32 devices in a mesh: cells: 4 (over y, x), genes: 8 (over z, core).
Axes of the slice: x: 2, y: 2, z: 4, core: 2. Of those that a mesh axis runs over, the one named last changes fastest.
Arguments:
- counts: bfloat16 [32768, 2560], P('cells', 'genes'), may hold values from 0 to 8, as said below
- library: float32 [32768], P('cells'), may hold values from 7 to 10
- noise: float32 [32768, 10], P('cells'), may hold values from -4 to 4
- batch_ids: int32 [32768], P('cells'), may hold values from 0 to 127
- gene_mask: int32 [2560], P('genes'), may hold values 0 or 1
- kl_weight: float32 [1], replicated, may hold values from 0.5 to 1
- enc_w: float32 [2560, 128], P('genes'), may hold values from -0.125 to 0.125
- enc_m: float32 [2560, 128], P('genes'), may hold values from -6.1035156e-05 to 6.1035156e-05
- enc_v: float32 [2560, 128], P('genes'), may hold values from 1.0172526e-11 to 4.0690104e-11
- dec_w: float32 [2, 128, 2560], P(None, None, 'genes'), may hold values from -0.5 to 0.5
- dec_m: float32 [2, 128, 2560], P(None, None, 'genes'), may hold values from -6.1035156e-05 to 6.1035156e-05
- dec_v: float32 [2, 128, 2560], P(None, None, 'genes'), may hold values from 1.0172526e-11 to 4.0690104e-11
- gene_par: float32 [3, 2560], P(None, 'genes'), may hold values from -3 to 3
- gene_m: float32 [3, 2560], P(None, 'genes'), may hold values from -0.00024414062 to 0.00024414062
- gene_v: float32 [3, 2560], P(None, 'genes'), may hold values from 1.6276042e-10 to 6.5104167e-10
- small_w: float32 [266, 128], replicated, may hold values from -3 to 3
- small_m: float32 [266, 128], replicated, may hold values from -3.0517578e-05 to 3.0517578e-05
- small_v: float32 [266, 128], replicated, may hold values from 3.0517578e-12 to 1.2207031e-11
- head_w: float32 [129, 20], replicated, may hold values from -0.5 to 0.5
- head_m: float32 [129, 20], replicated, may hold values from -0.00024414062 to 0.00024414062
- head_v: float32 [129, 20], replicated, may hold values from 1.6276042e-10 to 6.5104167e-10
- norm_par: float32 [4, 128], replicated, may hold values from 0.5 to 1.5
- norm_m: float32 [4, 128], replicated, may hold values from -0.00024414062 to 0.00024414062
- norm_v: float32 [4, 128], replicated, may hold values from 1.6276042e-10 to 6.5104167e-10
Outputs:
- enc_new: float32 [2560, 128], P('genes')
- enc_m_new: float32 [2560, 128], P('genes')
- enc_v_new: float32 [2560, 128], P('genes')
- enc_low: bfloat16 [2560, 128], P('genes')
- dec_new: float32 [2, 128, 2560], P(None, None, 'genes')
- dec_m_new: float32 [2, 128, 2560], P(None, None, 'genes')
- dec_v_new: float32 [2, 128, 2560], P(None, None, 'genes')
- dec_low: bfloat16 [2, 128, 2560], P(None, None, 'genes')
- gene_new: float32 [3, 2560], P(None, 'genes')
- gene_m_new: float32 [3, 2560], P(None, 'genes')
- gene_v_new: float32 [3, 2560], P(None, 'genes')
- small_new: float32 [266, 128], replicated
- small_m_new: float32 [266, 128], replicated
- small_v_new: float32 [266, 128], replicated
- head_new: float32 [129, 20], replicated
- head_m_new: float32 [129, 20], replicated
- head_v_new: float32 [129, 20], replicated
- norm_new: float32 [4, 128], replicated
- norm_m_new: float32 [4, 128], replicated
- norm_v_new: float32 [4, 128], replicated
- grad_norm: float32 [], replicated
- loss: float32 [32768], P(('cells', 'genes'))
The draws below stay inside these ranges and needn't reach their ends.
Inputs may be any that keep to these rules, and one draw needn't show every extreme that they name: `counts`: whole numbers.
All inputs are finite; a program needn't handle non-finite values. No bound on the sum of `gene_mask` on one device may be relied on, other than what follows from the above.
Results may differ from the reference program's by a relative error of at most 0.0047.
Values may be sent and summed in bfloat16 or wider, within the bound.
No kernel may reach another device: no remote copies, remote signals or barrier semaphores. Data moves between devices by JAX's collectives and lax.ppermute only.
A program may use at most 192 MiB of HBM per device.

```python
import math
import jax
import jax.numpy as jnp
from jax import lax

G = 2560
H = 128
L = 10
B = 128
CELLS_DEV = 8192
CELLS = 32768
N_CELLS = 4


def draw_counts(key, part):
    key_level, key_value = jax.random.split(jax.random.fold_in(key, 11))
    cell_level = jax.random.randint(key_level, (CELLS, 1), 3, 12)
    uniform_int = jax.random.randint(key_value, (CELLS, G), 0, 1000)
    count_value = jnp.maximum(uniform_int * cell_level // 1000 - 2, 0)
    return count_value.astype(jnp.float32).astype(jnp.bfloat16)


def plant(result, stream_key, smallest, high):
    longest = result.shape.index(max(result.shape))
    spots = []
    for shift in (0, 1):
        where = [jax.random.randint(jax.random.fold_in(stream_key, axis), (), 0, length) for axis, length in enumerate(result.shape)]
        where[longest] = (where[longest] + shift) % result.shape[longest]
        spots.append(tuple(where))
    return result.at[spots[0]].set(smallest).at[spots[1]].set(high)


def steps_of(rng, shape, cuts, smallest, high):
    def one(position, shards_of):
        draws = jax.random.uniform(jax.random.fold_in(jax.random.fold_in(rng, 6), position), (shards_of,), jnp.float32, smallest / len(cuts), high / len(cuts))
        return jnp.repeat(jnp.exp(draws), shape[position] // shards_of).reshape((-1,) + (1,) * (len(shape) - position - 1))

    factor_of = one(*cuts[0])
    for cut in cuts[1:]:
        factor_of = factor_of * one(*cut)
    return factor_of


def gaussian(rng, shape, deviation, reach, shards=(), held_as=jnp.bfloat16):
    values = jax.random.normal(rng, shape, jnp.float32) * deviation
    if len(shards) > 0:
        values = steps_of(rng, shape, shards, -0.22, 0.18) * values
    return jnp.clip(values, min=-reach, max=reach).astype(held_as)


def setup_inputs(seed: int = 0) -> dict:
    key_of = jax.random.split(jax.random.key(seed), 25)
    return {
        "counts": draw_counts(jax.random.fold_in(key_of[24], 71), 0),
        "library": jnp.clip(7.0 + 3.0 * jax.random.uniform(key_of[1], (CELLS,), jnp.float32) ** steps_of(key_of[1], (CELLS,), ((0, 4),), -0.2, 0.2), 7.0, 10.0),
        "noise": gaussian(key_of[2], (CELLS, L), 1.0, 4.0, ((0, 4),), jnp.float32),
        "batch_ids": plant(jax.random.randint(key_of[3], (CELLS,), 0, B), jax.random.fold_in(key_of[3], 1), 0, B - 1).astype(jnp.int32),
        "gene_mask": plant((jax.random.randint(key_of[4], (G,), 0, 16) < 15).astype(jnp.int32), jax.random.fold_in(key_of[4], 1), 0, 1),
        "kl_weight": jnp.clip(jax.random.uniform(key_of[5], (1,), jnp.float32, 0.5, 1.0), 0.5, 1.0),
        "enc_w": gaussian(key_of[6], (G, H), G ** -0.5, 0.125, ((0, 8),), jnp.float32),
        "enc_m": gaussian(key_of[7], (G, H), (0.011 / (3 * G * H) ** 0.5), 6.103515625e-05, ((0, 8),), jnp.float32),
        "enc_v": jnp.clip(jnp.exp(math.log(4.069010406393403e-11) - 1.3862944 * jax.random.uniform(key_of[8], (G, H), jnp.float32) ** steps_of(key_of[8], (G, H), ((0, 8),), -0.2, 0.2)), 1.0172526015983507e-11, 4.069010406393403e-11),
        "dec_w": gaussian(key_of[9], (2, H, G), H ** -0.5, 0.5, ((2, 8),), jnp.float32),
        "dec_m": gaussian(key_of[10], (2, H, G), (0.011 / (3 * G * H) ** 0.5), 6.103515625e-05, ((2, 8),), jnp.float32),
        "dec_v": jnp.clip(jnp.exp(math.log(4.069010406393403e-11) - 1.3862944 * jax.random.uniform(key_of[11], (2, H, G), jnp.float32) ** steps_of(key_of[11], (2, H, G), ((2, 8),), -0.2, 0.2)), 1.0172526015983507e-11, 4.069010406393403e-11),
        "gene_par": gaussian(key_of[12], (3, G), 1.0, 3.0, ((1, 8),), jnp.float32),
        "gene_m": gaussian(key_of[13], (3, G), (0.044 / (3 * G * H) ** 0.5), 0.00024414062, ((1, 8),), jnp.float32),
        "gene_v": jnp.clip(jnp.exp(math.log(6.510416650229445e-10) - 1.3862944 * jax.random.uniform(key_of[14], (3, G), jnp.float32) ** steps_of(key_of[14], (3, G), ((1, 8),), -0.2, 0.2)), 1.6276041625573612e-10, 6.510416650229445e-10),
        "small_w": gaussian(key_of[15], (2 * B + L, H), 0.5, 3.0, (), jnp.float32),
        "small_m": gaussian(key_of[16], (2 * B + L, H), (0.005 / (3 * G * H) ** 0.5), 3.0517578125e-05, (), jnp.float32),
        "small_v": jnp.clip(jnp.exp(jax.random.uniform(key_of[17], (2 * B + L, H), jnp.float32, math.log(3.051757848163139e-12), math.log(1.2207031392652556e-11))), 3.051757848163139e-12, 1.2207031392652556e-11),
        "head_w": gaussian(key_of[18], (H + 1, 2 * L), H ** -0.5, 0.5, (), jnp.float32),
        "head_m": gaussian(key_of[19], (H + 1, 2 * L), (0.044 / (3 * G * H) ** 0.5), 0.00024414062, (), jnp.float32),
        "head_v": jnp.clip(jnp.exp(jax.random.uniform(key_of[20], (H + 1, 2 * L), jnp.float32, math.log(1.6276041625573612e-10), math.log(6.510416650229445e-10))), 1.6276041625573612e-10, 6.510416650229445e-10),
        "norm_par": jnp.clip(jax.random.uniform(key_of[21], (4, H), jnp.float32, 0.5, 1.5), 0.5, 1.5),
        "norm_m": gaussian(key_of[22], (4, H), (0.044 / (3 * G * H) ** 0.5), 0.00024414062, (), jnp.float32),
        "norm_v": jnp.clip(jnp.exp(jax.random.uniform(key_of[23], (4, H), jnp.float32, math.log(1.6276041625573612e-10), math.log(6.510416650229445e-10))), 1.6276041625573612e-10, 6.510416650229445e-10),
    }


@jax.custom_vjp
def low(v):
    return lax.optimization_barrier(v.astype(jnp.bfloat16)).astype(jnp.float32)

@jax.custom_vjp
def low_back(v):
    return v

def low_keep(v):
    return (low(v), None)

def low_pass(kept, grad):
    return (grad,)

def back_keep(v):
    return (v, None)

def back_low(kept, grad):
    return (low(grad),)
low.defvjp(low_keep, low_pass)
low_back.defvjp(back_keep, back_low)
norm_epsilon = 0.001
zinb_epsilon = 1e-08
beta_one = 0.9
beta_two = 0.999
step_number = 5.0
decay_rate = 0.01
rate_genes = 0.03
rate_small = 0.2
max_norm = 0.1

def exact_dot(left, right):
    return jnp.dot(left, right, precision=lax.Precision.HIGHEST, preferred_element_type=jnp.float32)

def zinb_loglik(observed, log_mean, drop_logit, log_disp):
    dispersion = jnp.exp(log_disp)
    mean_rate = jnp.exp(log_mean)
    soft_drop = jax.nn.softplus(-drop_logit)
    log_disp_eps = jnp.log(dispersion + zinb_epsilon)
    log_both = jnp.log(dispersion + mean_rate + zinb_epsilon)
    drop_term = -drop_logit + dispersion * (log_disp_eps - log_both)
    case_zero = jax.nn.softplus(drop_term) - soft_drop
    case_other = -soft_drop + drop_term + observed * (jnp.log(mean_rate + zinb_epsilon) - log_both) + lax.lgamma(observed + dispersion) - lax.lgamma(dispersion) - lax.lgamma(observed + 1.0)
    return jnp.where(observed < zinb_epsilon, case_zero, case_other)

def batch_norm(pre_act, gain_row, shift_row):
    stat_mean = lax.optimization_barrier(jnp.mean(pre_act, axis=0))
    stat_var = lax.optimization_barrier(jnp.mean(jnp.square(pre_act - stat_mean), axis=0))
    return jax.nn.relu(gain_row * (pre_act - stat_mean) * lax.rsqrt(stat_var + norm_epsilon) + shift_row)

def adamw(weight, gradient, moment_one, moment_two, step_rate):
    moment_one = beta_one * moment_one + (1.0 - beta_one) * gradient
    moment_two = beta_two * moment_two + (1.0 - beta_two) * gradient * gradient
    fixed_one = moment_one / (1.0 - beta_one ** step_number)
    fixed_two = moment_two / (1.0 - beta_two ** step_number)
    update = fixed_one / (jnp.sqrt(fixed_two) + 1e-08) + decay_rate * weight
    return (weight - step_rate * update, moment_one, moment_two)

def reference(counts, library, noise, batch_ids, gene_mask, kl_weight, enc_w, enc_m, enc_v, dec_w, dec_m, dec_v, gene_par, gene_m, gene_v, small_w, small_m, small_v, head_w, head_m, head_v, norm_par, norm_m, norm_v):
    observed = counts.astype(jnp.float32)
    log_counts = jnp.log1p(observed)
    batch_table = (batch_ids[:, None] == jnp.arange(B, dtype=jnp.int32)[None, :]).astype(jnp.float32)
    gene_keep = gene_mask > 0

    def loss_of(enc_weight, dec_weight, gene_param, small_weight, head_weight, norm_param):
        pre_enc = low_back(exact_dot(low(log_counts), low(enc_weight))) + exact_dot(batch_table, small_weight[:B])
        hidden_enc = batch_norm(pre_enc, norm_param[0], norm_param[1])
        head_out = exact_dot(hidden_enc, head_weight[:H]) + head_weight[H]
        latent_mean = head_out[:, :L]
        latent_logvar = head_out[:, L:]
        latent_var = jnp.exp(latent_logvar) + 0.0001
        latent_draw = latent_mean + jnp.sqrt(latent_var) * noise
        pre_dec = exact_dot(latent_draw, small_weight[2 * B:]) + exact_dot(batch_table, small_weight[B:2 * B])
        hidden_dec = low(batch_norm(pre_dec, norm_param[2], norm_param[3]))
        scale_weight = low(dec_weight[0])
        drop_weight = low(dec_weight[1])

        def block_loss(block_args):
            rows_hidden, rows_counts, rows_library = block_args
            score = low_back(exact_dot(rows_hidden, scale_weight)) + gene_param[0]
            drop_logit = low_back(exact_dot(rows_hidden, drop_weight)) + gene_param[1]
            log_total = jax.nn.logsumexp(jnp.where(gene_keep, score, -1e+30), axis=1)
            log_mean = rows_library[:, None] + score - log_total[:, None]
            terms = zinb_loglik(rows_counts, log_mean, drop_logit, gene_param[2])
            return lax.optimization_barrier(jnp.sum(jnp.where(gene_keep, terms, 0.0), axis=1))
        block_sums = lax.map(jax.checkpoint(block_loss), (hidden_dec.reshape(N_CELLS, CELLS_DEV, H), observed.reshape(N_CELLS, CELLS_DEV, G), library.reshape(N_CELLS, CELLS_DEV)))
        recon_cells = block_sums.reshape(CELLS)
        diverge_cells = 0.5 * lax.optimization_barrier(jnp.sum(latent_var + latent_mean * latent_mean - 1.0 - jnp.log(latent_var), axis=1))
        cell_loss = kl_weight[0] * diverge_cells - recon_cells
        return (jnp.sum(cell_loss) / CELLS, cell_loss)
    weights = (enc_w, dec_w, gene_par, small_w, head_w, norm_par)
    objective, pullback, cell_loss = jax.vjp(loss_of, *weights, has_aux=True)
    grads = pullback(jnp.ones_like(objective))
    squares = sum((jnp.sum(gradient * gradient) for gradient in grads))
    norm_value = jnp.sqrt(squares)
    factor = jnp.minimum(1.0, max_norm / norm_value)
    firsts = (enc_m, dec_m, gene_m, small_m, head_m, norm_m)
    seconds = (enc_v, dec_v, gene_v, small_v, head_v, norm_v)
    rates = (rate_genes, rate_genes, rate_small, rate_small, rate_small, rate_small)
    results = [adamw(weights[index], grads[index] * factor, firsts[index], seconds[index], rates[index]) for index in range(6)]
    enc_res, dec_res, gene_res, small_res, head_res, norm_res = results
    return (enc_res[0], enc_res[1], enc_res[2], enc_res[0].astype(jnp.bfloat16), dec_res[0], dec_res[1], dec_res[2], dec_res[0].astype(jnp.bfloat16), gene_res[0], gene_res[1], gene_res[2], small_res[0], small_res[1], small_res[2], head_res[0], head_res[1], head_res[2], norm_res[0], norm_res[1], norm_res[2], norm_value, cell_loss)
```

```python
import jax
import jax.numpy as jnp
from jax import lax
from jax.experimental import pallas as pl
from jax.experimental.pallas import tpu as pltpu
from jax.sharding import PartitionSpec as P

norm_epsilon = 0.001
zinb_epsilon = 1e-08
beta_one = 0.9
beta_two = 0.999
step_number = 5.0
decay_rate = 0.01
rate_genes = 0.03
rate_small = 0.2
max_norm = 0.1

F32 = jnp.float32
BF = jnp.bfloat16
HI = lax.Precision.HIGHEST
VMEM_LIMIT = 56 * 1024 * 1024
COUNT_TOP = 8


def nn(left, right, precision=None):
    return lax.dot_general(
        left, right, (((1,), (0,)), ((), ())), precision=precision, preferred_element_type=F32
    )


def nt(left, right, precision=None):
    return lax.dot_general(
        left, right, (((1,), (1,)), ((), ())), precision=precision, preferred_element_type=F32
    )


def params():
    return pltpu.CompilerParams(vmem_limit_bytes=VMEM_LIMIT)


def whole(shape):
    return pl.BlockSpec(shape, lambda *_: (0,) * len(shape))


def call(kernel, grid, ins, outs, scratch=(), scalars=0, flops=0, moved=0):
    return pl.pallas_call(
        kernel,
        out_shape=[jax.ShapeDtypeStruct(shape, dtype) for shape, dtype, _ in outs],
        grid_spec=pltpu.PrefetchScalarGridSpec(
            num_scalar_prefetch=scalars,
            grid=grid,
            in_specs=[spec for _, spec in ins[scalars:]],
            out_specs=[spec for _, _, spec in outs],
            scratch_shapes=list(scratch),
        ),
        compiler_params=params(),
        cost_estimate=pl.CostEstimate(flops=flops, bytes_accessed=moved, transcendentals=0),
    )(*[array for array, _ in ins])


def swap(value, axis, bit):
    count = lax.axis_size(axis)
    return lax.ppermute(value, axis, [(i, i ^ bit) for i in range(count)])


def bit_groups(axis):
    count = lax.axis_size(axis)
    if axis == "genes":
        groups, bit = [[1]], 2
    else:
        groups, bit = [], 1
    while bit < count:
        groups.append([bit, 2 * bit] if 2 * bit < count else [bit])
        bit *= 4
    return groups


def total(value, axis):
    for group in bit_groups(axis):
        if len(group) == 1:
            value = value + swap(value, axis, group[0])
        else:
            low, high = group
            value = (value + swap(value, axis, low)) + (
                swap(value, axis, high) + swap(value, axis, low ^ high)
            )
    return value


def log_total_of(value, axis):
    for group in bit_groups(axis):
        if len(group) == 1:
            parts = [value, swap(value, axis, group[0])]
        else:
            low, high = group
            parts = [value] + [swap(value, axis, k) for k in (low, high, low ^ high)]
        top = parts[0]
        for part in parts[1:]:
            top = jnp.maximum(top, part)
        mass = sum(jnp.exp(part - top) for part in parts)
        value = top + jnp.log(mass)
    return value


def three(value):
    high = value.astype(BF)
    rest = value - high.astype(F32)
    mid = rest.astype(BF)
    low = (rest - mid.astype(F32)).astype(BF)
    return high, mid, low


def one_hot(batch_row, kinds):
    ids = lax.broadcasted_iota(jnp.int32, (kinds, batch_row.shape[1]), 0)
    return jnp.where(ids == batch_row, 1.0, 0.0)


def prep_kernel(enc_b_ref, dec_b_ref, lat_ref, enc_out, dec_out):
    hidden, kinds = enc_b_ref.shape
    for index, piece in enumerate(three(enc_b_ref[...])):
        enc_out[index * hidden : (index + 1) * hidden, :] = piece
    batch_pieces = three(dec_b_ref[...])
    lat = three(lat_ref[...])
    zero = jnp.zeros_like(lat[0])
    tails = ((lat[0], lat[0], lat[0]), (lat[1], lat[1], zero), (lat[2], zero, zero))
    for index in range(3):
        rows = slice(index * hidden, (index + 1) * hidden)
        dec_out[rows, :] = jnp.concatenate((batch_pieces[index],) + tails[index], axis=1)


def exact_rows(stacked, table):
    out = nn(stacked, table)
    hidden = out.shape[0] // 3
    return out[:hidden] + out[hidden : 2 * hidden] + out[2 * hidden :]


def dec_table(z, batch_row, kinds):
    high, mid, low = three(z)
    return jnp.concatenate((one_hot(batch_row, kinds).astype(BF), high, mid, low), axis=0)


def row_sums(value):
    return nt(jnp.ones((8, value.shape[1]), F32), value, HI)


def stat_rows(first, second, at):
    sums, squares = row_sums(first), row_sums(second)
    row = lax.broadcasted_iota(jnp.int32, sums.shape, 0)
    return jnp.where(row == at, sums, jnp.where(row == at + 1, squares, 0.0))


def enc_kernel(me_ref, x_ref, w_ref, keep_ref, send_ref):
    log_counts = jnp.log(1.0 + x_ref[...].astype(F32)).astype(BF)
    part = nn(w_ref[...], log_counts)
    odd = lax.rem(pl.program_id(0), 2)

    @pl.when(odd == 0)
    def _():
        keep_ref[0] = part

    @pl.when(odd == 1)
    def _():
        send_ref[0] = part.astype(BF)


def counts_kernel(rows, x_ref, lg_ref, dg_ref, logc_ref, cell_ref, disp_ref):
    step = pl.program_id(0)
    genes, width = x_ref.shape

    @pl.when(step == 0)
    def _():
        disp_ref[...] = jnp.zeros_like(disp_ref)

    def chunk(g, cell):
        at = pl.ds(pl.multiple_of(g * rows, rows), rows)
        digamma = disp_ref[at, :]
        out = []
        for tile in range(width // 128):
            lanes = slice(tile * 128, (tile + 1) * 128)
            x = x_ref[at, lanes].astype(F32)
            logc_ref[at, lanes] = jnp.log(1.0 + x).astype(BF)
            gam = jnp.zeros_like(x)
            dig = jnp.zeros_like(x)
            for k in range(COUNT_TOP):
                more = x > (k + 0.5)
                gam = jnp.where(more, lg_ref[k, at, :], gam)
                dig = jnp.where(more, dg_ref[k, at, :], dig)
            digamma = digamma + dig
            folded = gam[:8]
            for part in range(1, rows // 8):
                folded = folded + gam[part * 8 : (part + 1) * 8]
            out.append(cell[tile] + folded)
        disp_ref[at, :] = digamma
        return tuple(out)

    zero = tuple(jnp.zeros((8, 128), F32) for _ in range(width // 128))
    cell = lax.fori_loop(0, genes // rows, chunk, zero)
    cell_ref[pl.ds(step, 1), :] = jnp.sum(jnp.concatenate(cell, axis=1), axis=0, keepdims=True)


def own_kernel(me_ref, keep_ref, got_ref, one_ref, two_ref, six_ref, batch_ref, enc_b_ref, pre_ref, stat_ref):
    kinds = enc_b_ref.shape[1]
    gathered = (keep_ref[0] + got_ref[0].astype(F32) + one_ref[0].astype(F32)) + (
        two_ref[0].astype(F32) + six_ref[0].astype(F32)
    )
    table = one_hot(batch_ref[0], kinds).astype(BF)
    pre = gathered + exact_rows(enc_b_ref[...], table)
    pre_ref[...] = pre
    stat_ref[...] = stat_rows(pre, pre * pre, 0)


def norm_columns(stat, first, cells):
    turned = jnp.transpose(stat)
    mean = turned[:, first : first + 1] / cells
    var = turned[:, first + 1 : first + 2] / cells - mean * mean
    return mean, lax.rsqrt(var + norm_epsilon)


def norm_rows(stat, first, cells):
    mean = stat[first : first + 1] / cells
    var = stat[first + 1 : first + 2] / cells - mean * mean
    return mean, lax.rsqrt(var + norm_epsilon)


def latent_kernel(cells, latent, me_ref, pre_ref, stat_ref, norm_ref, head_ref, bias_ref, noise_ref, batch_ref, dec_b_ref, kinds_ref, z_ref, head_out_ref, kl_ref):
    kinds = kinds_ref.shape[1]
    mean, inv = norm_columns(stat_ref[...], 0, cells)
    phat = (pre_ref[...] - mean) * inv
    hidden = jnp.maximum(norm_ref[:, 0:1] * phat + norm_ref[:, 1:2], 0.0)
    out = nn(head_ref[...], hidden, HI) + bias_ref[:, 0:1]
    head_out_ref[...] = out
    lat_mean, lat_logvar = out[:16], out[16:]
    var = jnp.exp(lat_logvar) + 0.0001
    z = lat_mean + jnp.sqrt(var) * noise_ref[...]
    row = lax.broadcasted_iota(jnp.int32, z.shape, 0)
    terms = jnp.where(row < latent, var + lat_mean * lat_mean - 1.0 - jnp.log(var), 0.0)
    kl_ref[...] = 0.5 * jnp.sum(terms, axis=0, keepdims=True)
    pre_dec = exact_rows(dec_b_ref[...], dec_table(z, batch_ref[0], kinds))
    hidden_rows = pre_dec.shape[0]
    z_ref[...] = z
    stat = stat_rows(pre_dec, pre_dec * pre_dec, 0)
    z_ref[latent : latent + 1, 0:hidden_rows] = stat[0:1]
    z_ref[latent + 1 : latent + 2, 0:hidden_rows] = stat[1:2]


def decode_kernel(cells, latent, me_ref, z_ref, batch_ref, stat_ref, norm_ref, dec_b_ref, kinds_ref, w_ref, bias_ref, hid_ref, phat_ref, lse_ref, score_ref):
    kinds = kinds_ref.shape[1]
    step = pl.program_id(0)
    genes = w_ref.shape[0]
    mean, inv = norm_columns(stat_ref[...], latent - 8, cells)
    z = z_ref[0]
    row = lax.broadcasted_iota(jnp.int32, z.shape, 0)
    z = jnp.where(row < latent, z, 0.0)
    pre_dec = exact_rows(dec_b_ref[...], dec_table(z, batch_ref[0], kinds))
    phat = (pre_dec - mean) * inv
    phat_ref[...] = phat
    hidden = jnp.maximum(norm_ref[:, 2:3] * phat + norm_ref[:, 3:4], 0.0).astype(BF)
    hid_ref[...] = hidden
    score_ref[...] = nn(w_ref[...], hidden)
    width = score_ref.shape[1]
    tiles = width // 128

    def top(g, best):
        at = pl.ds(pl.multiple_of(g * 8, 8), 8)
        bias = bias_ref[at, :]
        new = []
        for tile in range(tiles):
            lanes = slice(tile * 128, (tile + 1) * 128)
            value = score_ref[at, lanes] + bias
            score_ref[at, lanes] = value
            new.append(jnp.maximum(best[tile], value))
        return tuple(new)

    best = lax.fori_loop(0, genes // 8, top, tuple(jnp.full((8, 128), -3e38, F32) for _ in range(tiles)))
    high = [jnp.max(part, axis=0, keepdims=True) for part in best]
    wide = [jnp.broadcast_to(part, (8, 128)) for part in high]

    def mass(g, sums):
        at = pl.ds(pl.multiple_of(g * 8, 8), 8)
        return tuple(
            sums[tile] + jnp.exp(score_ref[at, slice(tile * 128, (tile + 1) * 128)] - wide[tile])
            for tile in range(tiles)
        )

    sums = lax.fori_loop(0, genes // 8, mass, tuple(jnp.zeros((8, 128), F32) for _ in range(tiles)))
    lse = [high[tile] + jnp.log(jnp.sum(sums[tile], axis=0, keepdims=True)) for tile in range(tiles)]
    lse_ref[pl.ds(step, 1), :] = jnp.concatenate(lse, axis=1)


def zinb_kernel(rows, span, hid_ref, w_ref, x_ref, keep_ref, par_ref, lib_ref, lse_ref, gam_ref, gm_ref, gd_ref, rt_ref, mass_ref, recon_ref, acc_ref, sc_ref):
    step = pl.program_id(0)
    genes, width = x_ref.shape

    @pl.when(step == 0)
    def _():
        acc_ref[...] = jnp.zeros_like(acc_ref)

    sc_ref[...] = nn(w_ref[...], hid_ref[...])
    tiles = span // 128

    one_row = pl.ds(step, 1)
    lib_row, lse_row, gam_row = lib_ref[one_row, :], lse_ref[one_row, :], gam_ref[one_row, :]
    mass_out, recon_out = [], []
    for first in range(0, width, span):
        lanes = [slice(first + tile * 128, first + (tile + 1) * 128) for tile in range(tiles)]
        shift, ratio_of = [], []
        for tile in range(tiles):
            lib = lib_row[:, lanes[tile]]
            shift.append(jnp.broadcast_to(lib - lse_row[:, lanes[tile]], (rows, 128)))
            ratio_of.append(jnp.broadcast_to(jnp.exp(-lib), (rows, 128)))

        def chunk(g, state):
            at = pl.ds(pl.multiple_of(g * rows, rows), rows)
            at_drop = pl.ds(pl.multiple_of(genes + g * rows, rows), rows)
            bias_s, bias_d, the, th, log_the, part_th = (par_ref[i, at, :] for i in range(6))
            keep = keep_ref[at, :]
            sum_s, sum_d, sum_t = acc_ref[0, at, :], acc_ref[1, at, :], acc_ref[2, at, :]
            new = []
            for tile in range(tiles):
                rec, prod, back = state[tile]
                x = (x_ref[at, lanes[tile]] * keep).astype(F32)
                log_mean = (sc_ref[at, lanes[tile]] + bias_s) + shift[tile]
                drop = sc_ref[at_drop, lanes[tile]] + bias_d
                mu = jnp.exp(log_mean)
                both = mu + the
                r = 1.0 / both
                log_gap = log_the - jnp.log(both)
                log_both = log_the - log_gap
                u = th * log_gap - drop
                eu = jnp.exp(-jnp.abs(u))
                ed = jnp.exp(-jnp.abs(drop))
                is_zero = x < 0.5
                mu_eps = mu + zinb_epsilon
                den = jnp.where(is_zero, 1.0 + eu, mu_eps)
                q = 1.0 / den
                rd = 1.0 / (1.0 + ed)
                w0 = jnp.where(is_zero, jnp.where(u >= 0.0, 1.0, eu) * q, 1.0)
                rec_term = (
                    jnp.where(is_zero, jnp.maximum(u, 0.0), u)
                    + x * (jnp.log(mu_eps) - log_both)
                    + jnp.minimum(drop, 0.0)
                )
                factor = jnp.where(is_zero, den, 1.0) * rd
                y = (x + w0 * th) * r
                g_mean = mu * (x * q - y)
                g_drop = jnp.where(drop >= 0.0, ed, 1.0) * rd - w0
                g_disp = w0 * (log_gap + part_th) - y
                gm_ref[at, lanes[tile]] = g_mean.astype(BF)
                gd_ref[at, lanes[tile]] = g_drop.astype(BF)
                rt_ref[at, lanes[tile]] = (mu * ratio_of[tile]).astype(BF)
                sum_s = sum_s + g_mean
                sum_d = sum_d + g_drop
                sum_t = sum_t + g_disp
                for part in range(rows // 8):
                    sub = slice(part * 8, (part + 1) * 8)
                    rec = rec + rec_term[sub]
                    prod = prod * factor[sub]
                    back = back + g_mean[sub]
                new.append((rec, prod, back))
            acc_ref[0, at, :] = sum_s
            acc_ref[1, at, :] = sum_d
            acc_ref[2, at, :] = sum_t
            return tuple(new)

        zero = jnp.zeros((8, 128), F32)
        state = tuple((zero, zero + 1.0, zero) for _ in range(tiles))
        state = lax.fori_loop(0, genes // rows, chunk, state)
        for tile in range(tiles):
            rec, prod, back = state[tile]
            mass_out.append(jnp.sum(back, axis=0, keepdims=True))
            recon_out.append(jnp.sum(rec + jnp.log(prod), axis=0, keepdims=True))
    mass_ref[one_row, :] = jnp.concatenate(mass_out, axis=1)
    recon_ref[one_row, :] = jnp.concatenate(recon_out, axis=1) + gam_row


def back_kernel(gm_ref, gd_ref, rt_ref, hid_ref, w_ref, a_ref, r_ref, g_ref):
    genes = gm_ref.shape[0]

    @pl.when(pl.program_id(0) == 0)
    def _():
        g_ref[...] = jnp.zeros_like(g_ref)

    gm, gd, rt, hid = gm_ref[...], gd_ref[...], rt_ref[...], hid_ref[...]
    scale_w = w_ref[:, :genes]
    a_ref[...] = nn(scale_w, gm) + nn(w_ref[:, genes:], gd)
    r_ref[...] = nn(scale_w, rt)
    g_ref[:genes, :] += nt(gm, hid)
    g_ref[genes:, :] += nt(gd, hid)


def hidden_grad_kernel(cells, latent, me_ref, a_ref, r_ref, mass_ref, hid_ref, phat_ref, stat_ref, gain_ref, lat_ref, recon_ref, dy_ref, keep_ref, send_ref, sum_ref):
    step = pl.program_id(0)
    steps = pl.num_programs(0)
    place = step ^ me_ref[0]

    @pl.when(step == 0)
    def _():
        sum_ref[...] = jnp.zeros_like(sum_ref)

    back = mass_ref[pl.ds(step, 1), :]
    dy = jnp.where(hid_ref[...] > 0, (a_ref[...] - back * r_ref[...]) * (-1.0 / cells), 0.0)
    dy_ref[...] = dy
    hidden, width = dy.shape
    weighted = dy * phat_ref[...]
    first, second = dy[:, :128], weighted[:, :128]
    for tile in range(1, width // 128):
        lanes = slice(tile * 128, (tile + 1) * 128)
        first = first + dy[:, lanes]
        second = second + weighted[:, lanes]
    sum_ref[0] += first
    sum_ref[1] += second
    _, inv = norm_rows(stat_ref[...], latent - 8, cells)
    lat = lat_ref[...] * (gain_ref[2:3] * inv)
    lat_high, lat_mid, _ = three(lat)
    dy_high, dy_mid, _ = three(dy)
    table = jnp.concatenate((dy_high, dy_mid), axis=0)
    left = jnp.concatenate(
        (
            jnp.concatenate((lat_high, lat_high), axis=1),
            jnp.concatenate((lat_mid, jnp.zeros_like(lat_mid)), axis=1),
        ),
        axis=0,
    )
    both = nn(left, table)
    block = both[:16] + both[16:]
    row = lax.broadcasted_iota(jnp.int32, block.shape, 0)
    block = jnp.where(row == latent, recon_ref[pl.ds(step, 1), :], block)
    slot = lax.div(place, 2)

    @pl.when(lax.rem(place, 2) == 0)
    def _():
        keep_ref[slot] = block

    @pl.when(lax.rem(place, 2) == 1)
    def _():
        send_ref[slot] = block

    @pl.when(step == steps - 1)
    def _():
        one, two = row_sums(sum_ref[0]), row_sums(sum_ref[1])
        for ref in (keep_ref, send_ref):
            for index in range(ref.shape[0]):
                ref[index, latent + 1 : latent + 2, 0:hidden] = one[0:1]
                ref[index, latent + 2 : latent + 3, 0:hidden] = two[0:1]


def dec_grad_kernel(cells, latent, me_ref, rt_ref, hid_ref, mass_ref, dy_ref, z_ref, batch_ref, g_ref, acc_ref, dig_ref, th_ref, dec_ref, oh_ref, mix_ref):
    step = pl.program_id(0)
    steps = pl.num_programs(0)
    genes = rt_ref.shape[0]
    hidden = hid_ref.shape[0]
    kinds = oh_ref.shape[0] - 16

    @pl.when(step == 0)
    def _():
        mix_ref[...] = jnp.zeros_like(mix_ref)
        oh_ref[...] = jnp.zeros_like(oh_ref)

    back = mass_ref[pl.ds(step, 1), :]
    back_high, back_mid, back_low = three(back)
    row = lax.broadcasted_iota(jnp.int32, (16, back.shape[1]), 0)
    extra = jnp.where(row == 0, back_high.astype(F32), jnp.where(row == 1, back_mid.astype(F32), 0.0))
    scaled = (hid_ref[...].astype(F32) * back).astype(BF)
    mix_ref[...] += nt(rt_ref[...], jnp.concatenate((scaled, extra.astype(BF)), axis=0))
    z = z_ref[0]
    z = jnp.where(lax.broadcasted_iota(jnp.int32, z.shape, 0) < latent, z, 0.0)
    z_high, z_mid, _ = three(z)
    left = jnp.concatenate((one_hot(batch_ref[0], kinds).astype(BF), z_high, z_mid), axis=0)
    dy_high, dy_mid, _ = three(dy_ref[...])
    part = nt(left, dy_high) + nt(left, dy_mid)
    oh_ref[:kinds, :] += part[:kinds]
    oh_ref[kinds:, :] += part[kinds : kinds + 16] + part[kinds + 16 :]

    @pl.when(step == steps - 1)
    def _():
        scale = -1.0 / cells
        mix = mix_ref[...]
        dec_ref[:genes, :] = (g_ref[:genes, :] - mix[:, :hidden]) * scale
        dec_ref[genes : 2 * genes, :] = g_ref[genes:, :] * scale
        pick = jnp.where(lax.broadcasted_iota(jnp.int32, (8, 16), 1) < 2, 1.0, 0.0)
        score_row = row_sums(acc_ref[0]) - nt(pick, mix[:, hidden:], HI)
        drop_row = row_sums(acc_ref[1])
        disp_row = row_sums((acc_ref[2] + dig_ref[...]) * th_ref[...])
        line = lax.broadcasted_iota(jnp.int32, score_row.shape, 0)
        gene_rows = scale * jnp.where(
            line == 0, score_row, jnp.where(line == 1, drop_row, jnp.where(line == 2, disp_row, 0.0))
        )
        base = 2 * genes
        for index in range(pl.cdiv(genes, 128)):
            wide = min(128, genes - index * 128)
            piece = gene_rows[:, index * 128 : index * 128 + wide]
            if wide < 128:
                piece = jnp.concatenate((piece, jnp.zeros((8, 128 - wide), F32)), axis=1)
            dec_ref[base + index * 8 : base + (index + 1) * 8, :] = piece


def own_phat(pre, stat, first, cells):
    mean, inv = norm_columns(stat, first, cells)
    return (pre - mean) * inv


def head_grad_kernel(cells, latent, me_ref, d0_ref, d1_ref, d2_ref, d3_ref, d4_ref, sums_ref, phat_ref, stat_dec_ref, gain_ref, lat_ref, head_out_ref, noise_ref, kl_ref, klw_ref, pre_ref, stat_ref, norm_ref, head_ref, dy_ref, gh_ref, loss_ref, stat_out_ref):
    block = (d0_ref[0] + d1_ref[0] + d2_ref[0]) + (d3_ref[0] + d4_ref[0])
    loss_ref[...] = klw_ref[0:1, 0:1] * kl_ref[...] - block[latent : latent + 1]
    row = lax.broadcasted_iota(jnp.int32, block.shape, 0)
    _, inv = norm_rows(stat_dec_ref[...], latent - 8, cells)
    lat = lat_ref[...] * (gain_ref[2:3] * inv)
    at = latent + 1 - 8
    m_one = sums_ref[at : at + 1] * (1.0 / cells)
    m_two = sums_ref[at + 1 : at + 2] * (1.0 / cells)
    fixed = jnp.sum(lat * m_one, axis=1, keepdims=True)
    grad_z = block - fixed - nn(lat * m_two, phat_ref[...], HI)
    grad_z = jnp.where(row < latent, grad_z, 0.0)
    out = head_out_ref[...]
    lat_mean, lat_logvar = out[:16], out[16:]
    spread = jnp.exp(lat_logvar)
    var = spread + 0.0001
    std = jnp.sqrt(var)
    scale = klw_ref[0:1, 0:1] * (1.0 / cells)
    g_mean = grad_z + scale * lat_mean
    g_var = grad_z * noise_ref[...] * 0.5 * spread / std + scale * 0.5 * (spread - spread / var)
    g_var = jnp.where(row < latent, g_var, 0.0)
    g_head = jnp.concatenate((g_mean, g_var), axis=0)
    gh_ref[...] = g_head
    phat = own_phat(pre_ref[...], stat_ref[...], 0, cells)
    affine = norm_ref[:, 0:1] * phat + norm_ref[:, 1:2]
    dy = jnp.where(affine > 0, nn(head_ref[...], g_head, HI), 0.0)
    dy_ref[...] = dy
    stat_out_ref[...] = stat_rows(dy, dy * phat, 0)


def pre_grad_kernel(cells, dy_ref, pre_ref, stat_ref, norm_ref, sums_ref, out_ref, low_ref):
    mean, inv = norm_columns(stat_ref[...], 0, cells)
    phat = (pre_ref[...] - mean) * inv
    turned = jnp.transpose(sums_ref[...])
    grad = (norm_ref[:, 0:1] * inv) * (
        dy_ref[...] - turned[:, 0:1] * (1.0 / cells) - phat * (turned[:, 1:2] * (1.0 / cells))
    )
    out_ref[...] = grad
    low_ref[...] = grad.astype(BF)


def small_grad_kernel(cells, latent, me_ref, grad_ref, gh_ref, pre_ref, stat_ref, norm_ref, batch_ref, phat_ref, z_ref, oh_ref, sums_ref, stat_dec_ref, gain_ref, out_ref):
    kinds = oh_ref.shape[0] - 16
    table = one_hot(batch_ref[0], kinds)
    phat = own_phat(pre_ref[...], stat_ref[...], 0, cells)
    hidden = jnp.maximum(norm_ref[:, 0:1] * phat + norm_ref[:, 1:2], 0.0)
    out_ref[:kinds, :] = nt(table, grad_ref[...], HI)
    z = z_ref[...]
    z = jnp.where(lax.broadcasted_iota(jnp.int32, z.shape, 0) < latent, z, 0.0)
    left = jnp.concatenate((table, z), axis=0)
    _, inv = norm_rows(stat_dec_ref[...], latent - 8, cells)
    at = latent + 1 - 8
    m_one = sums_ref[at : at + 1] * (1.0 / cells)
    m_two = sums_ref[at + 1 : at + 2] * (1.0 / cells)
    held = jnp.sum(left, axis=1, keepdims=True)
    out_ref[kinds : 2 * kinds + 16, :] = (gain_ref[2:3] * inv) * (
        oh_ref[...] - held * m_one - nt(left, phat_ref[...], HI) * m_two
    )
    base = 2 * kinds + 16
    g_head = gh_ref[...]
    out_ref[base : base + 32, :] = nt(g_head, hidden, HI)
    out_ref[base + 32 : base + 64, :] = jnp.broadcast_to(
        jnp.sum(g_head, axis=1, keepdims=True), (32, out_ref.shape[1])
    )


def enc_grad_kernel(logc_ref, grad_ref, out_ref):
    @pl.when(pl.program_id(0) == 0)
    def _():
        out_ref[...] = jnp.zeros_like(out_ref)

    part = jnp.zeros(out_ref.shape, F32)
    share = grad_ref.shape[2]
    for index in range(grad_ref.shape[0]):
        part = part + nt(logc_ref[:, index * share : (index + 1) * share], grad_ref[index])
    out_ref[...] += part


def square_kernel(enc_ref, dec_ref, out_ref):
    enc, dec = enc_ref[...], dec_ref[...]
    whole_sum = jnp.sum(jnp.sum(enc * enc, axis=0, keepdims=True) + jnp.sum(dec * dec, axis=0, keepdims=True), axis=1, keepdims=True)
    out_ref[...] = jnp.broadcast_to(whole_sum, out_ref.shape)


def step_of(weight, gradient, first, second, rate):
    first = beta_one * first + (1.0 - beta_one) * gradient
    second = beta_two * second + (1.0 - beta_two) * gradient * gradient
    fixed_one = first * (1.0 / (1.0 - beta_one**step_number))
    fixed_two = second * (1.0 / (1.0 - beta_two**step_number))
    update = fixed_one / (jnp.sqrt(fixed_two) + 1e-08) + decay_rate * weight
    return weight - rate * update, first, second


def update_kernel(latent, square_ref, enc_g_ref, dec_g_ref, small_g_ref, enc_s_ref, dec_s_ref, *refs):
    ins, outs, scratch = refs[:18], refs[18:-1], refs[-1]
    enc, dec, gene, small, head, norm = (ins[3 * i : 3 * i + 3] for i in range(6))
    genes = enc[0].shape[0]
    hidden = enc[0].shape[1]
    kinds = (small[0].shape[0] - latent) // 2
    base = 2 * kinds + 16
    small_g = small_g_ref[...]
    at = latent + 1 - 8
    norm_g = (enc_s_ref[1:2], enc_s_ref[0:1], dec_s_ref[at + 1 : at + 2], dec_s_ref[at : at + 1])
    shared = small_g[: base + 32]
    tail = small_g[base + 32 : base + 64, 0:1]
    lanes = jnp.sum(shared * shared, axis=0, keepdims=True)
    for part in norm_g:
        lanes = lanes + part * part
    small_square = jnp.sum(lanes, axis=1, keepdims=True) + jnp.sum(tail * tail, axis=0, keepdims=True)
    value = jnp.sqrt(square_ref[0:1, 0:1] + small_square)
    factor = jnp.minimum(1.0, max_norm / value)
    (enc_n, enc_m, enc_v, enc_l, dec_n, dec_m, dec_v, dec_l, gene_n, gene_m, gene_v, small_n, small_m, small_v, head_n, head_m, head_v, norm_n, norm_m, norm_v, norm_out) = outs
    norm_out[...] = jnp.broadcast_to(value, norm_out.shape)
    new, first, second = step_of(enc[0][...], enc_g_ref[...] * factor, enc[1][...], enc[2][...], rate_genes)
    enc_n[...], enc_m[...], enc_v[...], enc_l[...] = new, first, second, new.astype(BF)
    for index in range(2):
        gradient = dec_g_ref[index * genes : (index + 1) * genes, :] * factor
        new, first, second = step_of(dec[0][index], gradient, dec[1][index], dec[2][index], rate_genes)
        dec_n[index], dec_m[index], dec_v[index], dec_l[index] = new, first, second, new.astype(BF)
    for index in range(pl.cdiv(genes, 128)):
        span = slice(index * 128, min(genes, (index + 1) * 128))
        gradient = dec_g_ref[2 * genes + index * 8 : 2 * genes + index * 8 + 3, 0 : span.stop - span.start] * factor
        new, first, second = step_of(gene[0][:, span], gradient, gene[1][:, span], gene[2][:, span], rate_small)
        gene_n[:, span], gene_m[:, span], gene_v[:, span] = new, first, second
    rows = 2 * kinds + latent
    new, first, second = step_of(small[0][...], small_g_ref[0:rows, :] * factor, small[1][...], small[2][...], rate_small)
    small_n[...], small_m[...], small_v[...] = new, first, second
    for half in range(2):
        take = slice(base + 16 * half, base + 16 * half + latent)
        take_bias = slice(base + 32 + 16 * half, base + 32 + 16 * half + latent)
        into = slice(half * latent, (half + 1) * latent)
        scratch[into, 0:hidden] = small_g_ref[take, :]
        scratch[into, hidden : 2 * hidden] = small_g_ref[take_bias, :]
    gradient = scratch[0 : 2 * latent, 0 : hidden + 1] * factor
    new, first, second = step_of(head[0][...], gradient, head[1][...], head[2][...], rate_small)
    head_n[...], head_m[...], head_v[...] = new, first, second
    for index in range(4):
        line = slice(index, index + 1)
        new, first, second = step_of(norm[0][line], norm_g[index] * factor, norm[1][line], norm[2][line], rate_small)
        norm_n[line], norm_m[line], norm_v[line] = new, first, second


def per_device(counts, library, noise, batch_ids, gene_mask, kl_weight, enc_w, enc_m, enc_v, dec_w, dec_m, dec_v, gene_par, gene_m, gene_v, small_w, small_m, small_v, head_w, head_m, head_v, norm_par, norm_m, norm_v):
    rows_all, genes = counts.shape
    cells = float(rows_all * lax.axis_size("cells"))
    groups = lax.axis_size("genes")
    hidden = enc_w.shape[1]
    latent = head_w.shape[1] // 2
    kinds = (small_w.shape[0] - latent) // 2
    share = rows_all // groups
    width = min(1024, rows_all)
    blocks = rows_all // width
    fast = groups == 8 and blocks == 8
    me = lax.axis_index("genes").astype(jnp.int32).reshape(1)
    chunk = 16

    x_t = counts.T
    enc_low = enc_w.T.astype(BF)
    dec_t = dec_w.transpose(0, 2, 1).astype(BF).reshape(2 * genes, hidden)
    dec_n = jnp.concatenate([dec_w[0], dec_w[1]], axis=1).astype(BF)
    keep = gene_mask > 0
    th_row = jnp.exp(gene_par[2])

    def tall(row):
        return jnp.broadcast_to(row[..., None], row.shape + (128,))

    the_row = th_row + zinb_epsilon
    par = tall(
        jnp.stack(
            [
                jnp.where(keep, gene_par[0], -1e30),
                jnp.where(keep, gene_par[1], 1e30),
                the_row,
                th_row,
                jnp.log(the_row),
                th_row / the_row,
            ]
        )
    )
    keep_bf = tall(keep.astype(BF))
    lg_rows, dg_rows = [jnp.zeros_like(th_row)], [jnp.zeros_like(th_row)]
    for k in range(COUNT_TOP):
        lg_rows.append(lg_rows[-1] + jnp.where(keep, jnp.log((th_row + k) / (1.0 + k)), 0.0))
        dg_rows.append(dg_rows[-1] + jnp.where(keep, 1.0 / (th_row + k), 0.0))
    lg_tab = tall(jnp.stack(lg_rows[1:]))
    dg_tab = tall(jnp.stack(dg_rows[1:]))
    enc_b_t = small_w[:kinds].T
    dec_b_t = small_w[kinds : 2 * kinds].T
    lat_row = jnp.pad(small_w[2 * kinds :], ((0, 16 - latent), (0, 0)))
    lat_t = lat_row.T
    norm_t = norm_par.T
    head_t = head_w.T
    pad = ((0, 16 - latent), (0, 0))
    head_all = jnp.concatenate([jnp.pad(head_t[:latent], pad), jnp.pad(head_t[latent:], pad)], axis=0)
    head_rows = head_all[:, :hidden]
    head_bias = jnp.broadcast_to(head_all[:, hidden:], (32, 128))
    head_cols = head_rows.T
    noise_t = jnp.pad(noise.T, pad)
    lib8 = library.reshape(blocks, width)
    batch_all = batch_ids.reshape(blocks, 1, width)
    batch_own = batch_ids.reshape(groups, 1, share)
    klw = jnp.broadcast_to(kl_weight.reshape(1, 1), (8, 128))

    own_block = pl.BlockSpec((1, 1, share), lambda i, m: (m[0], 0, 0))
    own_lanes = lambda rows: pl.BlockSpec((rows, share), lambda i, m: (0, m[0]))
    lane_block = lambda rows: pl.BlockSpec((rows, width), lambda i, *_: (0, i))

    enc_pieces, dec_pieces = call(
        prep_kernel,
        (1,),
        [(enc_b_t, whole((hidden, kinds))), (dec_b_t, whole((hidden, kinds))), (lat_t, whole((hidden, 16)))],
        [((3 * hidden, kinds), BF, whole((3 * hidden, kinds))), ((3 * hidden, kinds + 48), BF, whole((3 * hidden, kinds + 48)))],
    )

    keep_part, send_part = call(
        enc_kernel,
        (groups,),
        [
            (me if fast else me & 1, None),
            (x_t, pl.BlockSpec((genes, share), lambda i, m: (0, i ^ m[0]))),
            (enc_low, whole((hidden, genes))),
        ],
        [
            ((groups // 2, hidden, share), F32, pl.BlockSpec((1, hidden, share), lambda i, m: (i // 2, 0, 0))),
            ((groups // 2, hidden, share), BF, pl.BlockSpec((1, hidden, share), lambda i, m: (i // 2, 0, 0))),
        ],
        scalars=1,
        flops=2 * rows_all * genes * hidden,
        moved=2 * rows_all * genes,
    )
    got = swap(send_part, "genes", 1)
    slot = pl.BlockSpec((1, hidden, share), lambda i, m: (0, 0, 0))
    if fast:
        far = []
        for k in (2, 3, 1):
            mine = (keep_part[k : k + 1] + got[k : k + 1].astype(F32)).astype(BF)
            far.append(swap(mine, "genes", 2 * k))
        kept = keep_part
    else:
        summed = keep_part + got.astype(F32)
        summed = lax.psum_scatter(
            summed,
            "genes",
            scatter_dimension=0,
            axis_index_groups=[list(range(c, groups, 2)) for c in range(2)],
            tiled=True,
        )
        zero = jnp.zeros((1, hidden, share), BF)
        kept, got, far = summed, zero, [zero] * 3
    pre_enc, stat_enc = call(
        own_kernel,
        (1,),
        [(me, None), (kept, slot), (got, slot)]
        + [(part, slot) for part in far]
        + [(batch_own, own_block), (enc_pieces, whole((3 * hidden, kinds)))],
        [((hidden, share), F32, whole((hidden, share))), ((8, hidden), F32, whole((8, hidden)))],
        scalars=1,
        flops=2 * share * hidden * kinds * 3,
        moved=share * hidden * 16,
    )
    logc, gam_cell, dig_acc = call(
        lambda *refs: counts_kernel(chunk, *refs),
        (blocks,),
        [
            (x_t, lane_block(genes)),
            (lg_tab, whole((COUNT_TOP, genes, 128))),
            (dg_tab, whole((COUNT_TOP, genes, 128))),
        ],
        [
            ((genes, rows_all), BF, lane_block(genes)),
            ((blocks, width), F32, whole((blocks, width))),
            ((genes, 128), F32, whole((genes, 128))),
        ],
        flops=rows_all * genes * 30,
        moved=4 * rows_all * genes,
    )
    stat_enc = total(total(stat_enc, "genes"), "cells")

    stat8 = whole((8, hidden))
    z_own, head_out, kl_row = call(
        lambda *refs: latent_kernel(cells, latent, *refs),
        (1,),
        [
            (me, None),
            (pre_enc, whole((hidden, share))),
            (stat_enc, stat8),
            (norm_t, whole((hidden, 4))),
            (head_rows, whole((32, hidden))),
            (head_bias, whole((32, 128))),
            (noise_t, own_lanes(16)),
            (batch_own, own_block),
            (dec_pieces, whole((3 * hidden, kinds + 48))),
            (enc_b_t, whole((hidden, kinds))),
        ],
        [
            ((16, share), F32, whole((16, share))),
            ((32, share), F32, whole((32, share))),
            ((1, share), F32, whole((1, share))),
        ],
        scalars=1,
    )
    if fast:
        column = jnp.stack([z_own] + [swap(z_own, "genes", 2 * k) for k in (1, 2, 3)])
        z_all = jnp.concatenate([column, swap(column, "genes", 1)])
        stat_dec = jnp.sum(z_all[:, 8:, :hidden], axis=0)
        where_z = me
        z_spec = pl.BlockSpec((1, 16, width), lambda i, m: (((i ^ m[0]) % 2) * 4 + (i ^ m[0]) // 2, 0, 0))
    else:
        z_all = lax.all_gather(z_own, "genes", axis=0)
        stat_dec = jnp.sum(z_all[:, 8:, :hidden], axis=0)
        z_all = z_all.transpose(1, 0, 2).reshape(16, blocks, width).transpose(1, 0, 2)
        where_z = me
        z_spec = pl.BlockSpec((1, 16, width), lambda i, m: (i, 0, 0))
    stat_dec = total(stat_dec, "cells")

    batch_spec = pl.BlockSpec((1, 1, width), lambda i, *_: (i, 0, 0))
    hid, phat_dec, lse = call(
        lambda *refs: decode_kernel(cells, latent, *refs),
        (blocks,),
        [
            (where_z, None),
            (z_all, z_spec),
            (batch_all, batch_spec),
            (stat_dec, stat8),
            (norm_t, whole((hidden, 4))),
            (dec_pieces, whole((3 * hidden, kinds + 48))),
            (enc_b_t, whole((hidden, kinds))),
            (dec_t, pl.BlockSpec((genes, hidden), lambda i, m: (0, 0))),
            (par, pl.BlockSpec((None, genes, 128), lambda i, m: (0, 0, 0))),
        ],
        [
            ((hidden, rows_all), BF, lane_block(hidden)),
            ((hidden, rows_all), F32, lane_block(hidden)),
            ((blocks, width), F32, whole((blocks, width))),
        ],
        scratch=[pltpu.VMEM((genes, width), F32)],
        scalars=1,
        flops=2 * rows_all * genes * hidden,
        moved=rows_all * hidden * 6,
    )
    lse = log_total_of(lse, "genes")

    full8 = whole((blocks, width))
    gm, gd, rt, mass, recon, gene_acc = call(
        lambda *refs: zinb_kernel(chunk, min(256, width), *refs),
        (blocks,),
        [
            (hid, lane_block(hidden)),
            (dec_t, whole((2 * genes, hidden))),
            (x_t, lane_block(genes)),
            (keep_bf, whole((genes, 128))),
            (par, whole((6, genes, 128))),
            (lib8, full8),
            (lse, full8),
            (gam_cell, full8),
        ],
        [
            ((genes, rows_all), BF, lane_block(genes)),
            ((genes, rows_all), BF, lane_block(genes)),
            ((genes, rows_all), BF, lane_block(genes)),
            ((blocks, width), F32, full8),
            ((blocks, width), F32, full8),
            ((3, genes, 128), F32, whole((3, genes, 128))),
        ],
        scratch=[pltpu.VMEM((2 * genes, width), F32)],
        flops=rows_all * genes * 200,
        moved=8 * rows_all * genes,
    )
    mass = total(mass, "genes")
    part_a, part_r, dec_acc = call(
        back_kernel,
        (blocks,),
        [
            (gm, lane_block(genes)),
            (gd, lane_block(genes)),
            (rt, lane_block(genes)),
            (hid, lane_block(hidden)),
            (dec_n, whole((hidden, 2 * genes))),
        ],
        [
            ((hidden, rows_all), F32, lane_block(hidden)),
            ((hidden, rows_all), F32, lane_block(hidden)),
            ((2 * genes, hidden), F32, whole((2 * genes, hidden))),
        ],
        flops=2 * rows_all * genes * hidden * 5,
        moved=8 * rows_all * genes,
    )

    if fast:
        where_d = me
    else:
        where_d = jnp.zeros_like(me)
    half = whole((blocks // 2, 16, width))
    dy_dec, keep_d, send_d = call(
        lambda *refs: hidden_grad_kernel(cells, latent, *refs),
        (blocks,),
        [
            (where_d, None),
            (part_a, lane_block(hidden)),
            (part_r, lane_block(hidden)),
            (mass, full8),
            (hid, lane_block(hidden)),
            (phat_dec, lane_block(hidden)),
            (stat_dec, stat8),
            (norm_par, whole((4, hidden))),
            (lat_row, whole((16, hidden))),
            (recon, full8),
        ],
        [
            ((hidden, rows_all), F32, lane_block(hidden)),
            ((blocks // 2, 16, width), F32, half),
            ((blocks // 2, 16, width), F32, half),
        ],
        scratch=[pltpu.VMEM((2, hidden, 128), F32)],
        scalars=1,
    )
    slot_d = pl.BlockSpec((1, 16, share), lambda i, m: (0, 0, 0))
    if fast:
        got_d = swap(send_d, "genes", 1)
        pieces = [swap(keep_d[k : k + 1] + got_d[k : k + 1], "genes", 2 * k) for k in (1, 2, 3)]
        own_d = [keep_d, got_d] + pieces
    else:
        both = jnp.stack([keep_d, send_d], axis=1).reshape(blocks, 16, width)
        stat_part = both[0, 8:, :hidden]
        both = both.transpose(1, 0, 2).reshape(16, groups, share).transpose(1, 0, 2)
        mine = lax.psum_scatter(both, "genes", scatter_dimension=0, tiled=True)
        zero = jnp.zeros_like(mine)
        own_d = [mine, zero, zero, zero, zero]
    if fast:
        sums_dec = sum(part[0, 8:, :hidden] for part in own_d)
    else:
        sums_dec = lax.psum(stat_part, "genes")
    sums_dec = total(sums_dec, "cells")
    dec_part, oh_part = call(
        lambda *refs: dec_grad_kernel(cells, latent, *refs),
        (blocks,),
        [
            (where_z, None),
            (rt, lane_block(genes)),
            (hid, lane_block(hidden)),
            (mass, full8),
            (dy_dec, lane_block(hidden)),
            (z_all, z_spec),
            (batch_all, batch_spec),
            (dec_acc, whole((2 * genes, hidden))),
            (gene_acc, whole((3, genes, 128))),
            (dig_acc, whole((genes, 128))),
            (par, pl.BlockSpec((None, genes, 128), lambda i, m: (3, 0, 0))),
        ],
        [
            ((2 * genes + 8 * (-(-genes // 128)), hidden), F32, whole((2 * genes + 8 * (-(-genes // 128)), hidden))),
            ((kinds + 16, hidden), F32, whole((kinds + 16, hidden))),
        ],
        scratch=[pltpu.VMEM((genes, hidden + 16), F32)],
        scalars=1,
    )

    dy_enc, g_head, loss, stat_back = call(
        lambda *refs: head_grad_kernel(cells, latent, *refs),
        (1,),
        [(me, None)]
        + [(part, slot_d) for part in own_d]
        + [
            (sums_dec, stat8),
            (phat_dec, own_lanes(hidden)),
            (stat_dec, stat8),
            (norm_par, whole((4, hidden))),
            (lat_row, whole((16, hidden))),
            (head_out, whole((32, share))),
            (noise_t, own_lanes(16)),
            (kl_row, whole((1, share))),
            (klw, whole((8, 128))),
            (pre_enc, whole((hidden, share))),
            (stat_enc, stat8),
            (norm_t, whole((hidden, 4))),
            (head_cols, whole((hidden, 32))),
        ],
        [
            ((hidden, share), F32, whole((hidden, share))),
            ((32, share), F32, whole((32, share))),
            ((1, share), F32, whole((1, share))),
            ((8, hidden), F32, stat8),
        ],
        scalars=1,
    )
    stat_back = total(total(stat_back, "genes"), "cells")
    pre_grad, pre_low = call(
        lambda *refs: pre_grad_kernel(cells, *refs),
        (1,),
        [
            (dy_enc, whole((hidden, share))),
            (pre_enc, whole((hidden, share))),
            (stat_enc, stat8),
            (norm_t, whole((hidden, 4))),
            (stat_back, stat8),
        ],
        [((hidden, share), F32, whole((hidden, share))), ((hidden, share), BF, whole((hidden, share)))],
    )
    pre_all = lax.all_gather(pre_low, "genes", axis=0)
    small_rows = 2 * kinds + 16 + 64
    (small_part,) = call(
        lambda *refs: small_grad_kernel(cells, latent, *refs),
        (1,),
        [
            (me, None),
            (pre_grad, whole((hidden, share))),
            (g_head, whole((32, share))),
            (pre_enc, whole((hidden, share))),
            (stat_enc, stat8),
            (norm_t, whole((hidden, 4))),
            (batch_own, own_block),
            (phat_dec, own_lanes(hidden)),
            (z_own, whole((16, share))),
            (oh_part, whole((kinds + 16, hidden))),
            (sums_dec, stat8),
            (stat_dec, stat8),
            (norm_par, whole((4, hidden))),
        ],
        [((small_rows, hidden), F32, whole((small_rows, hidden)))],
        scalars=1,
    )
    small_g = total(total(small_part, "genes"), "cells")
    dec_g = total(dec_part, "cells")
    (enc_part,) = call(
        enc_grad_kernel,
        (blocks,),
        [
            (logc, lane_block(genes)),
            (pre_all, pl.BlockSpec((groups // blocks, hidden, share), lambda i: (i, 0, 0))),
        ],
        [((genes, hidden), F32, whole((genes, hidden)))],
        flops=2 * rows_all * genes * hidden,
        moved=2 * rows_all * genes,
    )
    enc_g = total(enc_part, "cells")

    (square,) = call(
        square_kernel,
        (1,),
        [(enc_g, whole(enc_g.shape)), (dec_g, whole(dec_g.shape))],
        [((8, 128), F32, whole((8, 128)))],
    )
    square = total(square, "genes")

    def turn(value):
        return value.transpose(0, 2, 1)

    state = [
        enc_w, enc_m, enc_v, turn(dec_w), turn(dec_m), turn(dec_v), gene_par, gene_m, gene_v,
        small_w, small_m, small_v, head_w.T, head_m.T, head_v.T, norm_par, norm_m, norm_v,
    ]
    ins = [square, enc_g, dec_g, small_g, stat_back, sums_dec] + state
    outs = []
    for index in range(6):
        one = state[3 * index]
        outs += [(one.shape, F32)] * 3
        if index < 2:
            outs.append((one.shape, BF))
    outs.append(((8, 128), F32))
    res = call(
        lambda *refs: update_kernel(latent, *refs),
        (1,),
        [(array, whole(array.shape)) for array in ins],
        [(shape, dtype, whole(shape)) for shape, dtype in outs],
        scratch=[pltpu.VMEM((24, 2 * hidden), F32)],
    )
    enc_res, dec_res = res[0:4], [turn(part) for part in res[4:8]]
    head_res = [part.T for part in res[14:17]]
    return (
        *enc_res,
        *dec_res,
        *res[8:14],
        *head_res,
        *res[17:20],
        res[20][0, 0],
        loss.reshape(share),
    )


def solution(mesh):
    placed = (
        P("cells", "genes"), P("cells"), P("cells", None), P("cells"), P("genes"), P(),
        P("genes", None), P("genes", None), P("genes", None),
        P(None, None, "genes"), P(None, None, "genes"), P(None, None, "genes"),
        P(None, "genes"), P(None, "genes"), P(None, "genes"),
        P(), P(), P(), P(), P(), P(), P(), P(), P(),
    )
    return jax.shard_map(
        per_device,
        mesh=mesh,
        in_specs=placed,
        out_specs=(
            P("genes", None), P("genes", None), P("genes", None), P("genes", None),
            P(None, None, "genes"), P(None, None, "genes"), P(None, None, "genes"), P(None, None, "genes"),
            P(None, "genes"), P(None, "genes"), P(None, "genes"),
            P(), P(), P(), P(), P(), P(), P(), P(), P(), P(),
            P(("cells", "genes")),
        ),
        check_vma=False,
    )
```

```python
import jax
import jax.numpy as jnp
from jax import lax
from jax.experimental import pallas as pl
from jax.experimental.pallas import tpu as pltpu
from jax.sharding import PartitionSpec as P

norm_epsilon = 0.001
zinb_epsilon = 1e-08
beta_one = 0.9
beta_two = 0.999
step_number = 5.0
decay_rate = 0.01
rate_genes = 0.03
rate_small = 0.2
max_norm = 0.1

F32 = jnp.float32
BF = jnp.bfloat16
HI = lax.Precision.HIGHEST
COUNT_TOP = 8
LOG2_E = 1.4426950408889634


def nn(left, right, precision=None):
    return lax.dot_general(
        left, right, (((1,), (0,)), ((), ())), precision=precision, preferred_element_type=F32
    )


def nt(left, right, precision=None):
    return lax.dot_general(
        left, right, (((1,), (1,)), ((), ())), precision=precision, preferred_element_type=F32
    )


def whole(shape):
    return pl.BlockSpec(shape, lambda *_: (0,) * len(shape))


def call(kernel, grid, ins, outs, scratch=(), scalars=0, flops=0, moved=0, mib=12):
    return pl.pallas_call(
        kernel,
        out_shape=[jax.ShapeDtypeStruct(shape, dtype) for shape, dtype, _ in outs],
        grid_spec=pltpu.PrefetchScalarGridSpec(
            num_scalar_prefetch=scalars,
            grid=grid,
            in_specs=[spec for _, spec in ins[scalars:]],
            out_specs=[spec for _, _, spec in outs],
            scratch_shapes=list(scratch),
        ),
        compiler_params=pltpu.CompilerParams(vmem_limit_bytes=mib * 1024 * 1024),
        cost_estimate=pl.CostEstimate(flops=flops, bytes_accessed=moved, transcendentals=0),
    )(*[array for array, _ in ins])


def swap(value, axis, bit):
    count = lax.axis_size(axis)
    return lax.ppermute(value, axis, [(i, i ^ bit) for i in range(count)])


def bit_groups(axis):
    count = lax.axis_size(axis)
    if axis == "genes":
        groups, bit = [[1]], 2
    else:
        groups, bit = [], 1
    while bit < count:
        groups.append([bit, 2 * bit] if 2 * bit < count else [bit])
        bit *= 4
    return groups


def total(value, axis):
    for group in bit_groups(axis):
        if len(group) == 1:
            value = value + swap(value, axis, group[0])
        else:
            low, high = group
            value = (value + swap(value, axis, low)) + (
                swap(value, axis, high) + swap(value, axis, low ^ high)
            )
    return value


def log_total_of(value, axis):
    for group in bit_groups(axis):
        if len(group) == 1:
            parts = [value, swap(value, axis, group[0])]
        else:
            low, high = group
            parts = [value] + [swap(value, axis, k) for k in (low, high, low ^ high)]
        top = parts[0]
        for part in parts[1:]:
            top = jnp.maximum(top, part)
        mass = sum(jnp.exp(part - top) for part in parts)
        value = top + jnp.log(mass)
    return value


def total_by_halves(value, axis, order):
    for bit in order:
        value = value + swap(value, axis, bit)
    return value


def after(value, *others):
    return lax.optimization_barrier((value,) + others)[0]


def three(value):
    high = value.astype(BF)
    rest = value - high.astype(F32)
    mid = rest.astype(BF)
    low = (rest - mid.astype(F32)).astype(BF)
    return high, mid, low


def one_hot(batch_row, kinds):
    ids = lax.broadcasted_iota(jnp.int32, (kinds, batch_row.shape[1]), 0)
    return jnp.where(ids == batch_row, 1.0, 0.0)


def columns(rows):
    return jnp.transpose(rows)


def prep_kernel(gene_ref, mask_ref, dec_ref, small_ref, head_ref, norm_ref, aug_ref, turn_ref, par_ref, lg_ref, dg_ref, enc_out, dec_out, lat_out, head_out, bias_out, cols_out, norm_out):
    genes = gene_ref.shape[1]
    hidden = norm_ref.shape[1]
    latent = head_ref.shape[0] // 2
    kinds = (small_ref.shape[0] - latent) // 2
    padded = pl.cdiv(genes, 128) * 128
    keep = mask_ref[...] > 0
    score_b = jnp.where(keep, gene_ref[0:1], -1e30)
    drop_b = jnp.where(keep, gene_ref[1:2], 1e30)
    th = jnp.exp(gene_ref[2:3])
    kept = jnp.where(keep, 1.0, 0.0)
    rows = jnp.concatenate((score_b, drop_b, th, kept, th, th, th, th), axis=0)
    if padded > genes:
        rows = jnp.concatenate((rows, jnp.ones((8, padded - genes), F32)), axis=1)
    turned = jnp.transpose(rows)[:genes]
    lane = lax.broadcasted_iota(jnp.int32, (genes, 16), 1)
    for half in range(2):
        at = slice(half * genes, (half + 1) * genes)
        aug_ref[at, 0:hidden] = dec_ref[half].astype(BF)
        high, mid, low = (jnp.broadcast_to(part.astype(F32), (genes, 16)) for part in three(turned[:, half : half + 1]))
        tail = jnp.where(lane == 0, high, jnp.where(lane == 1, mid, jnp.where(lane == 2, low, 0.0)))
        if half == 0:
            tail = jnp.where((lane >= 3) & (lane < 6), 1.0, tail)
        aug_ref[at, hidden : hidden + 16] = tail.astype(BF)
        turn_ref[:, at] = jnp.transpose(dec_ref[half]).astype(BF)
    th_w = jnp.broadcast_to(turned[:, 2:3], (genes, 128))
    keep_w = jnp.broadcast_to(turned[:, 3:4], (genes, 128))
    the_w = th_w + zinb_epsilon
    par_ref[0] = the_w
    par_ref[1] = th_w
    par_ref[2] = jnp.log(the_w)
    par_ref[3] = th_w / the_w
    par_ref[4] = keep_w
    gam = jnp.zeros_like(th_w)
    dig = jnp.zeros_like(th_w)
    for k in range(COUNT_TOP):
        more = th_w + float(k)
        gam = gam + keep_w * jnp.log(more * (1.0 / (1.0 + k)))
        dig = dig + keep_w / more
        lg_ref[k] = gam
        dg_ref[k] = dig
    for index, piece in enumerate(three(jnp.transpose(small_ref[0:kinds, :]))):
        enc_out[index * hidden : (index + 1) * hidden, :] = piece
    row = lax.broadcasted_iota(jnp.int32, (16, hidden), 0)
    lat_row = jnp.zeros((16, hidden), F32)
    for index in range(latent):
        lat_row = jnp.where(row == index, small_ref[2 * kinds + index : 2 * kinds + index + 1, :], lat_row)
    lat_out[...] = lat_row
    batch_pieces = three(jnp.transpose(small_ref[kinds : 2 * kinds, :]))
    lat = three(jnp.transpose(lat_row))
    zero = jnp.zeros_like(lat[0])
    tails = ((lat[0], lat[0], lat[0]), (lat[1], lat[1], zero), (lat[2], zero, zero))
    for index in range(3):
        at = slice(index * hidden, (index + 1) * hidden)
        dec_out[at, :] = jnp.concatenate((batch_pieces[index],) + tails[index], axis=1)
    full = lax.broadcasted_iota(jnp.int32, (32, hidden), 0)
    head = jnp.zeros((32, hidden), F32)
    bias = jnp.zeros((32, 1), F32)
    for index in range(2 * latent):
        to = index if index < latent else index - latent + 16
        head = jnp.where(full == to, head_ref[index : index + 1, 0:hidden], head)
        bias = jnp.where(full[:, 0:1] == to, head_ref[index : index + 1, hidden : hidden + 1], bias)
    head_out[...] = head
    bias_out[...] = jnp.broadcast_to(bias, (32, 128))
    high, mid, _ = three(jnp.transpose(head))
    cols_out[0:hidden, :] = jnp.concatenate((high, high), axis=1)
    cols_out[hidden : 2 * hidden, :] = jnp.concatenate((mid, jnp.zeros_like(mid)), axis=1)
    norm_out[...] = jnp.transpose(jnp.concatenate((norm_ref[...], norm_ref[...]), axis=0))


def exact_rows(stacked, table):
    out = nn(stacked, table)
    hidden = out.shape[0] // 3
    return out[:hidden] + out[hidden : 2 * hidden] + out[2 * hidden :]


def dec_table(z, batch_row, kinds):
    high, mid, low = three(z)
    return jnp.concatenate((one_hot(batch_row, kinds).astype(BF), high, mid, low), axis=0)


def row_sums(value):
    return nt(jnp.ones((8, value.shape[1]), F32), value, HI)


def stat_rows(first, second, at):
    sums, squares = row_sums(first), row_sums(second)
    row = lax.broadcasted_iota(jnp.int32, sums.shape, 0)
    return jnp.where(row == at, sums, jnp.where(row == at + 1, squares, 0.0))


def enc_kernel(me_ref, x_ref, w_ref, keep_ref, send_ref, turn_ref):
    step = pl.program_id(0)

    @pl.when(step == 0)
    def _():
        turn_ref[...] = jnp.transpose(w_ref[...]).astype(BF)

    log_counts = jnp.log(1.0 + x_ref[...].astype(F32)).astype(BF)
    part = nn(turn_ref[...], log_counts)
    odd = lax.rem(step, 2)

    @pl.when(odd == 0)
    def _():
        keep_ref[0] = part

    @pl.when(odd == 1)
    def _():
        send_ref[0] = part.astype(BF)


def lines(rows8, count):
    wide = rows8.shape[1]
    if wide < 128 * count:
        rows8 = jnp.concatenate((rows8, jnp.zeros((8, 128 * count - wide), F32)), axis=1)
    return jnp.concatenate([rows8[:, i * 128 : (i + 1) * 128] for i in range(count)], axis=0)


def counts_kernel(rows, span, x_ref, lg_ref, dg_ref, keep_ref, logc_ref, mask_ref, cell_ref, disp_ref, line_ref, sum_ref):
    step = pl.program_id(0)
    genes, width = x_ref.shape

    @pl.when(step == 0)
    def _():
        disp_ref[...] = jnp.zeros_like(disp_ref)
        sum_ref[...] = jnp.zeros_like(sum_ref)

    tiles = span // 128
    done = []
    for first in range(0, width, span):
        lanes = [slice(first + tile * 128, first + (tile + 1) * 128) for tile in range(tiles)]

        def chunk(g, cell):
            at = pl.ds(pl.multiple_of(g * rows, rows), rows)
            keep = keep_ref[at, :]
            xs = [x_ref[at, lanes[tile]].astype(F32) for tile in range(tiles)]
            logs = [jnp.log(1.0 + x) for x in xs]
            for tile in range(tiles):
                logc_ref[at, lanes[tile]] = logs[tile].astype(BF)
                mask_ref[at, lanes[tile]] = (xs[tile] * keep).astype(BF)
            sum_ref[at, :] += sum(part.astype(BF).astype(F32) for part in logs)
            gams = [jnp.zeros_like(xs[0]) for _ in range(tiles)]
            digs = [jnp.zeros_like(xs[0]) for _ in range(tiles)]
            for k in range(COUNT_TOP):
                lg, dg = lg_ref[k, at, :], dg_ref[k, at, :]
                for tile in range(tiles):
                    more = xs[tile] > (k + 0.5)
                    gams[tile] = jnp.where(more, lg, gams[tile])
                    digs[tile] = jnp.where(more, dg, digs[tile])
            disp_ref[at, :] += sum(digs)
            out = []
            for tile in range(tiles):
                folded = cell[tile]
                for part in range(rows // 8):
                    folded = folded + gams[tile][part * 8 : (part + 1) * 8]
                out.append(folded)
            return tuple(out)

        zero = tuple(jnp.zeros((8, 128), F32) for _ in range(tiles))
        done += list(lax.fori_loop(0, genes // rows, chunk, zero))
    cell_ref[pl.ds(step, 1), :] = jnp.sum(jnp.concatenate(done, axis=1), axis=0, keepdims=True)

    @pl.when(step == pl.num_programs(0) - 1)
    def _():
        line_ref[...] = lines(row_sums(sum_ref[...]), line_ref.shape[0] // 8)


def own_kernel(me_ref, keep_ref, got_ref, one_ref, two_ref, six_ref, batch_ref, enc_b_ref, pre_ref, stat_ref):
    kinds = enc_b_ref.shape[1]
    gathered = (keep_ref[0] + got_ref[0].astype(F32) + one_ref[0].astype(F32)) + (
        two_ref[0].astype(F32) + six_ref[0].astype(F32)
    )
    table = one_hot(batch_ref[0], kinds).astype(BF)
    pre = gathered + exact_rows(enc_b_ref[...], table)
    pre_ref[...] = pre
    stat_ref[...] = stat_rows(pre, pre * pre, 0)


def norm_columns(stat, first, cells):
    turned = jnp.transpose(stat)
    mean = turned[:, first : first + 1] / cells
    var = turned[:, first + 1 : first + 2] / cells - mean * mean
    return mean, lax.rsqrt(var + norm_epsilon)


def norm_rows(stat, first, cells):
    mean = stat[first : first + 1] / cells
    var = stat[first + 1 : first + 2] / cells - mean * mean
    return mean, lax.rsqrt(var + norm_epsilon)


def latent_kernel(cells, latent, me_ref, pre_ref, stat_ref, norm_ref, head_ref, bias_ref, noise_ref, batch_ref, dec_b_ref, pack_ref, aff_ref, kl_ref):
    kinds = dec_b_ref.shape[1] - 48
    mean, inv = norm_columns(stat_ref[...], 0, cells)
    phat = (pre_ref[...] - mean) * inv
    affine = norm_ref[:, 0:1] * phat + norm_ref[:, 1:2]
    aff_ref[...] = affine.astype(BF)
    out = nn(head_ref[...], jnp.maximum(affine, 0.0), HI) + bias_ref[:, 0:1]
    lat_mean, lat_logvar = out[:latent], out[16 : 16 + latent]
    var = jnp.exp(lat_logvar) + 0.0001
    z = lat_mean + jnp.sqrt(var) * noise_ref[...]
    terms = var + lat_mean * lat_mean - 1.0 - jnp.log(var)
    kl_ref[...] = 0.5 * jnp.sum(terms, axis=0, keepdims=True)
    pre_dec = exact_rows(dec_b_ref[...], dec_table(latent_rows(z), batch_ref[0], kinds))
    hidden = pre_dec.shape[0]
    stat = stat_rows(pre_dec, pre_dec * pre_dec, 0)
    pack_ref[0:latent, :] = lat_mean
    pack_ref[latent : latent + 6, :] = jnp.zeros((6, z.shape[1]), F32)
    pack_ref[latent : latent + 1, 0:hidden] = stat[0:1]
    pack_ref[latent + 1 : latent + 2, 0:hidden] = stat[1:2]
    pack_ref[16 : 16 + latent, :] = lat_logvar
    pack_ref[16 + latent : 32, :] = jnp.zeros((16 - latent, z.shape[1]), F32)


def latent_rows(z):
    if z.shape[0] == 16:
        return z
    return jnp.concatenate((z, jnp.zeros((16 - z.shape[0], z.shape[1]), F32)), axis=0)


def draw(latent, pack, noise):
    lat_mean, lat_logvar = pack[0:latent], pack[16 : 16 + latent]
    return lat_mean, lat_logvar, lat_mean + jnp.sqrt(jnp.exp(lat_logvar) + 0.0001) * noise


def pick(step, me_ref, fast, near_ref, far_ref):
    if not fast:
        return near_ref[0]
    return jnp.where(lax.rem(step ^ me_ref[0], 2) == 0, near_ref[0], far_ref[0])


def decode_kernel(cells, latent, fast, me_ref, near_ref, far_ref, noise_ref, batch_ref, stat_ref, norm_ref, dec_b_ref, w_ref, hid_ref, phat_ref, lse_ref, z_ref, score_ref):
    kinds = dec_b_ref.shape[1] - 48
    step = pl.program_id(0)
    genes = score_ref.shape[0]
    mean, inv = norm_columns(stat_ref[...], latent - 8, cells)
    _, _, z = draw(latent, pick(step, me_ref, fast, near_ref, far_ref), noise_ref[...])
    z = latent_rows(z)
    z_ref[...] = z
    pre_dec = exact_rows(dec_b_ref[...], dec_table(z, batch_ref[0], kinds))
    phat = (pre_dec - mean) * inv
    phat_ref[...] = phat
    hidden = jnp.maximum(norm_ref[:, 2:3] * phat + norm_ref[:, 3:4], 0.0).astype(BF)
    hid_ref[...] = hidden
    width = score_ref.shape[1]
    row = lax.broadcasted_iota(jnp.int32, (16, width), 0)
    table = jnp.concatenate((hidden, jnp.where(row < 3, 1.0, 0.0).astype(BF)), axis=0)
    score_ref[...] = nn(w_ref[...], table)
    tiles = width // 128
    rows = 32

    def top(g, best):
        at = pl.ds(pl.multiple_of(g * rows, rows), rows)
        new = []
        for tile in range(tiles):
            value = score_ref[at, slice(tile * 128, (tile + 1) * 128)]
            part = best[tile]
            for index in range(rows // 8):
                part = jnp.maximum(part, value[index * 8 : (index + 1) * 8])
            new.append(part)
        return tuple(new)

    best = lax.fori_loop(0, genes // rows, top, tuple(jnp.full((8, 128), -3e38, F32) for _ in range(tiles)))
    high = [jnp.max(part, axis=0, keepdims=True) for part in best]
    wide = [jnp.broadcast_to(part, (8, 128)) for part in high]

    def mass(g, sums):
        at = pl.ds(pl.multiple_of(g * rows, rows), rows)
        new = []
        for tile in range(tiles):
            value = score_ref[at, slice(tile * 128, (tile + 1) * 128)]
            part = sums[tile]
            for index in range(rows // 8):
                part = part + jnp.exp(value[index * 8 : (index + 1) * 8] - wide[tile])
            new.append(part)
        return tuple(new)

    sums = lax.fori_loop(0, genes // rows, mass, tuple(jnp.zeros((8, 128), F32) for _ in range(tiles)))
    lse = [high[tile] + jnp.log(jnp.sum(sums[tile], axis=0, keepdims=True)) for tile in range(tiles)]
    lse_ref[pl.ds(step, 1), :] = jnp.concatenate(lse, axis=1)


def enc_sums_kernel(fast, me_ref, logc_ref, near_ref, far_ref, batch_ref, lines_ref, out_ref):
    step = pl.program_id(0)
    genes = logc_ref.shape[0]
    kinds = out_ref.shape[0] - genes - lines_ref.shape[0] - 8

    @pl.when(step == 0)
    def _():
        out_ref[...] = jnp.zeros_like(out_ref)
        out_ref[genes + kinds : genes + kinds + lines_ref.shape[0], :] = lines_ref[...]

    affine = pick(step, me_ref, fast, near_ref, far_ref)
    table = one_hot(batch_ref[0], kinds)
    out_ref[0:genes, :] += nt(logc_ref[...], affine)
    out_ref[genes : genes + kinds, :] += nt(table.astype(BF), affine)
    out_ref[genes + kinds + lines_ref.shape[0] :, :] += row_sums(table)


def zinb_kernel(rows, span, hid_ref, w_ref, x_ref, par_ref, lib_ref, lse_ref, gam_ref, gm_ref, gd_ref, rt_ref, mass_ref, recon_ref, acc_ref, sc_ref):
    step = pl.program_id(0)
    genes, width = x_ref.shape

    @pl.when(step == 0)
    def _():
        acc_ref[...] = jnp.zeros_like(acc_ref)

    one_row = pl.ds(step, 1)
    gam_row = gam_ref[one_row, :]
    shift = lib_ref[one_row, :] - lse_ref[one_row, :]
    row = lax.broadcasted_iota(jnp.int32, (16, width), 0)
    hi, mid, lo = three(shift)
    extra = jnp.where(row < 3, 1.0, jnp.where(row == 3, hi.astype(F32), jnp.where(row == 4, mid.astype(F32), jnp.where(row == 5, lo.astype(F32), 0.0))))
    table = jnp.concatenate((hid_ref[...], extra.astype(BF)), axis=0)
    sc_ref[...] = nn(w_ref[...], table)
    tiles = span // 128
    mass_out, recon_out = [], []
    for first in range(0, width, span):
        lanes = [slice(first + tile * 128, first + (tile + 1) * 128) for tile in range(tiles)]
        def chunk(g, state):
            at = pl.ds(pl.multiple_of(g * rows, rows), rows)
            at_drop = pl.ds(pl.multiple_of(genes + g * rows, rows), rows)
            the, th, log_the, part_th = (par_ref[i, at, :] for i in range(4))
            sums = [acc_ref[i, at, :] for i in range(3)]
            new = []
            for tile in range(tiles):
                rec, prod, back = state[tile]
                x = x_ref[at, lanes[tile]].astype(F32)
                mu = jnp.exp(sc_ref[at, lanes[tile]])
                drop = sc_ref[at_drop, lanes[tile]]
                both = mu + the
                r = 1.0 / both
                log_both = jnp.log(both)
                gap = log_the - log_both
                th_gap = th * gap
                u = jnp.where(x < 0.5, th_gap - drop, 1e30)
                eu = jnp.exp2(jnp.abs(u) * (-LOG2_E))
                ed = jnp.exp2(jnp.abs(drop) * (-LOG2_E))
                den = 1.0 + eu
                mu_eps = mu + zinb_epsilon
                rd = 1.0 / (1.0 + ed)
                w0 = jnp.where(u >= 0.0, 1.0, eu) * (1.0 / den)
                term = (th_gap - jnp.maximum(drop, 0.0)) + (x * (jnp.log(mu_eps) - log_both) - jnp.minimum(u, 0.0))
                factor = den * rd
                y = (x + w0 * th) * r
                g_mean = mu * (x * (1.0 / mu_eps) - y)
                g_drop = jnp.where(drop >= 0.0, ed, 1.0) * rd - w0
                g_disp = w0 * (gap + part_th) - y
                gm_ref[at, lanes[tile]] = g_mean.astype(BF)
                gd_ref[at, lanes[tile]] = g_drop.astype(BF)
                rt_ref[at, lanes[tile]] = mu.astype(BF)
                sums = [a + b for a, b in zip(sums, (g_mean, g_drop, g_disp))]
                for part in range(rows // 8):
                    sub = slice(part * 8, (part + 1) * 8)
                    rec = rec + term[sub]
                    prod = prod * factor[sub]
                    back = back + g_mean[sub]
                new.append((rec, prod, back))
            for i in range(3):
                acc_ref[i, at, :] = sums[i]
            return tuple(new)
        zero = jnp.zeros((8, 128), F32)
        state = tuple((zero, zero + 1.0, zero) for _ in range(tiles))
        state = lax.fori_loop(0, genes // rows, chunk, state)
        for tile in range(tiles):
            rec, prod, back = state[tile]
            mass_out.append(jnp.sum(back, axis=0, keepdims=True))
            recon_out.append(jnp.sum(rec + jnp.log(prod), axis=0, keepdims=True))
    mass_ref[one_row, :] = jnp.concatenate(mass_out, axis=1)
    recon_ref[one_row, :] = jnp.concatenate(recon_out, axis=1) + gam_row


def back_kernel(gm_ref, gd_ref, rt_ref, hid_ref, w_ref, a_ref, r_ref, g_ref):
    genes = gm_ref.shape[0]

    @pl.when(pl.program_id(0) == 0)
    def _():
        g_ref[...] = jnp.zeros_like(g_ref)

    gm, gd, rt, hid = gm_ref[...], gd_ref[...], rt_ref[...], hid_ref[...]
    scale_w = w_ref[:, :genes]
    a_ref[...] = nn(scale_w, gm) + nn(w_ref[:, genes:], gd)
    r_ref[...] = nn(scale_w, rt)
    g_ref[:genes, :] += nt(gm, hid)
    g_ref[genes:, :] += nt(gd, hid)


def hidden_grad_kernel(cells, latent, me_ref, a_ref, r_ref, mass_ref, hid_ref, phat_ref, lib_ref, stat_ref, gain_ref, lat_ref, recon_ref, dy_ref, keep_ref, send_ref, sum_ref):
    step = pl.program_id(0)
    steps = pl.num_programs(0)
    place = step ^ me_ref[0]

    @pl.when(step == 0)
    def _():
        sum_ref[...] = jnp.zeros_like(sum_ref)

    back = mass_ref[pl.ds(step, 1), :] * jnp.exp(-lib_ref[pl.ds(step, 1), :])
    dy = jnp.where(hid_ref[...] > 0, (a_ref[...] - back * r_ref[...]) * (-1.0 / cells), 0.0)
    dy_ref[...] = dy
    hidden, width = dy.shape
    weighted = dy * phat_ref[...]
    first, second = dy[:, :128], weighted[:, :128]
    for tile in range(1, width // 128):
        lanes = slice(tile * 128, (tile + 1) * 128)
        first = first + dy[:, lanes]
        second = second + weighted[:, lanes]
    sum_ref[0] += first
    sum_ref[1] += second
    _, inv = norm_rows(stat_ref[...], latent - 8, cells)
    lat = lat_ref[...] * (gain_ref[2:3] * inv)
    lat_high, lat_mid, _ = three(lat)
    dy_high, dy_mid, _ = three(dy)
    table = jnp.concatenate((dy_high, dy_mid), axis=0)
    left = jnp.concatenate(
        (
            jnp.concatenate((lat_high, lat_high), axis=1),
            jnp.concatenate((lat_mid, jnp.zeros_like(lat_mid)), axis=1),
        ),
        axis=0,
    )
    both = nn(left, table)
    block = both[:16] + both[16:]
    row = lax.broadcasted_iota(jnp.int32, block.shape, 0)
    block = jnp.where(row == latent, recon_ref[pl.ds(step, 1), :], block)
    slot = lax.div(place, 2)

    @pl.when(lax.rem(place, 2) == 0)
    def _():
        keep_ref[slot] = block

    @pl.when(lax.rem(place, 2) == 1)
    def _():
        send_ref[slot] = block

    @pl.when(step == steps - 1)
    def _():
        one, two = row_sums(sum_ref[0]), row_sums(sum_ref[1])
        for ref in (keep_ref, send_ref):
            for index in range(ref.shape[0]):
                ref[index, latent + 1 : latent + 2, 0:hidden] = one[0:1]
                ref[index, latent + 2 : latent + 3, 0:hidden] = two[0:1]


def dec_grad_kernel(cells, rt_ref, hid_ref, mass_ref, lib_ref, dy_ref, z_ref, batch_ref, g_ref, acc_ref, dig_ref, th_ref, dec_ref, oh_ref, mix_ref):
    step = pl.program_id(0)
    steps = pl.num_programs(0)
    genes = rt_ref.shape[0]
    hidden = hid_ref.shape[0]
    kinds = oh_ref.shape[0] - 16

    @pl.when(step == 0)
    def _():
        mix_ref[...] = jnp.zeros_like(mix_ref)
        oh_ref[...] = jnp.zeros_like(oh_ref)

    back = mass_ref[pl.ds(step, 1), :] * jnp.exp(-lib_ref[pl.ds(step, 1), :])
    back_high, back_mid, back_low = three(back)
    row = lax.broadcasted_iota(jnp.int32, (16, back.shape[1]), 0)
    extra = jnp.where(row == 0, back_high.astype(F32), jnp.where(row == 1, back_mid.astype(F32), 0.0))
    scaled = (hid_ref[...].astype(F32) * back).astype(BF)
    mix_ref[...] += nt(rt_ref[...], jnp.concatenate((scaled, extra.astype(BF)), axis=0))
    z_high, z_mid, _ = three(z_ref[...])
    left = jnp.concatenate((one_hot(batch_ref[0], kinds).astype(BF), z_high, z_mid), axis=0)
    dy_high, dy_mid, _ = three(dy_ref[...])
    part = nt(left, dy_high) + nt(left, dy_mid)
    oh_ref[:kinds, :] += part[:kinds]
    oh_ref[kinds:, :] += part[kinds : kinds + 16] + part[kinds + 16 :]

    @pl.when(step == steps - 1)
    def _():
        scale = -1.0 / cells
        mix = mix_ref[...]
        dec_ref[:genes, :] = (g_ref[:genes, :] - mix[:, :hidden]) * scale
        dec_ref[genes : 2 * genes, :] = g_ref[genes:, :] * scale
        pick = jnp.where(lax.broadcasted_iota(jnp.int32, (8, 16), 1) < 2, 1.0, 0.0)
        score_row = row_sums(acc_ref[0]) - nt(pick, mix[:, hidden:], HI)
        drop_row = row_sums(acc_ref[1])
        disp_row = row_sums((acc_ref[2] + dig_ref[...]) * th_ref[...])
        line = lax.broadcasted_iota(jnp.int32, score_row.shape, 0)
        gene_rows = scale * jnp.where(
            line == 0, score_row, jnp.where(line == 1, drop_row, jnp.where(line == 2, disp_row, 0.0))
        )
        dec_ref[2 * genes :, :] = lines(gene_rows, pl.cdiv(genes, 128))


def enc_back_kernel(cells, latent, fast, me_ref, dnear_ref, dfar_ref, phat_ref, sums_ref, stat_ref, gain_ref, lat_ref, near_ref, far_ref, noise_ref, klw_ref, anear_ref, afar_ref, batch_ref, logc_ref, cols_ref, z_ref, enc_ref, rest_ref, lane_ref):
    step = pl.program_id(0)
    genes, width = logc_ref.shape
    hidden = phat_ref.shape[0]
    kinds = (rest_ref.shape[0] - 32 - 16 - 16) // 2

    @pl.when(step == 0)
    def _():
        enc_ref[...] = jnp.zeros_like(enc_ref)
        rest_ref[...] = jnp.zeros_like(rest_ref)
        lane_ref[...] = jnp.zeros_like(lane_ref)

    block = pick(step, me_ref, fast, dnear_ref, dfar_ref)
    _, inv = norm_rows(stat_ref[...], latent - 8, cells)
    scaled = gain_ref[2:3] * inv
    lat = lat_ref[...] * scaled
    at = latent + 1 - 8
    m_one = sums_ref[at : at + 1] * (1.0 / cells)
    m_two = sums_ref[at + 1 : at + 2] * (1.0 / cells)
    fixed = jnp.sum(lat * m_one, axis=1, keepdims=True)
    left_high, left_mid, _ = three(lat * m_two)
    phat_high, phat_mid, _ = three(phat_ref[...])
    both = nn(
        jnp.concatenate(
            (
                jnp.concatenate((left_high, left_high), axis=1),
                jnp.concatenate((left_mid, jnp.zeros_like(left_mid)), axis=1),
            ),
            axis=0,
        ),
        jnp.concatenate((phat_high, phat_mid), axis=0),
    )
    grad_z = (block - fixed - (both[:16] + both[16:]))[:latent]
    noise = noise_ref[...]
    lat_mean, lat_logvar, _ = draw(latent, pick(step, me_ref, fast, near_ref, far_ref), noise)
    spread = jnp.exp(lat_logvar)
    var = spread + 0.0001
    scale = klw_ref[0:1, 0:1] * (1.0 / cells)
    g_mean = latent_rows(grad_z + scale * lat_mean)
    g_var = latent_rows(
        grad_z * noise * 0.5 * spread * lax.rsqrt(var) + scale * 0.5 * (spread - spread / var)
    )
    g_head = jnp.concatenate((g_mean, g_var), axis=0)
    head_high, head_mid, _ = three(g_head)
    spread_out = nn(cols_ref[...], jnp.concatenate((head_high, head_mid), axis=0))
    affine = pick(step, me_ref, fast, anear_ref, afar_ref)
    wide = affine.astype(F32)
    dy = jnp.where(wide > 0, spread_out[:hidden] + spread_out[hidden:], 0.0)
    weighted = dy * wide
    first, second = dy[:, :128], weighted[:, :128]
    for tile in range(1, width // 128):
        lanes = slice(tile * 128, (tile + 1) * 128)
        first = first + dy[:, lanes]
        second = second + weighted[:, lanes]
    lane_ref[0] += first
    lane_ref[1] += second
    dy_low = dy.astype(BF)
    table = one_hot(batch_ref[0], kinds)
    hidden_low = jnp.maximum(wide, 0.0).astype(BF)
    enc_ref[...] += nt(logc_ref[...], dy_low)
    rest_ref[0:kinds, :] += nt(table.astype(BF), dy_low)
    rest_ref[kinds : kinds + 32, :] += nt(head_high, hidden_low) + nt(head_mid, hidden_low)
    base = kinds + 32
    z_high, z_mid, _ = three(z_ref[...])
    left = jnp.concatenate((table.astype(BF), z_high, z_mid), axis=0)
    part = nt(left, phat_high) + nt(left, phat_mid)
    held = jnp.sum(jnp.concatenate((table, z_ref[...]), axis=0), axis=1, keepdims=True)
    product = jnp.concatenate((part[:kinds], part[kinds : kinds + 16] + part[kinds + 16 :]), axis=0)
    rest_ref[base + 16 :, :] -= held * m_one + product * m_two
    bias = row_sums(g_head)
    rest_ref[base + 8 : base + 16, 0:32] += bias

    @pl.when(step == pl.num_programs(0) - 1)
    def _():
        one, two = row_sums(lane_ref[0]), row_sums(lane_ref[1])
        row = lax.broadcasted_iota(jnp.int32, one.shape, 0)
        rest_ref[base : base + 8, :] = jnp.where(row == 0, one, jnp.where(row == 1, two, 0.0))


def finish_kernel(cells, latent, enc_ref, rest_ref, dec_ref, fixed_ref, stat_enc_ref, stat_dec_ref, sums_ref, norm_ref, kl_ref, klw_ref, own_ref, enc_out, small_out, head_out, norm_out, square_out, loss_out):
    genes, hidden = enc_ref.shape
    kinds = (rest_ref.shape[0] - 32 - 16 - 16) // 2
    count = pl.cdiv(genes, 128)
    loss_out[...] = klw_ref[0:1, 0:1] * kl_ref[...] - own_ref[latent : latent + 1, :]
    gain, shift = norm_ref[0:1], norm_ref[1:2]
    _, inv = norm_rows(stat_enc_ref[...], 0, cells)
    base = kinds + 32
    n_one = rest_ref[base : base + 1]
    n_two = (rest_ref[base + 1 : base + 2] - shift * n_one) / gain
    one, two = n_one * (1.0 / cells), n_two * (1.0 / cells)
    lines_at = genes + kinds
    logs = jnp.concatenate([fixed_ref[lines_at + 8 * i : lines_at + 8 * (i + 1), :] for i in range(count)], axis=1)
    log_sum = jnp.transpose(logs)[:genes, 0:1]
    batch_sum = jnp.transpose(fixed_ref[lines_at + 8 * count : lines_at + 8 * count + 8, :])[:kinds, 0:1]

    def whole_gradient(part, product, plain):
        return (gain * inv) * (part - plain * one - ((product - plain * shift) / gain) * two)

    enc = whole_gradient(enc_ref[...], fixed_ref[0:genes, :], log_sum)
    enc_out[...] = enc
    dec = dec_ref[...]
    lane = jnp.sum(enc * enc, axis=0, keepdims=True) + jnp.sum(dec * dec, axis=0, keepdims=True)
    square_out[...] = jnp.broadcast_to(jnp.sum(lane, axis=1, keepdims=True), square_out.shape)
    small_out[0:kinds, :] = whole_gradient(rest_ref[0:kinds, :], fixed_ref[genes : genes + kinds, :], batch_sum)
    _, inv_dec = norm_rows(stat_dec_ref[...], latent - 8, cells)
    small_out[kinds:, :] = (norm_ref[2:3] * inv_dec) * rest_ref[base + 16 :, :]
    bias = jnp.transpose(rest_ref[base + 8 : base + 16, :])
    for half in range(2):
        rows = slice(half * latent, (half + 1) * latent)
        head_out[rows, 0:hidden] = rest_ref[kinds + 16 * half : kinds + 16 * half + latent, :]
        head_out[rows, hidden : hidden + 1] = bias[16 * half : 16 * half + latent, 0:1]
    at = latent + 1 - 8
    norm_out[0:1] = n_two
    norm_out[1:2] = n_one
    norm_out[2:3] = sums_ref[at + 1 : at + 2]
    norm_out[3:4] = sums_ref[at : at + 1]


def step_of(weight, gradient, first, second, rate):
    first = beta_one * first + (1.0 - beta_one) * gradient
    second = beta_two * second + (1.0 - beta_two) * gradient * gradient
    fixed_one = first * (1.0 / (1.0 - beta_one**step_number))
    fixed_two = second * (1.0 / (1.0 - beta_two**step_number))
    update = fixed_one / (jnp.sqrt(fixed_two) + 1e-08) + decay_rate * weight
    return weight - rate * update, first, second


def update_kernel(latent, square_ref, enc_g_ref, dec_g_ref, small_g_ref, head_g_ref, norm_g_ref, *refs):
    ins, outs = refs[:18], refs[18:]
    enc, dec, gene, small, head, norm = (ins[3 * i : 3 * i + 3] for i in range(6))
    genes = enc[0].shape[0]
    rows = small[0].shape[0]
    small_square = jnp.zeros((1, 1), F32)
    for part in (small_g_ref[0:rows, :], head_g_ref[...], norm_g_ref[...]):
        small_square = small_square + jnp.sum(jnp.sum(part * part, axis=0, keepdims=True), axis=1, keepdims=True)
    value = jnp.sqrt(square_ref[0:1, 0:1] + small_square)
    factor = jnp.minimum(1.0, max_norm / value)
    (enc_n, enc_m, enc_v, enc_l, dec_n, dec_m, dec_v, dec_l, gene_n, gene_m, gene_v, small_n, small_m, small_v, head_n, head_m, head_v, norm_n, norm_m, norm_v, norm_out) = outs
    norm_out[...] = jnp.broadcast_to(value, norm_out.shape)
    new, first, second = step_of(enc[0][...], enc_g_ref[...] * factor, enc[1][...], enc[2][...], rate_genes)
    enc_n[...], enc_m[...], enc_v[...], enc_l[...] = new, first, second, new.astype(BF)
    for index in range(2):
        gradient = dec_g_ref[index * genes : (index + 1) * genes, :] * factor
        new, first, second = step_of(dec[0][index], gradient, dec[1][index], dec[2][index], rate_genes)
        dec_n[index], dec_m[index], dec_v[index], dec_l[index] = new, first, second, new.astype(BF)
    for index in range(pl.cdiv(genes, 128)):
        span = slice(index * 128, min(genes, (index + 1) * 128))
        gradient = dec_g_ref[2 * genes + index * 8 : 2 * genes + index * 8 + 3, 0 : span.stop - span.start] * factor
        new, first, second = step_of(gene[0][:, span], gradient, gene[1][:, span], gene[2][:, span], rate_small)
        gene_n[:, span], gene_m[:, span], gene_v[:, span] = new, first, second
    new, first, second = step_of(small[0][...], small_g_ref[0:rows, :] * factor, small[1][...], small[2][...], rate_small)
    small_n[...], small_m[...], small_v[...] = new, first, second
    new, first, second = step_of(head[0][...], head_g_ref[...] * factor, head[1][...], head[2][...], rate_small)
    head_n[...], head_m[...], head_v[...] = new, first, second
    new, first, second = step_of(norm[0][...], norm_g_ref[...] * factor, norm[1][...], norm[2][...], rate_small)
    norm_n[...], norm_m[...], norm_v[...] = new, first, second


def gather_genes(value, fast, blocks, width):
    if fast:
        near = jnp.stack([value] + [swap(value, "genes", 2 * k) for k in (1, 2, 3)])
        return near, swap(near, "genes", 1)
    rows = value.shape[0]
    whole_rows = lax.all_gather(value, "genes", axis=0).transpose(1, 0, 2)
    near = whole_rows.reshape(rows, blocks, width).transpose(1, 0, 2)
    return near, near


def per_device(counts, library, noise, batch_ids, gene_mask, kl_weight, enc_w, enc_m, enc_v, dec_w, dec_m, dec_v, gene_par, gene_m, gene_v, small_w, small_m, small_v, head_w, head_m, head_v, norm_par, norm_m, norm_v):
    rows_all, genes = counts.shape
    cells = float(rows_all * lax.axis_size("cells"))
    groups = lax.axis_size("genes")
    hidden = enc_w.shape[1]
    latent = head_w.shape[1] // 2
    kinds = (small_w.shape[0] - latent) // 2
    share = rows_all // groups
    width = min(1024, rows_all)
    blocks = rows_all // width
    fast = groups == 8 and blocks == 8
    me = lax.axis_index("genes").astype(jnp.int32).reshape(1)
    gene_lines = -(-genes // 128)

    def turn(value):
        return value.transpose(0, 2, 1)

    x_t = counts.T
    noise_t = noise.T
    dec_t = turn(dec_w)
    head_t = head_w.T
    lib8 = library.reshape(blocks, width)
    batch_all = batch_ids.reshape(blocks, 1, width)
    batch_own = batch_ids.reshape(groups, 1, share)
    klw = jnp.broadcast_to(kl_weight.reshape(1, 1), (8, 128))

    own_block = pl.BlockSpec((1, 1, share), lambda i, m: (m[0], 0, 0))
    own_lanes = lambda rows: pl.BlockSpec((rows, share), lambda i, m: (0, m[0]))
    lane_block = lambda rows: pl.BlockSpec((rows, width), lambda i, *_: (0, i))
    full = lambda array: (array, whole(array.shape))
    new = lambda shape, dtype=F32: (shape, dtype, whole(shape))
    if fast:
        from_all = lambda rows: pl.BlockSpec((1, rows, width), lambda i, m: ((i ^ m[0]) // 2, 0, 0))
    else:
        from_all = lambda rows: pl.BlockSpec((1, rows, width), lambda i, m: (i, 0, 0))

    keep_part, send_part = call(
        enc_kernel,
        (groups,),
        [
            (me if fast else me & 1, None),
            (x_t, pl.BlockSpec((genes, share), lambda i, m: (0, i ^ m[0]))),
            full(enc_w),
        ],
        [
            ((groups // 2, hidden, share), F32, pl.BlockSpec((1, hidden, share), lambda i, m: (i // 2, 0, 0))),
            ((groups // 2, hidden, share), BF, pl.BlockSpec((1, hidden, share), lambda i, m: (i // 2, 0, 0))),
        ],
        scratch=[pltpu.VMEM((hidden, genes), BF)],
        scalars=1,
        flops=2 * rows_all * genes * hidden,
        moved=2 * rows_all * genes,
    )
    got = swap(send_part, "genes", 1)
    slot = pl.BlockSpec((1, hidden, share), lambda i, m: (0, 0, 0))
    if fast:
        mine = [(keep_part[k : k + 1] + got[k : k + 1].astype(F32)).astype(BF) for k in (2, 3, 1)]
        far = [swap(part, "genes", 2 * k) for part, k in zip(mine, (2, 3, 1))]
        kept = keep_part
        ready = mine[2]
    else:
        summed = lax.psum_scatter(
            keep_part + got.astype(F32),
            "genes",
            scatter_dimension=0,
            axis_index_groups=[list(range(c, groups, 2)) for c in range(2)],
            tiled=True,
        )
        zero = jnp.zeros((1, hidden, share), BF)
        kept, got, far = summed, zero, [zero] * 3
        ready = keep_part

    mask_late = after(gene_mask.reshape(1, genes), ready)
    aug, dec_n, par, lg_tab, dg_tab, enc_pieces, dec_pieces, lat_row, head_rows, head_bias, head_cols, norm_t = call(
        prep_kernel,
        (1,),
        [full(gene_par), full(mask_late), full(dec_t), full(small_w), full(head_t), full(norm_par)],
        [
            new((2 * genes, hidden + 16), BF),
            new((hidden, 2 * genes), BF),
            new((5, genes, 128)),
            new((COUNT_TOP, genes, 128)),
            new((COUNT_TOP, genes, 128)),
            new((3 * hidden, kinds), BF),
            new((3 * hidden, kinds + 48), BF),
            new((16, hidden)),
            new((32, hidden)),
            new((32, 128)),
            new((2 * hidden, 64), BF),
            new((hidden, 8)),
        ],
    )
    logc, x_kept, gam_cell, dig_acc, log_lines = call(
        lambda *refs: counts_kernel(16, min(512, width), *refs),
        (blocks,),
        [
            (x_t, lane_block(genes)),
            full(lg_tab),
            full(dg_tab),
            (par, pl.BlockSpec((None, genes, 128), lambda i: (4, 0, 0))),
        ],
        [
            ((genes, rows_all), BF, lane_block(genes)),
            ((genes, rows_all), BF, lane_block(genes)),
            new((blocks, width)),
            new((genes, 128)),
            new((8 * gene_lines, 128)),
        ],
        scratch=[pltpu.VMEM((genes, 128), F32)],
        flops=rows_all * genes * 30,
        moved=4 * rows_all * genes,
        mib=16,
    )
    enc_late = after(enc_pieces, log_lines)
    stat8 = whole((8, hidden))
    pre_enc, stat_enc = call(
        own_kernel,
        (1,),
        [(me, None), (kept, slot), (got, slot)]
        + [(part, slot) for part in far]
        + [(batch_own, own_block), full(enc_late)],
        [new((hidden, share)), new((8, hidden))],
        scalars=1,
        flops=2 * share * hidden * kinds * 3,
        moved=share * hidden * 16,
    )
    stat_enc = total(total(stat_enc, "genes"), "cells")

    pack, aff_own, kl_row = call(
        lambda *refs: latent_kernel(cells, latent, *refs),
        (1,),
        [
            (me, None),
            full(pre_enc),
            full(stat_enc),
            full(norm_t),
            full(head_rows),
            full(head_bias),
            (noise_t, own_lanes(latent)),
            (batch_own, own_block),
            full(dec_pieces),
        ],
        [new((32, share)), new((hidden, share), BF), new((1, share))],
        scalars=1,
    )
    near, far_pack = gather_genes(pack, fast, blocks, width)
    if fast:
        stat_dec = jnp.sum(near[:, 8:16, :hidden], axis=0) + jnp.sum(far_pack[:, 8:16, :hidden], axis=0)
    else:
        stat_dec = lax.psum(pack[8:16, :hidden], "genes")
    stat_dec = total(stat_dec, "cells")

    batch_spec = pl.BlockSpec((1, 1, width), lambda i, *_: (i, 0, 0))
    hid, phat_dec, lse, z_all = call(
        lambda *refs: decode_kernel(cells, latent, fast, *refs),
        (blocks,),
        [
            (me, None),
            (near, from_all(32)),
            (far_pack, from_all(32)),
            (noise_t, lane_block(latent)),
            (batch_all, batch_spec),
            full(stat_dec),
            full(norm_t),
            full(dec_pieces),
            (aug, pl.BlockSpec((genes, hidden + 16), lambda i, m: (0, 0))),
        ],
        [
            ((hidden, rows_all), BF, lane_block(hidden)),
            ((hidden, rows_all), F32, lane_block(hidden)),
            new((blocks, width)),
            ((16, rows_all), F32, lane_block(16)),
        ],
        scratch=[pltpu.VMEM((genes, width), F32)],
        scalars=1,
        flops=2 * rows_all * genes * hidden,
        moved=rows_all * hidden * 6,
    )
    lse_all = log_total_of(lse, "genes")

    aff_near, aff_far = gather_genes(after(aff_own, stat_dec), fast, blocks, width)
    fixed_rows = genes + kinds + 8 * gene_lines + 8
    (fixed,) = call(
        lambda *refs: enc_sums_kernel(fast, *refs),
        (blocks,),
        [
            (me, None),
            (logc, lane_block(genes)),
            (aff_near, from_all(hidden)),
            (aff_far, from_all(hidden)),
            (batch_all, batch_spec),
            full(log_lines),
        ],
        [new((fixed_rows, hidden))],
        scalars=1,
    )
    fixed = total_by_halves(fixed, "cells", (1, 2))

    full8 = whole((blocks, width))
    gm, gd, rt, mass, recon, gene_acc = call(
        lambda *refs: zinb_kernel(32, min(512, width), *refs),
        (blocks,),
        [
            (hid, lane_block(hidden)),
            full(aug),
            (x_kept, lane_block(genes)),
            (par, pl.BlockSpec((4, genes, 128), lambda i: (0, 0, 0))),
            full(lib8),
            full(lse_all),
            full(gam_cell),
        ],
        [((genes, rows_all), BF, lane_block(genes))] * 3
        + [new((blocks, width)), new((blocks, width)), new((3, genes, 128))],
        scratch=[pltpu.VMEM((2 * genes, width), F32)],
        flops=rows_all * genes * 200,
        moved=8 * rows_all * genes,
        mib=20,
    )
    mass = total(mass, "genes")
    part_a, part_r, dec_acc = call(
        back_kernel,
        (blocks,),
        [
            (gm, lane_block(genes)),
            (gd, lane_block(genes)),
            (rt, lane_block(genes)),
            (hid, lane_block(hidden)),
            full(dec_n),
        ],
        [
            ((hidden, rows_all), F32, lane_block(hidden)),
            ((hidden, rows_all), F32, lane_block(hidden)),
            new((2 * genes, hidden)),
        ],
        flops=2 * rows_all * genes * hidden * 5,
        moved=8 * rows_all * genes,
        mib=16,
    )

    dy_dec, keep_d, send_d = call(
        lambda *refs: hidden_grad_kernel(cells, latent, *refs),
        (blocks,),
        [
            (me if fast else jnp.zeros_like(me), None),
            (part_a, lane_block(hidden)),
            (part_r, lane_block(hidden)),
            (mass, full8),
            (hid, lane_block(hidden)),
            (phat_dec, lane_block(hidden)),
            full(lib8),
            full(stat_dec),
            full(norm_par),
            full(lat_row),
            full(recon),
        ],
        [
            ((hidden, rows_all), F32, lane_block(hidden)),
            new((blocks // 2, 16, width)),
            new((blocks // 2, 16, width)),
        ],
        scratch=[pltpu.VMEM((2, hidden, 128), F32)],
        scalars=1,
    )
    if fast:
        got_d = swap(send_d, "genes", 1)
        pieces = [swap(keep_d[k] + got_d[k], "genes", 2 * k) for k in (1, 2, 3)]
        own_d = (keep_d[0] + got_d[0] + pieces[0]) + (pieces[1] + pieces[2])
        sums_dec = own_d[8:, :hidden]
    else:
        both = jnp.stack([keep_d, send_d], axis=1).reshape(blocks, 16, width)
        sums_dec = lax.psum(both[0, 8:, :hidden], "genes")
        both = both.transpose(1, 0, 2).reshape(16, groups, share).transpose(1, 0, 2)
        own_d = lax.psum_scatter(both, "genes", scatter_dimension=0, tiled=True)[0]
    sums_dec = total(sums_dec, "cells")
    d_near, d_far = gather_genes(own_d, fast, blocks, width)
    dec_part, oh_part = call(
        lambda *refs: dec_grad_kernel(cells, *refs),
        (blocks,),
        [
            (rt, lane_block(genes)),
            (hid, lane_block(hidden)),
            (mass, full8),
            full(lib8),
            (dy_dec, lane_block(hidden)),
            (z_all, lane_block(16)),
            (batch_all, batch_spec),
            full(dec_acc),
            full(gene_acc),
            full(dig_acc),
            (par, pl.BlockSpec((None, genes, 128), lambda i: (1, 0, 0))),
        ],
        [new((2 * genes + 8 * gene_lines, hidden)), new((kinds + 16, hidden))],
        scratch=[pltpu.VMEM((genes, hidden + 16), F32)],
    )
    oh_part = total(oh_part, "genes")
    dec_g = total_by_halves(dec_part, "cells", (2, 1))

    rest_rows = 2 * kinds + 16 + 32 + 16
    enc_part, rest = call(
        lambda *refs: enc_back_kernel(cells, latent, fast, *refs),
        (blocks,),
        [
            (me, None),
            (d_near, from_all(16)),
            (d_far, from_all(16)),
            (phat_dec, lane_block(hidden)),
            full(sums_dec),
            full(stat_dec),
            full(norm_par),
            full(lat_row),
            (near, from_all(32)),
            (far_pack, from_all(32)),
            (noise_t, lane_block(latent)),
            full(klw),
            (aff_near, from_all(hidden)),
            (aff_far, from_all(hidden)),
            (batch_all, batch_spec),
            (logc, lane_block(genes)),
            full(head_cols),
            (z_all, lane_block(16)),
        ],
        [new((genes, hidden)), new((rest_rows, hidden))],
        scratch=[pltpu.VMEM((2, hidden, 128), F32)],
        scalars=1,
        flops=2 * rows_all * genes * hidden,
        moved=2 * rows_all * genes,
    )
    rest = jnp.concatenate([rest[: kinds + 48], rest[kinds + 48 :] + oh_part])
    enc_sum = total_by_halves(enc_part, "cells", (1, 2))
    rest = total_by_halves(rest, "cells", (2, 1))

    enc_g, small_g, head_g, norm_g, square, loss = call(
        lambda *refs: finish_kernel(cells, latent, *refs),
        (1,),
        [full(a) for a in (enc_sum, rest, dec_g, fixed, stat_enc, stat_dec, sums_dec, norm_par, kl_row, klw, own_d)],
        [
            new((genes, hidden)),
            new((2 * kinds + 16, hidden)),
            new((2 * latent, hidden + 1)),
            new((4, hidden)),
            new((8, 128)),
            new((1, share)),
        ],
    )
    square = total(square, "genes")

    state = [
        enc_w, enc_m, enc_v, dec_t, turn(dec_m), turn(dec_v), gene_par, gene_m, gene_v,
        small_w, small_m, small_v, head_t, head_m.T, head_v.T, norm_par, norm_m, norm_v,
    ]
    ins = [square, enc_g, dec_g, small_g, head_g, norm_g] + state
    outs = []
    for index in range(6):
        one = state[3 * index]
        outs += [(one.shape, F32)] * 3
        if index < 2:
            outs.append((one.shape, BF))
    outs.append(((8, 128), F32))
    res = call(
        lambda *refs: update_kernel(latent, *refs),
        (1,),
        [full(array) for array in ins],
        [new(shape, dtype) for shape, dtype in outs],
        mib=16,
    )
    enc_res, dec_res = res[0:4], [turn(part) for part in res[4:8]]
    head_res = [part.T for part in res[14:17]]
    return (
        *enc_res,
        *dec_res,
        *res[8:14],
        *head_res,
        *res[17:20],
        res[20][0, 0],
        loss.reshape(share),
    )


def solution(mesh):
    placed = (
        P("cells", "genes"), P("cells"), P("cells", None), P("cells"), P("genes"), P(),
        P("genes", None), P("genes", None), P("genes", None),
        P(None, None, "genes"), P(None, None, "genes"), P(None, None, "genes"),
        P(None, "genes"), P(None, "genes"), P(None, "genes"),
        P(), P(), P(), P(), P(), P(), P(), P(), P(),
    )
    return jax.shard_map(
        per_device,
        mesh=mesh,
        in_specs=placed,
        out_specs=(
            P("genes", None), P("genes", None), P("genes", None), P("genes", None),
            P(None, None, "genes"), P(None, None, "genes"), P(None, None, "genes"), P(None, None, "genes"),
            P(None, "genes"), P(None, "genes"), P(None, "genes"),
            P(), P(), P(), P(), P(), P(), P(), P(), P(), P(),
            P(("cells", "genes")),
        ),
        check_vma=False,
    )
```

```python
import jax
import jax.numpy as jnp
from jax import lax
from jax.experimental import pallas as pl
from jax.experimental.pallas import tpu as pltpu
from jax.sharding import PartitionSpec as P

norm_epsilon = 0.001
zinb_epsilon = 1e-08
beta_one = 0.9
beta_two = 0.999
step_number = 5.0
decay_rate = 0.01
rate_genes = 0.03
rate_small = 0.2
max_norm = 0.1

F32 = jnp.float32
BF = jnp.bfloat16
HI = lax.Precision.HIGHEST
COUNT_TOP = 8
LOG2_E = 1.4426950408889634


def nn(left, right, precision=None):
    return lax.dot_general(
        left, right, (((1,), (0,)), ((), ())), precision=precision, preferred_element_type=F32
    )


def nt(left, right, precision=None):
    return lax.dot_general(
        left, right, (((1,), (1,)), ((), ())), precision=precision, preferred_element_type=F32
    )


def whole(shape):
    return pl.BlockSpec(shape, lambda *_: (0,) * len(shape))


def call(kernel, grid, ins, outs, scratch=(), scalars=0, us=2.0, mib=12):
    return pl.pallas_call(
        kernel,
        out_shape=[jax.ShapeDtypeStruct(shape, dtype) for shape, dtype, _ in outs],
        grid_spec=pltpu.PrefetchScalarGridSpec(
            num_scalar_prefetch=scalars,
            grid=grid,
            in_specs=[spec for _, spec in ins[scalars:]],
            out_specs=[spec for _, _, spec in outs],
            scratch_shapes=list(scratch),
        ),
        compiler_params=pltpu.CompilerParams(vmem_limit_bytes=mib * 1024 * 1024),
        cost_estimate=pl.CostEstimate(flops=0, bytes_accessed=int(us * 3.69e6), transcendentals=0),
    )(*[array for array, _ in ins])


def swap(value, axis, bit):
    count = lax.axis_size(axis)
    return lax.ppermute(value, axis, [(i, i ^ bit) for i in range(count)])


def bit_groups(axis):
    count = lax.axis_size(axis)
    if axis == "genes":
        groups, bit = [[1]], 2
    else:
        groups, bit = [], 1
    while bit < count:
        groups.append([bit, 2 * bit] if 2 * bit < count else [bit])
        bit *= 4
    return groups


def total(value, axis):
    for group in bit_groups(axis):
        if len(group) == 1:
            value = value + swap(value, axis, group[0])
        else:
            low, high = group
            value = (value + swap(value, axis, low)) + (
                swap(value, axis, high) + swap(value, axis, low ^ high)
            )
    return value


def log_total_of(value, axis):
    for group in bit_groups(axis):
        if len(group) == 1:
            parts = [value, swap(value, axis, group[0])]
        else:
            low, high = group
            parts = [value] + [swap(value, axis, k) for k in (low, high, low ^ high)]
        top = parts[0]
        for part in parts[1:]:
            top = jnp.maximum(top, part)
        mass = sum(jnp.exp(part - top) for part in parts)
        value = top + jnp.log(mass)
    return value


def total_by_halves(value, axis, order):
    for bit in order:
        value = value + swap(value, axis, bit)
    return value


def after(value, *others):
    return lax.optimization_barrier((value,) + others)[0]


def three(value):
    high = value.astype(BF)
    rest = value - high.astype(F32)
    mid = rest.astype(BF)
    low = (rest - mid.astype(F32)).astype(BF)
    return high, mid, low


def one_hot(batch_row, kinds):
    ids = lax.broadcasted_iota(jnp.int32, (kinds, batch_row.shape[1]), 0)
    return jnp.where(ids == batch_row, 1.0, 0.0)


def columns(rows):
    return jnp.transpose(rows)


def prep_kernel(gene_ref, mask_ref, dec_ref, small_ref, head_ref, norm_ref, aug_ref, turn_ref, par_ref, lg_ref, dg_ref, enc_out, dec_out, lat_out, head_out, bias_out, cols_out, norm_out):
    genes = gene_ref.shape[1]
    hidden = norm_ref.shape[1]
    latent = head_ref.shape[0] // 2
    kinds = (small_ref.shape[0] - latent) // 2
    padded = pl.cdiv(genes, 128) * 128
    keep = mask_ref[...] > 0
    score_b = jnp.where(keep, gene_ref[0:1], -1e30)
    drop_b = jnp.where(keep, gene_ref[1:2], 1e30)
    th = jnp.exp(gene_ref[2:3])
    kept = jnp.where(keep, 1.0, 0.0)
    rows = jnp.concatenate((score_b, drop_b, th, kept, th, th, th, th), axis=0)
    if padded > genes:
        rows = jnp.concatenate((rows, jnp.ones((8, padded - genes), F32)), axis=1)
    turned = jnp.transpose(rows)[:genes]
    lane = lax.broadcasted_iota(jnp.int32, (genes, 16), 1)
    for half in range(2):
        at = slice(half * genes, (half + 1) * genes)
        aug_ref[at, 0:hidden] = dec_ref[half].astype(BF)
        high, mid, low = (jnp.broadcast_to(part.astype(F32), (genes, 16)) for part in three(turned[:, half : half + 1]))
        tail = jnp.where(lane == 0, high, jnp.where(lane == 1, mid, jnp.where(lane == 2, low, 0.0)))
        if half == 0:
            tail = jnp.where((lane >= 3) & (lane < 6), 1.0, tail)
        aug_ref[at, hidden : hidden + 16] = tail.astype(BF)
        turn_ref[:, at] = jnp.transpose(dec_ref[half]).astype(BF)
    th_w = jnp.broadcast_to(turned[:, 2:3], (genes, 128))
    keep_w = jnp.broadcast_to(turned[:, 3:4], (genes, 128))
    the_w = th_w + zinb_epsilon
    par_ref[0] = the_w
    par_ref[1] = th_w
    par_ref[2] = jnp.log(the_w)
    par_ref[3] = th_w / the_w
    par_ref[4] = keep_w
    gam = jnp.zeros_like(th_w)
    dig = jnp.zeros_like(th_w)
    for k in range(COUNT_TOP):
        more = th_w + float(k)
        gam = gam + keep_w * jnp.log(more * (1.0 / (1.0 + k)))
        dig = dig + keep_w / more
        lg_ref[k] = gam
        dg_ref[k] = dig
    for index, piece in enumerate(three(jnp.transpose(small_ref[0:kinds, :]))):
        enc_out[index * hidden : (index + 1) * hidden, :] = piece
    row = lax.broadcasted_iota(jnp.int32, (16, hidden), 0)
    lat_row = jnp.zeros((16, hidden), F32)
    for index in range(latent):
        lat_row = jnp.where(row == index, small_ref[2 * kinds + index : 2 * kinds + index + 1, :], lat_row)
    lat_out[...] = lat_row
    batch_pieces = three(jnp.transpose(small_ref[kinds : 2 * kinds, :]))
    lat = three(jnp.transpose(lat_row))
    zero = jnp.zeros_like(lat[0])
    tails = ((lat[0], lat[0], lat[0]), (lat[1], lat[1], zero), (lat[2], zero, zero))
    for index in range(3):
        at = slice(index * hidden, (index + 1) * hidden)
        dec_out[at, :] = jnp.concatenate((batch_pieces[index],) + tails[index], axis=1)
    full = lax.broadcasted_iota(jnp.int32, (32, hidden), 0)
    head = jnp.zeros((32, hidden), F32)
    bias = jnp.zeros((32, 1), F32)
    for index in range(2 * latent):
        to = index if index < latent else index - latent + 16
        head = jnp.where(full == to, head_ref[index : index + 1, 0:hidden], head)
        bias = jnp.where(full[:, 0:1] == to, head_ref[index : index + 1, hidden : hidden + 1], bias)
    head_out[...] = head
    bias_out[...] = jnp.broadcast_to(bias, (32, 128))
    high, mid, _ = three(jnp.transpose(head))
    cols_out[0:hidden, :] = jnp.concatenate((high, high), axis=1)
    cols_out[hidden : 2 * hidden, :] = jnp.concatenate((mid, jnp.zeros_like(mid)), axis=1)
    norm_out[...] = jnp.transpose(jnp.concatenate((norm_ref[...], norm_ref[...]), axis=0))


def exact_rows(stacked, table):
    out = nn(stacked, table)
    hidden = out.shape[0] // 3
    return out[:hidden] + out[hidden : 2 * hidden] + out[2 * hidden :]


def dec_table(z, batch_row, kinds):
    high, mid, low = three(z)
    return jnp.concatenate((one_hot(batch_row, kinds).astype(BF), high, mid, low), axis=0)


def row_sums(value):
    return nt(jnp.ones((8, value.shape[1]), F32), value, HI)


def stat_rows(first, second, at):
    sums, squares = row_sums(first), row_sums(second)
    row = lax.broadcasted_iota(jnp.int32, sums.shape, 0)
    return jnp.where(row == at, sums, jnp.where(row == at + 1, squares, 0.0))


def enc_kernel(me_ref, x_ref, w_ref, keep_ref, send_ref, turn_ref):
    step = pl.program_id(0)

    @pl.when(step == 0)
    def _():
        turn_ref[...] = jnp.transpose(w_ref[...]).astype(BF)

    log_counts = jnp.log(1.0 + x_ref[...].astype(F32)).astype(BF)
    part = nn(turn_ref[...], log_counts)
    odd = lax.rem(step, 2)

    @pl.when(odd == 0)
    def _():
        keep_ref[0] = part

    @pl.when(odd == 1)
    def _():
        send_ref[0] = part.astype(BF)


def lines(rows8, count):
    wide = rows8.shape[1]
    if wide < 128 * count:
        rows8 = jnp.concatenate((rows8, jnp.zeros((8, 128 * count - wide), F32)), axis=1)
    return jnp.concatenate([rows8[:, i * 128 : (i + 1) * 128] for i in range(count)], axis=0)


def counts_kernel(rows, span, x_ref, lg_ref, dg_ref, keep_ref, logc_ref, mask_ref, cell_ref, disp_ref, line_ref, sum_ref):
    step = pl.program_id(0)
    genes, width = x_ref.shape

    @pl.when(step == 0)
    def _():
        disp_ref[...] = jnp.zeros_like(disp_ref)
        sum_ref[...] = jnp.zeros_like(sum_ref)

    tiles = span // 128
    done = []
    for first in range(0, width, span):
        lanes = [slice(first + tile * 128, first + (tile + 1) * 128) for tile in range(tiles)]

        def chunk(g, cell):
            at = pl.ds(pl.multiple_of(g * rows, rows), rows)
            keep = keep_ref[at, :]
            xs = [x_ref[at, lanes[tile]].astype(F32) for tile in range(tiles)]
            logs = [jnp.log(1.0 + x) for x in xs]
            for tile in range(tiles):
                logc_ref[at, lanes[tile]] = logs[tile].astype(BF)
                mask_ref[at, lanes[tile]] = (xs[tile] * keep).astype(BF)
            sum_ref[at, :] += sum(part.astype(BF).astype(F32) for part in logs)
            gams = [jnp.zeros_like(xs[0]) for _ in range(tiles)]
            digs = [jnp.zeros_like(xs[0]) for _ in range(tiles)]
            for k in range(COUNT_TOP):
                lg, dg = lg_ref[k, at, :], dg_ref[k, at, :]
                for tile in range(tiles):
                    more = xs[tile] > (k + 0.5)
                    gams[tile] = jnp.where(more, lg, gams[tile])
                    digs[tile] = jnp.where(more, dg, digs[tile])
            disp_ref[at, :] += sum(digs)
            out = []
            for tile in range(tiles):
                folded = cell[tile]
                for part in range(rows // 8):
                    folded = folded + gams[tile][part * 8 : (part + 1) * 8]
                out.append(folded)
            return tuple(out)

        zero = tuple(jnp.zeros((8, 128), F32) for _ in range(tiles))
        done += list(lax.fori_loop(0, genes // rows, chunk, zero))
    cell_ref[pl.ds(step, 1), :] = jnp.sum(jnp.concatenate(done, axis=1), axis=0, keepdims=True)

    @pl.when(step == pl.num_programs(0) - 1)
    def _():
        line_ref[...] = lines(row_sums(sum_ref[...]), line_ref.shape[0] // 8)


def own_kernel(me_ref, keep_ref, got_ref, one_ref, two_ref, six_ref, batch_ref, enc_b_ref, pre_ref, stat_ref):
    kinds = enc_b_ref.shape[1]
    gathered = (keep_ref[0] + got_ref[0].astype(F32) + one_ref[0].astype(F32)) + (
        two_ref[0].astype(F32) + six_ref[0].astype(F32)
    )
    table = one_hot(batch_ref[0], kinds).astype(BF)
    pre = gathered + exact_rows(enc_b_ref[...], table)
    pre_ref[...] = pre
    stat_ref[...] = stat_rows(pre, pre * pre, 0)


def norm_columns(stat, first, cells):
    turned = jnp.transpose(stat)
    mean = turned[:, first : first + 1] / cells
    var = turned[:, first + 1 : first + 2] / cells - mean * mean
    return mean, lax.rsqrt(var + norm_epsilon)


def norm_rows(stat, first, cells):
    mean = stat[first : first + 1] / cells
    var = stat[first + 1 : first + 2] / cells - mean * mean
    return mean, lax.rsqrt(var + norm_epsilon)


def latent_kernel(cells, latent, me_ref, pre_ref, stat_ref, norm_ref, head_ref, bias_ref, noise_ref, batch_ref, dec_b_ref, pack_ref, aff_ref, kl_ref):
    kinds = dec_b_ref.shape[1] - 48
    hidden = pre_ref.shape[0]
    mean, inv = norm_columns(stat_ref[...], 0, cells)
    phat = (pre_ref[...] - mean) * inv
    affine = norm_ref[:, 0:1] * phat + norm_ref[:, 1:2]
    out = nn(head_ref[...], jnp.maximum(affine, 0.0), HI) + bias_ref[:, 0:1]
    lat_mean, lat_logvar = out[:latent], out[16 : 16 + latent]
    high, mid, low = three(latent_rows(lat_logvar))
    aff_ref[...] = jnp.concatenate((affine.astype(BF), high, mid, low), axis=0)
    var = jnp.exp(lat_logvar) + 0.0001
    z = latent_rows(lat_mean + jnp.sqrt(var) * noise_ref[...])
    terms = var + lat_mean * lat_mean - 1.0 - jnp.log(var)
    kl_ref[...] = 0.5 * jnp.sum(terms, axis=0, keepdims=True)
    pre_dec = exact_rows(dec_b_ref[...], dec_table(z, batch_ref[0], kinds))
    stat = stat_rows(pre_dec, pre_dec * pre_dec, 0)
    pack_ref[...] = z
    pack_ref[latent : latent + 1, 0:hidden] = stat[0:1]
    pack_ref[latent + 1 : latent + 2, 0:hidden] = stat[1:2]


def latent_rows(z):
    if z.shape[0] == 16:
        return z
    return jnp.concatenate((z, jnp.zeros((16 - z.shape[0], z.shape[1]), F32)), axis=0)


def pick(step, me_ref, fast, near_ref, far_ref):
    if not fast:
        return near_ref[0]
    return jnp.where(lax.rem(step ^ me_ref[0], 2) == 0, near_ref[0], far_ref[0])


def decode_kernel(cells, latent, fast, me_ref, near_ref, far_ref, batch_ref, stat_ref, norm_ref, dec_b_ref, w_ref, hid_ref, phat_ref, lse_ref, z_ref, score_ref):
    kinds = dec_b_ref.shape[1] - 48
    step = pl.program_id(0)
    genes = score_ref.shape[0]
    mean, inv = norm_columns(stat_ref[...], latent - 8, cells)
    z = pick(step, me_ref, fast, near_ref, far_ref)
    z = jnp.where(lax.broadcasted_iota(jnp.int32, z.shape, 0) < latent, z, 0.0)
    z_ref[...] = z
    pre_dec = exact_rows(dec_b_ref[...], dec_table(z, batch_ref[0], kinds))
    phat = (pre_dec - mean) * inv
    phat_ref[...] = phat
    hidden = jnp.maximum(norm_ref[:, 2:3] * phat + norm_ref[:, 3:4], 0.0).astype(BF)
    hid_ref[...] = hidden
    width = score_ref.shape[1]
    row = lax.broadcasted_iota(jnp.int32, (16, width), 0)
    table = jnp.concatenate((hidden, jnp.where(row < 3, 1.0, 0.0).astype(BF)), axis=0)
    score_ref[...] = nn(w_ref[...], table)
    tiles = width // 128
    rows = 32

    def top(g, best):
        at = pl.ds(pl.multiple_of(g * rows, rows), rows)
        new = []
        for tile in range(tiles):
            value = score_ref[at, slice(tile * 128, (tile + 1) * 128)]
            part = best[tile]
            for index in range(rows // 8):
                part = jnp.maximum(part, value[index * 8 : (index + 1) * 8])
            new.append(part)
        return tuple(new)

    best = lax.fori_loop(0, genes // rows, top, tuple(jnp.full((8, 128), -3e38, F32) for _ in range(tiles)))
    high = [jnp.max(part, axis=0, keepdims=True) for part in best]
    wide = [jnp.broadcast_to(part, (8, 128)) for part in high]

    def mass(g, sums):
        at = pl.ds(pl.multiple_of(g * rows, rows), rows)
        new = []
        for tile in range(tiles):
            value = score_ref[at, slice(tile * 128, (tile + 1) * 128)]
            part = sums[tile]
            for index in range(rows // 8):
                part = part + jnp.exp(value[index * 8 : (index + 1) * 8] - wide[tile])
            new.append(part)
        return tuple(new)

    sums = lax.fori_loop(0, genes // rows, mass, tuple(jnp.zeros((8, 128), F32) for _ in range(tiles)))
    lse = [high[tile] + jnp.log(jnp.sum(sums[tile], axis=0, keepdims=True)) for tile in range(tiles)]
    lse_ref[pl.ds(step, 1), :] = jnp.concatenate(lse, axis=1)


def enc_sums_kernel(fast, me_ref, logc_ref, near_ref, far_ref, batch_ref, lines_ref, out_ref):
    step = pl.program_id(0)
    genes = logc_ref.shape[0]
    kinds = out_ref.shape[0] - genes - lines_ref.shape[0] - 8

    @pl.when(step == 0)
    def _():
        out_ref[...] = jnp.zeros_like(out_ref)
        out_ref[genes + kinds : genes + kinds + lines_ref.shape[0], :] = lines_ref[...]

    affine = pick(step, me_ref, fast, near_ref, far_ref)[: out_ref.shape[1]]
    table = one_hot(batch_ref[0], kinds).astype(BF)
    out_ref[0:genes, :] += nt(logc_ref[...], affine)
    out_ref[genes : genes + kinds, :] += nt(table, affine)
    out_ref[genes + kinds + lines_ref.shape[0] :, :] += nt(jnp.ones((8, table.shape[1]), BF), table)


def zinb_kernel(rows, span, hid_ref, w_ref, x_ref, par_ref, lib_ref, lse_ref, gam_ref, gm_ref, gd_ref, rt_ref, mass_ref, recon_ref, acc_ref, sc_ref):
    step = pl.program_id(0)
    genes, width = x_ref.shape

    @pl.when(step == 0)
    def _():
        acc_ref[...] = jnp.zeros_like(acc_ref)

    one_row = pl.ds(step, 1)
    gam_row = gam_ref[one_row, :]
    shift = lib_ref[one_row, :] - lse_ref[one_row, :]
    row = lax.broadcasted_iota(jnp.int32, (16, width), 0)
    hi, mid, lo = three(shift)
    extra = jnp.where(row < 3, 1.0, jnp.where(row == 3, hi.astype(F32), jnp.where(row == 4, mid.astype(F32), jnp.where(row == 5, lo.astype(F32), 0.0))))
    table = jnp.concatenate((hid_ref[...], extra.astype(BF)), axis=0)
    sc_ref[...] = nn(w_ref[...], table)
    tiles = span // 128
    mass_out, recon_out = [], []
    for first in range(0, width, span):
        lanes = [slice(first + tile * 128, first + (tile + 1) * 128) for tile in range(tiles)]
        def chunk(g, state):
            at = pl.ds(pl.multiple_of(g * rows, rows), rows)
            at_drop = pl.ds(pl.multiple_of(genes + g * rows, rows), rows)
            the, th, log_the, part_th = (par_ref[i, at, :] for i in range(4))
            sums = [acc_ref[i, at, :] for i in range(3)]
            new = []
            for tile in range(tiles):
                rec, prod, back = state[tile]
                x = x_ref[at, lanes[tile]].astype(F32)
                mu = jnp.exp(sc_ref[at, lanes[tile]])
                drop = sc_ref[at_drop, lanes[tile]]
                both = mu + the
                r = 1.0 / both
                log_both = jnp.log(both)
                gap = log_the - log_both
                th_gap = th * gap
                u = jnp.where(x < 0.5, th_gap - drop, 1e30)
                eu = jnp.exp2(jnp.abs(u) * (-LOG2_E))
                ed = jnp.exp2(jnp.abs(drop) * (-LOG2_E))
                den = 1.0 + eu
                mu_eps = mu + zinb_epsilon
                rd = 1.0 / (1.0 + ed)
                w0 = jnp.where(u >= 0.0, 1.0, eu) * (1.0 / den)
                term = (th_gap - jnp.maximum(drop, 0.0)) + (x * (jnp.log(mu_eps) - log_both) - jnp.minimum(u, 0.0))
                factor = den * rd
                y = (x + w0 * th) * r
                g_mean = mu * (x * (1.0 / mu_eps) - y)
                g_drop = jnp.where(drop >= 0.0, ed, 1.0) * rd - w0
                g_disp = w0 * (gap + part_th) - y
                gm_ref[at, lanes[tile]] = g_mean.astype(BF)
                gd_ref[at, lanes[tile]] = g_drop.astype(BF)
                rt_ref[at, lanes[tile]] = mu.astype(BF)
                sums = [a + b for a, b in zip(sums, (g_mean, g_drop, g_disp))]
                for part in range(rows // 8):
                    sub = slice(part * 8, (part + 1) * 8)
                    rec = rec + term[sub]
                    prod = prod * factor[sub]
                    back = back + g_mean[sub]
                new.append((rec, prod, back))
            for i in range(3):
                acc_ref[i, at, :] = sums[i]
            return tuple(new)
        zero = jnp.zeros((8, 128), F32)
        state = tuple((zero, zero + 1.0, zero) for _ in range(tiles))
        state = lax.fori_loop(0, genes // rows, chunk, state)
        for tile in range(tiles):
            rec, prod, back = state[tile]
            mass_out.append(jnp.sum(back, axis=0, keepdims=True))
            recon_out.append(jnp.sum(rec + jnp.log(prod), axis=0, keepdims=True))
    mass_ref[one_row, :] = jnp.concatenate(mass_out, axis=1)
    recon_ref[one_row, :] = jnp.concatenate(recon_out, axis=1) + gam_row


def back_kernel(gm_ref, gd_ref, rt_ref, hid_ref, w_ref, a_ref, r_ref, g_ref):
    genes = gm_ref.shape[0]

    @pl.when(pl.program_id(0) == 0)
    def _():
        g_ref[...] = jnp.zeros_like(g_ref)

    gm, gd, rt, hid = gm_ref[...], gd_ref[...], rt_ref[...], hid_ref[...]
    scale_w = w_ref[:, :genes]
    a_ref[...] = nn(scale_w, gm) + nn(w_ref[:, genes:], gd)
    r_ref[...] = nn(scale_w, rt)
    g_ref[:genes, :] += nt(gm, hid)
    g_ref[genes:, :] += nt(gd, hid)


def hidden_grad_kernel(cells, latent, me_ref, a_ref, r_ref, mass_ref, hid_ref, phat_ref, lib_ref, stat_ref, gain_ref, lat_ref, recon_ref, z_ref, batch_ref, keep_ref, send_ref, sum_ref, oh_ref):
    step = pl.program_id(0)
    steps = pl.num_programs(0)
    place = step ^ me_ref[0]

    @pl.when(step == 0)
    def _():
        sum_ref[...] = jnp.zeros_like(sum_ref)
        oh_ref[...] = jnp.zeros_like(oh_ref)

    back = mass_ref[pl.ds(step, 1), :] * jnp.exp(-lib_ref[pl.ds(step, 1), :])
    dy = jnp.where(hid_ref[...] > 0, (a_ref[...] - back * r_ref[...]) * (-1.0 / cells), 0.0)
    hidden, width = dy.shape
    weighted = dy * phat_ref[...]
    first, second = dy[:, :128], weighted[:, :128]
    for tile in range(1, width // 128):
        lanes = slice(tile * 128, (tile + 1) * 128)
        first = first + dy[:, lanes]
        second = second + weighted[:, lanes]
    sum_ref[0] += first
    sum_ref[1] += second
    _, inv = norm_rows(stat_ref[...], latent - 8, cells)
    lat = lat_ref[...] * (gain_ref[2:3] * inv)
    lat_high, lat_mid, _ = three(lat)
    dy_high, dy_mid, _ = three(dy)
    table = jnp.concatenate((dy_high, dy_mid), axis=0)
    left = jnp.concatenate(
        (
            jnp.concatenate((lat_high, lat_high), axis=1),
            jnp.concatenate((lat_mid, jnp.zeros_like(lat_mid)), axis=1),
        ),
        axis=0,
    )
    kinds = oh_ref.shape[0] - 16
    z_high, z_mid, _ = three(z_ref[...])
    held = jnp.concatenate((one_hot(batch_ref[0], kinds).astype(BF), z_high, z_mid), axis=0)
    product = nt(held, table)
    product = product[:, :hidden] + product[:, hidden:]
    oh_ref[:kinds, :] += product[:kinds]
    oh_ref[kinds:, :] += product[kinds : kinds + 16] + product[kinds + 16 :]
    both = nn(left, table)
    block = both[:16] + both[16:]
    row = lax.broadcasted_iota(jnp.int32, block.shape, 0)
    block = jnp.where(row == latent, recon_ref[pl.ds(step, 1), :], block)
    slot = lax.div(place, 2)

    @pl.when(lax.rem(place, 2) == 0)
    def _():
        keep_ref[slot] = block

    @pl.when(lax.rem(place, 2) == 1)
    def _():
        send_ref[slot] = block

    @pl.when(step == steps - 1)
    def _():
        one, two = row_sums(sum_ref[0]), row_sums(sum_ref[1])
        part = oh_ref.shape[0] // steps
        for core, ref in enumerate((keep_ref, send_ref)):
            for index in range(ref.shape[0]):
                ref[index, latent + 1 : latent + 2, 0:hidden] = one[0:1]
                ref[index, latent + 2 : latent + 3, 0:hidden] = two[0:1]
                owner = me_ref[0] ^ (2 * index + core)
                for k in range(part):
                    line = latent + 3 + k // 8
                    lanes = slice((k % 8) * hidden, (k % 8 + 1) * hidden)
                    ref[index, line : line + 1, lanes] = oh_ref[pl.ds(owner * part + k, 1), :]


def dec_grad_kernel(cells, rt_ref, hid_ref, mass_ref, lib_ref, g_ref, acc_ref, dig_ref, th_ref, dec_ref, mix_ref):
    step = pl.program_id(0)
    steps = pl.num_programs(0)
    genes = rt_ref.shape[0]
    hidden = hid_ref.shape[0]

    @pl.when(step == 0)
    def _():
        mix_ref[...] = jnp.zeros_like(mix_ref)

    back = mass_ref[pl.ds(step, 1), :] * jnp.exp(-lib_ref[pl.ds(step, 1), :])
    back_high, back_mid, back_low = three(back)
    row = lax.broadcasted_iota(jnp.int32, (16, back.shape[1]), 0)
    extra = jnp.where(row == 0, back_high.astype(F32), jnp.where(row == 1, back_mid.astype(F32), 0.0))
    scaled = (hid_ref[...].astype(F32) * back).astype(BF)
    mix_ref[...] += nt(rt_ref[...], jnp.concatenate((scaled, extra.astype(BF)), axis=0))

    @pl.when(step == steps - 1)
    def _():
        scale = -1.0 / cells
        mix = mix_ref[...]
        dec_ref[:genes, :] = (g_ref[:genes, :] - mix[:, :hidden]) * scale
        dec_ref[genes : 2 * genes, :] = g_ref[genes:, :] * scale
        pick = jnp.where(lax.broadcasted_iota(jnp.int32, (8, 16), 1) < 2, 1.0, 0.0)
        score_row = row_sums(acc_ref[0]) - nt(pick, mix[:, hidden:], HI)
        drop_row = row_sums(acc_ref[1])
        disp_row = row_sums((acc_ref[2] + dig_ref[...]) * th_ref[...])
        line = lax.broadcasted_iota(jnp.int32, score_row.shape, 0)
        gene_rows = scale * jnp.where(
            line == 0, score_row, jnp.where(line == 1, drop_row, jnp.where(line == 2, disp_row, 0.0))
        )
        dec_ref[2 * genes :, :] = lines(gene_rows, pl.cdiv(genes, 128))


def enc_back_kernel(cells, latent, fast, me_ref, own_ref, dnear_ref, dfar_ref, phat_ref, sums_ref, stat_ref, gain_ref, lat_ref, noise_ref, klw_ref, anear_ref, afar_ref, batch_ref, logc_ref, cols_ref, z_ref, out_ref, rest_ref, lane_ref):
    step = pl.program_id(0)
    genes, width = logc_ref.shape
    hidden = phat_ref.shape[0]
    kinds = (rest_ref.shape[0] - 64) // 2
    steps = pl.num_programs(0)

    @pl.when(step == 0)
    def _():
        out_ref[...] = jnp.zeros_like(out_ref)
        rest_ref[...] = jnp.zeros_like(rest_ref)
        lane_ref[...] = jnp.zeros_like(lane_ref)

    block = pick(step, me_ref, fast, dnear_ref, dfar_ref)
    _, inv = norm_rows(stat_ref[...], latent - 8, cells)
    scaled = gain_ref[2:3] * inv
    lat = lat_ref[...] * scaled
    at = latent + 1 - 8
    m_one = sums_ref[at : at + 1] * (1.0 / cells)
    m_two = sums_ref[at + 1 : at + 2] * (1.0 / cells)
    fixed = jnp.sum(lat * m_one, axis=1, keepdims=True)
    left_high, left_mid, _ = three(lat * m_two)
    phat_high, phat_mid, _ = three(phat_ref[...])
    both = nn(
        jnp.concatenate(
            (
                jnp.concatenate((left_high, left_high), axis=1),
                jnp.concatenate((left_mid, jnp.zeros_like(left_mid)), axis=1),
            ),
            axis=0,
        ),
        jnp.concatenate((phat_high, phat_mid), axis=0),
    )
    grad_z = (block - fixed - (both[:16] + both[16:]))[:latent]
    noise = noise_ref[...]
    rows = pick(step, me_ref, fast, anear_ref, afar_ref)
    pieces = rows[hidden:].astype(F32)
    lat_logvar = (pieces[:latent] + pieces[16 : 16 + latent]) + pieces[32 : 32 + latent]
    spread = jnp.exp(lat_logvar)
    var = spread + 0.0001
    lat_mean = z_ref[0:latent, :] - jnp.sqrt(var) * noise
    scale = klw_ref[0:1, 0:1] * (1.0 / cells)
    g_mean = latent_rows(grad_z + scale * lat_mean)
    g_var = latent_rows(
        grad_z * noise * 0.5 * spread * lax.rsqrt(var) + scale * 0.5 * (spread - spread / var)
    )
    g_head = jnp.concatenate((g_mean, g_var), axis=0)
    head_high, head_mid, _ = three(g_head)
    spread_out = nn(cols_ref[...], jnp.concatenate((head_high, head_mid), axis=0))
    wide = rows[:hidden].astype(F32)
    dy = jnp.where(wide > 0, spread_out[:hidden] + spread_out[hidden:], 0.0)
    weighted = dy * wide
    first, second = dy[:, :128], weighted[:, :128]
    for tile in range(1, width // 128):
        lanes = slice(tile * 128, (tile + 1) * 128)
        first = first + dy[:, lanes]
        second = second + weighted[:, lanes]
    lane_ref[0] += first
    lane_ref[1] += second
    dy_low = dy.astype(BF)
    table = one_hot(batch_ref[0], kinds)
    hidden_low = jnp.maximum(wide, 0.0).astype(BF)
    out_ref[0:genes, :] += nt(logc_ref[...], dy_low)
    rest_ref[0:kinds, :] += nt(table.astype(BF), dy_low)
    rest_ref[kinds : kinds + 32, :] += nt(head_high, hidden_low) + nt(head_mid, hidden_low)
    rest_ref[kinds + 32 : kinds + 40, 0:32] += row_sums(g_head)
    base = kinds + 40
    z_high, z_mid, _ = three(z_ref[...])
    left = jnp.concatenate((table.astype(BF), z_high, z_mid), axis=0)
    part = nt(left, jnp.concatenate((phat_high, phat_mid), axis=0))
    part = part[:, :hidden] + part[:, hidden:]
    held = jnp.sum(jnp.concatenate((table, z_ref[...]), axis=0), axis=1, keepdims=True)
    product = jnp.concatenate((part[:kinds], part[kinds : kinds + 16] + part[kinds + 16 :]), axis=0)
    rest_ref[base : base + kinds + 16, :] -= held * m_one + product * m_two
    count = (kinds + 16) // steps
    for k in range(count):
        line = latent + 3 + k // 8
        rest_ref[pl.ds(base + step * count + k, 1), :] += block[line : line + 1, (k % 8) * hidden : (k % 8 + 1) * hidden]

    @pl.when(step == steps - 1)
    def _():
        one, two = row_sums(lane_ref[0]), row_sums(lane_ref[1])
        row = lax.broadcasted_iota(jnp.int32, one.shape, 0)
        out_ref[genes : genes + 8, :] = jnp.where(row == 0, one, jnp.where(row == 1, two, 0.0))
        size = rest_ref.shape[0] // 8
        out_ref[genes + 8 :, :] = rest_ref[pl.ds(pl.multiple_of((own_ref[0] & 7) * size, 8), size), :]


def whole_gradient(part, product, plain, gain, shift, inv, one, two):
    return (gain * inv) * (part - plain * one - ((product - plain * shift) / gain) * two)


def norm_sums(rows, norm_ref):
    return rows[0:1], (rows[1:2] - norm_ref[1:2] * rows[0:1]) / norm_ref[0:1]


def finish_kernel(cells, latent, sum_ref, dec_ref, fixed_ref, stat_enc_ref, norm_ref, kl_ref, klw_ref, own_ref, enc_out, tail_out, loss_out):
    genes = enc_out.shape[0]
    size = tail_out.shape[0] - 8
    count = pl.cdiv(genes, 128)
    kinds = fixed_ref.shape[0] - genes - 8 * count - 8
    loss_out[...] = klw_ref[0:1, 0:1] * kl_ref[...] - own_ref[latent : latent + 1, :]
    _, inv = norm_rows(stat_enc_ref[...], 0, cells)
    n_one, n_two = norm_sums(sum_ref[genes : genes + 8, :], norm_ref)
    at = genes + kinds
    logs = jnp.concatenate([fixed_ref[at + 8 * i : at + 8 * (i + 1), :] for i in range(count)], axis=1)
    log_sum = jnp.transpose(logs)[:genes, 0:1]
    enc = whole_gradient(
        sum_ref[0:genes, :], fixed_ref[0:genes, :], log_sum, norm_ref[0:1], norm_ref[1:2], inv, n_one * (1.0 / cells), n_two * (1.0 / cells)
    )
    enc_out[...] = enc
    dec = dec_ref[...]
    lane = jnp.sum(enc * enc, axis=0, keepdims=True) + jnp.sum(dec * dec, axis=0, keepdims=True)
    tail_out[0:size, :] = sum_ref[genes + 8 :, :]
    tail_out[size:, :] = jnp.broadcast_to(jnp.sum(lane, axis=1, keepdims=True), (8, tail_out.shape[1]))


def step_of(weight, gradient, first, second, rate):
    first = beta_one * first + (1.0 - beta_one) * gradient
    second = beta_two * second + (1.0 - beta_two) * gradient * gradient
    fixed_one = first * (1.0 / (1.0 - beta_one**step_number))
    fixed_two = second * (1.0 / (1.0 - beta_two**step_number))
    update = fixed_one / (jnp.sqrt(fixed_two) + 1e-08) + decay_rate * weight
    return weight - rate * update, first, second


def update_kernel(cells, latent, me_ref, near_ref, far_ref, enc_g_ref, dec_g_ref, sum_ref, fixed_ref, stat_enc_ref, stat_dec_ref, sums_ref, *refs):
    ins, outs, (rest_ref, small_g_ref, head_g_ref, norm_g_ref) = refs[:18], refs[18:-4], refs[-4:]
    enc, dec, gene, small, head, norm = (ins[3 * i : 3 * i + 3] for i in range(6))
    genes, hidden = enc[0].shape
    rows = small[0].shape[0]
    kinds = (rows - latent) // 2
    count = pl.cdiv(genes, 128)
    size = near_ref.shape[1]
    for core, ref in enumerate((near_ref, far_ref)):
        for index in range(ref.shape[0]):
            owner = me_ref[0] ^ (2 * index + core)
            rest_ref[pl.ds(pl.multiple_of(owner * size, 8), size), :] = ref[index]
    whole_rest = [rest_ref[i * size : i * size + size - 8, :] for i in range(8)]
    square = jnp.zeros((1, 1), F32)
    for i in range(8):
        square = square + rest_ref[(i + 1) * size - 8 : (i + 1) * size - 7, 0:1]
    rest = jnp.concatenate(whole_rest, axis=0)
    gains = norm[0]
    gain, shift = gains[0:1], gains[1:2]
    n_one, n_two = norm_sums(sum_ref[genes : genes + 8, :], gains)
    _, inv = norm_rows(stat_enc_ref[...], 0, cells)
    _, inv_dec = norm_rows(stat_dec_ref[...], latent - 8, cells)
    at = genes + kinds + 8 * count
    batch_sum = jnp.transpose(fixed_ref[at : at + 8, :])[:kinds, 0:1]
    small_g_ref[0:kinds, :] = whole_gradient(
        rest[0:kinds], fixed_ref[genes : genes + kinds, :], batch_sum, gain, shift, inv, n_one * (1.0 / cells), n_two * (1.0 / cells)
    )
    small_g_ref[kinds:, :] = (gains[2:3] * inv_dec) * rest[kinds + 40 : 2 * kinds + 56]
    bias = jnp.transpose(rest[kinds + 32 : kinds + 40])
    for half in range(2):
        into = slice(half * latent, (half + 1) * latent)
        head_g_ref[into, 0:hidden] = rest[kinds + 16 * half : kinds + 16 * half + latent]
        head_g_ref[into, hidden : hidden + 1] = bias[16 * half : 16 * half + latent, 0:1]
    at = latent + 1 - 8
    norm_g_ref[0:1] = n_two
    norm_g_ref[1:2] = n_one
    norm_g_ref[2:3] = sums_ref[at + 1 : at + 2]
    norm_g_ref[3:4] = sums_ref[at : at + 1]
    small_square = jnp.zeros((1, 1), F32)
    for part in (small_g_ref[0:rows, :], head_g_ref[...], norm_g_ref[...]):
        small_square = small_square + jnp.sum(jnp.sum(part * part, axis=0, keepdims=True), axis=1, keepdims=True)
    value = jnp.sqrt(square + small_square)
    factor = jnp.minimum(1.0, max_norm / value)
    (enc_n, enc_m, enc_v, enc_l, dec_n, dec_m, dec_v, dec_l, gene_n, gene_m, gene_v, small_n, small_m, small_v, head_n, head_m, head_v, norm_n, norm_m, norm_v, norm_out) = outs
    norm_out[...] = jnp.broadcast_to(value, norm_out.shape)
    new, first, second = step_of(enc[0][...], enc_g_ref[...] * factor, enc[1][...], enc[2][...], rate_genes)
    enc_n[...], enc_m[...], enc_v[...], enc_l[...] = new, first, second, new.astype(BF)
    for index in range(2):
        gradient = dec_g_ref[index * genes : (index + 1) * genes, :] * factor
        new, first, second = step_of(dec[0][index], gradient, dec[1][index], dec[2][index], rate_genes)
        dec_n[index], dec_m[index], dec_v[index], dec_l[index] = new, first, second, new.astype(BF)
    for index in range(pl.cdiv(genes, 128)):
        span = slice(index * 128, min(genes, (index + 1) * 128))
        gradient = dec_g_ref[2 * genes + index * 8 : 2 * genes + index * 8 + 3, 0 : span.stop - span.start] * factor
        new, first, second = step_of(gene[0][:, span], gradient, gene[1][:, span], gene[2][:, span], rate_small)
        gene_n[:, span], gene_m[:, span], gene_v[:, span] = new, first, second
    new, first, second = step_of(small[0][...], small_g_ref[0:rows, :] * factor, small[1][...], small[2][...], rate_small)
    small_n[...], small_m[...], small_v[...] = new, first, second
    new, first, second = step_of(head[0][...], head_g_ref[...] * factor, head[1][...], head[2][...], rate_small)
    head_n[...], head_m[...], head_v[...] = new, first, second
    new, first, second = step_of(norm[0][...], norm_g_ref[...] * factor, norm[1][...], norm[2][...], rate_small)
    norm_n[...], norm_m[...], norm_v[...] = new, first, second


def gather_genes(value, fast, blocks, width, late=None):
    if fast:
        near = jnp.stack([value] + [swap(value, "genes", 2 * k) for k in (1, 2, 3)])
        near = near if late is None else after(near, late)
        return near, swap(near, "genes", 1)
    rows = value.shape[0]
    whole_rows = lax.all_gather(value, "genes", axis=0).transpose(1, 0, 2)
    near = whole_rows.reshape(rows, blocks, width).transpose(1, 0, 2)
    return near, near


def per_device(counts, library, noise, batch_ids, gene_mask, kl_weight, enc_w, enc_m, enc_v, dec_w, dec_m, dec_v, gene_par, gene_m, gene_v, small_w, small_m, small_v, head_w, head_m, head_v, norm_par, norm_m, norm_v):
    rows_all, genes = counts.shape
    cells = float(rows_all * lax.axis_size("cells"))
    groups = lax.axis_size("genes")
    hidden = enc_w.shape[1]
    latent = head_w.shape[1] // 2
    kinds = (small_w.shape[0] - latent) // 2
    share = rows_all // groups
    width = min(1024, rows_all)
    blocks = rows_all // width
    fast = groups == 8 and blocks == 8
    me = lax.axis_index("genes").astype(jnp.int32).reshape(1)
    gene_lines = -(-genes // 128)

    def turn(value):
        return value.transpose(0, 2, 1)

    x_t = counts.T
    noise_t = noise.T
    dec_t = turn(dec_w)
    head_t = head_w.T
    lib8 = library.reshape(blocks, width)
    batch_all = batch_ids.reshape(blocks, 1, width)
    batch_own = batch_ids.reshape(groups, 1, share)
    klw = jnp.broadcast_to(kl_weight.reshape(1, 1), (8, 128))

    own_block = pl.BlockSpec((1, 1, share), lambda i, m: (m[0], 0, 0))
    own_lanes = lambda rows: pl.BlockSpec((rows, share), lambda i, m: (0, m[0]))
    lane_block = lambda rows: pl.BlockSpec((rows, width), lambda i, *_: (0, i))
    full = lambda array: (array, whole(array.shape))
    new = lambda shape, dtype=F32: (shape, dtype, whole(shape))
    if fast:
        from_all = lambda rows: pl.BlockSpec((1, rows, width), lambda i, m, *_: ((i ^ m[0]) // 2, 0, 0))
    else:
        from_all = lambda rows: pl.BlockSpec((1, rows, width), lambda i, m, *_: (i, 0, 0))

    keep_part, send_part = call(
        enc_kernel,
        (groups,),
        [
            (me if fast else me & 1, None),
            (x_t, pl.BlockSpec((genes, share), lambda i, m: (0, i ^ m[0]))),
            full(enc_w),
        ],
        [
            ((groups // 2, hidden, share), F32, pl.BlockSpec((1, hidden, share), lambda i, m: (i // 2, 0, 0))),
            ((groups // 2, hidden, share), BF, pl.BlockSpec((1, hidden, share), lambda i, m: (i // 2, 0, 0))),
        ],
        scratch=[pltpu.VMEM((hidden, genes), BF)],
        scalars=1,
        us=4.0,
    )
    got = swap(send_part, "genes", 1)
    slot = pl.BlockSpec((1, hidden, share), lambda i, m: (0, 0, 0))
    if fast:
        mine = [(keep_part[k : k + 1] + got[k : k + 1].astype(F32)).astype(BF) for k in (2, 3, 1)]
        far = [swap(part, "genes", 2 * k) for part, k in zip(mine, (2, 3, 1))]
        kept = keep_part
        ready = mine[2]
    else:
        summed = lax.psum_scatter(
            keep_part + got.astype(F32),
            "genes",
            scatter_dimension=0,
            axis_index_groups=[list(range(c, groups, 2)) for c in range(2)],
            tiled=True,
        )
        zero = jnp.zeros((1, hidden, share), BF)
        kept, got, far = summed, zero, [zero] * 3
        ready = keep_part

    mask_late = after(gene_mask.reshape(1, genes), ready)
    aug, dec_n, par, lg_tab, dg_tab, enc_pieces, dec_pieces, lat_row, head_rows, head_bias, head_cols, norm_t = call(
        prep_kernel,
        (1,),
        [full(gene_par), full(mask_late), full(dec_t), full(small_w), full(head_t), full(norm_par)],
        [
            new((2 * genes, hidden + 16), BF),
            new((hidden, 2 * genes), BF),
            new((5, genes, 128)),
            new((COUNT_TOP, genes, 128)),
            new((COUNT_TOP, genes, 128)),
            new((3 * hidden, kinds), BF),
            new((3 * hidden, kinds + 48), BF),
            new((16, hidden)),
            new((32, hidden)),
            new((32, 128)),
            new((2 * hidden, 64), BF),
            new((hidden, 8)),
        ],
    )
    logc, x_kept, gam_cell, dig_acc, log_lines = call(
        lambda *refs: counts_kernel(16, min(512, width), *refs),
        (blocks,),
        [
            (x_t, lane_block(genes)),
            full(lg_tab),
            full(dg_tab),
            (par, pl.BlockSpec((None, genes, 128), lambda i: (4, 0, 0))),
        ],
        [
            ((genes, rows_all), BF, lane_block(genes)),
            ((genes, rows_all), BF, lane_block(genes)),
            new((blocks, width)),
            new((genes, 128)),
            new((8 * gene_lines, 128)),
        ],
        scratch=[pltpu.VMEM((genes, 128), F32)],
        mib=16,
        us=15.0,
    )
    enc_late = after(enc_pieces, log_lines)
    stat8 = whole((8, hidden))
    pre_enc, stat_enc = call(
        own_kernel,
        (1,),
        [(me, None), (kept, slot), (got, slot)]
        + [(part, slot) for part in far]
        + [(batch_own, own_block), full(enc_late)],
        [new((hidden, share)), new((8, hidden))],
        scalars=1,
    )
    stat_enc = total(total(stat_enc, "genes"), "cells")

    pack, aff_own, kl_row = call(
        lambda *refs: latent_kernel(cells, latent, *refs),
        (1,),
        [
            (me, None),
            full(pre_enc),
            full(stat_enc),
            full(norm_t),
            full(head_rows),
            full(head_bias),
            (noise_t, own_lanes(latent)),
            (batch_own, own_block),
            full(dec_pieces),
        ],
        [new((16, share)), new((hidden + 48, share), BF), new((1, share))],
        scalars=1,
    )
    near, far_pack = gather_genes(pack, fast, blocks, width)
    if fast:
        stat_dec = jnp.sum(near[:, 8:16, :hidden], axis=0) + jnp.sum(far_pack[:, 8:16, :hidden], axis=0)
    else:
        stat_dec = lax.psum(pack[8:16, :hidden], "genes")
    stat_dec = total(stat_dec, "cells")

    batch_spec = pl.BlockSpec((1, 1, width), lambda i, *_: (i, 0, 0))
    hid, phat_dec, lse, z_all = call(
        lambda *refs: decode_kernel(cells, latent, fast, *refs),
        (blocks,),
        [
            (me, None),
            (near, from_all(16)),
            (far_pack, from_all(16)),
            (batch_all, batch_spec),
            full(stat_dec),
            full(norm_t),
            full(dec_pieces),
            (aug, pl.BlockSpec((genes, hidden + 16), lambda i, m: (0, 0))),
        ],
        [
            ((hidden, rows_all), BF, lane_block(hidden)),
            ((hidden, rows_all), F32, lane_block(hidden)),
            new((blocks, width)),
            ((16, rows_all), F32, lane_block(16)),
        ],
        scratch=[pltpu.VMEM((genes, width), F32)],
        scalars=1,
        us=8.0,
    )
    lse_all = log_total_of(lse, "genes")

    full8 = whole((blocks, width))
    gm, gd, rt, mass, recon, gene_acc = call(
        lambda *refs: zinb_kernel(32, min(512, width), *refs),
        (blocks,),
        [
            (hid, lane_block(hidden)),
            full(aug),
            (x_kept, lane_block(genes)),
            (par, pl.BlockSpec((4, genes, 128), lambda i: (0, 0, 0))),
            full(lib8),
            full(lse_all),
            full(gam_cell),
        ],
        [((genes, rows_all), BF, lane_block(genes))] * 3
        + [new((blocks, width)), new((blocks, width)), new((3, genes, 128))],
        scratch=[pltpu.VMEM((2 * genes, width), F32)],
        mib=20,
        us=28.0,
    )
    mass_own, mass = mass, total(mass, "genes")
    part_a, part_r, dec_acc = call(
        back_kernel,
        (blocks,),
        [
            (gm, lane_block(genes)),
            (gd, lane_block(genes)),
            (rt, lane_block(genes)),
            (hid, lane_block(hidden)),
            full(dec_n),
        ],
        [
            ((hidden, rows_all), F32, lane_block(hidden)),
            ((hidden, rows_all), F32, lane_block(hidden)),
            new((2 * genes, hidden)),
        ],
        mib=16,
        us=9.0,
    )

    aff_near, aff_far = gather_genes(after(aff_own, lse_all), fast, blocks, width, mass_own)
    fixed_rows = genes + kinds + 8 * gene_lines + 8
    (fixed,) = call(
        lambda *refs: enc_sums_kernel(fast, *refs),
        (blocks,),
        [
            (me, None),
            (logc, lane_block(genes)),
            (aff_near, from_all(hidden + 48)),
            (aff_far, from_all(hidden + 48)),
            (batch_all, batch_spec),
            full(log_lines),
        ],
        [new((fixed_rows, hidden))],
        scalars=1,
        us=4.0,
    )
    fixed = total_by_halves(fixed, "cells", (1, 2))

    keep_d, send_d = call(
        lambda *refs: hidden_grad_kernel(cells, latent, *refs),
        (blocks,),
        [
            (me if fast else jnp.zeros_like(me), None),
            (part_a, lane_block(hidden)),
            (part_r, lane_block(hidden)),
            (mass, full8),
            (hid, lane_block(hidden)),
            (phat_dec, lane_block(hidden)),
            full(lib8),
            full(stat_dec),
            full(norm_par),
            full(lat_row),
            full(recon),
            (z_all, lane_block(16)),
            (batch_all, batch_spec),
        ],
        [
            new((blocks // 2, 16, width)),
            new((blocks // 2, 16, width)),
        ],
        scratch=[pltpu.VMEM((2, hidden, 128), F32), pltpu.VMEM((kinds + 16, hidden), F32)],
        scalars=1,
        us=5.0,
    )
    if fast:
        got_d = swap(send_d, "genes", 1)
        pieces = [swap(keep_d[k] + got_d[k], "genes", 2 * k) for k in (1, 2, 3)]
        own_d = (keep_d[0] + got_d[0] + pieces[0]) + (pieces[1] + pieces[2])
        sums_dec = own_d[8:, :hidden]
    else:
        both = jnp.stack([keep_d, send_d], axis=1).reshape(blocks, 16, width)
        sums_dec = lax.psum(both[0, 8:, :hidden], "genes")
        both = both.transpose(1, 0, 2).reshape(16, groups, share).transpose(1, 0, 2)
        own_d = lax.psum_scatter(both, "genes", scatter_dimension=0, tiled=True)[0]
    sums_dec = total(sums_dec, "cells")
    d_near, d_far = gather_genes(own_d, fast, blocks, width)
    (dec_part,) = call(
        lambda *refs: dec_grad_kernel(cells, *refs),
        (blocks,),
        [
            (rt, lane_block(genes)),
            (hid, lane_block(hidden)),
            (mass, full8),
            full(lib8),
            full(dec_acc),
            full(gene_acc),
            full(dig_acc),
            (par, pl.BlockSpec((None, genes, 128), lambda i: (1, 0, 0))),
        ],
        [new((2 * genes + 8 * gene_lines, hidden))],
        scratch=[pltpu.VMEM((genes, hidden + 16), F32)],
        us=5.0,
    )
    dec_g = total_by_halves(dec_part, "cells", (2, 1))

    size = (2 * kinds + 64) // 8
    (enc_part,) = call(
        lambda *refs: enc_back_kernel(cells, latent, fast, *refs),
        (blocks,),
        [
            (me, None),
            (me, None),
            (d_near, from_all(16)),
            (d_far, from_all(16)),
            (phat_dec, lane_block(hidden)),
            full(sums_dec),
            full(stat_dec),
            full(norm_par),
            full(lat_row),
            (noise_t, lane_block(latent)),
            full(klw),
            (aff_near, from_all(hidden + 48)),
            (aff_far, from_all(hidden + 48)),
            (batch_all, batch_spec),
            (logc, lane_block(genes)),
            full(head_cols),
            (z_all, lane_block(16)),
        ],
        [new((genes + 8 + size, hidden))],
        scratch=[pltpu.VMEM((2 * kinds + 64, hidden), F32), pltpu.VMEM((2, hidden, 128), F32)],
        scalars=2,
        us=11.0,
    )
    enc_sum = total_by_halves(enc_part, "cells", (1, 2))
    enc_g, tail, loss = call(
        lambda *refs: finish_kernel(cells, latent, *refs),
        (1,),
        [full(a) for a in (enc_sum, dec_g, fixed, stat_enc, norm_par, kl_row, klw, own_d)],
        [new((genes, hidden)), new((size + 8, hidden)), new((1, share))],
    )
    if fast:
        tail_near = jnp.stack([tail] + [swap(tail, "genes", 2 * k) for k in (1, 2, 3)])
        tail_far = swap(tail_near, "genes", 1)
    else:
        tails = lax.all_gather(tail, "genes", axis=0)
        square = jnp.sum(tails[:, size:], axis=0)
        tails = tails[:8].at[:, size:].set(0.0).at[0, size:].set(square)
        tail_near, tail_far = tails[0::2], tails[1::2]

    state = [
        enc_w, enc_m, enc_v, dec_t, turn(dec_m), turn(dec_v), gene_par, gene_m, gene_v,
        small_w, small_m, small_v, head_t, head_m.T, head_v.T, norm_par, norm_m, norm_v,
    ]
    ins = [tail_near, tail_far, enc_g, dec_g, enc_sum, fixed, stat_enc, stat_dec, sums_dec] + state
    outs = []
    for index in range(6):
        one = state[3 * index]
        outs += [(one.shape, F32)] * 3
        if index < 2:
            outs.append((one.shape, BF))
    outs.append(((8, 128), F32))
    res = call(
        lambda *refs: update_kernel(cells, latent, *refs),
        (1,),
        [(me if fast else jnp.zeros_like(me), None)] + [full(array) for array in ins],
        [new(shape, dtype) for shape, dtype in outs],
        scratch=[
            pltpu.VMEM((8 * (size + 8), hidden), F32),
            pltpu.VMEM((2 * kinds + 16, hidden), F32),
            pltpu.VMEM((2 * latent, hidden + 1), F32),
            pltpu.VMEM((4, hidden), F32),
        ],
        scalars=1,
        mib=16,
    )
    enc_res, dec_res = res[0:4], [turn(part) for part in res[4:8]]
    head_res = [part.T for part in res[14:17]]
    return (
        *enc_res,
        *dec_res,
        *res[8:14],
        *head_res,
        *res[17:20],
        res[20][0, 0],
        loss.reshape(share),
    )


def solution(mesh):
    placed = (
        P("cells", "genes"), P("cells"), P("cells", None), P("cells"), P("genes"), P(),
        P("genes", None), P("genes", None), P("genes", None),
        P(None, None, "genes"), P(None, None, "genes"), P(None, None, "genes"),
        P(None, "genes"), P(None, "genes"), P(None, "genes"),
        P(), P(), P(), P(), P(), P(), P(), P(), P(),
    )
    return jax.shard_map(
        per_device,
        mesh=mesh,
        in_specs=placed,
        out_specs=(
            P("genes", None), P("genes", None), P("genes", None), P("genes", None),
            P(None, None, "genes"), P(None, None, "genes"), P(None, None, "genes"), P(None, None, "genes"),
            P(None, "genes"), P(None, "genes"), P(None, "genes"),
            P(), P(), P(), P(), P(), P(), P(), P(), P(), P(),
            P(("cells", "genes")),
        ),
        check_vma=False,
    )
```

```python
import jax
import jax.numpy as jnp
from jax import lax
from jax.experimental import pallas as pl
from jax.experimental.pallas import tpu as pltpu
from jax.sharding import PartitionSpec as P

norm_epsilon = 0.001
zinb_epsilon = 1e-08
beta_one = 0.9
beta_two = 0.999
step_number = 5.0
decay_rate = 0.01
rate_genes = 0.03
rate_small = 0.2
max_norm = 0.1

F32 = jnp.float32
BF = jnp.bfloat16
HI = lax.Precision.HIGHEST
COUNT_TOP = 8
LOG2_E = 1.4426950408889634


def nn(left, right, precision=None):
    return lax.dot_general(
        left, right, (((1,), (0,)), ((), ())), precision=precision, preferred_element_type=F32
    )


def nt(left, right, precision=None):
    return lax.dot_general(
        left, right, (((1,), (1,)), ((), ())), precision=precision, preferred_element_type=F32
    )


def whole(shape):
    return pl.BlockSpec(shape, lambda *_: (0,) * len(shape))


def in_hbm(array):
    return pltpu.with_memory_space_constraint(array, pltpu.HBM)


def call(kernel, grid, ins, outs, scratch=(), scalars=0, us=2.0, mib=12):
    return pl.pallas_call(
        kernel,
        out_shape=[pltpu.HBM(out[0], out[1]) if len(out) == 4 else jax.ShapeDtypeStruct(out[0], out[1]) for out in outs],
        grid_spec=pltpu.PrefetchScalarGridSpec(
            num_scalar_prefetch=scalars,
            grid=grid,
            in_specs=[spec for _, spec in ins[scalars:]],
            out_specs=[out[2] for out in outs],
            scratch_shapes=list(scratch),
        ),
        compiler_params=pltpu.CompilerParams(vmem_limit_bytes=mib * 1024 * 1024),
        cost_estimate=pl.CostEstimate(flops=0, bytes_accessed=int(us * 3.69e6), transcendentals=0),
    )(*[array for array, _ in ins])


def swap(value, axis, bit):
    count = lax.axis_size(axis)
    return lax.ppermute(value, axis, [(i, i ^ bit) for i in range(count)])


def bit_groups(axis):
    count = lax.axis_size(axis)
    if axis == "genes":
        groups, bit = [[1]], 2
    else:
        groups, bit = [], 1
    while bit < count:
        groups.append([bit, 2 * bit] if 2 * bit < count else [bit])
        bit *= 4
    return groups


def total(value, axis):
    for group in bit_groups(axis):
        if len(group) == 1:
            value = value + swap(value, axis, group[0])
        else:
            low, high = group
            value = (value + swap(value, axis, low)) + (
                swap(value, axis, high) + swap(value, axis, low ^ high)
            )
    return value


def log_total_of(value, axis):
    for group in bit_groups(axis):
        if len(group) == 1:
            parts = [value, swap(value, axis, group[0])]
        else:
            low, high = group
            parts = [value] + [swap(value, axis, k) for k in (low, high, low ^ high)]
        top = parts[0]
        for part in parts[1:]:
            top = jnp.maximum(top, part)
        mass = sum(jnp.exp(part - top) for part in parts)
        value = top + jnp.log(mass)
    return value


def total_by_halves(value, axis, order):
    for bit in order:
        value = value + swap(value, axis, bit)
    return value


def after(value, *others):
    return lax.optimization_barrier((value,) + others)[0]


def three(value):
    high = value.astype(BF)
    rest = value - high.astype(F32)
    mid = rest.astype(BF)
    low = (rest - mid.astype(F32)).astype(BF)
    return high, mid, low


def one_hot(batch_row, kinds):
    ids = lax.broadcasted_iota(jnp.int32, (kinds, batch_row.shape[1]), 0)
    return jnp.where(ids == batch_row, 1.0, 0.0)


def columns(rows):
    return jnp.transpose(rows)


def prep_kernel(gene_ref, mask_ref, dec_ref, small_ref, head_ref, norm_ref, aug_ref, turn_ref, par_ref, lg_ref, dg_ref, enc_out, dec_out, plain_out, lat_out, head_out, bias_out, cols_out, norm_out):
    genes = gene_ref.shape[1]
    hidden = norm_ref.shape[1]
    latent = head_ref.shape[0] // 2
    kinds = (small_ref.shape[0] - latent) // 2
    padded = pl.cdiv(genes, 128) * 128
    keep = mask_ref[...] > 0
    score_b = jnp.where(keep, gene_ref[0:1], -1e30)
    drop_b = jnp.where(keep, gene_ref[1:2], 1e30)
    th = jnp.exp(gene_ref[2:3])
    kept = jnp.where(keep, 1.0, 0.0)
    rows = jnp.concatenate((score_b, drop_b, th, kept, th, th, th, th), axis=0)
    if padded > genes:
        rows = jnp.concatenate((rows, jnp.ones((8, padded - genes), F32)), axis=1)
    turned = jnp.transpose(rows)[:genes]
    lane = lax.broadcasted_iota(jnp.int32, (genes, 16), 1)
    for half in range(2):
        at = slice(half * genes, (half + 1) * genes)
        aug_ref[at, 0:hidden] = dec_ref[half].astype(BF)
        high, mid, low = (jnp.broadcast_to(part.astype(F32), (genes, 16)) for part in three(turned[:, half : half + 1]))
        tail = jnp.where(lane == 0, high, jnp.where(lane == 1, mid, jnp.where(lane == 2, low, 0.0)))
        if half == 0:
            tail = jnp.where((lane >= 3) & (lane < 6), 1.0, tail)
        aug_ref[at, hidden : hidden + 16] = tail.astype(BF)
        turn_ref[:, at] = jnp.transpose(dec_ref[half]).astype(BF)
    th_w = jnp.broadcast_to(turned[:, 2:3], (genes, 128))
    keep_w = jnp.broadcast_to(turned[:, 3:4], (genes, 128))
    the_w = th_w + zinb_epsilon
    par_ref[0] = the_w
    par_ref[1] = th_w
    par_ref[2] = jnp.log(the_w)
    par_ref[3] = th_w / the_w
    par_ref[4] = keep_w
    gam = jnp.zeros_like(th_w)
    dig = jnp.zeros_like(th_w)
    for k in range(COUNT_TOP):
        more = th_w + float(k)
        gam = gam + keep_w * jnp.log(more * (1.0 / (1.0 + k)))
        dig = dig + keep_w / more
        lg_ref[k] = gam
        dg_ref[k] = dig
    for index, piece in enumerate(three(jnp.transpose(small_ref[0:kinds, :]))):
        enc_out[index * hidden : (index + 1) * hidden, :] = piece
    row = lax.broadcasted_iota(jnp.int32, (16, hidden), 0)
    lat_row = jnp.zeros((16, hidden), F32)
    for index in range(latent):
        lat_row = jnp.where(row == index, small_ref[2 * kinds + index : 2 * kinds + index + 1, :], lat_row)
    lat_out[...] = lat_row
    batch_turned, lat_turned = jnp.transpose(small_ref[kinds : 2 * kinds, :]), jnp.transpose(lat_row)
    plain_out[...] = jnp.concatenate((batch_turned, lat_turned), axis=1)
    batch_pieces = three(batch_turned)
    lat = three(lat_turned)
    zero = jnp.zeros_like(lat[0])
    tails = ((lat[0], lat[0], lat[0]), (lat[1], lat[1], zero), (lat[2], zero, zero))
    for index in range(3):
        at = slice(index * hidden, (index + 1) * hidden)
        dec_out[at, :] = jnp.concatenate((batch_pieces[index],) + tails[index], axis=1)
    full = lax.broadcasted_iota(jnp.int32, (32, hidden), 0)
    head = jnp.zeros((32, hidden), F32)
    bias = jnp.zeros((32, 1), F32)
    for index in range(2 * latent):
        to = index if index < latent else index - latent + 16
        head = jnp.where(full == to, head_ref[index : index + 1, 0:hidden], head)
        bias = jnp.where(full[:, 0:1] == to, head_ref[index : index + 1, hidden : hidden + 1], bias)
    head_out[...] = head
    bias_out[...] = jnp.broadcast_to(bias, (32, 128))
    high, mid, _ = three(jnp.transpose(head))
    cols_out[...] = jnp.concatenate((high, high, mid), axis=1)
    norm_out[...] = jnp.transpose(jnp.concatenate((norm_ref[...], norm_ref[...]), axis=0))


def exact_rows(stacked, table):
    out = nn(stacked, table)
    hidden = out.shape[0] // 3
    return out[:hidden] + out[hidden : 2 * hidden] + out[2 * hidden :]


def dec_table(z, batch_row, kinds):
    high, mid, low = three(z)
    return jnp.concatenate((one_hot(batch_row, kinds).astype(BF), high, mid, low), axis=0)


def row_sums(value):
    return nt(jnp.ones((8, value.shape[1]), F32), value, HI)


def stat_rows(first, second, at):
    sums, squares = row_sums(first), row_sums(second)
    row = lax.broadcasted_iota(jnp.int32, sums.shape, 0)
    return jnp.where(row == at, sums, jnp.where(row == at + 1, squares, 0.0))


def enc_kernel(low, me_ref, x_ref, w_ref, keep_ref, send_ref, buffer_ref, turn_ref, arrived):
    count, _, share = buffer_ref.shape

    def block(i):
        at = pl.multiple_of(((low + i) ^ me_ref[0]) * share, share)
        return pltpu.make_async_copy(x_ref.at[:, pl.ds(at, share)], buffer_ref.at[i], arrived.at[i])

    for i in range(count):
        block(i).start()
    turn_ref[...] = jnp.transpose(w_ref[...]).astype(BF)

    def pair(half, carry):
        for odd in range(2):
            i = 2 * half + odd
            block(i).wait()
            log_counts = jnp.log(1.0 + buffer_ref[i].astype(F32)).astype(BF)
            part = nn(turn_ref[...], log_counts)
            if odd:
                send_ref[half] = part.astype(BF)
            else:
                keep_ref[half] = part
        return carry

    lax.fori_loop(0, count // 2, pair, 0)


def lines(rows8, count):
    wide = rows8.shape[1]
    if wide < 128 * count:
        rows8 = jnp.concatenate((rows8, jnp.zeros((8, 128 * count - wide), F32)), axis=1)
    return jnp.concatenate([rows8[:, i * 128 : (i + 1) * 128] for i in range(count)], axis=0)


def counts_kernel(rows, span, x_ref, lg_ref, dg_ref, keep_ref, batch_ref, logc_ref, mask_ref, side_ref, cell_ref, disp_ref, line_ref, held_ref, sum_ref):
    step = pl.program_id(0)
    genes, width = x_ref.shape

    @pl.when(step == 0)
    def _():
        disp_ref[...] = jnp.zeros_like(disp_ref)
        sum_ref[...] = jnp.zeros_like(sum_ref)
        held_ref[...] = jnp.zeros_like(held_ref)

    kinds = held_ref.shape[0]
    table = one_hot(batch_ref[0], kinds)
    held_ref[...] += sum(table[:, t : t + 128] for t in range(0, width, 128))
    row = lax.broadcasted_iota(jnp.int32, (16, width), 0)
    side_ref[0:kinds, :] = table.astype(BF)
    side_ref[kinds:, :] = jnp.where(row == 0, 1.0, 0.0).astype(BF)
    tiles = span // 128
    done = []
    for first in range(0, width, span):
        lanes = [slice(first + tile * 128, first + (tile + 1) * 128) for tile in range(tiles)]

        def chunk(g, cell):
            at = pl.ds(pl.multiple_of(g * rows, rows), rows)
            keep = keep_ref[at, :]
            xs = [x_ref[at, lanes[tile]].astype(F32) for tile in range(tiles)]
            logs = [jnp.log(1.0 + x) for x in xs]
            for tile in range(tiles):
                logc_ref[at, lanes[tile]] = logs[tile].astype(BF)
                mask_ref[at, lanes[tile]] = (xs[tile] * keep).astype(BF)
            sum_ref[at, :] += sum(part.astype(BF).astype(F32) for part in logs)
            gams = [jnp.zeros_like(xs[0]) for _ in range(tiles)]
            digs = [jnp.zeros_like(xs[0]) for _ in range(tiles)]
            for k in range(COUNT_TOP):
                lg, dg = lg_ref[k, at, :], dg_ref[k, at, :]
                for tile in range(tiles):
                    more = xs[tile] > (k + 0.5)
                    gams[tile] = jnp.where(more, lg, gams[tile])
                    digs[tile] = jnp.where(more, dg, digs[tile])
            disp_ref[at, :] += sum(digs)
            out = []
            for tile in range(tiles):
                folded = cell[tile]
                for part in range(rows // 8):
                    folded = folded + gams[tile][part * 8 : (part + 1) * 8]
                out.append(folded)
            return tuple(out)

        zero = tuple(jnp.zeros((8, 128), F32) for _ in range(tiles))
        done += list(lax.fori_loop(0, genes // rows, chunk, zero))
    cell_ref[pl.ds(step, 1), :] = jnp.sum(jnp.concatenate(done, axis=1), axis=0, keepdims=True)

    @pl.when(step == pl.num_programs(0) - 1)
    def _():
        most = line_ref.shape[0] - 8
        line_ref[0:most, :] = lines(row_sums(sum_ref[...]), most // 8)
        line_ref[most:, :] = row_sums(held_ref[...])


def own_kernel(me_ref, keep_ref, got_ref, one_ref, two_ref, six_ref, batch_ref, enc_b_ref, pre_ref, stat_ref):
    kinds = enc_b_ref.shape[1]
    gathered = (keep_ref[0] + got_ref[0].astype(F32) + one_ref[0].astype(F32)) + (
        two_ref[0].astype(F32) + six_ref[0].astype(F32)
    )
    table = one_hot(batch_ref[0], kinds).astype(BF)
    pre = gathered + exact_rows(enc_b_ref[...], table)
    pre_ref[...] = pre
    stat_ref[...] = stat_rows(pre, pre * pre, 0)


def norm_columns(stat, first, cells):
    turned = jnp.transpose(stat)
    mean = turned[:, first : first + 1] / cells
    var = turned[:, first + 1 : first + 2] / cells - mean * mean
    return mean, lax.rsqrt(var + norm_epsilon)


def norm_rows(stat, first, cells):
    mean = stat[first : first + 1] / cells
    var = stat[first + 1 : first + 2] / cells - mean * mean
    return mean, lax.rsqrt(var + norm_epsilon)


def latent_kernel(cells, latent, me_ref, pre_ref, stat_ref, norm_ref, head_ref, bias_ref, noise_ref, batch_ref, dec_b_ref, pack_ref, aff_ref, kl_ref):
    kinds = dec_b_ref.shape[1] - 48
    hidden = pre_ref.shape[0]
    mean, inv = norm_columns(stat_ref[...], 0, cells)
    phat = (pre_ref[...] - mean) * inv
    affine = norm_ref[:, 0:1] * phat + norm_ref[:, 1:2]
    out = nn(head_ref[...], jnp.maximum(affine, 0.0), HI) + bias_ref[:, 0:1]
    lat_mean, lat_logvar = out[:latent], out[16 : 16 + latent]
    high, mid, low = three(latent_rows(lat_logvar))
    aff_ref[...] = jnp.concatenate((affine.astype(BF), high, mid, low), axis=0)
    var = jnp.exp(lat_logvar) + 0.0001
    z = latent_rows(lat_mean + jnp.sqrt(var) * noise_ref[...])
    terms = var + lat_mean * lat_mean - 1.0 - jnp.log(var)
    kl_ref[...] = 0.5 * jnp.sum(terms, axis=0, keepdims=True)
    pre_dec = exact_rows(dec_b_ref[...], dec_table(z, batch_ref[0], kinds))
    stat = stat_rows(pre_dec, pre_dec * pre_dec, 0)
    pack_ref[...] = z
    pack_ref[latent : latent + 1, 0:hidden] = stat[0:1]
    pack_ref[latent + 1 : latent + 2, 0:hidden] = stat[1:2]


def latent_rows(z):
    if z.shape[0] == 16:
        return z
    return jnp.concatenate((z, jnp.zeros((16 - z.shape[0], z.shape[1]), F32)), axis=0)


def part_of(step, width):
    return pl.ds(pl.multiple_of(step * width, 128), width)


def relu_low(affine):
    return jnp.maximum(affine, jnp.zeros_like(affine))


def pick(step, me_ref, fast, near_ref, far_ref):
    if not fast:
        return near_ref[step]
    place = step ^ me_ref[0]
    return jnp.where(lax.rem(place, 2) == 0, near_ref[lax.div(place, 2)], far_ref[lax.div(place, 2)])


def decode_kernel(cells, latent, fast, me_ref, near_ref, far_ref, side_ref, stat_ref, norm_ref, plain_ref, w_ref, aff_ref, lse_ref, z_ref, score_ref, left_ref):
    kinds = plain_ref.shape[1] - 16
    step = pl.program_id(0)
    cells_at = part_of(step, score_ref.shape[1])
    genes = score_ref.shape[0]
    hidden_rows = aff_ref.shape[0]

    @pl.when(step == 0)
    def _():
        mean, inv = norm_columns(stat_ref[...], latent - 8, cells)
        scaled = norm_ref[:, 2:3] * inv
        weights = plain_ref[...] * scaled
        high, mid, _ = three(weights)
        lane = lax.broadcasted_iota(jnp.int32, (hidden_rows, 16), 1)
        shift = jnp.broadcast_to(norm_ref[:, 3:4] - scaled * mean, (hidden_rows, 16))
        one, two, rest = (part.astype(F32) for part in three(shift))
        tail = jnp.where(lane == 0, one, jnp.where(lane == 1, two, jnp.where(lane == 2, rest, 0.0))).astype(BF)
        zero = jnp.zeros_like(tail)
        left_ref[:hidden_rows, :] = jnp.concatenate((high, high[:, kinds:], tail), axis=1)
        left_ref[hidden_rows:, :] = jnp.concatenate((mid, zero, zero), axis=1)

    z = pick(step, me_ref, fast, near_ref, far_ref)
    z = jnp.where(lax.broadcasted_iota(jnp.int32, z.shape, 0) < latent, z, 0.0)
    z_ref[:, cells_at] = z
    z_high, z_mid, _ = three(z)
    ones = jnp.where(lax.broadcasted_iota(jnp.int32, z.shape, 0) < 3, 1.0, 0.0).astype(BF)
    table = jnp.concatenate((side_ref[0:kinds, cells_at], z_high, z_mid, ones), axis=0)
    both = nn(left_ref[...], table)
    affine = (both[:hidden_rows] + both[hidden_rows:]).astype(BF)
    aff_ref[:, cells_at] = affine
    hidden = relu_low(affine)
    width = score_ref.shape[1]
    score_ref[...] = nn(w_ref[...], jnp.concatenate((hidden, ones), axis=0))
    tiles = width // 128
    rows = 32

    def top(g, best):
        at = pl.ds(pl.multiple_of(g * rows, rows), rows)
        new = []
        for tile in range(tiles):
            value = score_ref[at, slice(tile * 128, (tile + 1) * 128)]
            part = best[tile]
            for index in range(rows // 8):
                part = jnp.maximum(part, value[index * 8 : (index + 1) * 8])
            new.append(part)
        return tuple(new)

    best = lax.fori_loop(0, genes // rows, top, tuple(jnp.full((8, 128), -3e38, F32) for _ in range(tiles)), unroll=5)
    high = [jnp.max(part, axis=0, keepdims=True) for part in best]
    wide = [jnp.broadcast_to(part, (8, 128)) for part in high]

    def mass(g, sums):
        at = pl.ds(pl.multiple_of(g * rows, rows), rows)
        new = []
        for tile in range(tiles):
            value = score_ref[at, slice(tile * 128, (tile + 1) * 128)]
            part = sums[tile]
            for index in range(rows // 8):
                part = part + jnp.exp(value[index * 8 : (index + 1) * 8] - wide[tile])
            new.append(part)
        return tuple(new)

    sums = lax.fori_loop(0, genes // rows, mass, tuple(jnp.zeros((8, 128), F32) for _ in range(tiles)), unroll=5)
    lse = [high[tile] + jnp.log(jnp.sum(sums[tile], axis=0, keepdims=True)) for tile in range(tiles)]
    lse_ref[pl.ds(step, 1), :] = jnp.concatenate(lse, axis=1)


def enc_sums_kernel(fast, me_ref, logc_ref, near_ref, far_ref, side_ref, lines_ref, out_ref):
    step = pl.program_id(0)
    genes = logc_ref.shape[0]
    kinds = side_ref.shape[0] - 16

    @pl.when(step == 0)
    def _():
        out_ref[...] = jnp.zeros_like(out_ref)
        out_ref[genes + kinds :, :] = lines_ref[...]

    cells_at = part_of(step, near_ref.shape[2])
    affine = pick(step, me_ref, fast, near_ref, far_ref)[: out_ref.shape[1]]
    out_ref[0:genes, :] += nt(logc_ref[:, cells_at], affine)
    out_ref[genes : genes + kinds, :] += nt(side_ref[0:kinds, cells_at], affine)


def zinb_kernel(rows, span, hid_ref, w_ref, x_ref, par_ref, lib_ref, lse_ref, gam_ref, g_ref, rt_ref, mass_ref, recon_ref, acc_ref, sc_ref):
    step = pl.program_id(0)
    genes, width = x_ref.shape

    @pl.when(step == 0)
    def _():
        acc_ref[...] = jnp.zeros_like(acc_ref)

    one_row = pl.ds(step, 1)
    gam_row = gam_ref[one_row, :]
    shift = lib_ref[one_row, :] - lse_ref[one_row, :]
    row = lax.broadcasted_iota(jnp.int32, (16, width), 0)
    hi, mid, lo = three(shift)
    extra = jnp.where(row < 3, 1.0, jnp.where(row == 3, hi.astype(F32), jnp.where(row == 4, mid.astype(F32), jnp.where(row == 5, lo.astype(F32), 0.0))))
    table = jnp.concatenate((relu_low(hid_ref[:, part_of(step, width)]), extra.astype(BF)), axis=0)
    sc_ref[...] = nn(w_ref[...], table)
    tiles = span // 128
    mass_out, recon_out = [], []
    for first in range(0, width, span):
        lanes = [slice(first + tile * 128, first + (tile + 1) * 128) for tile in range(tiles)]
        far_lanes = [pl.ds(pl.multiple_of(step * width + first + tile * 128, 128), 128) for tile in range(tiles)]
        def chunk(g, state):
            at = pl.ds(pl.multiple_of(g * rows, rows), rows)
            at_drop = pl.ds(pl.multiple_of(genes + g * rows, rows), rows)
            the, th, log_the, part_th = (par_ref[i, at, :] for i in range(4))
            sums = [acc_ref[i, at, :] for i in range(3)]
            new = []
            for tile in range(tiles):
                rec, prod, back = state[tile]
                x = x_ref[at, lanes[tile]].astype(F32)
                mu = jnp.exp(sc_ref[at, lanes[tile]])
                drop = sc_ref[at_drop, lanes[tile]]
                both = mu + the
                r = 1.0 / both
                log_both = jnp.log(both)
                gap = log_the - log_both
                th_gap = th * gap
                u = jnp.where(x < 0.5, th_gap - drop, 1e30)
                eu = jnp.exp2(jnp.abs(u) * (-LOG2_E))
                ed = jnp.exp2(jnp.abs(drop) * (-LOG2_E))
                den = 1.0 + eu
                mu_eps = mu + zinb_epsilon
                rd = 1.0 / (1.0 + ed)
                w0 = jnp.where(u >= 0.0, 1.0, eu) * (1.0 / den)
                term = (th_gap - jnp.maximum(drop, 0.0)) + (x * (jnp.log(mu_eps) - log_both) - jnp.minimum(u, 0.0))
                factor = den * rd
                y = (x + w0 * th) * r
                g_mean = mu * (x * (1.0 / mu_eps) - y)
                g_drop = jnp.where(drop >= 0.0, ed, 1.0) * rd - w0
                g_disp = w0 * (gap + part_th) - y
                g_ref[at, far_lanes[tile]] = g_mean.astype(BF)
                g_ref[at_drop, far_lanes[tile]] = g_drop.astype(BF)
                rt_ref[at, far_lanes[tile]] = mu.astype(BF)
                sums = [a + b for a, b in zip(sums, (g_mean, g_drop, g_disp))]
                for part in range(rows // 8):
                    sub = slice(part * 8, (part + 1) * 8)
                    rec = rec + term[sub]
                    prod = prod * factor[sub]
                    back = back + g_mean[sub]
                new.append((rec, prod, back))
            for i in range(3):
                acc_ref[i, at, :] = sums[i]
            return tuple(new)
        zero = jnp.zeros((8, 128), F32)
        state = tuple((zero, zero + 1.0, zero) for _ in range(tiles))
        state = lax.fori_loop(0, genes // rows, chunk, state)
        for tile in range(tiles):
            rec, prod, back = state[tile]
            mass_out.append(jnp.sum(back, axis=0, keepdims=True))
            recon_out.append(jnp.sum(rec + jnp.log(prod), axis=0, keepdims=True))
    mass_ref[one_row, :] = jnp.concatenate(mass_out, axis=1)
    recon_ref[one_row, :] = jnp.concatenate(recon_out, axis=1) + gam_row


def back_kernel(width, g_in_ref, rt_ref, aff_ref, w_ref, a_ref, r_ref, g_ref):
    genes = rt_ref.shape[0]
    step = pl.program_id(0)
    cells_at = part_of(step, width)

    @pl.when(step == 0)
    def _():
        g_ref[...] = jnp.zeros_like(g_ref)

    a_ref[:, cells_at] = nn(w_ref[...], g_in_ref[:, cells_at])
    r_ref[:, cells_at] = nn(w_ref[:, :genes], rt_ref[:, cells_at])
    g_ref[...] += nt(g_in_ref[:, cells_at], relu_low(aff_ref[:, cells_at]))


def hidden_grad_kernel(cells, latent, me_ref, a_ref, r_ref, mass_ref, aff_ref, lib_ref, stat_ref, gain_ref, lat_ref, recon_ref, z_ref, side_ref, keep_ref, send_ref, lane_ref, oh_ref):
    step = pl.program_id(0)
    steps = pl.num_programs(0)
    place = step ^ me_ref[0]
    hidden, width = a_ref.shape[0], mass_ref.shape[1]
    cells_at = part_of(step, width)
    kinds = side_ref.shape[0] - 16

    @pl.when(step == 0)
    def _():
        lane_ref[...] = jnp.zeros_like(lane_ref)
        oh_ref[...] = jnp.zeros_like(oh_ref)

    back = mass_ref[pl.ds(step, 1), :] * jnp.exp(-lib_ref[pl.ds(step, 1), :])
    wide = aff_ref[:, cells_at].astype(F32)
    dy = jnp.where(wide > 0, a_ref[:, cells_at] - back * r_ref[:, cells_at], 0.0)
    weighted = dy * wide
    lane_ref[...] += sum(weighted[:, t : t + 128] for t in range(0, width, 128))
    dy_low = dy.astype(BF)
    oh_ref[...] += nt(jnp.concatenate((side_ref[:, cells_at], z_ref[:, cells_at].astype(BF)), axis=0), dy_low)
    _, inv = norm_rows(stat_ref[...], latent - 8, cells)
    lat_high, lat_mid, _ = three(lat_ref[...] * (gain_ref[2:3] * inv) * (-1.0 / cells))
    both = nn(jnp.concatenate((lat_high, lat_mid), axis=0), dy_low)
    block = both[:16] + both[16:]
    row = lax.broadcasted_iota(jnp.int32, block.shape, 0)
    block = jnp.where(row == latent, recon_ref[pl.ds(step, 1), :], block)
    slot = lax.div(place, 2)

    @pl.when(lax.rem(place, 2) == 0)
    def _():
        keep_ref[slot] = block

    @pl.when(lax.rem(place, 2) == 1)
    def _():
        send_ref[slot] = block

    @pl.when(step == steps - 1)
    def _():
        scale = -1.0 / cells
        one, two = oh_ref[kinds : kinds + 1, :] * scale, row_sums(lane_ref[...])[0:1] * scale
        oh_ref[kinds : kinds + 16, :] = oh_ref[kinds + 16 :, :]
        part = (kinds + 16) // steps
        for core, ref in enumerate((keep_ref, send_ref)):
            for index in range(ref.shape[0]):
                ref[index, latent + 1 : latent + 2, 0:hidden] = one
                ref[index, latent + 2 : latent + 3, 0:hidden] = two
                owner = me_ref[0] ^ (2 * index + core)
                for k in range(part):
                    line = latent + 3 + k // 8
                    lanes = slice((k % 8) * hidden, (k % 8 + 1) * hidden)
                    ref[index, line : line + 1, lanes] = oh_ref[pl.ds(owner * part + k, 1), :] * scale


def dec_grad_kernel(cells, rt_ref, hid_ref, mass_ref, lib_ref, g_ref, acc_ref, dig_ref, th_ref, dec_ref, mix_ref):
    step = pl.program_id(0)
    steps = pl.num_programs(0)
    genes = rt_ref.shape[0]
    cells_at = part_of(step, mass_ref.shape[1])
    hidden = hid_ref.shape[0]

    @pl.when(step == 0)
    def _():
        mix_ref[...] = jnp.zeros_like(mix_ref)

    back = mass_ref[pl.ds(step, 1), :] * jnp.exp(-lib_ref[pl.ds(step, 1), :])
    back_high, back_mid, back_low = three(back)
    row = lax.broadcasted_iota(jnp.int32, (16, back.shape[1]), 0)
    extra = jnp.where(row == 0, back_high.astype(F32), jnp.where(row == 1, back_mid.astype(F32), 0.0))
    scaled = (relu_low(hid_ref[:, cells_at]).astype(F32) * back).astype(BF)
    mix_ref[...] += nt(rt_ref[:, cells_at], jnp.concatenate((scaled, extra.astype(BF)), axis=0))

    @pl.when(step == steps - 1)
    def _():
        scale = -1.0 / cells
        mix = mix_ref[...]
        dec_ref[:genes, :] = (g_ref[:genes, :] - mix[:, :hidden]) * scale
        dec_ref[genes : 2 * genes, :] = g_ref[genes:, :] * scale
        pick = jnp.where(lax.broadcasted_iota(jnp.int32, (8, 16), 1) < 2, 1.0, 0.0)
        score_row = row_sums(acc_ref[0]) - nt(pick, mix[:, hidden:], HI)
        drop_row = row_sums(acc_ref[1])
        disp_row = row_sums((acc_ref[2] + dig_ref[...]) * th_ref[...])
        line = lax.broadcasted_iota(jnp.int32, score_row.shape, 0)
        gene_rows = scale * jnp.where(
            line == 0, score_row, jnp.where(line == 1, drop_row, jnp.where(line == 2, disp_row, 0.0))
        )
        dec_ref[2 * genes :, :] = lines(gene_rows, pl.cdiv(genes, 128))


def enc_back_kernel(cells, latent, fast, span, me_ref, own_ref, dnear_ref, dfar_ref, aff_dec_ref, sums_ref, stat_ref, gain_ref, lat_ref, noise_ref, klw_ref, anear_ref, afar_ref, side_ref, held_ref, logc_ref, cols_ref, z_ref, out_ref, rest_ref, lane_ref, left_ref, fixed_ref, one_ref, kept_ref, sum_ref):
    step = pl.program_id(0)
    steps = kept_ref.shape[0]
    genes, width = logc_ref.shape[0], dnear_ref.shape[2]
    hidden = aff_dec_ref.shape[0]
    cells_at = part_of(step, width)
    place = (step ^ me_ref[0]) if fast else step
    kinds = (rest_ref.shape[0] - 64) // 2
    at = latent + 1 - 8
    m_one, m_two = norm_sums(sums_ref[at : at + 2], gain_ref, 2)
    m_two = m_two / gain_ref[2:3] * (1.0 / cells)
    m_one = m_one * (1.0 / cells) - m_two * gain_ref[3:4]

    @pl.when(step == 0)
    def _():
        out_ref[...] = jnp.zeros_like(out_ref)
        rest_ref[...] = jnp.zeros_like(rest_ref)
        lane_ref[...] = jnp.zeros_like(lane_ref)
        sum_ref[...] = jnp.zeros_like(sum_ref)
        _, inv = norm_rows(stat_ref[...], latent - 8, cells)
        lat = lat_ref[...] * (gain_ref[2:3] * inv)
        fixed_ref[...] = jnp.broadcast_to(jnp.sum(lat * m_one, axis=1, keepdims=True), fixed_ref.shape)
        high, mid, _ = three(lat * m_two)
        left_ref[...] = jnp.concatenate((high, mid), axis=0)

    index = lax.div(place, 2) if fast else place
    near = (lax.rem(place, 2) == 0) if fast else None

    def take(near_ref, far_ref, rows, lanes):
        if not fast:
            return near_ref[index, rows, lanes]
        return jnp.where(near, near_ref[index, rows, lanes], far_ref[index, rows, lanes])

    every = slice(0, width)
    scale = klw_ref[0:1, 0:1] * (1.0 / cells)
    affine_dec = aff_dec_ref[:, cells_at]
    both = nn(left_ref[...], affine_dec)
    block = take(dnear_ref, dfar_ref, slice(0, 16), every)
    kept_ref[step] = block[8:]
    grad_z = (block - fixed_ref[:, 0:1] - (both[:16] + both[16:]))[:latent]
    noise = noise_ref[:, cells_at]
    pieces = take(anear_ref, afar_ref, slice(hidden, hidden + 48), every).astype(F32)
    lat_logvar = (pieces[:latent] + pieces[16 : 16 + latent]) + pieces[32 : 32 + latent]
    spread = jnp.exp(lat_logvar)
    var = spread + 0.0001
    inv_std = lax.rsqrt(var)
    z = z_ref[:, cells_at]
    lat_mean = z[0:latent] - var * inv_std * noise
    g_mean = latent_rows(grad_z + scale * lat_mean)
    g_var = latent_rows(spread * (grad_z * noise * (0.5 * inv_std) + (0.5 * scale) * (1.0 - inv_std * inv_std)))
    g_head = jnp.concatenate((g_mean, g_var), axis=0)
    sum_ref[0:32, :] += sum(g_head[:, t : t + 128] for t in range(0, width, 128))
    sum_ref[32:, :] += sum(z[:, t : t + 128] for t in range(0, width, 128))
    head_high, head_mid, _ = three(g_head)
    heads = jnp.concatenate((head_high, head_mid, head_high), axis=0)
    for begin in range(0, width, span):
        lanes = slice(begin, begin + span)
        affine = take(anear_ref, afar_ref, slice(0, hidden), lanes)
        one_ref[hidden:, lanes] = relu_low(affine)
        wide = affine.astype(F32)
        dy = jnp.where(wide > 0, nn(cols_ref[...], heads[:, lanes]), 0.0)
        one_ref[0:hidden, lanes] = dy.astype(BF)
        weighted = dy * wide
        lane_ref[...] += sum(weighted[:, t : t + 128] for t in range(0, span, 128))
    dy_low = one_ref[0:hidden, :]
    side = side_ref[:, cells_at]
    out_ref[0:genes, :] += nt(logc_ref[:, cells_at], dy_low)
    mixed = nt(side, dy_low)
    rest_ref[0:kinds, :] += mixed[:kinds]
    out_ref[genes : genes + 1, :] += mixed[kinds : kinds + 1]
    rest_ref[kinds : kinds + 32, :] += nt(head_high, one_ref[hidden:, :])
    base = kinds + 40
    product = nt(jnp.concatenate((side, z.astype(BF)), axis=0), affine_dec)
    rest_ref[base : base + kinds, :] -= product[:kinds] * m_two
    rest_ref[base + kinds : base + kinds + 16, :] -= product[kinds + 16 :] * m_two

    @pl.when(step == steps - 1)
    def _():
        out_ref[genes + 1 : genes + 2, :] = row_sums(lane_ref[...])[0:1]
        rest_ref[kinds + 32 : kinds + 40, 0:32] = row_sums(sum_ref[0:32, :])
        held = jnp.concatenate((held_ref[...], sum_ref[32:, :]), axis=0)
        rest_ref[base : base + kinds + 16, :] -= jnp.sum(held, axis=1, keepdims=True) * m_one
        count = (kinds + 16) // steps
        for owner in range(steps):
            for k in range(count):
                line = latent + 3 + k // 8 - 8
                at = slice(base + owner * count + k, base + owner * count + k + 1)
                rest_ref[at, :] += kept_ref[owner, line : line + 1, (k % 8) * hidden : (k % 8 + 1) * hidden]
        size = rest_ref.shape[0] // 8
        out_ref[genes + 8 :, :] = rest_ref[pl.ds(pl.multiple_of((own_ref[0] & 7) * size, 8), size), :]


def whole_gradient(part, product, plain, gain, shift, inv, one, two):
    return (gain * inv) * (part - plain * one - ((product - plain * shift) / gain) * two)


def norm_sums(rows, norm_ref, at):
    return rows[0:1], (rows[1:2] - norm_ref[at + 1 : at + 2] * rows[0:1]) / norm_ref[at : at + 1]


def finish_kernel(cells, latent, sum_ref, dec_ref, fixed_ref, stat_enc_ref, norm_ref, kl_ref, klw_ref, own_ref, enc_out, tail_out, loss_out):
    genes = enc_out.shape[0]
    size = tail_out.shape[0] - 8
    count = pl.cdiv(genes, 128)
    kinds = fixed_ref.shape[0] - genes - 8 * count - 8
    loss_out[...] = klw_ref[0:1, 0:1] * kl_ref[...] - own_ref[latent : latent + 1, :]
    _, inv = norm_rows(stat_enc_ref[...], 0, cells)
    n_one, n_two = norm_sums(sum_ref[genes : genes + 8, :], norm_ref, 0)
    at = genes + kinds
    logs = jnp.concatenate([fixed_ref[at + 8 * i : at + 8 * (i + 1), :] for i in range(count)], axis=1)
    log_sum = jnp.transpose(logs)[:genes, 0:1]
    enc = whole_gradient(
        sum_ref[0:genes, :], fixed_ref[0:genes, :], log_sum, norm_ref[0:1], norm_ref[1:2], inv, n_one * (1.0 / cells), n_two * (1.0 / cells)
    )
    enc_out[...] = enc
    dec = dec_ref[...]
    lane = jnp.sum(enc * enc, axis=0, keepdims=True) + jnp.sum(dec * dec, axis=0, keepdims=True)
    tail_out[0:size, :] = sum_ref[genes + 8 :, :]
    tail_out[size:, :] = jnp.broadcast_to(jnp.sum(lane, axis=1, keepdims=True), (8, tail_out.shape[1]))


def step_of(weight, gradient, first, second, rate):
    first = beta_one * first + (1.0 - beta_one) * gradient
    second = beta_two * second + (1.0 - beta_two) * gradient * gradient
    fixed_one = first * (1.0 / (1.0 - beta_one**step_number))
    fixed_two = second * (1.0 / (1.0 - beta_two**step_number))
    update = fixed_one / (jnp.sqrt(fixed_two) + 1e-08) + decay_rate * weight
    return weight - rate * update, first, second


def update_kernel(cells, latent, me_ref, near_ref, far_ref, enc_g_ref, dec_g_ref, sum_ref, fixed_ref, stat_enc_ref, stat_dec_ref, sums_ref, *refs):
    ins, outs, (rest_ref, small_g_ref, head_g_ref, norm_g_ref) = refs[:18], refs[18:-4], refs[-4:]
    enc, dec, gene, small, head, norm = (ins[3 * i : 3 * i + 3] for i in range(6))
    genes, hidden = enc[0].shape
    rows = small[0].shape[0]
    kinds = (rows - latent) // 2
    count = pl.cdiv(genes, 128)
    size = near_ref.shape[1]
    for core, ref in enumerate((near_ref, far_ref)):
        for index in range(ref.shape[0]):
            owner = me_ref[0] ^ (2 * index + core)
            rest_ref[pl.ds(pl.multiple_of(owner * size, 8), size), :] = ref[index]
    whole_rest = [rest_ref[i * size : i * size + size - 8, :] for i in range(8)]
    square = jnp.zeros((1, 1), F32)
    for i in range(8):
        square = square + rest_ref[(i + 1) * size - 8 : (i + 1) * size - 7, 0:1]
    rest = jnp.concatenate(whole_rest, axis=0)
    gains = norm[0]
    gain, shift = gains[0:1], gains[1:2]
    n_one, n_two = norm_sums(sum_ref[genes : genes + 8, :], gains, 0)
    _, inv = norm_rows(stat_enc_ref[...], 0, cells)
    _, inv_dec = norm_rows(stat_dec_ref[...], latent - 8, cells)
    at = genes + kinds + 8 * count
    batch_sum = jnp.transpose(fixed_ref[at : at + 8, :])[:kinds, 0:1]
    small_g_ref[0:kinds, :] = whole_gradient(
        rest[0:kinds], fixed_ref[genes : genes + kinds, :], batch_sum, gain, shift, inv, n_one * (1.0 / cells), n_two * (1.0 / cells)
    )
    small_g_ref[kinds:, :] = (gains[2:3] * inv_dec) * rest[kinds + 40 : 2 * kinds + 56]
    bias = jnp.transpose(rest[kinds + 32 : kinds + 40])
    for half in range(2):
        into = slice(half * latent, (half + 1) * latent)
        head_g_ref[into, 0:hidden] = rest[kinds + 16 * half : kinds + 16 * half + latent]
        head_g_ref[into, hidden : hidden + 1] = bias[16 * half : 16 * half + latent, 0:1]
    at = latent + 1 - 8
    norm_g_ref[0:1] = n_two
    norm_g_ref[1:2] = n_one
    m_one, m_two = norm_sums(sums_ref[at : at + 2], gains, 2)
    norm_g_ref[2:3] = m_two
    norm_g_ref[3:4] = m_one
    small_square = jnp.zeros((1, 1), F32)
    for part in (small_g_ref[0:rows, :], head_g_ref[...], norm_g_ref[...]):
        small_square = small_square + jnp.sum(jnp.sum(part * part, axis=0, keepdims=True), axis=1, keepdims=True)
    value = jnp.sqrt(square + small_square)
    factor = jnp.minimum(1.0, max_norm / value)
    (enc_n, enc_m, enc_v, enc_l, dec_n, dec_m, dec_v, dec_l, gene_n, gene_m, gene_v, small_n, small_m, small_v, head_n, head_m, head_v, norm_n, norm_m, norm_v, norm_out) = outs
    norm_out[...] = jnp.broadcast_to(value, norm_out.shape)
    new, first, second = step_of(enc[0][...], enc_g_ref[...] * factor, enc[1][...], enc[2][...], rate_genes)
    enc_n[...], enc_m[...], enc_v[...], enc_l[...] = new, first, second, new.astype(BF)
    for index in range(2):
        gradient = dec_g_ref[index * genes : (index + 1) * genes, :] * factor
        new, first, second = step_of(dec[0][index], gradient, dec[1][index], dec[2][index], rate_genes)
        dec_n[index], dec_m[index], dec_v[index], dec_l[index] = new, first, second, new.astype(BF)
    for index in range(pl.cdiv(genes, 128)):
        span = slice(index * 128, min(genes, (index + 1) * 128))
        gradient = dec_g_ref[2 * genes + index * 8 : 2 * genes + index * 8 + 3, 0 : span.stop - span.start] * factor
        new, first, second = step_of(gene[0][:, span], gradient, gene[1][:, span], gene[2][:, span], rate_small)
        gene_n[:, span], gene_m[:, span], gene_v[:, span] = new, first, second
    new, first, second = step_of(small[0][...], small_g_ref[0:rows, :] * factor, small[1][...], small[2][...], rate_small)
    small_n[...], small_m[...], small_v[...] = new, first, second
    new, first, second = step_of(head[0][...], head_g_ref[...] * factor, head[1][...], head[2][...], rate_small)
    head_n[...], head_m[...], head_v[...] = new, first, second
    new, first, second = step_of(norm[0][...], norm_g_ref[...] * factor, norm[1][...], norm[2][...], rate_small)
    norm_n[...], norm_m[...], norm_v[...] = new, first, second


def gather_genes(value, fast, blocks, width, late=None):
    if fast:
        near = jnp.stack([value] + [swap(value, "genes", 2 * k) for k in (1, 2, 3)])
        near = near if late is None else after(near, late)
        return near, swap(near, "genes", 1)
    rows = value.shape[0]
    whole_rows = lax.all_gather(value, "genes", axis=0).transpose(1, 0, 2)
    near = whole_rows.reshape(rows, blocks, width).transpose(1, 0, 2)
    return near, near


def per_device(counts, library, noise, batch_ids, gene_mask, kl_weight, enc_w, enc_m, enc_v, dec_w, dec_m, dec_v, gene_par, gene_m, gene_v, small_w, small_m, small_v, head_w, head_m, head_v, norm_par, norm_m, norm_v):
    rows_all, genes = counts.shape
    cells = float(rows_all * lax.axis_size("cells"))
    groups = lax.axis_size("genes")
    hidden = enc_w.shape[1]
    latent = head_w.shape[1] // 2
    kinds = (small_w.shape[0] - latent) // 2
    share = rows_all // groups
    width = min(1024, rows_all)
    blocks = rows_all // width
    fast = groups == 8 and blocks == 8
    me = lax.axis_index("genes").astype(jnp.int32).reshape(1)
    gene_lines = -(-genes // 128)

    def turn(value):
        return value.transpose(0, 2, 1)

    x_t = counts.T
    noise_t = noise.T
    dec_t = turn(dec_w)
    head_t = head_w.T
    lib8 = library.reshape(blocks, width)
    batch_all = batch_ids.reshape(blocks, 1, width)
    batch_own = batch_ids.reshape(groups, 1, share)
    klw = jnp.broadcast_to(kl_weight.reshape(1, 1), (8, 128))

    own_block = pl.BlockSpec((1, 1, share), lambda i, m: (m[0], 0, 0))
    own_lanes = lambda rows: pl.BlockSpec((rows, share), lambda i, m: (0, m[0]))
    lane_block = lambda rows: pl.BlockSpec((rows, width), lambda i, *_: (0, i))
    full = lambda array: (array, whole(array.shape))
    here = pl.BlockSpec(memory_space=pltpu.VMEM)
    new = lambda shape, dtype=F32: (shape, dtype, whole(shape))

    def encode(low, count, weight):
        return call(
            lambda *refs: enc_kernel(low, *refs),
            (1,),
            [
                (me if fast else me & 1, None),
                (in_hbm(x_t), pl.BlockSpec(memory_space=pl.ANY)),
                full(weight),
            ],
            [new((count // 2, hidden, share)), new((count // 2, hidden, share), BF)],
            scratch=[
                pltpu.VMEM((count, genes, share), BF),
                pltpu.VMEM((hidden, genes), BF),
                pltpu.SemaphoreType.DMA((count,)),
            ],
            scalars=1,
            us=3.0,
            mib=20,
        )

    slot = pl.BlockSpec((1, hidden, share), lambda i, m: (0, 0, 0))
    if fast:
        keep_far, send_far = encode(4, 4, enc_w)
        got_far = swap(send_far, "genes", 1)
        keep_near, send_near = encode(0, 4, after(enc_w, send_far))
        far = [
            swap((keep_far[k : k + 1] + got_far[k : k + 1].astype(F32)).astype(BF), "genes", 4 + 2 * k)
            for k in range(2)
        ]
        got = swap(send_near, "genes", 1)
        ready = (keep_near[1:2] + got[1:2].astype(F32)).astype(BF)
        far.append(swap(ready, "genes", 2))
        kept = keep_near
    else:
        keep_part, send_part = encode(0, groups, enc_w)
        got = swap(send_part, "genes", 1)
        summed = lax.psum_scatter(
            keep_part + got.astype(F32),
            "genes",
            scatter_dimension=0,
            axis_index_groups=[list(range(c, groups, 2)) for c in range(2)],
            tiled=True,
        )
        zero = jnp.zeros((1, hidden, share), BF)
        kept, got, far = summed, zero, [zero] * 3
        ready = keep_part

    mask_late = after(gene_mask.reshape(1, genes), ready)
    aug, dec_n, par, lg_tab, dg_tab, enc_pieces, dec_pieces, dec_plain, lat_row, head_rows, head_bias, head_cols, norm_t = call(
        prep_kernel,
        (1,),
        [full(gene_par), full(mask_late), full(dec_t), full(small_w), full(head_t), full(norm_par)],
        [
            new((2 * genes, hidden + 16), BF),
            new((hidden, 2 * genes), BF),
            new((5, genes, 128)),
            new((COUNT_TOP, genes, 128)),
            new((COUNT_TOP, genes, 128)),
            new((3 * hidden, kinds), BF),
            new((3 * hidden, kinds + 48), BF),
            new((hidden, kinds + 16)),
            new((16, hidden)),
            new((32, hidden)),
            new((32, 128)),
            new((hidden, 96), BF),
            new((hidden, 8)),
        ],
    )
    batch_spec = pl.BlockSpec((1, 1, width), lambda i, *_: (i, 0, 0))
    logc, x_kept, side, gam_cell, dig_acc, log_lines, held = call(
        lambda *refs: counts_kernel(16, min(512, width), *refs),
        (blocks,),
        [
            (x_t, lane_block(genes)),
            full(lg_tab),
            full(dg_tab),
            (par, pl.BlockSpec((None, genes, 128), lambda i: (4, 0, 0))),
            (batch_all, batch_spec),
        ],
        [
            ((genes, rows_all), BF, lane_block(genes), True),
            ((genes, rows_all), BF, lane_block(genes), True),
            ((kinds + 16, rows_all), BF, lane_block(kinds + 16)),
            new((blocks, width)),
            new((genes, 128)),
            new((8 * gene_lines + 8, 128)),
            new((kinds, 128)),
        ],
        scratch=[pltpu.VMEM((genes, 128), F32)],
        mib=16,
        us=15.0,
    )
    enc_late = after(enc_pieces, log_lines)
    stat8 = whole((8, hidden))
    pre_enc, stat_enc = call(
        own_kernel,
        (1,),
        [(me, None), (kept, slot), (got, slot)]
        + [(part, slot) for part in far]
        + [(batch_own, own_block), full(enc_late)],
        [new((hidden, share)), new((8, hidden))],
        scalars=1,
    )
    stat_enc = total(total(stat_enc, "genes"), "cells")

    pack, aff_own, kl_row = call(
        lambda *refs: latent_kernel(cells, latent, *refs),
        (1,),
        [
            (me, None),
            full(pre_enc),
            full(stat_enc),
            full(norm_t),
            full(head_rows),
            full(head_bias),
            (noise_t, own_lanes(latent)),
            (batch_own, own_block),
            full(dec_pieces),
        ],
        [new((16, share)), new((hidden + 48, share), BF), new((1, share))],
        scalars=1,
    )
    near, far_pack = gather_genes(pack, fast, blocks, width)
    if fast:
        stat_dec = jnp.sum(near[:, 8:16, :hidden], axis=0) + jnp.sum(far_pack[:, 8:16, :hidden], axis=0)
    else:
        stat_dec = lax.psum(pack[8:16, :hidden], "genes")
    stat_dec = total(stat_dec, "cells")

    aff_dec, lse, z_all = call(
        lambda *refs: decode_kernel(cells, latent, fast, *refs),
        (blocks,),
        [
            (me, None),
            (near, here),
            (far_pack, here),
            (side, here),
            full(stat_dec),
            full(norm_t),
            full(dec_plain),
            (aug, pl.BlockSpec((genes, hidden + 16), lambda i, m: (0, 0))),
        ],
        [
            ((hidden, rows_all), BF, here),
            new((blocks, width)),
            ((16, rows_all), F32, here),
        ],
        scratch=[pltpu.VMEM((genes, width), F32), pltpu.VMEM((2 * hidden, kinds + 48), BF)],
        scalars=1,
        us=8.0,
    )
    lse_all = log_total_of(lse, "genes")

    full8 = whole((blocks, width))
    g_both, rt, mass, recon, gene_acc = call(
        lambda *refs: zinb_kernel(64, min(512, width), *refs),
        (blocks,),
        [
            (aff_dec, here),
            full(aug),
            (in_hbm(x_kept), lane_block(genes)),
            (par, pl.BlockSpec((4, genes, 128), lambda i: (0, 0, 0))),
            full(lib8),
            full(lse_all),
            full(gam_cell),
        ],
        [((2 * genes, rows_all), BF, here), ((genes, rows_all), BF, here)]
        + [new((blocks, width)), new((blocks, width)), new((3, genes, 128))],
        scratch=[pltpu.VMEM((2 * genes, width), F32)],
        mib=20,
        us=28.0,
    )
    mass_own, mass = mass, total(mass, "genes")
    part_a, part_r, dec_acc = call(
        lambda *refs: back_kernel(width, *refs),
        (blocks,),
        [
            (g_both, here),
            (rt, here),
            (aff_dec, here),
            full(dec_n),
        ],
        [
            ((hidden, rows_all), F32, here),
            ((hidden, rows_all), F32, here),
            new((2 * genes, hidden)),
        ],
        mib=16,
        us=9.0,
    )

    aff_near, aff_far = gather_genes(after(aff_own, lse_all), fast, blocks, width, mass_own)
    fixed_rows = genes + kinds + 8 * gene_lines + 8
    (fixed,) = call(
        lambda *refs: enc_sums_kernel(fast, *refs),
        (blocks,),
        [
            (me, None),
            (logc, here),
            (aff_near, here),
            (aff_far, here),
            (side, here),
            full(log_lines),
        ],
        [new((fixed_rows, hidden))],
        scalars=1,
        us=4.0,
    )
    fixed = total_by_halves(fixed, "cells", (1, 2))

    keep_d, send_d = call(
        lambda *refs: hidden_grad_kernel(cells, latent, *refs),
        (blocks,),
        [
            (me if fast else jnp.zeros_like(me), None),
            (part_a, here),
            (part_r, here),
            (mass, full8),
            (aff_dec, here),
            full(lib8),
            full(stat_dec),
            full(norm_par),
            full(lat_row),
            full(recon),
            (z_all, here),
            (side, here),
        ],
        [
            new((blocks // 2, 16, width)),
            new((blocks // 2, 16, width)),
        ],
        scratch=[pltpu.VMEM((hidden, 128), F32), pltpu.VMEM((kinds + 32, hidden), F32)],
        scalars=1,
        us=5.0,
    )
    if fast:
        got_d = swap(send_d, "genes", 1)
        pieces = [swap(keep_d[k] + got_d[k], "genes", 2 * k) for k in (1, 2, 3)]
        own_d = (keep_d[0] + got_d[0] + pieces[0]) + (pieces[1] + pieces[2])
        sums_dec = own_d[8:, :hidden]
    else:
        both = jnp.stack([keep_d, send_d], axis=1).reshape(blocks, 16, width)
        sums_dec = lax.psum(both[0, 8:, :hidden], "genes")
        both = both.transpose(1, 0, 2).reshape(16, groups, share).transpose(1, 0, 2)
        own_d = lax.psum_scatter(both, "genes", scatter_dimension=0, tiled=True)[0]
    sums_dec = total(sums_dec, "cells")
    d_near, d_far = gather_genes(own_d, fast, blocks, width)
    (dec_part,) = call(
        lambda *refs: dec_grad_kernel(cells, *refs),
        (blocks,),
        [
            (rt, here),
            (aff_dec, here),
            (mass, full8),
            full(lib8),
            full(dec_acc),
            full(gene_acc),
            full(dig_acc),
            (par, pl.BlockSpec((None, genes, 128), lambda i: (1, 0, 0))),
        ],
        [new((2 * genes + 8 * gene_lines, hidden))],
        scratch=[pltpu.VMEM((genes, hidden + 16), F32)],
        us=5.0,
    )
    dec_g = total_by_halves(dec_part, "cells", (2, 1))

    size = (2 * kinds + 64) // 8
    (enc_part,) = call(
        lambda *refs: enc_back_kernel(cells, latent, fast, min(256, width), *refs),
        (blocks,),
        [
            (me, None),
            (me, None),
            (d_near, here),
            (d_far, here),
            (aff_dec, here),
            full(sums_dec),
            full(stat_dec),
            full(norm_par),
            full(lat_row),
            (noise_t, here),
            full(klw),
            (aff_near, here),
            (aff_far, here),
            (side, here),
            full(held),
            (logc, here),
            full(head_cols),
            (z_all, here),
        ],
        [new((genes + 8 + size, hidden))],
        scratch=[
            pltpu.VMEM((2 * kinds + 64, hidden), F32),
            pltpu.VMEM((hidden, 128), F32),
            pltpu.VMEM((32, hidden), BF),
            pltpu.VMEM((16, 128), F32),
            pltpu.VMEM((2 * hidden, width), BF),
            pltpu.VMEM((blocks, 8, width), F32),
            pltpu.VMEM((48, 128), F32),
        ],
        scalars=2,
        us=11.0,
    )
    enc_sum = total_by_halves(enc_part, "cells", (1, 2))
    enc_g, tail, loss = call(
        lambda *refs: finish_kernel(cells, latent, *refs),
        (1,),
        [full(a) for a in (enc_sum, dec_g, fixed, stat_enc, norm_par, kl_row, klw, own_d)],
        [new((genes, hidden)), new((size + 8, hidden)), new((1, share))],
    )
    if fast:
        tail_near = jnp.stack([tail] + [swap(tail, "genes", 2 * k) for k in (1, 2, 3)])
        tail_far = swap(tail_near, "genes", 1)
    else:
        tails = lax.all_gather(tail, "genes", axis=0)
        square = jnp.sum(tails[:, size:], axis=0)
        tails = tails[:8].at[:, size:].set(0.0).at[0, size:].set(square)
        tail_near, tail_far = tails[0::2], tails[1::2]

    state = [
        enc_w, enc_m, enc_v, dec_t, turn(dec_m), turn(dec_v), gene_par, gene_m, gene_v,
        small_w, small_m, small_v, head_t, head_m.T, head_v.T, norm_par, norm_m, norm_v,
    ]
    ins = [tail_near, tail_far, enc_g, dec_g, enc_sum, fixed, stat_enc, stat_dec, sums_dec] + state
    outs = []
    for index in range(6):
        one = state[3 * index]
        outs += [(one.shape, F32)] * 3
        if index < 2:
            outs.append((one.shape, BF))
    outs.append(((8, 128), F32))
    res = call(
        lambda *refs: update_kernel(cells, latent, *refs),
        (1,),
        [(me if fast else jnp.zeros_like(me), None)] + [full(array) for array in ins],
        [new(shape, dtype) for shape, dtype in outs],
        scratch=[
            pltpu.VMEM((8 * (size + 8), hidden), F32),
            pltpu.VMEM((2 * kinds + 16, hidden), F32),
            pltpu.VMEM((2 * latent, hidden + 1), F32),
            pltpu.VMEM((4, hidden), F32),
        ],
        scalars=1,
        mib=16,
    )
    enc_res, dec_res = res[0:4], [turn(part) for part in res[4:8]]
    head_res = [part.T for part in res[14:17]]
    return (
        *enc_res,
        *dec_res,
        *res[8:14],
        *head_res,
        *res[17:20],
        res[20][0, 0],
        loss.reshape(share),
    )


def solution(mesh):
    placed = (
        P("cells", "genes"), P("cells"), P("cells", None), P("cells"), P("genes"), P(),
        P("genes", None), P("genes", None), P("genes", None),
        P(None, None, "genes"), P(None, None, "genes"), P(None, None, "genes"),
        P(None, "genes"), P(None, "genes"), P(None, "genes"),
        P(), P(), P(), P(), P(), P(), P(), P(), P(),
    )
    return jax.shard_map(
        per_device,
        mesh=mesh,
        in_specs=placed,
        out_specs=(
            P("genes", None), P("genes", None), P("genes", None), P("genes", None),
            P(None, None, "genes"), P(None, None, "genes"), P(None, None, "genes"), P(None, None, "genes"),
            P(None, "genes"), P(None, "genes"), P(None, "genes"),
            P(), P(), P(), P(), P(), P(), P(), P(), P(), P(),
            P(("cells", "genes")),
        ),
        check_vma=False,
    )
```

```python
import jax
import jax.numpy as jnp
from jax import lax
from jax.experimental import pallas as pl
from jax.experimental.pallas import tpu as pltpu
from jax.sharding import PartitionSpec as P

norm_epsilon = 0.001
zinb_epsilon = 1e-08
beta_one = 0.9
beta_two = 0.999
step_number = 5.0
decay_rate = 0.01
rate_genes = 0.03
rate_small = 0.2
max_norm = 0.1

F32 = jnp.float32
BF = jnp.bfloat16
HI = lax.Precision.HIGHEST
COUNT_TOP = 8
LOG2_E = 1.4426950408889634


def nn(left, right, precision=None):
    return lax.dot_general(
        left, right, (((1,), (0,)), ((), ())), precision=precision, preferred_element_type=F32
    )


def nt(left, right, precision=None):
    return lax.dot_general(
        left, right, (((1,), (1,)), ((), ())), precision=precision, preferred_element_type=F32
    )


def whole(shape):
    return pl.BlockSpec(shape, lambda *_: (0,) * len(shape))


def in_hbm(array):
    return pltpu.with_memory_space_constraint(array, pltpu.HBM)


def call(kernel, grid, ins, outs, scratch=(), scalars=0, us=2.0, mib=12):
    return pl.pallas_call(
        kernel,
        out_shape=[pltpu.HBM(out[0], out[1]) if len(out) == 4 else jax.ShapeDtypeStruct(out[0], out[1]) for out in outs],
        grid_spec=pltpu.PrefetchScalarGridSpec(
            num_scalar_prefetch=scalars,
            grid=grid,
            in_specs=[spec for _, spec in ins[scalars:]],
            out_specs=[out[2] for out in outs],
            scratch_shapes=list(scratch),
        ),
        compiler_params=pltpu.CompilerParams(vmem_limit_bytes=mib * 1024 * 1024),
        cost_estimate=pl.CostEstimate(flops=0, bytes_accessed=int(us * 3.69e6), transcendentals=0),
    )(*[array for array, _ in ins])


def swap(value, axis, bit):
    count = lax.axis_size(axis)
    return lax.ppermute(value, axis, [(i, i ^ bit) for i in range(count)])


def bit_groups(axis):
    count = lax.axis_size(axis)
    if axis == "genes":
        groups, bit = [[1]], 2
    else:
        groups, bit = [], 1
    while bit < count:
        groups.append([bit, 2 * bit] if 2 * bit < count else [bit])
        bit *= 4
    return groups


def total(value, axis, done=0):
    for group in bit_groups(axis)[done:]:
        if len(group) == 1:
            value = value + swap(value, axis, group[0])
        else:
            low, high = group
            value = (value + swap(value, axis, low)) + (
                swap(value, axis, high) + swap(value, axis, low ^ high)
            )
    return value


def log_total_of(value, axis):
    for group in bit_groups(axis):
        if len(group) == 1:
            parts = [value, swap(value, axis, group[0])]
        else:
            low, high = group
            parts = [value] + [swap(value, axis, k) for k in (low, high, low ^ high)]
        top = parts[0]
        for part in parts[1:]:
            top = jnp.maximum(top, part)
        mass = sum(jnp.exp(part - top) for part in parts)
        value = top + jnp.log(mass)
    return value


def total_by_halves(value, axis, order):
    for bit in order:
        value = value + swap(value, axis, bit)
    return value


def after(value, *others):
    return lax.optimization_barrier((value,) + others)[0]


def three(value):
    high = value.astype(BF)
    rest = value - high.astype(F32)
    mid = rest.astype(BF)
    low = (rest - mid.astype(F32)).astype(BF)
    return high, mid, low


def one_hot(batch_row, kinds):
    ids = lax.broadcasted_iota(jnp.int32, (kinds, batch_row.shape[1]), 0)
    return jnp.where(ids == batch_row, 1.0, 0.0)


def columns(rows):
    return jnp.transpose(rows)


def prep_kernel(gene_ref, mask_ref, dec_ref, small_ref, head_ref, norm_ref, aug_ref, turn_ref, par_ref, lg_ref, dg_ref, enc_out, dec_out, plain_out, lat_out, head_out, bias_out, cols_out, norm_out):
    genes = gene_ref.shape[1]
    hidden = norm_ref.shape[1]
    latent = head_ref.shape[0] // 2
    kinds = (small_ref.shape[0] - latent) // 2
    padded = pl.cdiv(genes, 128) * 128
    keep = mask_ref[...] > 0
    score_b = jnp.where(keep, gene_ref[0:1], -1e30)
    drop_b = jnp.where(keep, gene_ref[1:2], 1e30)
    th = jnp.exp(gene_ref[2:3])
    kept = jnp.where(keep, 1.0, 0.0)
    rows = jnp.concatenate((score_b, drop_b, th, kept, th, th, th, th), axis=0)
    if padded > genes:
        rows = jnp.concatenate((rows, jnp.ones((8, padded - genes), F32)), axis=1)
    turned = jnp.transpose(rows)[:genes]
    lane = lax.broadcasted_iota(jnp.int32, (genes, 16), 1)
    for half in range(2):
        at = slice(half * genes, (half + 1) * genes)
        aug_ref[at, 0:hidden] = dec_ref[half].astype(BF)
        high, mid, low = (jnp.broadcast_to(part.astype(F32), (genes, 16)) for part in three(turned[:, half : half + 1]))
        tail = jnp.where(lane == 0, high, jnp.where(lane == 1, mid, jnp.where(lane == 2, low, 0.0)))
        if half == 0:
            tail = jnp.where((lane >= 3) & (lane < 6), 1.0, tail)
        aug_ref[at, hidden : hidden + 16] = tail.astype(BF)
        turn_ref[:, at] = jnp.transpose(dec_ref[half]).astype(BF)
    th_w = jnp.broadcast_to(turned[:, 2:3], (genes, 128))
    keep_w = jnp.broadcast_to(turned[:, 3:4], (genes, 128))
    the_w = th_w + zinb_epsilon
    par_ref[0] = the_w
    par_ref[1] = th_w
    par_ref[2] = jnp.log(the_w)
    par_ref[3] = th_w / the_w
    par_ref[4] = keep_w
    gam = jnp.zeros_like(th_w)
    dig = jnp.zeros_like(th_w)
    for k in range(COUNT_TOP):
        more = th_w + float(k)
        gam = gam + keep_w * jnp.log(more * (1.0 / (1.0 + k)))
        dig = dig + keep_w / more
        lg_ref[k] = gam
        dg_ref[k] = dig
    for index, piece in enumerate(three(jnp.transpose(small_ref[0:kinds, :]))):
        enc_out[index * hidden : (index + 1) * hidden, :] = piece
    row = lax.broadcasted_iota(jnp.int32, (16, hidden), 0)
    lat_row = jnp.zeros((16, hidden), F32)
    for index in range(latent):
        lat_row = jnp.where(row == index, small_ref[2 * kinds + index : 2 * kinds + index + 1, :], lat_row)
    lat_out[...] = lat_row
    batch_turned, lat_turned = jnp.transpose(small_ref[kinds : 2 * kinds, :]), jnp.transpose(lat_row)
    plain_out[...] = jnp.concatenate((batch_turned, lat_turned), axis=1)
    batch_pieces = three(batch_turned)
    lat = three(lat_turned)
    zero = jnp.zeros_like(lat[0])
    tails = ((lat[0], lat[0], lat[0]), (lat[1], lat[1], zero), (lat[2], zero, zero))
    for index in range(3):
        at = slice(index * hidden, (index + 1) * hidden)
        dec_out[at, :] = jnp.concatenate((batch_pieces[index],) + tails[index], axis=1)
    full = lax.broadcasted_iota(jnp.int32, (32, hidden), 0)
    head = jnp.zeros((32, hidden), F32)
    bias = jnp.zeros((32, 1), F32)
    for index in range(2 * latent):
        to = index if index < latent else index - latent + 16
        head = jnp.where(full == to, head_ref[index : index + 1, 0:hidden], head)
        bias = jnp.where(full[:, 0:1] == to, head_ref[index : index + 1, hidden : hidden + 1], bias)
    head_out[...] = head
    bias_out[...] = jnp.broadcast_to(bias, (32, 128))
    high, mid, _ = three(jnp.transpose(head))
    cols_out[...] = jnp.concatenate((high, high, mid), axis=1)
    norm_out[...] = jnp.transpose(jnp.concatenate((norm_ref[...], norm_ref[...]), axis=0))


def exact_rows(stacked, table):
    out = nn(stacked, table)
    hidden = out.shape[0] // 3
    return out[:hidden] + out[hidden : 2 * hidden] + out[2 * hidden :]


def dec_table(z, batch_row, kinds):
    high, mid, low = three(z)
    return jnp.concatenate((one_hot(batch_row, kinds).astype(BF), high, mid, low), axis=0)


def row_sums(value):
    return nt(jnp.ones((8, value.shape[1]), F32), value, HI)


def stat_rows(first, second, at):
    sums, squares = row_sums(first), row_sums(second)
    row = lax.broadcasted_iota(jnp.int32, sums.shape, 0)
    return jnp.where(row == at, sums, jnp.where(row == at + 1, squares, 0.0))


def enc_kernel(low, count, share, near, me_ref, x_ref, w_ref, keep_ref, send_ref, weight_ref, turn_ref, arrived, *buffers):
    def at(i):
        return pl.ds(pl.multiple_of(((low + i) ^ me_ref[0]) * share, share), share)

    weight = pltpu.make_async_copy(w_ref, weight_ref, arrived.at[count])
    weight.start()
    if not near:
        (buffer_ref,) = buffers

        def block(i):
            return pltpu.make_async_copy(x_ref.at[:, at(i)], buffer_ref.at[i], arrived.at[i])

        for i in range(count):
            block(i).start()
    weight.wait()
    turn_ref[...] = jnp.transpose(weight_ref[...]).astype(BF)

    def pair(half, carry):
        for odd in range(2):
            i = 2 * half + odd
            if near:
                x = x_ref[:, at(i)]
            else:
                block(i).wait()
                x = buffer_ref[i]
            part = nn(turn_ref[...], jnp.log(1.0 + x.astype(F32)).astype(BF))
            if odd:
                send_ref[half] = part.astype(BF)
            else:
                keep_ref[half] = part
        return carry

    lax.fori_loop(0, count // 2, pair, 0)


def lines(rows8, count):
    wide = rows8.shape[1]
    if wide < 128 * count:
        rows8 = jnp.concatenate((rows8, jnp.zeros((8, 128 * count - wide), F32)), axis=1)
    return jnp.concatenate([rows8[:, i * 128 : (i + 1) * 128] for i in range(count)], axis=0)


def counts_kernel(rows, span, x_ref, lg_ref, dg_ref, par_ref, batch_ref, lib_ref, logc_ref, mask_ref, side_ref, lib_out, cell_ref, disp_ref, line_ref, held_ref, sum_ref):
    step = pl.program_id(0)
    genes, width = mask_ref.shape

    @pl.when(step == 0)
    def _():
        disp_ref[...] = jnp.zeros_like(disp_ref)
        sum_ref[...] = jnp.zeros_like(sum_ref)
        held_ref[...] = jnp.zeros_like(held_ref)

    kinds = held_ref.shape[0]
    table = one_hot(batch_ref[0], kinds)
    held_ref[...] += sum(table[:, t : t + 128] for t in range(0, width, 128))
    row = lax.broadcasted_iota(jnp.int32, (16, width), 0)
    side_ref[0:kinds, part_of(step, width)] = table.astype(BF)
    side_ref[kinds:, part_of(step, width)] = jnp.where(row == 0, 1.0, 0.0).astype(BF)
    lib_out[...] = lib_ref[...]
    tiles = span // 128
    done = []
    for first in range(0, width, span):
        lanes = [slice(first + tile * 128, first + (tile + 1) * 128) for tile in range(tiles)]
        far_lanes = [pl.ds(pl.multiple_of(step * width + first + tile * 128, 128), 128) for tile in range(tiles)]

        def chunk(g, cell):
            at = pl.ds(pl.multiple_of(g * rows, rows), rows)
            keep = par_ref[4, at, :]
            xs = [x_ref[at, far_lanes[tile]].astype(F32) for tile in range(tiles)]
            logs = [jnp.log(1.0 + x) for x in xs]
            for tile in range(tiles):
                logc_ref[at, lanes[tile]] = logs[tile].astype(BF)
                mask_ref[at, lanes[tile]] = (xs[tile] * keep).astype(BF)
            sum_ref[at, :] += sum(part.astype(BF).astype(F32) for part in logs)
            gams = [jnp.zeros_like(xs[0]) for _ in range(tiles)]
            digs = [jnp.zeros_like(xs[0]) for _ in range(tiles)]
            for k in range(COUNT_TOP):
                lg, dg = lg_ref[k, at, :], dg_ref[k, at, :]
                for tile in range(tiles):
                    more = xs[tile] > (k + 0.5)
                    gams[tile] = jnp.where(more, lg, gams[tile])
                    digs[tile] = jnp.where(more, dg, digs[tile])
            disp_ref[at, :] += sum(digs)
            out = []
            for tile in range(tiles):
                folded = cell[tile]
                for part in range(rows // 8):
                    folded = folded + gams[tile][part * 8 : (part + 1) * 8]
                out.append(folded)
            return tuple(out)

        zero = tuple(jnp.zeros((8, 128), F32) for _ in range(tiles))
        done += list(lax.fori_loop(0, genes // rows, chunk, zero))
    cell_ref[pl.ds(step, 1), :] = jnp.sum(jnp.concatenate(done, axis=1), axis=0, keepdims=True)

    @pl.when(step == pl.num_programs(0) - 1)
    def _():
        most = line_ref.shape[0] - 8
        line_ref[0:most, :] = lines(row_sums(sum_ref[...]), most // 8)
        line_ref[most:, :] = row_sums(held_ref[...])


def own_kernel(me_ref, keep_ref, got_ref, one_ref, two_ref, six_ref, batch_ref, enc_b_ref, pre_ref, stat_ref):
    kinds = enc_b_ref.shape[1]
    gathered = (keep_ref[0] + got_ref[0].astype(F32) + one_ref[0].astype(F32)) + (
        two_ref[0].astype(F32) + six_ref[0].astype(F32)
    )
    table = one_hot(batch_ref[0], kinds).astype(BF)
    pre = gathered + exact_rows(enc_b_ref[...], table)
    pre_ref[...] = pre
    stat_ref[...] = stat_rows(pre, pre * pre, 0)


def norm_columns(stat, first, cells):
    turned = jnp.transpose(stat)
    mean = turned[:, first : first + 1] / cells
    var = turned[:, first + 1 : first + 2] / cells - mean * mean
    return mean, lax.rsqrt(var + norm_epsilon)


def norm_rows(stat, first, cells):
    mean = stat[first : first + 1] / cells
    var = stat[first + 1 : first + 2] / cells - mean * mean
    return mean, lax.rsqrt(var + norm_epsilon)


def latent_kernel(cells, latent, me_ref, pre_ref, stat_ref, norm_ref, head_ref, bias_ref, noise_ref, batch_ref, dec_b_ref, pack_ref, aff_ref, kl_ref):
    kinds = dec_b_ref.shape[1] - 48
    hidden = pre_ref.shape[0]
    mean, inv = norm_columns(stat_ref[...], 0, cells)
    phat = (pre_ref[...] - mean) * inv
    affine = norm_ref[:, 0:1] * phat + norm_ref[:, 1:2]
    out = nn(head_ref[...], jnp.maximum(affine, 0.0), HI) + bias_ref[:, 0:1]
    lat_mean, lat_logvar = out[:latent], out[16 : 16 + latent]
    high, mid, low = three(latent_rows(lat_logvar))
    aff_ref[...] = jnp.concatenate((affine.astype(BF), high, mid, low), axis=0)
    var = jnp.exp(lat_logvar) + 0.0001
    z = latent_rows(lat_mean + jnp.sqrt(var) * noise_ref[...])
    terms = var + lat_mean * lat_mean - 1.0 - jnp.log(var)
    kl_ref[...] = 0.5 * jnp.sum(terms, axis=0, keepdims=True)
    pre_dec = exact_rows(dec_b_ref[...], dec_table(z, batch_ref[0], kinds))
    stat = stat_rows(pre_dec, pre_dec * pre_dec, 0)
    pack_ref[...] = z
    pack_ref[latent : latent + 1, 0:hidden] = stat[0:1]
    pack_ref[latent + 1 : latent + 2, 0:hidden] = stat[1:2]


def latent_rows(z):
    if z.shape[0] == 16:
        return z
    return jnp.concatenate((z, jnp.zeros((16 - z.shape[0], z.shape[1]), F32)), axis=0)


def part_of(step, width):
    return pl.ds(pl.multiple_of(step * width, 128), width)


def relu_low(affine):
    return jnp.maximum(affine, jnp.zeros_like(affine))


def pick(step, me_ref, fast, near_ref, far_ref):
    if not fast:
        return near_ref[step]
    place = step ^ me_ref[0]
    return jnp.where(lax.rem(place, 2) == 0, near_ref[lax.div(place, 2)], far_ref[lax.div(place, 2)])


def decode_kernel(cells, latent, fast, me_ref, near_ref, far_ref, side_ref, stat_ref, norm_ref, plain_ref, w_ref, aff_ref, lse_ref, z_ref, top_ref, mass_ref, score_ref, left_ref):
    kinds = plain_ref.shape[1] - 16
    step = pl.program_id(0)
    cells_at = part_of(step, score_ref.shape[1])
    genes = score_ref.shape[0]
    hidden_rows = aff_ref.shape[0]

    @pl.when(step == 0)
    def _():
        mean, inv = norm_columns(stat_ref[...], latent - 8, cells)
        scaled = norm_ref[:, 2:3] * inv
        weights = plain_ref[...] * scaled
        high, mid, _ = three(weights)
        lane = lax.broadcasted_iota(jnp.int32, (hidden_rows, 16), 1)
        shift = jnp.broadcast_to(norm_ref[:, 3:4] - scaled * mean, (hidden_rows, 16))
        one, two, rest = (part.astype(F32) for part in three(shift))
        tail = jnp.where(lane == 0, one, jnp.where(lane == 1, two, jnp.where(lane == 2, rest, 0.0))).astype(BF)
        zero = jnp.zeros_like(tail)
        left_ref[:hidden_rows, :] = jnp.concatenate((high, high[:, kinds:], tail), axis=1)
        left_ref[hidden_rows:, :] = jnp.concatenate((mid, zero, zero), axis=1)

    z = pick(step, me_ref, fast, near_ref, far_ref)
    z = jnp.where(lax.broadcasted_iota(jnp.int32, z.shape, 0) < latent, z, 0.0)
    z_ref[:, cells_at] = z
    z_high, z_mid, _ = three(z)
    ones = jnp.where(lax.broadcasted_iota(jnp.int32, z.shape, 0) < 3, 1.0, 0.0).astype(BF)
    table = jnp.concatenate((side_ref[0:kinds, cells_at], z_high, z_mid, ones), axis=0)
    both = nn(left_ref[...], table)
    affine = (both[:hidden_rows] + both[hidden_rows:]).astype(BF)
    aff_ref[:, cells_at] = affine
    hidden = relu_low(affine)
    width = score_ref.shape[1]
    score_ref[...] = nn(w_ref[0:genes, :], jnp.concatenate((hidden, ones), axis=0))
    tiles = width // 128
    rows = 32

    def top(g, best):
        at = pl.ds(pl.multiple_of(g * rows, rows), rows)
        new = []
        for tile in range(tiles):
            value = score_ref[at, slice(tile * 128, (tile + 1) * 128)]
            part = best[tile]
            for index in range(rows // 8):
                part = jnp.maximum(part, value[index * 8 : (index + 1) * 8])
            new.append(part)
        return tuple(new)

    best = lax.fori_loop(0, genes // rows, top, tuple(jnp.full((8, 128), -3e38, F32) for _ in range(tiles)), unroll=5)
    high = [jnp.max(part, axis=0, keepdims=True) for part in best]
    wide = [jnp.broadcast_to(part, (8, 128)) for part in high]

    far_lanes = [pl.ds(pl.multiple_of(step * width + tile * 128, 128), 128) for tile in range(tiles)]

    def mass(g, sums):
        at = pl.ds(pl.multiple_of(g * rows, rows), rows)
        new = []
        for tile in range(tiles):
            value = score_ref[at, slice(tile * 128, (tile + 1) * 128)]
            part = sums[tile]
            pieces = []
            for index in range(rows // 8):
                pieces.append(jnp.exp(value[index * 8 : (index + 1) * 8] - wide[tile]))
                part = part + pieces[-1]
            mass_ref[at, far_lanes[tile]] = jnp.concatenate(pieces, axis=0)
            new.append(part)
        return tuple(new)

    sums = lax.fori_loop(0, genes // rows, mass, tuple(jnp.zeros((8, 128), F32) for _ in range(tiles)), unroll=5)
    top_ref[pl.ds(step, 1), :] = jnp.concatenate(high, axis=1)
    lse = [high[tile] + jnp.log(jnp.sum(sums[tile], axis=0, keepdims=True)) for tile in range(tiles)]
    lse_ref[pl.ds(step, 1), :] = jnp.concatenate(lse, axis=1)


def enc_sums_kernel(fast, me_ref, logc_ref, near_ref, far_ref, side_ref, lines_ref, out_ref):
    step = pl.program_id(0)
    genes = logc_ref.shape[0]
    kinds = side_ref.shape[0] - 16

    @pl.when(step == 0)
    def _():
        out_ref[...] = jnp.zeros_like(out_ref)
        out_ref[genes + kinds :, :] = lines_ref[...]

    cells_at = part_of(step, near_ref.shape[2])
    affine = pick(step, me_ref, fast, near_ref, far_ref)[: out_ref.shape[1]]
    out_ref[0:genes, :] += nt(logc_ref[:, cells_at], affine)
    out_ref[genes : genes + kinds, :] += nt(side_ref[0:kinds, cells_at], affine)


def zinb_kernel(rows, span, hid_ref, e_ref, top_ref, w_ref, x_ref, par_ref, lib_ref, lse_ref, gam_ref, g_ref, rt_ref, mass_ref, recon_ref, acc_ref, sc_ref):
    step = pl.program_id(0)
    genes, width = x_ref.shape

    @pl.when(step == 0)
    def _():
        acc_ref[...] = jnp.zeros_like(acc_ref)

    one_row = pl.ds(step, 1)
    gam_row = gam_ref[one_row, :]
    level = jnp.exp(top_ref[one_row, :] + (lib_ref[one_row, :] - lse_ref[one_row, :]))
    row = lax.broadcasted_iota(jnp.int32, (16, width), 0)
    ones = jnp.where(row < 3, 1.0, 0.0).astype(BF)
    sc_ref[...] = nn(w_ref[genes:, :], jnp.concatenate((relu_low(hid_ref[:, part_of(step, width)]), ones), axis=0))
    tiles = span // 128
    mass_out, recon_out = [], []
    for first in range(0, width, span):
        lanes = [slice(first + tile * 128, first + (tile + 1) * 128) for tile in range(tiles)]
        far_lanes = [pl.ds(pl.multiple_of(step * width + first + tile * 128, 128), 128) for tile in range(tiles)]
        scale = [jnp.broadcast_to(level[:, lanes[tile]], (rows, 128)) for tile in range(tiles)]

        def chunk(g, state):
            at = pl.ds(pl.multiple_of(g * rows, rows), rows)
            at_drop = pl.ds(pl.multiple_of(genes + g * rows, rows), rows)
            the, th, log_the, part_th = (par_ref[i, at, :] for i in range(4))
            sums = [acc_ref[i, at, :] for i in range(3)]
            new = []
            for tile in range(tiles):
                rec, prod, back = state[tile]
                x = x_ref[at, lanes[tile]].astype(F32)
                mu = e_ref[at, far_lanes[tile]] * scale[tile]
                drop = sc_ref[at, lanes[tile]]
                both = mu + the
                r = 1.0 / both
                log_both = jnp.log(both)
                gap = log_the - log_both
                th_gap = th * gap
                u = jnp.where(x < 0.5, th_gap - drop, 1e30)
                eu = jnp.exp2(jnp.abs(u) * (-LOG2_E))
                ed = jnp.exp2(jnp.abs(drop) * (-LOG2_E))
                den = 1.0 + eu
                mu_eps = mu + zinb_epsilon
                rd = 1.0 / (1.0 + ed)
                w0 = jnp.where(u >= 0.0, 1.0, eu) * (1.0 / den)
                term = (th_gap - jnp.maximum(drop, 0.0)) + (x * (jnp.log(mu_eps) - log_both) - jnp.minimum(u, 0.0))
                factor = den * rd
                y = (x + w0 * th) * r
                g_mean = mu * (x * (1.0 / mu_eps) - y)
                g_drop = jnp.where(drop >= 0.0, ed, 1.0) * rd - w0
                g_disp = w0 * (gap + part_th) - y
                g_ref[at, far_lanes[tile]] = g_mean.astype(BF)
                g_ref[at_drop, far_lanes[tile]] = g_drop.astype(BF)
                rt_ref[at, far_lanes[tile]] = mu.astype(BF)
                sums = [a + b for a, b in zip(sums, (g_mean, g_drop, g_disp))]
                for part in range(rows // 8):
                    sub = slice(part * 8, (part + 1) * 8)
                    rec = rec + term[sub]
                    prod = prod * factor[sub]
                    back = back + g_mean[sub]
                new.append((rec, prod, back))
            for i in range(3):
                acc_ref[i, at, :] = sums[i]
            return tuple(new)
        zero = jnp.zeros((8, 128), F32)
        state = tuple((zero, zero + 1.0, zero) for _ in range(tiles))
        state = lax.fori_loop(0, genes // rows, chunk, state)
        for tile in range(tiles):
            rec, prod, back = state[tile]
            mass_out.append(jnp.sum(back, axis=0, keepdims=True))
            recon_out.append(jnp.sum(rec + jnp.log(prod), axis=0, keepdims=True))
    mass_ref[one_row, :] = jnp.concatenate(mass_out, axis=1)
    recon_ref[one_row, :] = jnp.concatenate(recon_out, axis=1) + gam_row


def back_kernel(width, g_in_ref, rt_ref, aff_ref, w_ref, a_ref, r_ref, g_ref):
    genes = rt_ref.shape[0]
    step = pl.program_id(0)
    cells_at = part_of(step, width)

    @pl.when(step == 0)
    def _():
        g_ref[...] = jnp.zeros_like(g_ref)

    a_ref[:, cells_at] = nn(w_ref[...], g_in_ref[:, cells_at])
    r_ref[:, cells_at] = nn(w_ref[:, :genes], rt_ref[:, cells_at])
    g_ref[...] += nt(g_in_ref[:, cells_at], relu_low(aff_ref[:, cells_at]))


def hidden_grad_kernel(cells, latent, me_ref, a_ref, r_ref, mass_ref, aff_ref, lib_ref, stat_ref, gain_ref, lat_ref, recon_ref, z_ref, side_ref, keep_ref, send_ref, lane_ref, oh_ref):
    step = pl.program_id(0)
    steps = pl.num_programs(0)
    place = step ^ me_ref[0]
    hidden, width = a_ref.shape[0], mass_ref.shape[1]
    cells_at = part_of(step, width)
    kinds = side_ref.shape[0] - 16

    @pl.when(step == 0)
    def _():
        lane_ref[...] = jnp.zeros_like(lane_ref)
        oh_ref[...] = jnp.zeros_like(oh_ref)

    back = mass_ref[pl.ds(step, 1), :] * jnp.exp(-lib_ref[pl.ds(step, 1), :])
    wide = aff_ref[:, cells_at].astype(F32)
    dy = jnp.where(wide > 0, a_ref[:, cells_at] - back * r_ref[:, cells_at], 0.0)
    weighted = dy * wide
    lane_ref[...] += sum(weighted[:, t : t + 128] for t in range(0, width, 128))
    dy_low = dy.astype(BF)
    oh_ref[...] += nt(jnp.concatenate((side_ref[:, cells_at], z_ref[:, cells_at].astype(BF)), axis=0), dy_low)
    _, inv = norm_rows(stat_ref[...], latent - 8, cells)
    lat_high, lat_mid, _ = three(lat_ref[...] * (gain_ref[2:3] * inv) * (-1.0 / cells))
    both = nn(jnp.concatenate((lat_high, lat_mid), axis=0), dy_low)
    block = both[:16] + both[16:]
    row = lax.broadcasted_iota(jnp.int32, block.shape, 0)
    block = jnp.where(row == latent, recon_ref[pl.ds(step, 1), :], block)
    slot = lax.div(place, 2)

    @pl.when(lax.rem(place, 2) == 0)
    def _():
        keep_ref[slot] = block

    @pl.when(lax.rem(place, 2) == 1)
    def _():
        send_ref[slot] = block

    @pl.when(step == steps - 1)
    def _():
        scale = -1.0 / cells
        one, two = oh_ref[kinds : kinds + 1, :] * scale, row_sums(lane_ref[...])[0:1] * scale
        oh_ref[kinds : kinds + 16, :] = oh_ref[kinds + 16 :, :]
        part = (kinds + 16) // steps
        for core, ref in enumerate((keep_ref, send_ref)):
            for index in range(ref.shape[0]):
                ref[index, latent + 1 : latent + 2, 0:hidden] = one
                ref[index, latent + 2 : latent + 3, 0:hidden] = two
                owner = me_ref[0] ^ (2 * index + core)
                for k in range(part):
                    line = latent + 3 + k // 8
                    lanes = slice((k % 8) * hidden, (k % 8 + 1) * hidden)
                    ref[index, line : line + 1, lanes] = oh_ref[pl.ds(owner * part + k, 1), :] * scale


def dec_grad_kernel(cells, rt_ref, hid_ref, mass_ref, lib_ref, g_ref, acc_ref, dig_ref, par_ref, dec_ref, mix_ref):
    step = pl.program_id(0)
    steps = pl.num_programs(0)
    genes = rt_ref.shape[0]
    cells_at = part_of(step, mass_ref.shape[1])
    hidden = hid_ref.shape[0]

    @pl.when(step == 0)
    def _():
        mix_ref[...] = jnp.zeros_like(mix_ref)

    back = mass_ref[pl.ds(step, 1), :] * jnp.exp(-lib_ref[pl.ds(step, 1), :])
    back_high, back_mid, back_low = three(back)
    row = lax.broadcasted_iota(jnp.int32, (16, back.shape[1]), 0)
    extra = jnp.where(row == 0, back_high.astype(F32), jnp.where(row == 1, back_mid.astype(F32), 0.0))
    scaled = (relu_low(hid_ref[:, cells_at]).astype(F32) * back).astype(BF)
    mix_ref[...] += nt(rt_ref[:, cells_at], jnp.concatenate((scaled, extra.astype(BF)), axis=0))

    @pl.when(step == steps - 1)
    def _():
        scale = -1.0 / cells
        mix = mix_ref[...]
        dec_ref[:genes, :] = (g_ref[:genes, :] - mix[:, :hidden]) * scale
        dec_ref[genes : 2 * genes, :] = g_ref[genes:, :] * scale
        pick = jnp.where(lax.broadcasted_iota(jnp.int32, (8, 16), 1) < 2, 1.0, 0.0)
        score_row = row_sums(acc_ref[0]) - nt(pick, mix[:, hidden:], HI)
        drop_row = row_sums(acc_ref[1])
        disp_row = row_sums((acc_ref[2] + dig_ref[...]) * par_ref[1])
        line = lax.broadcasted_iota(jnp.int32, score_row.shape, 0)
        gene_rows = scale * jnp.where(
            line == 0, score_row, jnp.where(line == 1, drop_row, jnp.where(line == 2, disp_row, 0.0))
        )
        dec_ref[2 * genes :, :] = lines(gene_rows, pl.cdiv(genes, 128))


def enc_back_kernel(cells, latent, fast, span, me_ref, own_ref, dnear_ref, dfar_ref, aff_dec_ref, sums_ref, stat_ref, gain_ref, lat_ref, noise_ref, klw_ref, anear_ref, afar_ref, side_ref, held_ref, logc_ref, cols_ref, z_ref, out_ref, rest_ref, lane_ref, left_ref, fixed_ref, one_ref, kept_ref, sum_ref):
    step = pl.program_id(0)
    steps = kept_ref.shape[0]
    genes, width = logc_ref.shape[0], dnear_ref.shape[2]
    hidden = aff_dec_ref.shape[0]
    cells_at = part_of(step, width)
    place = (step ^ me_ref[0]) if fast else step
    kinds = (rest_ref.shape[0] - 64) // 2
    at = latent + 1 - 8
    m_one, m_two = norm_sums(sums_ref[at : at + 2], gain_ref, 2)
    m_two = m_two / gain_ref[2:3] * (1.0 / cells)
    m_one = m_one * (1.0 / cells) - m_two * gain_ref[3:4]

    @pl.when(step == 0)
    def _():
        out_ref[...] = jnp.zeros_like(out_ref)
        rest_ref[...] = jnp.zeros_like(rest_ref)
        lane_ref[...] = jnp.zeros_like(lane_ref)
        sum_ref[...] = jnp.zeros_like(sum_ref)
        _, inv = norm_rows(stat_ref[...], latent - 8, cells)
        lat = lat_ref[...] * (gain_ref[2:3] * inv)
        fixed_ref[...] = jnp.broadcast_to(jnp.sum(lat * m_one, axis=1, keepdims=True), fixed_ref.shape)
        high, mid, _ = three(lat * m_two)
        left_ref[...] = jnp.concatenate((high, mid), axis=0)

    index = lax.div(place, 2) if fast else place
    near = (lax.rem(place, 2) == 0) if fast else None

    def take(near_ref, far_ref, rows, lanes):
        if not fast:
            return near_ref[index, rows, lanes]
        return jnp.where(near, near_ref[index, rows, lanes], far_ref[index, rows, lanes])

    every = slice(0, width)
    scale = klw_ref[0:1, 0:1] * (1.0 / cells)
    affine_dec = aff_dec_ref[:, cells_at]
    both = nn(left_ref[...], affine_dec)
    block = take(dnear_ref, dfar_ref, slice(0, 16), every)
    kept_ref[step] = block[8:]
    grad_z = (block - fixed_ref[:, 0:1] - (both[:16] + both[16:]))[:latent]
    noise = noise_ref[:, cells_at]
    pieces = take(anear_ref, afar_ref, slice(hidden, hidden + 48), every).astype(F32)
    lat_logvar = (pieces[:latent] + pieces[16 : 16 + latent]) + pieces[32 : 32 + latent]
    spread = jnp.exp(lat_logvar)
    var = spread + 0.0001
    inv_std = lax.rsqrt(var)
    z = z_ref[:, cells_at]
    lat_mean = z[0:latent] - var * inv_std * noise
    g_mean = latent_rows(grad_z + scale * lat_mean)
    g_var = latent_rows(spread * (grad_z * noise * (0.5 * inv_std) + (0.5 * scale) * (1.0 - inv_std * inv_std)))
    g_head = jnp.concatenate((g_mean, g_var), axis=0)
    sum_ref[0:32, :] += sum(g_head[:, t : t + 128] for t in range(0, width, 128))
    sum_ref[32:, :] += sum(z[:, t : t + 128] for t in range(0, width, 128))
    head_high, head_mid, _ = three(g_head)
    heads = jnp.concatenate((head_high, head_mid, head_high), axis=0)
    for begin in range(0, width, span):
        lanes = slice(begin, begin + span)
        affine = take(anear_ref, afar_ref, slice(0, hidden), lanes)
        one_ref[hidden:, lanes] = relu_low(affine)
        wide = affine.astype(F32)
        dy = jnp.where(wide > 0, nn(cols_ref[...], heads[:, lanes]), 0.0)
        one_ref[0:hidden, lanes] = dy.astype(BF)
        weighted = dy * wide
        lane_ref[...] += sum(weighted[:, t : t + 128] for t in range(0, span, 128))
    dy_low = one_ref[0:hidden, :]
    side = side_ref[:, cells_at]
    out_ref[0:genes, :] += nt(logc_ref[:, cells_at], dy_low)
    mixed = nt(side, dy_low)
    rest_ref[0:kinds, :] += mixed[:kinds]
    out_ref[genes : genes + 1, :] += mixed[kinds : kinds + 1]
    rest_ref[kinds : kinds + 32, :] += nt(head_high, one_ref[hidden:, :])
    base = kinds + 40
    product = nt(jnp.concatenate((side, z.astype(BF)), axis=0), affine_dec)
    rest_ref[base : base + kinds, :] -= product[:kinds] * m_two
    rest_ref[base + kinds : base + kinds + 16, :] -= product[kinds + 16 :] * m_two

    @pl.when(step == steps - 1)
    def _():
        out_ref[genes + 1 : genes + 2, :] = row_sums(lane_ref[...])[0:1]
        rest_ref[kinds + 32 : kinds + 40, 0:32] = row_sums(sum_ref[0:32, :])
        held = jnp.concatenate((held_ref[...], sum_ref[32:, :]), axis=0)
        rest_ref[base : base + kinds + 16, :] -= jnp.sum(held, axis=1, keepdims=True) * m_one
        count = (kinds + 16) // steps
        for owner in range(steps):
            for k in range(count):
                line = latent + 3 + k // 8 - 8
                at = slice(base + owner * count + k, base + owner * count + k + 1)
                rest_ref[at, :] += kept_ref[owner, line : line + 1, (k % 8) * hidden : (k % 8 + 1) * hidden]
        size = rest_ref.shape[0] // 8
        out_ref[genes + 8 :, :] = rest_ref[pl.ds(pl.multiple_of((own_ref[0] & 7) * size, 8), size), :]


def whole_gradient(part, product, plain, gain, shift, inv, one, two):
    return (gain * inv) * (part - plain * one - ((product - plain * shift) / gain) * two)


def norm_sums(rows, norm_ref, at):
    return rows[0:1], (rows[1:2] - norm_ref[at + 1 : at + 2] * rows[0:1]) / norm_ref[at : at + 1]


def finish_kernel(cells, latent, sum_ref, dec_ref, fixed_ref, stat_enc_ref, norm_ref, kl_ref, klw_ref, own_ref, enc_out, tail_out, loss_out):
    genes = enc_out.shape[0]
    size = tail_out.shape[0] - 8
    count = pl.cdiv(genes, 128)
    kinds = fixed_ref.shape[0] - genes - 8 * count - 8
    loss_out[...] = klw_ref[0:1, 0:1] * kl_ref[...] - own_ref[latent : latent + 1, :]
    _, inv = norm_rows(stat_enc_ref[...], 0, cells)
    n_one, n_two = norm_sums(sum_ref[genes : genes + 8, :], norm_ref, 0)
    at = genes + kinds
    logs = jnp.concatenate([fixed_ref[at + 8 * i : at + 8 * (i + 1), :] for i in range(count)], axis=1)
    log_sum = jnp.transpose(logs)[:genes, 0:1]
    enc = whole_gradient(
        sum_ref[0:genes, :], fixed_ref[0:genes, :], log_sum, norm_ref[0:1], norm_ref[1:2], inv, n_one * (1.0 / cells), n_two * (1.0 / cells)
    )
    enc_out[...] = enc
    dec = dec_ref[...]
    lane = jnp.sum(enc * enc, axis=0, keepdims=True) + jnp.sum(dec * dec, axis=0, keepdims=True)
    tail_out[0:size, :] = sum_ref[genes + 8 :, :]
    tail_out[size:, :] = jnp.broadcast_to(jnp.sum(lane, axis=1, keepdims=True), (8, tail_out.shape[1]))


def step_of(weight, gradient, first, second, rate):
    first = beta_one * first + (1.0 - beta_one) * gradient
    second = beta_two * second + (1.0 - beta_two) * gradient * gradient
    fixed_one = first * (1.0 / (1.0 - beta_one**step_number))
    fixed_two = second * (1.0 / (1.0 - beta_two**step_number))
    update = fixed_one / (jnp.sqrt(fixed_two) + 1e-08) + decay_rate * weight
    return weight - rate * update, first, second


def update_kernel(cells, latent, me_ref, near_ref, far_ref, enc_g_ref, dec_g_ref, sum_ref, fixed_ref, stat_enc_ref, stat_dec_ref, sums_ref, *refs):
    ins, outs, (rest_ref, small_g_ref, head_g_ref, norm_g_ref) = refs[:18], refs[18:-4], refs[-4:]
    enc, dec, gene, small, head, norm = (ins[3 * i : 3 * i + 3] for i in range(6))
    genes, hidden = enc[0].shape
    rows = small[0].shape[0]
    kinds = (rows - latent) // 2
    count = pl.cdiv(genes, 128)
    size = near_ref.shape[1]
    for core, ref in enumerate((near_ref, far_ref)):
        for index in range(ref.shape[0]):
            owner = me_ref[0] ^ (2 * index + core)
            rest_ref[pl.ds(pl.multiple_of(owner * size, 8), size), :] = ref[index]
    whole_rest = [rest_ref[i * size : i * size + size - 8, :] for i in range(8)]
    square = jnp.zeros((1, 1), F32)
    for i in range(8):
        square = square + rest_ref[(i + 1) * size - 8 : (i + 1) * size - 7, 0:1]
    rest = jnp.concatenate(whole_rest, axis=0)
    gains = norm[0]
    gain, shift = gains[0:1], gains[1:2]
    n_one, n_two = norm_sums(sum_ref[genes : genes + 8, :], gains, 0)
    _, inv = norm_rows(stat_enc_ref[...], 0, cells)
    _, inv_dec = norm_rows(stat_dec_ref[...], latent - 8, cells)
    at = genes + kinds + 8 * count
    batch_sum = jnp.transpose(fixed_ref[at : at + 8, :])[:kinds, 0:1]
    small_g_ref[0:kinds, :] = whole_gradient(
        rest[0:kinds], fixed_ref[genes : genes + kinds, :], batch_sum, gain, shift, inv, n_one * (1.0 / cells), n_two * (1.0 / cells)
    )
    small_g_ref[kinds:, :] = (gains[2:3] * inv_dec) * rest[kinds + 40 : 2 * kinds + 56]
    bias = jnp.transpose(rest[kinds + 32 : kinds + 40])
    for half in range(2):
        into = slice(half * latent, (half + 1) * latent)
        head_g_ref[into, 0:hidden] = rest[kinds + 16 * half : kinds + 16 * half + latent]
        head_g_ref[into, hidden : hidden + 1] = bias[16 * half : 16 * half + latent, 0:1]
    at = latent + 1 - 8
    norm_g_ref[0:1] = n_two
    norm_g_ref[1:2] = n_one
    m_one, m_two = norm_sums(sums_ref[at : at + 2], gains, 2)
    norm_g_ref[2:3] = m_two
    norm_g_ref[3:4] = m_one
    small_square = jnp.zeros((1, 1), F32)
    for part in (small_g_ref[0:rows, :], head_g_ref[...], norm_g_ref[...]):
        small_square = small_square + jnp.sum(jnp.sum(part * part, axis=0, keepdims=True), axis=1, keepdims=True)
    value = jnp.sqrt(square + small_square)
    factor = jnp.minimum(1.0, max_norm / value)
    (enc_n, enc_m, enc_v, enc_l, dec_n, dec_m, dec_v, dec_l, gene_n, gene_m, gene_v, small_n, small_m, small_v, head_n, head_m, head_v, norm_n, norm_m, norm_v, norm_out) = outs
    norm_out[...] = value
    new, first, second = step_of(enc[0][...], enc_g_ref[...] * factor, enc[1][...], enc[2][...], rate_genes)
    enc_n[...], enc_m[...], enc_v[...], enc_l[...] = new, first, second, new.astype(BF)
    for index in range(2):
        gradient = dec_g_ref[index * genes : (index + 1) * genes, :] * factor
        new, first, second = step_of(dec[0][index], gradient, dec[1][index], dec[2][index], rate_genes)
        dec_n[index], dec_m[index], dec_v[index], dec_l[index] = new, first, second, new.astype(BF)
    for index in range(pl.cdiv(genes, 128)):
        span = slice(index * 128, min(genes, (index + 1) * 128))
        gradient = dec_g_ref[2 * genes + index * 8 : 2 * genes + index * 8 + 3, 0 : span.stop - span.start] * factor
        new, first, second = step_of(gene[0][:, span], gradient, gene[1][:, span], gene[2][:, span], rate_small)
        gene_n[:, span], gene_m[:, span], gene_v[:, span] = new, first, second
    new, first, second = step_of(small[0][...], small_g_ref[0:rows, :] * factor, small[1][...], small[2][...], rate_small)
    small_n[...], small_m[...], small_v[...] = new, first, second
    new, first, second = step_of(head[0][...], head_g_ref[...] * factor, head[1][...], head[2][...], rate_small)
    head_n[...], head_m[...], head_v[...] = new, first, second
    new, first, second = step_of(norm[0][...], norm_g_ref[...] * factor, norm[1][...], norm[2][...], rate_small)
    norm_n[...], norm_m[...], norm_v[...] = new, first, second


def gather_genes(value, fast, blocks, width, late=None):
    if fast:
        near = jnp.stack([value] + [swap(value, "genes", 2 * k) for k in (1, 2, 3)])
        near = near if late is None else after(near, late)
        return near, swap(near, "genes", 1)
    rows = value.shape[0]
    whole_rows = lax.all_gather(value, "genes", axis=0).transpose(1, 0, 2)
    near = whole_rows.reshape(rows, blocks, width).transpose(1, 0, 2)
    return near, near


def per_device(counts, library, noise, batch_ids, gene_mask, kl_weight, enc_w, enc_m, enc_v, dec_w, dec_m, dec_v, gene_par, gene_m, gene_v, small_w, small_m, small_v, head_w, head_m, head_v, norm_par, norm_m, norm_v):
    rows_all, genes = counts.shape
    cells = float(rows_all * lax.axis_size("cells"))
    groups = lax.axis_size("genes")
    hidden = enc_w.shape[1]
    latent = head_w.shape[1] // 2
    kinds = (small_w.shape[0] - latent) // 2
    share = rows_all // groups
    width = min(1024, rows_all)
    blocks = rows_all // width
    fast = groups == 8 and blocks == 8
    me = lax.axis_index("genes").astype(jnp.int32).reshape(1)
    gene_lines = -(-genes // 128)

    def turn(value):
        return value.transpose(0, 2, 1)

    x_t = counts.T
    noise_t = noise.T
    dec_t = turn(dec_w)
    head_t = head_w.T
    lib8 = library.reshape(blocks, width)
    batch_all = batch_ids.reshape(blocks, 1, width)
    batch_own = batch_ids.reshape(groups, 1, share)
    klw = jnp.broadcast_to(kl_weight.reshape(1, 1), (8, 128))

    own_block = pl.BlockSpec((1, 1, share), lambda i, m: (m[0], 0, 0))
    own_lanes = lambda rows: pl.BlockSpec((rows, share), lambda i, m: (0, m[0]))
    lane_block = lambda rows: pl.BlockSpec((rows, width), lambda i, *_: (0, i))
    here = pl.BlockSpec(memory_space=pltpu.VMEM)
    full = lambda array: (array, here)
    out_of = lambda shape, dtype=F32: (shape, dtype, whole(shape))
    new = lambda shape, dtype=F32: (shape, dtype, here)

    def encode(low, count, weight, near=False):
        return call(
            lambda *refs: enc_kernel(low, count, share, near, *refs),
            (1,),
            [
                (me if fast else me & 1, None),
                (x_t, here) if near else (in_hbm(x_t), pl.BlockSpec(memory_space=pl.ANY)),
                (in_hbm(weight), pl.BlockSpec(memory_space=pl.ANY)),
            ],
            [new((count // 2, hidden, share)), new((count // 2, hidden, share), BF)],
            scratch=[
                pltpu.VMEM((genes, hidden), F32),
                pltpu.VMEM((hidden, genes), BF),
                pltpu.SemaphoreType.DMA((count + 1,)),
            ]
            + ([] if near else [pltpu.VMEM((count, genes, share), BF)]),
            scalars=1,
            us=2.0 if near else 3.0,
            mib=16,
        )

    slot = pl.BlockSpec((1, hidden, share), lambda i, m: (0, 0, 0))
    if fast:
        keep_far, send_far = encode(4, 4, enc_w)
        got_far = swap(send_far, "genes", 1)
        keep_near, send_near = encode(0, 4, after(enc_w, send_far), True)
        far = [
            swap((keep_far[k : k + 1] + got_far[k : k + 1].astype(F32)).astype(BF), "genes", 4 + 2 * k)
            for k in range(2)
        ]
        got = swap(send_near, "genes", 1)
        ready = (keep_near[1:2] + got[1:2].astype(F32)).astype(BF)
        far.append(swap(ready, "genes", 2))
        kept = keep_near
    else:
        keep_part, send_part = encode(0, groups, enc_w)
        got = swap(send_part, "genes", 1)
        summed = lax.psum_scatter(
            keep_part + got.astype(F32),
            "genes",
            scatter_dimension=0,
            axis_index_groups=[list(range(c, groups, 2)) for c in range(2)],
            tiled=True,
        )
        zero = jnp.zeros((1, hidden, share), BF)
        kept, got, far = summed, zero, [zero] * 3
        ready = keep_part

    mask_late = after(gene_mask.reshape(1, genes), ready)
    aug, dec_n, par, lg_tab, dg_tab, enc_pieces, dec_pieces, dec_plain, lat_row, head_rows, head_bias, head_cols, norm_t = call(
        prep_kernel,
        (1,),
        [full(gene_par), full(mask_late), full(dec_t), full(small_w), full(head_t), full(norm_par)],
        [
            new((2 * genes, hidden + 16), BF),
            new((hidden, 2 * genes), BF),
            new((5, genes, 128)),
            new((COUNT_TOP, genes, 128)),
            new((COUNT_TOP, genes, 128)),
            new((3 * hidden, kinds), BF),
            new((3 * hidden, kinds + 48), BF),
            new((hidden, kinds + 16)),
            new((16, hidden)),
            new((32, hidden)),
            new((32, 128)),
            new((hidden, 96), BF),
            new((hidden, 8)),
        ],
    )
    batch_spec = pl.BlockSpec((1, 1, width), lambda i, *_: (i, 0, 0))
    logc, x_kept, side, lib8, gam_cell, dig_acc, log_lines, held = call(
        lambda *refs: counts_kernel(16, min(512, width), *refs),
        (blocks,),
        [
            (x_t, here),
            full(lg_tab),
            full(dg_tab),
            full(par),
            (batch_all, batch_spec),
            full(lib8),
        ],
        [
            ((genes, rows_all), BF, lane_block(genes), True),
            ((genes, rows_all), BF, lane_block(genes), True),
            ((kinds + 16, rows_all), BF, here),
            new((blocks, width)),
            new((blocks, width)),
            new((genes, 128)),
            new((8 * gene_lines + 8, 128)),
            new((kinds, 128)),
        ],
        scratch=[pltpu.VMEM((genes, 128), F32)],
        mib=16,
        us=15.0,
    )
    enc_late = after(enc_pieces, log_lines)
    stat8 = whole((8, hidden))
    pre_enc, stat_enc = call(
        own_kernel,
        (1,),
        [(me, None), (kept, slot), (got, slot)]
        + [(part, slot) for part in far]
        + [(batch_own, own_block), full(enc_late)],
        [new((hidden, share)), new((8, hidden))],
        scalars=1,
    )
    stat_enc = total(total(stat_enc, "genes"), "cells")

    pack, aff_own, kl_row = call(
        lambda *refs: latent_kernel(cells, latent, *refs),
        (1,),
        [
            (me, None),
            full(pre_enc),
            full(stat_enc),
            full(norm_t),
            full(head_rows),
            full(head_bias),
            (noise_t, own_lanes(latent)),
            (batch_own, own_block),
            full(dec_pieces),
        ],
        [new((16, share)), new((hidden + 48, share), BF), new((1, share))],
        scalars=1,
    )
    near, far_pack = gather_genes(pack, fast, blocks, width)
    if fast:
        stat_dec = jnp.sum(near[:, 8:16, :hidden], axis=0) + jnp.sum(far_pack[:, 8:16, :hidden], axis=0)
    else:
        stat_dec = lax.psum(pack[8:16, :hidden], "genes")
    stat_dec = total(stat_dec, "cells")

    aff_dec, lse, z_all, top, mass_all = call(
        lambda *refs: decode_kernel(cells, latent, fast, *refs),
        (blocks,),
        [
            (me, None),
            (near, here),
            (far_pack, here),
            (side, here),
            full(stat_dec),
            full(norm_t),
            full(dec_plain),
            full(aug),
        ],
        [
            ((hidden, rows_all), BF, here),
            new((blocks, width)),
            ((16, rows_all), F32, here),
            new((blocks, width)),
            ((genes, rows_all), F32, here),
        ],
        scratch=[pltpu.VMEM((genes, width), F32), pltpu.VMEM((2 * hidden, kinds + 48), BF)],
        scalars=1,
        us=8.0,
    )
    lse_all = log_total_of(lse, "genes")

    full8 = whole((blocks, width))
    g_both, rt, mass, recon, gene_acc = call(
        lambda *refs: zinb_kernel(64, min(512, width), *refs),
        (blocks,),
        [
            (aff_dec, here),
            (mass_all, here),
            full(top),
            full(aug),
            (in_hbm(x_kept), lane_block(genes)),
            full(par),
            full(lib8),
            full(lse_all),
            full(gam_cell),
        ],
        [((2 * genes, rows_all), BF, here), ((genes, rows_all), BF, here)]
        + [new((blocks, width)), new((blocks, width)), new((3, genes, 128))],
        scratch=[pltpu.VMEM((genes, width), F32)],
        mib=20,
        us=28.0,
    )
    mass_low = mass + swap(mass, "genes", 1)
    mass = total(mass_low, "genes", 1)
    part_a, part_r, dec_acc = call(
        lambda *refs: back_kernel(width, *refs),
        (blocks,),
        [
            (g_both, here),
            (rt, here),
            (aff_dec, here),
            full(dec_n),
        ],
        [
            ((hidden, rows_all), F32, here),
            ((hidden, rows_all), F32, here),
            new((2 * genes, hidden)),
        ],
        mib=16,
        us=9.0,
    )

    aff_near, aff_far = gather_genes(after(aff_own, lse_all), fast, blocks, width, mass_low)
    fixed_rows = genes + kinds + 8 * gene_lines + 8
    (fixed,) = call(
        lambda *refs: enc_sums_kernel(fast, *refs),
        (blocks,),
        [
            (me, None),
            (logc, here),
            (aff_near, here),
            (aff_far, here),
            (side, here),
            full(log_lines),
        ],
        [new((fixed_rows, hidden))],
        scalars=1,
        us=4.0,
    )
    fixed = total_by_halves(fixed, "cells", (1, 2))

    keep_d, send_d = call(
        lambda *refs: hidden_grad_kernel(cells, latent, *refs),
        (blocks,),
        [
            (me if fast else jnp.zeros_like(me), None),
            (part_a, here),
            (part_r, here),
            (mass, here),
            (aff_dec, here),
            full(lib8),
            full(stat_dec),
            full(norm_par),
            full(lat_row),
            full(recon),
            (z_all, here),
            (side, here),
        ],
        [
            new((blocks // 2, 16, width)),
            new((blocks // 2, 16, width)),
        ],
        scratch=[pltpu.VMEM((hidden, 128), F32), pltpu.VMEM((kinds + 32, hidden), F32)],
        scalars=1,
        us=5.0,
    )
    (dec_part,) = call(
        lambda *refs: dec_grad_kernel(cells, *refs),
        (blocks,),
        [
            (rt, here),
            (aff_dec, here),
            (mass, here),
            full(lib8),
            full(dec_acc),
            full(gene_acc),
            full(dig_acc),
            full(par),
        ],
        [new((2 * genes + 8 * gene_lines, hidden))],
        scratch=[pltpu.VMEM((genes, hidden + 16), F32)],
        us=5.0,
    )
    if fast:
        got_d = swap(send_d, "genes", 1)
        pieces = [swap(keep_d[k] + got_d[k], "genes", 2 * k) for k in (1, 2, 3)]
        pieces = [after(piece, dec_part) for piece in pieces]
        own_d = (keep_d[0] + got_d[0] + pieces[0]) + (pieces[1] + pieces[2])
        sums_dec = own_d[8:, :hidden]
    else:
        both = jnp.stack([keep_d, send_d], axis=1).reshape(blocks, 16, width)
        sums_dec = lax.psum(both[0, 8:, :hidden], "genes")
        both = both.transpose(1, 0, 2).reshape(16, groups, share).transpose(1, 0, 2)
        own_d = lax.psum_scatter(both, "genes", scatter_dimension=0, tiled=True)[0]
    sums_dec = total(sums_dec, "cells")
    d_near, d_far = gather_genes(own_d, fast, blocks, width)
    dec_g = total_by_halves(dec_part, "cells", (2, 1))

    size = (2 * kinds + 64) // 8
    (enc_part,) = call(
        lambda *refs: enc_back_kernel(cells, latent, fast, min(256, width), *refs),
        (blocks,),
        [
            (me, None),
            (me, None),
            (d_near, here),
            (d_far, here),
            (aff_dec, here),
            full(sums_dec),
            full(stat_dec),
            full(norm_par),
            full(lat_row),
            (noise_t, here),
            full(klw),
            (aff_near, here),
            (aff_far, here),
            (side, here),
            full(held),
            (logc, here),
            full(head_cols),
            (z_all, here),
        ],
        [new((genes + 8 + size, hidden))],
        scratch=[
            pltpu.VMEM((2 * kinds + 64, hidden), F32),
            pltpu.VMEM((hidden, 128), F32),
            pltpu.VMEM((32, hidden), BF),
            pltpu.VMEM((16, 128), F32),
            pltpu.VMEM((2 * hidden, width), BF),
            pltpu.VMEM((blocks, 8, width), F32),
            pltpu.VMEM((48, 128), F32),
        ],
        scalars=2,
        us=11.0,
    )
    enc_sum = total_by_halves(enc_part, "cells", (1, 2))
    enc_g, tail, loss = call(
        lambda *refs: finish_kernel(cells, latent, *refs),
        (1,),
        [full(a) for a in (enc_sum, dec_g, fixed, stat_enc, norm_par, kl_row, klw, own_d)],
        [new((genes, hidden)), new((size + 8, hidden)), new((1, share))],
    )
    if fast:
        tail_near = jnp.stack([tail] + [swap(tail, "genes", 2 * k) for k in (1, 2, 3)])
        tail_far = swap(tail_near, "genes", 1)
    else:
        tails = lax.all_gather(tail, "genes", axis=0)
        square = jnp.sum(tails[:, size:], axis=0)
        tails = tails[:8].at[:, size:].set(0.0).at[0, size:].set(square)
        tail_near, tail_far = tails[0::2], tails[1::2]

    state = [
        enc_w, enc_m, enc_v, dec_t, turn(dec_m), turn(dec_v), gene_par, gene_m, gene_v,
        small_w, small_m, small_v, head_t, head_m.T, head_v.T, norm_par, norm_m, norm_v,
    ]
    ins = [tail_near, tail_far, enc_g, dec_g, enc_sum, fixed, stat_enc, stat_dec, sums_dec] + state
    outs = []
    for index in range(6):
        one = state[3 * index]
        outs += [(one.shape, F32)] * 3
        if index < 2:
            outs.append((one.shape, BF))
    outs.append(((1, 1), F32))
    res = call(
        lambda *refs: update_kernel(cells, latent, *refs),
        (1,),
        [(me if fast else jnp.zeros_like(me), None)] + [full(array) for array in ins],
        [out_of(shape, dtype) for shape, dtype in outs],
        scratch=[
            pltpu.VMEM((8 * (size + 8), hidden), F32),
            pltpu.VMEM((2 * kinds + 16, hidden), F32),
            pltpu.VMEM((2 * latent, hidden + 1), F32),
            pltpu.VMEM((4, hidden), F32),
        ],
        scalars=1,
        mib=16,
    )
    enc_res, dec_res = res[0:4], [turn(part) for part in res[4:8]]
    head_res = [part.T for part in res[14:17]]
    return (
        *enc_res,
        *dec_res,
        *res[8:14],
        *head_res,
        *res[17:20],
        res[20].reshape(()),
        loss.reshape(share),
    )


def solution(mesh):
    placed = (
        P("cells", "genes"), P("cells"), P("cells", None), P("cells"), P("genes"), P(),
        P("genes", None), P("genes", None), P("genes", None),
        P(None, None, "genes"), P(None, None, "genes"), P(None, None, "genes"),
        P(None, "genes"), P(None, "genes"), P(None, "genes"),
        P(), P(), P(), P(), P(), P(), P(), P(), P(),
    )
    return jax.shard_map(
        per_device,
        mesh=mesh,
        in_specs=placed,
        out_specs=(
            P("genes", None), P("genes", None), P("genes", None), P("genes", None),
            P(None, None, "genes"), P(None, None, "genes"), P(None, None, "genes"), P(None, None, "genes"),
            P(None, "genes"), P(None, "genes"), P(None, "genes"),
            P(), P(), P(), P(), P(), P(), P(), P(), P(), P(),
            P(("cells", "genes")),
        ),
        check_vma=False,
    )
```

```python
import jax
import jax.numpy as jnp
from jax import lax
from jax.experimental import pallas as pl
from jax.experimental.pallas import tpu as pltpu
from jax.sharding import PartitionSpec as P

norm_epsilon = 0.001
zinb_epsilon = 1e-08
beta_one = 0.9
beta_two = 0.999
step_number = 5.0
decay_rate = 0.01
rate_genes = 0.03
rate_small = 0.2
max_norm = 0.1

F32 = jnp.float32
BF = jnp.bfloat16
HI = lax.Precision.HIGHEST
COUNT_TOP = 8
LOG2_E = 1.4426950408889634


def nn(left, right, precision=None):
    return lax.dot_general(
        left, right, (((1,), (0,)), ((), ())), precision=precision, preferred_element_type=F32
    )


def nt(left, right, precision=None):
    return lax.dot_general(
        left, right, (((1,), (1,)), ((), ())), precision=precision, preferred_element_type=F32
    )


def whole(shape):
    return pl.BlockSpec(shape, lambda *_: (0,) * len(shape))


def in_hbm(array):
    return pltpu.with_memory_space_constraint(array, pltpu.HBM)


def call(kernel, grid, ins, outs, scratch=(), scalars=0, us=2.0, mib=12):
    return pl.pallas_call(
        kernel,
        out_shape=[pltpu.HBM(out[0], out[1]) if len(out) == 4 else jax.ShapeDtypeStruct(out[0], out[1]) for out in outs],
        grid_spec=pltpu.PrefetchScalarGridSpec(
            num_scalar_prefetch=scalars,
            grid=grid,
            in_specs=[spec for _, spec in ins[scalars:]],
            out_specs=[out[2] for out in outs],
            scratch_shapes=list(scratch),
        ),
        compiler_params=pltpu.CompilerParams(vmem_limit_bytes=mib * 1024 * 1024),
        cost_estimate=pl.CostEstimate(flops=0, bytes_accessed=int(us * 3.69e6), transcendentals=0),
    )(*[array for array, _ in ins])


def swap(value, axis, bit):
    count = lax.axis_size(axis)
    return lax.ppermute(value, axis, [(i, i ^ bit) for i in range(count)])


def bit_groups(axis):
    count = lax.axis_size(axis)
    if axis == "genes":
        groups, bit = [[1]], 2
    else:
        groups, bit = [], 1
    while bit < count:
        groups.append([bit, 2 * bit] if 2 * bit < count else [bit])
        bit *= 4
    return groups


def total(value, axis, done=0):
    for group in bit_groups(axis)[done:]:
        if len(group) == 1:
            value = value + swap(value, axis, group[0])
        else:
            low, high = group
            value = (value + swap(value, axis, low)) + (
                swap(value, axis, high) + swap(value, axis, low ^ high)
            )
    return value


def log_total_of(value, axis):
    for group in bit_groups(axis):
        if len(group) == 1:
            parts = [value, swap(value, axis, group[0])]
        else:
            low, high = group
            parts = [value] + [swap(value, axis, k) for k in (low, high, low ^ high)]
        top = parts[0]
        for part in parts[1:]:
            top = jnp.maximum(top, part)
        mass = sum(jnp.exp(part - top) for part in parts)
        value = top + jnp.log(mass)
    return value


def total_by_halves(value, axis, order):
    for bit in order:
        value = value + swap(value, axis, bit)
    return value


def after(value, *others):
    return lax.optimization_barrier((value,) + others)[0]


def three(value):
    high = value.astype(BF)
    rest = value - high.astype(F32)
    mid = rest.astype(BF)
    low = (rest - mid.astype(F32)).astype(BF)
    return high, mid, low


def one_hot(batch_row, kinds):
    ids = lax.broadcasted_iota(jnp.int32, (kinds, batch_row.shape[1]), 0)
    return jnp.where(ids == batch_row, 1.0, 0.0)


def columns(rows):
    return jnp.transpose(rows)


def prep_kernel(gene_ref, mask_ref, dec_ref, small_ref, head_ref, norm_ref, aug_ref, turn_ref, par_ref, lg_ref, dg_ref, enc_out, dec_out, plain_out, lat_out, head_out, bias_out, cols_out, norm_out):
    genes = gene_ref.shape[1]
    hidden = norm_ref.shape[1]
    latent = head_ref.shape[0] // 2
    kinds = (small_ref.shape[0] - latent) // 2
    padded = pl.cdiv(genes, 128) * 128
    keep = mask_ref[...] > 0
    score_b = jnp.where(keep, gene_ref[0:1], -1e30)
    drop_b = jnp.where(keep, gene_ref[1:2], 1e30)
    th = jnp.exp(gene_ref[2:3])
    kept = jnp.where(keep, 1.0, 0.0)
    rows = jnp.concatenate((score_b, drop_b, th, kept, th, th, th, th), axis=0)
    if padded > genes:
        rows = jnp.concatenate((rows, jnp.ones((8, padded - genes), F32)), axis=1)
    turned = jnp.transpose(rows)[:genes]
    lane = lax.broadcasted_iota(jnp.int32, (genes, 16), 1)
    for half in range(2):
        at = slice(half * genes, (half + 1) * genes)
        aug_ref[at, 0:hidden] = dec_ref[half].astype(BF)
        high, mid, low = (jnp.broadcast_to(part.astype(F32), (genes, 16)) for part in three(turned[:, half : half + 1]))
        tail = jnp.where(lane == 0, high, jnp.where(lane == 1, mid, jnp.where(lane == 2, low, 0.0)))
        if half == 0:
            tail = jnp.where((lane >= 3) & (lane < 6), 1.0, tail)
        aug_ref[at, hidden : hidden + 16] = tail.astype(BF)
        turn_ref[:, at] = jnp.transpose(dec_ref[half]).astype(BF)
    th_w = jnp.broadcast_to(turned[:, 2:3], (genes, 128))
    keep_w = jnp.broadcast_to(turned[:, 3:4], (genes, 128))
    the_w = th_w + zinb_epsilon
    par_ref[0] = the_w
    par_ref[1] = th_w
    par_ref[2] = jnp.log(the_w)
    par_ref[3] = th_w / the_w
    par_ref[4] = keep_w
    gam = jnp.zeros_like(th_w)
    dig = jnp.zeros_like(th_w)
    for k in range(COUNT_TOP):
        more = th_w + float(k)
        gam = gam + keep_w * jnp.log(more * (1.0 / (1.0 + k)))
        dig = dig + keep_w / more
        lg_ref[k] = gam
        dg_ref[k] = dig
    for index, piece in enumerate(three(jnp.transpose(small_ref[0:kinds, :]))):
        enc_out[index * hidden : (index + 1) * hidden, :] = piece
    row = lax.broadcasted_iota(jnp.int32, (16, hidden), 0)
    lat_row = jnp.zeros((16, hidden), F32)
    for index in range(latent):
        lat_row = jnp.where(row == index, small_ref[2 * kinds + index : 2 * kinds + index + 1, :], lat_row)
    lat_out[...] = lat_row
    batch_turned, lat_turned = jnp.transpose(small_ref[kinds : 2 * kinds, :]), jnp.transpose(lat_row)
    plain_out[...] = jnp.concatenate((batch_turned, lat_turned), axis=1)
    batch_pieces = three(batch_turned)
    lat = three(lat_turned)
    zero = jnp.zeros_like(lat[0])
    tails = ((lat[0], lat[0], lat[0]), (lat[1], lat[1], zero), (lat[2], zero, zero))
    for index in range(3):
        at = slice(index * hidden, (index + 1) * hidden)
        dec_out[at, :] = jnp.concatenate((batch_pieces[index],) + tails[index], axis=1)
    full = lax.broadcasted_iota(jnp.int32, (32, hidden), 0)
    head = jnp.zeros((32, hidden), F32)
    bias = jnp.zeros((32, 1), F32)
    for index in range(2 * latent):
        to = index if index < latent else index - latent + 16
        head = jnp.where(full == to, head_ref[index : index + 1, 0:hidden], head)
        bias = jnp.where(full[:, 0:1] == to, head_ref[index : index + 1, hidden : hidden + 1], bias)
    head_out[...] = head
    bias_out[...] = jnp.broadcast_to(bias, (32, 128))
    high, mid, _ = three(jnp.transpose(head))
    cols_out[...] = jnp.concatenate((high, high, mid), axis=1)
    norm_out[...] = jnp.transpose(jnp.concatenate((norm_ref[...], norm_ref[...]), axis=0))


def exact_rows(stacked, table):
    out = nn(stacked, table)
    hidden = out.shape[0] // 3
    return out[:hidden] + out[hidden : 2 * hidden] + out[2 * hidden :]


def dec_table(z, batch_row, kinds):
    high, mid, low = three(z)
    return jnp.concatenate((one_hot(batch_row, kinds).astype(BF), high, mid, low), axis=0)


def row_sums(value):
    return nt(jnp.ones((8, value.shape[1]), F32), value, HI)


def stat_rows(first, second, at):
    sums, squares = row_sums(first), row_sums(second)
    row = lax.broadcasted_iota(jnp.int32, sums.shape, 0)
    return jnp.where(row == at, sums, jnp.where(row == at + 1, squares, 0.0))


def enc_kernel(low, count, share, near, me_ref, x_ref, w_ref, keep_ref, send_ref, weight_ref, turn_ref, arrived, *buffers):
    def at(i):
        return pl.ds(pl.multiple_of(((low + i) ^ me_ref[0]) * share, share), share)

    weight = pltpu.make_async_copy(w_ref, weight_ref, arrived.at[count])
    weight.start()
    if not near:
        (buffer_ref,) = buffers

        def block(i):
            return pltpu.make_async_copy(x_ref.at[:, at(i)], buffer_ref.at[i], arrived.at[i])

        for i in range(count):
            block(i).start()
    weight.wait()
    turn_ref[...] = jnp.transpose(weight_ref[...]).astype(BF)

    def pair(half, carry):
        for odd in range(2):
            i = 2 * half + odd
            if near:
                x = x_ref[:, at(i)]
            else:
                block(i).wait()
                x = buffer_ref[i]
            part = nn(turn_ref[...], jnp.log(1.0 + x.astype(F32)).astype(BF))
            if odd:
                send_ref[half] = part.astype(BF)
            else:
                keep_ref[half] = part
        return carry

    lax.fori_loop(0, count // 2, pair, 0)


def lines(rows8, count):
    wide = rows8.shape[1]
    if wide < 128 * count:
        rows8 = jnp.concatenate((rows8, jnp.zeros((8, 128 * count - wide), F32)), axis=1)
    return jnp.concatenate([rows8[:, i * 128 : (i + 1) * 128] for i in range(count)], axis=0)


def counts_kernel(rows, span, x_ref, lg_ref, dg_ref, par_ref, batch_ref, lib_ref, logc_ref, mask_ref, side_ref, lib_out, cell_ref, disp_ref, line_ref, held_ref):
    step = pl.program_id(0)
    genes, width = mask_ref.shape

    @pl.when(step == 0)
    def _():
        disp_ref[...] = jnp.zeros_like(disp_ref)
        held_ref[...] = jnp.zeros_like(held_ref)

    kinds = held_ref.shape[0]
    table = one_hot(batch_ref[0], kinds)
    held_ref[...] += sum(table[:, t : t + 128] for t in range(0, width, 128))
    row = lax.broadcasted_iota(jnp.int32, (16, width), 0)
    side_ref[0:kinds, part_of(step, width)] = table.astype(BF)
    side_ref[kinds:, part_of(step, width)] = jnp.where(row == 0, 1.0, 0.0).astype(BF)
    lib_out[...] = lib_ref[...]
    tiles = span // 128
    done = []
    for first in range(0, width, span):
        lanes = [slice(first + tile * 128, first + (tile + 1) * 128) for tile in range(tiles)]

        def chunk(g, cell):
            at = pl.ds(pl.multiple_of(g * rows, rows), rows)
            keep = par_ref[4, at, :].astype(BF)
            lows = [x_ref[at, lanes[tile]] for tile in range(tiles)]
            xs = [low.astype(F32) for low in lows]
            logs = [jnp.log(1.0 + x) for x in xs]
            for tile in range(tiles):
                logc_ref[at, lanes[tile]] = logs[tile].astype(BF)
                mask_ref[at, lanes[tile]] = lows[tile] * keep
            gams = [jnp.zeros_like(xs[0]) for _ in range(tiles)]
            digs = [jnp.zeros_like(xs[0]) for _ in range(tiles)]
            for k in range(COUNT_TOP):
                lg, dg = lg_ref[k, at, :], dg_ref[k, at, :]
                for tile in range(tiles):
                    more = xs[tile] > (k + 0.5)
                    gams[tile] = jnp.where(more, lg, gams[tile])
                    digs[tile] = jnp.where(more, dg, digs[tile])
            disp_ref[at, :] += sum(digs)
            out = []
            for tile in range(tiles):
                folded = cell[tile]
                for part in range(rows // 8):
                    folded = folded + gams[tile][part * 8 : (part + 1) * 8]
                out.append(folded)
            return tuple(out)

        zero = tuple(jnp.zeros((8, 128), F32) for _ in range(tiles))
        done += list(lax.fori_loop(0, genes // rows, chunk, zero))
    cell_ref[pl.ds(step, 1), :] = jnp.sum(jnp.concatenate(done, axis=1), axis=0, keepdims=True)

    @pl.when(step == pl.num_programs(0) - 1)
    def _():
        line_ref[...] = row_sums(held_ref[...])


def own_kernel(me_ref, keep_ref, got_ref, one_ref, two_ref, six_ref, batch_ref, enc_b_ref, pre_ref, stat_ref):
    kinds = enc_b_ref.shape[1]
    gathered = (keep_ref[0] + got_ref[0].astype(F32) + one_ref[0].astype(F32)) + (
        two_ref[0].astype(F32) + six_ref[0].astype(F32)
    )
    table = one_hot(batch_ref[0], kinds).astype(BF)
    pre = gathered + exact_rows(enc_b_ref[...], table)
    pre_ref[...] = pre
    stat_ref[...] = stat_rows(pre, pre * pre, 0)


def norm_columns(stat, first, cells):
    turned = jnp.transpose(stat)
    mean = turned[:, first : first + 1] / cells
    var = turned[:, first + 1 : first + 2] / cells - mean * mean
    return mean, lax.rsqrt(var + norm_epsilon)


def norm_rows(stat, first, cells):
    mean = stat[first : first + 1] / cells
    var = stat[first + 1 : first + 2] / cells - mean * mean
    return mean, lax.rsqrt(var + norm_epsilon)


def latent_kernel(cells, latent, me_ref, pre_ref, stat_ref, norm_ref, head_ref, bias_ref, noise_ref, batch_ref, dec_b_ref, pack_ref, aff_ref, kl_ref):
    kinds = dec_b_ref.shape[1] - 48
    hidden = pre_ref.shape[0]
    mean, inv = norm_columns(stat_ref[...], 0, cells)
    phat = (pre_ref[...] - mean) * inv
    affine = norm_ref[:, 0:1] * phat + norm_ref[:, 1:2]
    out = nn(head_ref[...], jnp.maximum(affine, 0.0), HI) + bias_ref[:, 0:1]
    lat_mean, lat_logvar = out[:latent], out[16 : 16 + latent]
    high, mid, _ = three(latent_rows(lat_logvar))
    aff_ref[...] = jnp.concatenate((affine.astype(BF), high, mid), axis=0)
    var = jnp.exp(lat_logvar) + 0.0001
    z = latent_rows(lat_mean + jnp.sqrt(var) * noise_ref[...])
    terms = var + lat_mean * lat_mean - 1.0 - jnp.log(var)
    kl_ref[...] = 0.5 * jnp.sum(terms, axis=0, keepdims=True)
    pre_dec = exact_rows(dec_b_ref[...], dec_table(z, batch_ref[0], kinds))
    stat = stat_rows(pre_dec, pre_dec * pre_dec, 0)
    pack_ref[...] = z
    pack_ref[latent : latent + 1, 0:hidden] = stat[0:1]
    pack_ref[latent + 1 : latent + 2, 0:hidden] = stat[1:2]


def latent_rows(z):
    if z.shape[0] == 16:
        return z
    return jnp.concatenate((z, jnp.zeros((16 - z.shape[0], z.shape[1]), F32)), axis=0)


def part_of(step, width):
    return pl.ds(pl.multiple_of(step * width, 128), width)


def relu_low(affine):
    return jnp.maximum(affine, jnp.zeros_like(affine))


def pick(step, me_ref, fast, near_ref, far_ref):
    if not fast:
        return near_ref[step]
    place = step ^ me_ref[0]
    return jnp.where(lax.rem(place, 2) == 0, near_ref[lax.div(place, 2)], far_ref[lax.div(place, 2)])


def decode_kernel(cells, latent, fast, me_ref, near_ref, far_ref, side_ref, stat_ref, norm_ref, plain_ref, w_ref, aff_ref, lse_ref, z_ref, top_ref, mass_ref, score_ref, left_ref):
    kinds = plain_ref.shape[1] - 16
    step = pl.program_id(0)
    cells_at = part_of(step, score_ref.shape[1])
    genes = score_ref.shape[0]
    hidden_rows = aff_ref.shape[0]

    @pl.when(step == 0)
    def _():
        mean, inv = norm_columns(stat_ref[...], latent - 8, cells)
        scaled = norm_ref[:, 2:3] * inv
        weights = plain_ref[...] * scaled
        high, mid, _ = three(weights)
        lane = lax.broadcasted_iota(jnp.int32, (hidden_rows, 16), 1)
        shift = jnp.broadcast_to(norm_ref[:, 3:4] - scaled * mean, (hidden_rows, 16))
        one, two, rest = (part.astype(F32) for part in three(shift))
        tail = jnp.where(lane == 0, one, jnp.where(lane == 1, two, jnp.where(lane == 2, rest, 0.0))).astype(BF)
        zero = jnp.zeros_like(tail)
        left_ref[:hidden_rows, :] = jnp.concatenate((high, high[:, kinds:], tail), axis=1)
        left_ref[hidden_rows:, :] = jnp.concatenate((mid, zero, zero), axis=1)

    z = pick(step, me_ref, fast, near_ref, far_ref)
    z = jnp.where(lax.broadcasted_iota(jnp.int32, z.shape, 0) < latent, z, 0.0)
    z_ref[:, cells_at] = z
    z_high, z_mid, _ = three(z)
    ones = jnp.where(lax.broadcasted_iota(jnp.int32, z.shape, 0) < 3, 1.0, 0.0).astype(BF)
    table = jnp.concatenate((side_ref[0:kinds, cells_at], z_high, z_mid, ones), axis=0)
    both = nn(left_ref[...], table)
    affine = (both[:hidden_rows] + both[hidden_rows:]).astype(BF)
    aff_ref[:, cells_at] = affine
    hidden = relu_low(affine)
    width = score_ref.shape[1]
    score_ref[...] = nn(w_ref[0:genes, :], jnp.concatenate((hidden, ones), axis=0))
    tiles = width // 128
    rows = 32

    def top(g, best):
        at = pl.ds(pl.multiple_of(g * rows, rows), rows)
        new = []
        for tile in range(tiles):
            value = score_ref[at, slice(tile * 128, (tile + 1) * 128)]
            part = best[tile]
            for index in range(rows // 8):
                part = jnp.maximum(part, value[index * 8 : (index + 1) * 8])
            new.append(part)
        return tuple(new)

    best = lax.fori_loop(0, genes // rows, top, tuple(jnp.full((8, 128), -3e38, F32) for _ in range(tiles)), unroll=5)
    high = [jnp.max(part, axis=0, keepdims=True) for part in best]
    wide = [jnp.broadcast_to(part, (8, 128)) for part in high]

    far_lanes = [pl.ds(pl.multiple_of(step * width + tile * 128, 128), 128) for tile in range(tiles)]

    def mass(g, sums):
        at = pl.ds(pl.multiple_of(g * rows, rows), rows)
        new = []
        for tile in range(tiles):
            value = score_ref[at, slice(tile * 128, (tile + 1) * 128)]
            part = sums[tile]
            pieces = []
            for index in range(rows // 8):
                pieces.append(jnp.exp(value[index * 8 : (index + 1) * 8] - wide[tile]))
                part = part + pieces[-1]
            mass_ref[at, far_lanes[tile]] = jnp.concatenate(pieces, axis=0)
            new.append(part)
        return tuple(new)

    sums = lax.fori_loop(0, genes // rows, mass, tuple(jnp.zeros((8, 128), F32) for _ in range(tiles)), unroll=5)
    top_ref[pl.ds(step, 1), :] = jnp.concatenate(high, axis=1)
    lse = [high[tile] + jnp.log(jnp.sum(sums[tile], axis=0, keepdims=True)) for tile in range(tiles)]
    lse_ref[pl.ds(step, 1), :] = jnp.concatenate(lse, axis=1)


def enc_sums_kernel(fast, me_ref, logc_ref, near_ref, far_ref, side_ref, line_ref, out_ref, sum_ref):
    step = pl.program_id(0)
    genes = logc_ref.shape[0]
    hidden = out_ref.shape[1]
    kinds = side_ref.shape[0] - 16

    @pl.when(step == 0)
    def _():
        out_ref[...] = jnp.zeros_like(out_ref)
        sum_ref[...] = jnp.zeros_like(sum_ref)

    cells_at = part_of(step, near_ref.shape[2])
    affine = pick(step, me_ref, fast, near_ref, far_ref)[:hidden]
    part = nt(logc_ref[:, cells_at], jnp.concatenate((affine, side_ref[kinds:, cells_at]), axis=0))
    out_ref[0:genes, :] += part[:, :hidden]
    sum_ref[...] += part[:, hidden:]
    out_ref[genes : genes + kinds, :] += nt(side_ref[0:kinds, cells_at], affine)

    @pl.when(step == pl.num_programs(0) - 1)
    def _():
        pick_first = jnp.where(lax.broadcasted_iota(jnp.int32, (8, 16), 1) == 0, 1.0, 0.0)
        base = genes + kinds
        count = pl.cdiv(genes, 128)
        out_ref[base : base + 8 * count, :] = lines(nt(pick_first, sum_ref[...], HI), count)
        out_ref[base + 8 * count :, :] = line_ref[...]


def zinb_kernel(rows, span, hid_ref, e_ref, top_ref, w_ref, x_ref, par_ref, lib_ref, lse_ref, gam_ref, g_ref, rt_ref, mass_ref, recon_ref, acc_ref, sc_ref):
    step = pl.program_id(0)
    genes, width = x_ref.shape

    @pl.when(step == 0)
    def _():
        acc_ref[...] = jnp.zeros_like(acc_ref)

    one_row = pl.ds(step, 1)
    gam_row = gam_ref[one_row, :]
    level = jnp.exp(top_ref[one_row, :] + (lib_ref[one_row, :] - lse_ref[one_row, :]))
    row = lax.broadcasted_iota(jnp.int32, (16, width), 0)
    ones = jnp.where(row < 3, 1.0, 0.0).astype(BF)
    sc_ref[...] = nn(w_ref[genes:, :], jnp.concatenate((relu_low(hid_ref[:, part_of(step, width)]), ones), axis=0))
    tiles = span // 128
    mass_out, recon_out = [], []
    for first in range(0, width, span):
        lanes = [slice(first + tile * 128, first + (tile + 1) * 128) for tile in range(tiles)]
        far_lanes = [pl.ds(pl.multiple_of(step * width + first + tile * 128, 128), 128) for tile in range(tiles)]
        scale = [jnp.broadcast_to(level[:, lanes[tile]], (rows, 128)) for tile in range(tiles)]

        def chunk(g, state):
            at = pl.ds(pl.multiple_of(g * rows, rows), rows)
            at_drop = pl.ds(pl.multiple_of(genes + g * rows, rows), rows)
            the, th, log_the, part_th = (par_ref[i, at, :] for i in range(4))
            sum_t = acc_ref[at, :]
            new = []
            for tile in range(tiles):
                rec, prod, back = state[tile]
                x = x_ref[at, lanes[tile]].astype(F32)
                mu = e_ref[at, far_lanes[tile]] * scale[tile]
                drop = sc_ref[at, lanes[tile]]
                both = mu + the
                r = 1.0 / both
                log_both = jnp.log(both)
                gap = log_the - log_both
                th_gap = th * gap
                u = jnp.where(x < 0.5, th_gap - drop, 1e30)
                eu = jnp.exp2(jnp.abs(u) * (-LOG2_E))
                ed = jnp.exp2(jnp.abs(drop) * (-LOG2_E))
                den = 1.0 + eu
                mu_eps = mu + zinb_epsilon
                rd = 1.0 / (1.0 + ed)
                w0 = jnp.where(u >= 0.0, 1.0, eu) * (1.0 / den)
                term = (th_gap - jnp.maximum(drop, 0.0)) + (x * (jnp.log(mu_eps) - log_both) - jnp.minimum(u, 0.0))
                factor = den * rd
                y = (x + w0 * th) * r
                g_mean = mu * (x * (1.0 / mu_eps) - y)
                g_drop = jnp.where(drop >= 0.0, ed, 1.0) * rd - w0
                g_disp = w0 * (gap + part_th) - y
                g_ref[at, far_lanes[tile]] = g_mean.astype(BF)
                g_ref[at_drop, far_lanes[tile]] = g_drop.astype(BF)
                rt_ref[at, far_lanes[tile]] = mu.astype(BF)
                sum_t = sum_t + g_disp
                for part in range(rows // 8):
                    sub = slice(part * 8, (part + 1) * 8)
                    rec = rec + term[sub]
                    prod = prod * factor[sub]
                    back = back + g_mean[sub]
                new.append((rec, prod, back))
            acc_ref[at, :] = sum_t
            return tuple(new)
        zero = jnp.zeros((8, 128), F32)
        state = tuple((zero, zero + 1.0, zero) for _ in range(tiles))
        state = lax.fori_loop(0, genes // rows, chunk, state)
        for tile in range(tiles):
            rec, prod, back = state[tile]
            mass_out.append(jnp.sum(back, axis=0, keepdims=True))
            recon_out.append(jnp.sum(rec + jnp.log(prod), axis=0, keepdims=True))
    mass_ref[one_row, :] = jnp.concatenate(mass_out, axis=1)
    recon_ref[one_row, :] = jnp.concatenate(recon_out, axis=1) + gam_row


def back_kernel(width, g_in_ref, rt_ref, aff_ref, w_ref, a_ref, r_ref, g_ref):
    genes = rt_ref.shape[0]
    step = pl.program_id(0)
    cells_at = part_of(step, width)

    @pl.when(step == 0)
    def _():
        g_ref[...] = jnp.zeros_like(g_ref)

    a_ref[:, cells_at] = nn(w_ref[...], g_in_ref[:, cells_at])
    r_ref[:, cells_at] = nn(w_ref[:, :genes], rt_ref[:, cells_at])
    row = lax.broadcasted_iota(jnp.int32, (16, width), 0)
    ones = jnp.where(row == 0, 1.0, 0.0).astype(BF)
    g_ref[...] += nt(g_in_ref[:, cells_at], jnp.concatenate((relu_low(aff_ref[:, cells_at]), ones), axis=0))


def hidden_grad_kernel(cells, latent, me_ref, a_ref, r_ref, mass_ref, aff_ref, lib_ref, stat_ref, gain_ref, lat_ref, recon_ref, z_ref, side_ref, keep_ref, send_ref, lane_ref, oh_ref):
    step = pl.program_id(0)
    steps = pl.num_programs(0)
    place = step ^ me_ref[0]
    hidden, width = a_ref.shape[0], mass_ref.shape[1]
    cells_at = part_of(step, width)
    kinds = side_ref.shape[0] - 16

    @pl.when(step == 0)
    def _():
        lane_ref[...] = jnp.zeros_like(lane_ref)
        oh_ref[...] = jnp.zeros_like(oh_ref)

    back = mass_ref[pl.ds(step, 1), :] * jnp.exp(-lib_ref[pl.ds(step, 1), :])
    wide = aff_ref[:, cells_at].astype(F32)
    dy = jnp.where(wide > 0, a_ref[:, cells_at] - back * r_ref[:, cells_at], 0.0)
    weighted = dy * wide
    lane_ref[...] += sum(weighted[:, t : t + 128] for t in range(0, width, 128))
    dy_low = dy.astype(BF)
    oh_ref[...] += nt(jnp.concatenate((side_ref[:, cells_at], z_ref[:, cells_at].astype(BF)), axis=0), dy_low)
    _, inv = norm_rows(stat_ref[...], latent - 8, cells)
    lat_high, lat_mid, _ = three(lat_ref[...] * (gain_ref[2:3] * inv) * (-1.0 / cells))
    both = nn(jnp.concatenate((lat_high, lat_mid), axis=0), dy_low)
    block = both[:16] + both[16:]
    row = lax.broadcasted_iota(jnp.int32, block.shape, 0)
    block = jnp.where(row == latent, recon_ref[pl.ds(step, 1), :], block)
    slot = lax.div(place, 2)

    @pl.when(lax.rem(place, 2) == 0)
    def _():
        keep_ref[slot] = block

    @pl.when(lax.rem(place, 2) == 1)
    def _():
        send_ref[slot] = block

    @pl.when(step == steps - 1)
    def _():
        scale = -1.0 / cells
        one, two = oh_ref[kinds : kinds + 1, :] * scale, row_sums(lane_ref[...])[0:1] * scale
        oh_ref[kinds : kinds + 16, :] = oh_ref[kinds + 16 :, :]
        part = (kinds + 16) // steps
        for core, ref in enumerate((keep_ref, send_ref)):
            for index in range(ref.shape[0]):
                ref[index, latent + 1 : latent + 2, 0:hidden] = one
                ref[index, latent + 2 : latent + 3, 0:hidden] = two
                owner = me_ref[0] ^ (2 * index + core)
                for k in range(part):
                    line = latent + 3 + k // 8
                    lanes = slice((k % 8) * hidden, (k % 8 + 1) * hidden)
                    ref[index, line : line + 1, lanes] = oh_ref[pl.ds(owner * part + k, 1), :] * scale


def dec_grad_kernel(cells, rt_ref, hid_ref, mass_ref, lib_ref, g_ref, acc_ref, dig_ref, par_ref, dec_ref, mix_ref):
    step = pl.program_id(0)
    steps = pl.num_programs(0)
    genes = rt_ref.shape[0]
    cells_at = part_of(step, mass_ref.shape[1])
    hidden = hid_ref.shape[0]

    @pl.when(step == 0)
    def _():
        mix_ref[...] = jnp.zeros_like(mix_ref)

    back = mass_ref[pl.ds(step, 1), :] * jnp.exp(-lib_ref[pl.ds(step, 1), :])
    back_high, back_mid, back_low = three(back)
    row = lax.broadcasted_iota(jnp.int32, (16, back.shape[1]), 0)
    extra = jnp.where(row == 0, back_high.astype(F32), jnp.where(row == 1, back_mid.astype(F32), 0.0))
    scaled = (relu_low(hid_ref[:, cells_at]).astype(F32) * back).astype(BF)
    mix_ref[...] += nt(rt_ref[:, cells_at], jnp.concatenate((scaled, extra.astype(BF)), axis=0))

    @pl.when(step == steps - 1)
    def _():
        scale = -1.0 / cells
        mix = mix_ref[...]
        dec_ref[:genes, :] = (g_ref[:genes, :hidden] - mix[:, :hidden]) * scale
        dec_ref[genes : 2 * genes, :] = g_ref[genes:, :hidden] * scale
        pick = jnp.where(lax.broadcasted_iota(jnp.int32, (8, 16), 1) < 2, 1.0, 0.0)
        score_row = nt(pick, g_ref[:genes, hidden:] - mix[:, hidden:], HI)
        drop_row = nt(pick, g_ref[genes:, hidden:], HI)
        disp_row = row_sums((acc_ref[...] + dig_ref[...]) * par_ref[1])
        line = lax.broadcasted_iota(jnp.int32, score_row.shape, 0)
        gene_rows = scale * jnp.where(
            line == 0, score_row, jnp.where(line == 1, drop_row, jnp.where(line == 2, disp_row, 0.0))
        )
        dec_ref[2 * genes :, :] = lines(gene_rows, pl.cdiv(genes, 128))


def enc_back_kernel(cells, latent, fast, span, me_ref, own_ref, dnear_ref, dfar_ref, aff_dec_ref, sums_ref, stat_ref, gain_ref, lat_ref, noise_ref, klw_ref, anear_ref, afar_ref, side_ref, held_ref, logc_ref, cols_ref, z_ref, out_ref, rest_ref, lane_ref, left_ref, fixed_ref, one_ref, kept_ref, sum_ref):
    step = pl.program_id(0)
    steps = kept_ref.shape[0]
    genes, width = logc_ref.shape[0], dnear_ref.shape[2]
    hidden = aff_dec_ref.shape[0]
    cells_at = part_of(step, width)
    place = (step ^ me_ref[0]) if fast else step
    kinds = (rest_ref.shape[0] - 64) // 2
    at = latent + 1 - 8
    m_one, m_two = norm_sums(sums_ref[at : at + 2], gain_ref, 2)
    m_two = m_two / gain_ref[2:3] * (1.0 / cells)
    m_one = m_one * (1.0 / cells) - m_two * gain_ref[3:4]

    @pl.when(step == 0)
    def _():
        out_ref[...] = jnp.zeros_like(out_ref)
        rest_ref[...] = jnp.zeros_like(rest_ref)
        lane_ref[...] = jnp.zeros_like(lane_ref)
        sum_ref[...] = jnp.zeros_like(sum_ref)
        _, inv = norm_rows(stat_ref[...], latent - 8, cells)
        lat = lat_ref[...] * (gain_ref[2:3] * inv)
        fixed_ref[...] = jnp.broadcast_to(jnp.sum(lat * m_one, axis=1, keepdims=True), fixed_ref.shape)
        high, mid, _ = three(lat * m_two)
        left_ref[...] = jnp.concatenate((high, mid), axis=0)

    index = lax.div(place, 2) if fast else place
    near = (lax.rem(place, 2) == 0) if fast else None

    def take(near_ref, far_ref, rows, lanes):
        if not fast:
            return near_ref[index, rows, lanes]
        return jnp.where(near, near_ref[index, rows, lanes], far_ref[index, rows, lanes])

    every = slice(0, width)
    scale = klw_ref[0:1, 0:1] * (1.0 / cells)
    affine_dec = aff_dec_ref[:, cells_at]
    both = nn(left_ref[...], affine_dec)
    block = take(dnear_ref, dfar_ref, slice(0, 16), every)
    kept_ref[step] = block[8:]
    grad_z = (block - fixed_ref[:, 0:1] - (both[:16] + both[16:]))[:latent]
    noise = noise_ref[:, cells_at]
    pieces = take(anear_ref, afar_ref, slice(hidden, hidden + 32), every).astype(F32)
    lat_logvar = pieces[:latent] + pieces[16 : 16 + latent]
    spread = jnp.exp(lat_logvar)
    var = spread + 0.0001
    inv_std = lax.rsqrt(var)
    z = z_ref[:, cells_at]
    lat_mean = z[0:latent] - var * inv_std * noise
    g_mean = latent_rows(grad_z + scale * lat_mean)
    g_var = latent_rows(spread * (grad_z * noise * (0.5 * inv_std) + (0.5 * scale) * (1.0 - inv_std * inv_std)))
    g_head = jnp.concatenate((g_mean, g_var), axis=0)
    sum_ref[0:32, :] += sum(g_head[:, t : t + 128] for t in range(0, width, 128))
    sum_ref[32:, :] += sum(z[:, t : t + 128] for t in range(0, width, 128))
    head_high, head_mid, _ = three(g_head)
    heads = jnp.concatenate((head_high, head_mid, head_high), axis=0)
    for begin in range(0, width, span):
        lanes = slice(begin, begin + span)
        affine = take(anear_ref, afar_ref, slice(0, hidden), lanes)
        one_ref[hidden:, lanes] = relu_low(affine)
        wide = affine.astype(F32)
        dy = jnp.where(wide > 0, nn(cols_ref[...], heads[:, lanes]), 0.0)
        one_ref[0:hidden, lanes] = dy.astype(BF)
        weighted = dy * wide
        lane_ref[...] += sum(weighted[:, t : t + 128] for t in range(0, span, 128))
    dy_low = one_ref[0:hidden, :]
    side = side_ref[:, cells_at]
    out_ref[0:genes, :] += nt(logc_ref[:, cells_at], dy_low)
    mixed = nt(side, dy_low)
    rest_ref[0:kinds, :] += mixed[:kinds]
    out_ref[genes : genes + 1, :] += mixed[kinds : kinds + 1]
    rest_ref[kinds : kinds + 32, :] += nt(head_high, one_ref[hidden:, :])
    base = kinds + 40
    product = nt(jnp.concatenate((side, z.astype(BF)), axis=0), affine_dec)
    rest_ref[base : base + kinds, :] -= product[:kinds] * m_two
    rest_ref[base + kinds : base + kinds + 16, :] -= product[kinds + 16 :] * m_two

    @pl.when(step == steps - 1)
    def _():
        out_ref[genes + 1 : genes + 2, :] = row_sums(lane_ref[...])[0:1]
        rest_ref[kinds + 32 : kinds + 40, 0:32] = row_sums(sum_ref[0:32, :])
        held = jnp.concatenate((held_ref[...], sum_ref[32:, :]), axis=0)
        rest_ref[base : base + kinds + 16, :] -= jnp.sum(held, axis=1, keepdims=True) * m_one
        count = (kinds + 16) // steps
        for owner in range(steps):
            for k in range(count):
                line = latent + 3 + k // 8 - 8
                at = slice(base + owner * count + k, base + owner * count + k + 1)
                rest_ref[at, :] += kept_ref[owner, line : line + 1, (k % 8) * hidden : (k % 8 + 1) * hidden]
        size = rest_ref.shape[0] // 8
        out_ref[genes + 8 :, :] = rest_ref[pl.ds(pl.multiple_of((own_ref[0] & 7) * size, 8), size), :]


def whole_gradient(part, product, plain, gain, shift, inv, one, two):
    return (gain * inv) * (part - plain * one - ((product - plain * shift) / gain) * two)


def norm_sums(rows, norm_ref, at):
    return rows[0:1], (rows[1:2] - norm_ref[at + 1 : at + 2] * rows[0:1]) / norm_ref[at : at + 1]


def finish_kernel(cells, latent, sum_ref, dec_ref, fixed_ref, stat_enc_ref, norm_ref, kl_ref, klw_ref, own_ref, enc_out, tail_out, loss_out):
    genes = enc_out.shape[0]
    size = tail_out.shape[0] - 8
    count = pl.cdiv(genes, 128)
    kinds = fixed_ref.shape[0] - genes - 8 * count - 8
    loss_out[...] = klw_ref[0:1, 0:1] * kl_ref[...] - own_ref[latent : latent + 1, :]
    _, inv = norm_rows(stat_enc_ref[...], 0, cells)
    n_one, n_two = norm_sums(sum_ref[genes : genes + 8, :], norm_ref, 0)
    at = genes + kinds
    logs = jnp.concatenate([fixed_ref[at + 8 * i : at + 8 * (i + 1), :] for i in range(count)], axis=1)
    log_sum = jnp.transpose(logs)[:genes, 0:1]
    enc = whole_gradient(
        sum_ref[0:genes, :], fixed_ref[0:genes, :], log_sum, norm_ref[0:1], norm_ref[1:2], inv, n_one * (1.0 / cells), n_two * (1.0 / cells)
    )
    enc_out[...] = enc
    dec = dec_ref[...]
    lane = jnp.sum(enc * enc, axis=0, keepdims=True) + jnp.sum(dec * dec, axis=0, keepdims=True)
    tail_out[0:size, :] = sum_ref[genes + 8 :, :]
    tail_out[size:, :] = jnp.broadcast_to(jnp.sum(lane, axis=1, keepdims=True), (8, tail_out.shape[1]))


def step_of(weight, gradient, first, second, rate):
    first = beta_one * first + (1.0 - beta_one) * gradient
    second = beta_two * second + (1.0 - beta_two) * gradient * gradient
    fixed_one = first * (1.0 / (1.0 - beta_one**step_number))
    fixed_two = second * (1.0 / (1.0 - beta_two**step_number))
    update = fixed_one / (jnp.sqrt(fixed_two) + 1e-08) + decay_rate * weight
    return weight - rate * update, first, second


def update_kernel(cells, latent, me_ref, near_ref, far_ref, enc_g_ref, dec_g_ref, sum_ref, fixed_ref, stat_enc_ref, stat_dec_ref, sums_ref, *refs):
    ins, outs, (rest_ref, small_g_ref, head_g_ref, norm_g_ref) = refs[:18], refs[18:-4], refs[-4:]
    enc, dec, gene, small, head, norm = (ins[3 * i : 3 * i + 3] for i in range(6))
    genes, hidden = enc[0].shape
    rows = small[0].shape[0]
    kinds = (rows - latent) // 2
    count = pl.cdiv(genes, 128)
    size = near_ref.shape[1]
    for core, ref in enumerate((near_ref, far_ref)):
        for index in range(ref.shape[0]):
            owner = me_ref[0] ^ (2 * index + core)
            rest_ref[pl.ds(pl.multiple_of(owner * size, 8), size), :] = ref[index]
    whole_rest = [rest_ref[i * size : i * size + size - 8, :] for i in range(8)]
    square = jnp.zeros((1, 1), F32)
    for i in range(8):
        square = square + rest_ref[(i + 1) * size - 8 : (i + 1) * size - 7, 0:1]
    rest = jnp.concatenate(whole_rest, axis=0)
    gains = norm[0]
    gain, shift = gains[0:1], gains[1:2]
    n_one, n_two = norm_sums(sum_ref[genes : genes + 8, :], gains, 0)
    _, inv = norm_rows(stat_enc_ref[...], 0, cells)
    _, inv_dec = norm_rows(stat_dec_ref[...], latent - 8, cells)
    at = genes + kinds + 8 * count
    batch_sum = jnp.transpose(fixed_ref[at : at + 8, :])[:kinds, 0:1]
    small_g_ref[0:kinds, :] = whole_gradient(
        rest[0:kinds], fixed_ref[genes : genes + kinds, :], batch_sum, gain, shift, inv, n_one * (1.0 / cells), n_two * (1.0 / cells)
    )
    small_g_ref[kinds:, :] = (gains[2:3] * inv_dec) * rest[kinds + 40 : 2 * kinds + 56]
    bias = jnp.transpose(rest[kinds + 32 : kinds + 40])
    for half in range(2):
        into = slice(half * latent, (half + 1) * latent)
        head_g_ref[into, 0:hidden] = rest[kinds + 16 * half : kinds + 16 * half + latent]
        head_g_ref[into, hidden : hidden + 1] = bias[16 * half : 16 * half + latent, 0:1]
    at = latent + 1 - 8
    norm_g_ref[0:1] = n_two
    norm_g_ref[1:2] = n_one
    m_one, m_two = norm_sums(sums_ref[at : at + 2], gains, 2)
    norm_g_ref[2:3] = m_two
    norm_g_ref[3:4] = m_one
    small_square = jnp.zeros((1, 1), F32)
    for part in (small_g_ref[0:rows, :], head_g_ref[...], norm_g_ref[...]):
        small_square = small_square + jnp.sum(jnp.sum(part * part, axis=0, keepdims=True), axis=1, keepdims=True)
    value = jnp.sqrt(square + small_square)
    factor = jnp.minimum(1.0, max_norm / value)
    (enc_n, enc_m, enc_v, enc_l, dec_n, dec_m, dec_v, dec_l, gene_n, gene_m, gene_v, small_n, small_m, small_v, head_n, head_m, head_v, norm_n, norm_m, norm_v, norm_out) = outs
    norm_out[...] = value
    new, first, second = step_of(enc[0][...], enc_g_ref[...] * factor, enc[1][...], enc[2][...], rate_genes)
    enc_n[...], enc_m[...], enc_v[...], enc_l[...] = new, first, second, new.astype(BF)
    for index in range(2):
        gradient = dec_g_ref[index * genes : (index + 1) * genes, :] * factor
        new, first, second = step_of(dec[0][index], gradient, dec[1][index], dec[2][index], rate_genes)
        dec_n[index], dec_m[index], dec_v[index], dec_l[index] = new, first, second, new.astype(BF)
    for index in range(pl.cdiv(genes, 128)):
        span = slice(index * 128, min(genes, (index + 1) * 128))
        gradient = dec_g_ref[2 * genes + index * 8 : 2 * genes + index * 8 + 3, 0 : span.stop - span.start] * factor
        new, first, second = step_of(gene[0][:, span], gradient, gene[1][:, span], gene[2][:, span], rate_small)
        gene_n[:, span], gene_m[:, span], gene_v[:, span] = new, first, second
    new, first, second = step_of(small[0][...], small_g_ref[0:rows, :] * factor, small[1][...], small[2][...], rate_small)
    small_n[...], small_m[...], small_v[...] = new, first, second
    new, first, second = step_of(head[0][...], head_g_ref[...] * factor, head[1][...], head[2][...], rate_small)
    head_n[...], head_m[...], head_v[...] = new, first, second
    new, first, second = step_of(norm[0][...], norm_g_ref[...] * factor, norm[1][...], norm[2][...], rate_small)
    norm_n[...], norm_m[...], norm_v[...] = new, first, second


def gather_genes(value, fast, blocks, width, late=None):
    if fast:
        near = jnp.stack([value] + [swap(value, "genes", 2 * k) for k in (1, 2, 3)])
        near = near if late is None else after(near, late)
        return near, swap(near, "genes", 1)
    rows = value.shape[0]
    whole_rows = lax.all_gather(value, "genes", axis=0).transpose(1, 0, 2)
    near = whole_rows.reshape(rows, blocks, width).transpose(1, 0, 2)
    return near, near


def per_device(counts, library, noise, batch_ids, gene_mask, kl_weight, enc_w, enc_m, enc_v, dec_w, dec_m, dec_v, gene_par, gene_m, gene_v, small_w, small_m, small_v, head_w, head_m, head_v, norm_par, norm_m, norm_v):
    rows_all, genes = counts.shape
    cells = float(rows_all * lax.axis_size("cells"))
    groups = lax.axis_size("genes")
    hidden = enc_w.shape[1]
    latent = head_w.shape[1] // 2
    kinds = (small_w.shape[0] - latent) // 2
    share = rows_all // groups
    width = min(1024, rows_all)
    blocks = rows_all // width
    fast = groups == 8 and blocks == 8
    me = lax.axis_index("genes").astype(jnp.int32).reshape(1)
    gene_lines = -(-genes // 128)

    def turn(value):
        return value.transpose(0, 2, 1)

    x_t = counts.T
    noise_t = noise.T
    dec_t = turn(dec_w)
    head_t = head_w.T
    lib8 = library.reshape(blocks, width)
    batch_all = batch_ids.reshape(blocks, 1, width)
    batch_own = batch_ids.reshape(groups, 1, share)
    klw = jnp.broadcast_to(kl_weight.reshape(1, 1), (8, 128))

    own_block = pl.BlockSpec((1, 1, share), lambda i, m: (m[0], 0, 0))
    own_lanes = lambda rows: pl.BlockSpec((rows, share), lambda i, m: (0, m[0]))
    lane_block = lambda rows: pl.BlockSpec((rows, width), lambda i, *_: (0, i))
    here = pl.BlockSpec(memory_space=pltpu.VMEM)
    full = lambda array: (array, here)
    out_of = lambda shape, dtype=F32: (shape, dtype, whole(shape))
    new = lambda shape, dtype=F32: (shape, dtype, here)

    def encode(low, count, weight, near=False):
        return call(
            lambda *refs: enc_kernel(low, count, share, near, *refs),
            (1,),
            [
                (me if fast else me & 1, None),
                (x_t, here) if near else (in_hbm(x_t), pl.BlockSpec(memory_space=pl.ANY)),
                (in_hbm(weight), pl.BlockSpec(memory_space=pl.ANY)),
            ],
            [new((count // 2, hidden, share)), new((count // 2, hidden, share), BF)],
            scratch=[
                pltpu.VMEM((genes, hidden), F32),
                pltpu.VMEM((hidden, genes), BF),
                pltpu.SemaphoreType.DMA((count + 1,)),
            ]
            + ([] if near else [pltpu.VMEM((count, genes, share), BF)]),
            scalars=1,
            us=2.0 if near else 3.0,
            mib=6 if near else 8,
        )

    slot = pl.BlockSpec((1, hidden, share), lambda i, m: (0, 0, 0))
    if fast:
        keep_far, send_far = encode(4, 4, enc_w)
        got_far = swap(send_far, "genes", 1)
        keep_near, send_near = encode(0, 4, after(enc_w, send_far), True)
        far = [
            swap((keep_far[k : k + 1] + got_far[k : k + 1].astype(F32)).astype(BF), "genes", 4 + 2 * k)
            for k in range(2)
        ]
        got = swap(send_near, "genes", 1)
        ready = (keep_near[1:2] + got[1:2].astype(F32)).astype(BF)
        far.append(swap(ready, "genes", 2))
        kept = keep_near
    else:
        keep_part, send_part = encode(0, groups, enc_w)
        got = swap(send_part, "genes", 1)
        summed = lax.psum_scatter(
            keep_part + got.astype(F32),
            "genes",
            scatter_dimension=0,
            axis_index_groups=[list(range(c, groups, 2)) for c in range(2)],
            tiled=True,
        )
        zero = jnp.zeros((1, hidden, share), BF)
        kept, got, far = summed, zero, [zero] * 3
        ready = keep_part

    mask_late = after(gene_mask.reshape(1, genes), ready)
    aug, dec_n, par, lg_tab, dg_tab, enc_pieces, dec_pieces, dec_plain, lat_row, head_rows, head_bias, head_cols, norm_t = call(
        prep_kernel,
        (1,),
        [full(gene_par), full(mask_late), full(dec_t), full(small_w), full(head_t), full(norm_par)],
        [
            new((2 * genes, hidden + 16), BF),
            new((hidden, 2 * genes), BF),
            new((5, genes, 128)),
            new((COUNT_TOP, genes, 128)),
            new((COUNT_TOP, genes, 128)),
            new((3 * hidden, kinds), BF),
            new((3 * hidden, kinds + 48), BF),
            new((hidden, kinds + 16)),
            new((16, hidden)),
            new((32, hidden)),
            new((32, 128)),
            new((hidden, 96), BF),
            new((hidden, 8)),
        ],
    )
    batch_spec = pl.BlockSpec((1, 1, width), lambda i, *_: (i, 0, 0))
    logc, x_kept, side, lib8, gam_cell, dig_acc, log_lines, held = call(
        lambda *refs: counts_kernel(16, min(512, width), *refs),
        (blocks,),
        [
            (in_hbm(x_t), lane_block(genes)),
            full(lg_tab),
            full(dg_tab),
            full(par),
            (batch_all, batch_spec),
            full(lib8),
        ],
        [
            ((genes, rows_all), BF, lane_block(genes), True),
            ((genes, rows_all), BF, lane_block(genes), True),
            ((kinds + 16, rows_all), BF, here),
            new((blocks, width)),
            new((blocks, width)),
            new((genes, 128)),
            new((8, 128)),
            new((kinds, 128)),
        ],
        mib=8,
        us=15.0,
    )
    enc_late = after(enc_pieces, log_lines)
    stat8 = whole((8, hidden))
    pre_enc, stat_enc = call(
        own_kernel,
        (1,),
        [(me, None), (kept, slot), (got, slot)]
        + [(part, slot) for part in far]
        + [(batch_own, own_block), full(enc_late)],
        [new((hidden, share)), new((8, hidden))],
        scalars=1,
    )
    stat_enc = total(total(stat_enc, "genes"), "cells")

    pack, aff_own, kl_row = call(
        lambda *refs: latent_kernel(cells, latent, *refs),
        (1,),
        [
            (me, None),
            full(pre_enc),
            full(stat_enc),
            full(norm_t),
            full(head_rows),
            full(head_bias),
            (noise_t, own_lanes(latent)),
            (batch_own, own_block),
            full(dec_pieces),
        ],
        [new((16, share)), new((hidden + 32, share), BF), new((1, share))],
        scalars=1,
    )
    near, far_pack = gather_genes(pack, fast, blocks, width)
    if fast:
        stat_dec = jnp.sum(near[:, 8:16, :hidden], axis=0) + jnp.sum(far_pack[:, 8:16, :hidden], axis=0)
    else:
        stat_dec = lax.psum(pack[8:16, :hidden], "genes")
    stat_dec = total(stat_dec, "cells")

    aff_dec, lse, z_all, top, mass_all = call(
        lambda *refs: decode_kernel(cells, latent, fast, *refs),
        (blocks,),
        [
            (me, None),
            (near, here),
            (far_pack, here),
            (side, here),
            full(stat_dec),
            full(norm_t),
            full(dec_plain),
            full(aug),
        ],
        [
            ((hidden, rows_all), BF, here),
            new((blocks, width)),
            ((16, rows_all), F32, here),
            new((blocks, width)),
            ((genes, rows_all), F32, here),
        ],
        scratch=[pltpu.VMEM((genes, width), F32), pltpu.VMEM((2 * hidden, kinds + 48), BF)],
        scalars=1,
        us=8.0,
    )
    lse_all = log_total_of(lse, "genes")

    full8 = whole((blocks, width))
    g_both, rt, mass, recon, gene_acc = call(
        lambda *refs: zinb_kernel(64, min(1024, width), *refs),
        (blocks,),
        [
            (aff_dec, here),
            (mass_all, here),
            full(top),
            full(aug),
            (in_hbm(x_kept), lane_block(genes)),
            full(par),
            full(lib8),
            full(lse_all),
            full(gam_cell),
        ],
        [((2 * genes, rows_all), BF, here), ((genes, rows_all), BF, here)]
        + [new((blocks, width)), new((blocks, width)), new((genes, 128))],
        scratch=[pltpu.VMEM((genes, width), F32)],
        mib=16,
        us=28.0,
    )
    mass_low = mass + swap(mass, "genes", 1)
    mass = total(mass_low, "genes", 1)
    part_a, part_r, dec_acc = call(
        lambda *refs: back_kernel(width, *refs),
        (blocks,),
        [
            (g_both, here),
            (rt, here),
            (aff_dec, here),
            full(dec_n),
        ],
        [
            ((hidden, rows_all), F32, here),
            ((hidden, rows_all), F32, here),
            new((2 * genes, hidden + 16)),
        ],
        mib=16,
        us=9.0,
    )

    aff_near, aff_far = gather_genes(after(aff_own, lse_all), fast, blocks, width, mass_low)
    fixed_rows = genes + kinds + 8 * gene_lines + 8
    (fixed,) = call(
        lambda *refs: enc_sums_kernel(fast, *refs),
        (blocks,),
        [
            (me, None),
            (logc, here),
            (aff_near, here),
            (aff_far, here),
            (side, here),
            full(log_lines),
        ],
        [new((fixed_rows, hidden))],
        scratch=[pltpu.VMEM((genes, 16), F32)],
        scalars=1,
        us=4.0,
    )
    fixed = total_by_halves(fixed, "cells", (1, 2))

    keep_d, send_d = call(
        lambda *refs: hidden_grad_kernel(cells, latent, *refs),
        (blocks,),
        [
            (me if fast else jnp.zeros_like(me), None),
            (part_a, here),
            (part_r, here),
            (mass, here),
            (aff_dec, here),
            full(lib8),
            full(stat_dec),
            full(norm_par),
            full(lat_row),
            full(recon),
            (z_all, here),
            (side, here),
        ],
        [
            new((blocks // 2, 16, width)),
            new((blocks // 2, 16, width)),
        ],
        scratch=[pltpu.VMEM((hidden, 128), F32), pltpu.VMEM((kinds + 32, hidden), F32)],
        scalars=1,
        us=5.0,
    )
    (dec_part,) = call(
        lambda *refs: dec_grad_kernel(cells, *refs),
        (blocks,),
        [
            (rt, here),
            (aff_dec, here),
            (mass, here),
            full(lib8),
            full(dec_acc),
            full(gene_acc),
            full(dig_acc),
            full(par),
        ],
        [new((2 * genes + 8 * gene_lines, hidden))],
        scratch=[pltpu.VMEM((genes, hidden + 16), F32)],
        us=5.0,
    )
    if fast:
        got_d = swap(send_d, "genes", 1)
        pieces = [swap(keep_d[k] + got_d[k], "genes", 2 * k) for k in (1, 2, 3)]
        pieces = [after(piece, dec_part) for piece in pieces]
        own_d = (keep_d[0] + got_d[0] + pieces[0]) + (pieces[1] + pieces[2])
        sums_dec = own_d[8:, :hidden]
    else:
        both = jnp.stack([keep_d, send_d], axis=1).reshape(blocks, 16, width)
        sums_dec = lax.psum(both[0, 8:, :hidden], "genes")
        both = both.transpose(1, 0, 2).reshape(16, groups, share).transpose(1, 0, 2)
        own_d = lax.psum_scatter(both, "genes", scatter_dimension=0, tiled=True)[0]
    sums_dec = total(sums_dec, "cells")
    d_near, d_far = gather_genes(own_d, fast, blocks, width)
    dec_g = total_by_halves(dec_part, "cells", (2, 1))

    size = (2 * kinds + 64) // 8
    (enc_part,) = call(
        lambda *refs: enc_back_kernel(cells, latent, fast, min(256, width), *refs),
        (blocks,),
        [
            (me, None),
            (me, None),
            (d_near, here),
            (d_far, here),
            (aff_dec, here),
            full(sums_dec),
            full(stat_dec),
            full(norm_par),
            full(lat_row),
            (noise_t, here),
            full(klw),
            (aff_near, here),
            (aff_far, here),
            (side, here),
            full(held),
            (logc, here),
            full(head_cols),
            (z_all, here),
        ],
        [new((genes + 8 + size, hidden))],
        scratch=[
            pltpu.VMEM((2 * kinds + 64, hidden), F32),
            pltpu.VMEM((hidden, 128), F32),
            pltpu.VMEM((32, hidden), BF),
            pltpu.VMEM((16, 128), F32),
            pltpu.VMEM((2 * hidden, width), BF),
            pltpu.VMEM((blocks, 8, width), F32),
            pltpu.VMEM((48, 128), F32),
        ],
        scalars=2,
        us=11.0,
    )
    enc_sum = total_by_halves(enc_part, "cells", (1, 2))
    enc_g, tail, loss = call(
        lambda *refs: finish_kernel(cells, latent, *refs),
        (1,),
        [full(a) for a in (enc_sum, dec_g, fixed, stat_enc, norm_par, kl_row, klw, own_d)],
        [new((genes, hidden)), new((size + 8, hidden)), new((1, share))],
    )
    if fast:
        tail_near = jnp.stack([tail] + [swap(tail, "genes", 2 * k) for k in (1, 2, 3)])
        tail_far = swap(tail_near, "genes", 1)
    else:
        tails = lax.all_gather(tail, "genes", axis=0)
        square = jnp.sum(tails[:, size:], axis=0)
        tails = tails[:8].at[:, size:].set(0.0).at[0, size:].set(square)
        tail_near, tail_far = tails[0::2], tails[1::2]

    state = [
        enc_w, enc_m, enc_v, dec_t, turn(dec_m), turn(dec_v), gene_par, gene_m, gene_v,
        small_w, small_m, small_v, head_t, head_m.T, head_v.T, norm_par, norm_m, norm_v,
    ]
    ins = [tail_near, tail_far, enc_g, dec_g, enc_sum, fixed, stat_enc, stat_dec, sums_dec] + state
    outs = []
    for index in range(6):
        one = state[3 * index]
        outs += [(one.shape, F32)] * 3
        if index < 2:
            outs.append((one.shape, BF))
    outs.append(((1, 1), F32))
    res = call(
        lambda *refs: update_kernel(cells, latent, *refs),
        (1,),
        [(me if fast else jnp.zeros_like(me), None)] + [full(array) for array in ins],
        [out_of(shape, dtype) for shape, dtype in outs],
        scratch=[
            pltpu.VMEM((8 * (size + 8), hidden), F32),
            pltpu.VMEM((2 * kinds + 16, hidden), F32),
            pltpu.VMEM((2 * latent, hidden + 1), F32),
            pltpu.VMEM((4, hidden), F32),
        ],
        scalars=1,
        mib=16,
    )
    enc_res, dec_res = res[0:4], [turn(part) for part in res[4:8]]
    head_res = [part.T for part in res[14:17]]
    return (
        *enc_res,
        *dec_res,
        *res[8:14],
        *head_res,
        *res[17:20],
        res[20].reshape(()),
        loss.reshape(share),
    )


def solution(mesh):
    placed = (
        P("cells", "genes"), P("cells"), P("cells", None), P("cells"), P("genes"), P(),
        P("genes", None), P("genes", None), P("genes", None),
        P(None, None, "genes"), P(None, None, "genes"), P(None, None, "genes"),
        P(None, "genes"), P(None, "genes"), P(None, "genes"),
        P(), P(), P(), P(), P(), P(), P(), P(), P(),
    )
    return jax.shard_map(
        per_device,
        mesh=mesh,
        in_specs=placed,
        out_specs=(
            P("genes", None), P("genes", None), P("genes", None), P("genes", None),
            P(None, None, "genes"), P(None, None, "genes"), P(None, None, "genes"), P(None, None, "genes"),
            P(None, "genes"), P(None, "genes"), P(None, "genes"),
            P(), P(), P(), P(), P(), P(), P(), P(), P(), P(),
            P(("cells", "genes")),
        ),
        check_vma=False,
    )
```

```python
import jax
import jax.numpy as jnp
from jax import lax
from jax.experimental import pallas as pl
from jax.experimental.pallas import tpu as pltpu
from jax.sharding import PartitionSpec as P

norm_epsilon = 0.001
zinb_epsilon = 1e-08
beta_one = 0.9
beta_two = 0.999
step_number = 5.0
decay_rate = 0.01
rate_genes = 0.03
rate_small = 0.2
max_norm = 0.1

F32 = jnp.float32
BF = jnp.bfloat16
HI = lax.Precision.HIGHEST
COUNT_TOP = 8
LOG2_E = 1.4426950408889634


def nn(left, right, precision=None):
    return lax.dot_general(
        left, right, (((1,), (0,)), ((), ())), precision=precision, preferred_element_type=F32
    )


def nt(left, right, precision=None):
    return lax.dot_general(
        left, right, (((1,), (1,)), ((), ())), precision=precision, preferred_element_type=F32
    )


def whole(shape):
    return pl.BlockSpec(shape, lambda *_: (0,) * len(shape))


def in_hbm(array):
    return pltpu.with_memory_space_constraint(array, pltpu.HBM)


def call(kernel, grid, ins, outs, scratch=(), scalars=0, us=2.0, mib=12):
    return pl.pallas_call(
        kernel,
        out_shape=[pltpu.HBM(out[0], out[1]) if len(out) == 4 else jax.ShapeDtypeStruct(out[0], out[1]) for out in outs],
        grid_spec=pltpu.PrefetchScalarGridSpec(
            num_scalar_prefetch=scalars,
            grid=grid,
            in_specs=[spec for _, spec in ins[scalars:]],
            out_specs=[out[2] for out in outs],
            scratch_shapes=list(scratch),
        ),
        compiler_params=pltpu.CompilerParams(vmem_limit_bytes=mib * 1024 * 1024),
        cost_estimate=pl.CostEstimate(flops=0, bytes_accessed=int(us * 3.69e6), transcendentals=0),
    )(*[array for array, _ in ins])


def swap(value, axis, bit):
    count = lax.axis_size(axis)
    return lax.ppermute(value, axis, [(i, i ^ bit) for i in range(count)])


def bit_groups(axis):
    count = lax.axis_size(axis)
    if axis == "genes":
        groups, bit = [[1]], 2
    else:
        groups, bit = [], 1
    while bit < count:
        groups.append([bit, 2 * bit] if 2 * bit < count else [bit])
        bit *= 4
    return groups


def total(value, axis, done=0):
    for group in bit_groups(axis)[done:]:
        if len(group) == 1:
            value = value + swap(value, axis, group[0])
        else:
            low, high = group
            value = (value + swap(value, axis, low)) + (
                swap(value, axis, high) + swap(value, axis, low ^ high)
            )
    return value


def log_total_of(value, axis):
    for group in bit_groups(axis):
        if len(group) == 1:
            parts = [value, swap(value, axis, group[0])]
        else:
            low, high = group
            parts = [value] + [swap(value, axis, k) for k in (low, high, low ^ high)]
        top = parts[0]
        for part in parts[1:]:
            top = jnp.maximum(top, part)
        mass = sum(jnp.exp(part - top) for part in parts)
        value = top + jnp.log(mass)
    return value


def total_by_halves(value, axis, order):
    for bit in order:
        value = value + swap(value, axis, bit)
    return value


def after(value, *others):
    return lax.optimization_barrier((value,) + others)[0]


def three(value):
    high = value.astype(BF)
    rest = value - high.astype(F32)
    mid = rest.astype(BF)
    low = (rest - mid.astype(F32)).astype(BF)
    return high, mid, low


def one_hot(batch_row, kinds):
    ids = lax.broadcasted_iota(jnp.int32, (kinds, batch_row.shape[1]), 0)
    return jnp.where(ids == batch_row, 1.0, 0.0)


def columns(rows):
    return jnp.transpose(rows)


def prep_kernel(gene_ref, mask_ref, dec_ref, small_ref, head_ref, norm_ref, aug_ref, turn_ref, par_ref, lg_ref, dg_ref, enc_out, dec_out, plain_out, lat_out, head_out, bias_out, cols_out, norm_out):
    genes = gene_ref.shape[1]
    hidden = norm_ref.shape[1]
    latent = head_ref.shape[0] // 2
    kinds = (small_ref.shape[0] - latent) // 2
    padded = pl.cdiv(genes, 128) * 128
    keep = mask_ref[...] > 0
    score_b = jnp.where(keep, gene_ref[0:1], -1e30)
    drop_b = jnp.where(keep, gene_ref[1:2], 1e30)
    th = jnp.exp(gene_ref[2:3])
    kept = jnp.where(keep, 1.0, 0.0)
    rows = jnp.concatenate((score_b, drop_b, th, kept, th, th, th, th), axis=0)
    if padded > genes:
        rows = jnp.concatenate((rows, jnp.ones((8, padded - genes), F32)), axis=1)
    turned = jnp.transpose(rows)[:genes]
    lane = lax.broadcasted_iota(jnp.int32, (genes, 16), 1)
    for half in range(2):
        at = slice(half * genes, (half + 1) * genes)
        aug_ref[at, 0:hidden] = dec_ref[half].astype(BF)
        high, mid, low = (jnp.broadcast_to(part.astype(F32), (genes, 16)) for part in three(turned[:, half : half + 1]))
        tail = jnp.where(lane == 0, high, jnp.where(lane == 1, mid, jnp.where(lane == 2, low, 0.0)))
        if half == 0:
            tail = jnp.where((lane >= 3) & (lane < 6), 1.0, tail)
        aug_ref[at, hidden : hidden + 16] = tail.astype(BF)
        turn_ref[:, at] = jnp.transpose(dec_ref[half]).astype(BF)
    th_w = jnp.broadcast_to(turned[:, 2:3], (genes, 128))
    keep_w = jnp.broadcast_to(turned[:, 3:4], (genes, 128))
    the_w = th_w + zinb_epsilon
    par_ref[0] = the_w
    par_ref[1] = th_w
    par_ref[2] = jnp.log(the_w)
    par_ref[3] = th_w / the_w
    par_ref[4] = keep_w
    gam = jnp.zeros_like(th_w)
    dig = jnp.zeros_like(th_w)
    for k in range(COUNT_TOP):
        more = th_w + float(k)
        gam = gam + keep_w * jnp.log(more * (1.0 / (1.0 + k)))
        dig = dig + keep_w / more
        lg_ref[k] = gam
        dg_ref[k] = dig
    for index, piece in enumerate(three(jnp.transpose(small_ref[0:kinds, :]))):
        enc_out[index * hidden : (index + 1) * hidden, :] = piece
    row = lax.broadcasted_iota(jnp.int32, (16, hidden), 0)
    lat_row = jnp.zeros((16, hidden), F32)
    for index in range(latent):
        lat_row = jnp.where(row == index, small_ref[2 * kinds + index : 2 * kinds + index + 1, :], lat_row)
    lat_out[...] = lat_row
    batch_turned, lat_turned = jnp.transpose(small_ref[kinds : 2 * kinds, :]), jnp.transpose(lat_row)
    plain_out[...] = jnp.concatenate((batch_turned, lat_turned), axis=1)
    batch_pieces = three(batch_turned)
    lat = three(lat_turned)
    zero = jnp.zeros_like(lat[0])
    tails = ((lat[0], lat[0], lat[0]), (lat[1], lat[1], zero), (lat[2], zero, zero))
    for index in range(3):
        at = slice(index * hidden, (index + 1) * hidden)
        dec_out[at, :] = jnp.concatenate((batch_pieces[index],) + tails[index], axis=1)
    full = lax.broadcasted_iota(jnp.int32, (32, hidden), 0)
    head = jnp.zeros((32, hidden), F32)
    bias = jnp.zeros((32, 1), F32)
    for index in range(2 * latent):
        to = index if index < latent else index - latent + 16
        head = jnp.where(full == to, head_ref[index : index + 1, 0:hidden], head)
        bias = jnp.where(full[:, 0:1] == to, head_ref[index : index + 1, hidden : hidden + 1], bias)
    head_out[...] = head
    bias_out[...] = jnp.broadcast_to(bias, (32, 128))
    high, mid, _ = three(jnp.transpose(head))
    cols_out[...] = jnp.concatenate((high, high, mid), axis=1)
    norm_out[...] = jnp.transpose(jnp.concatenate((norm_ref[...], norm_ref[...]), axis=0))


def exact_rows(stacked, table):
    out = nn(stacked, table)
    hidden = out.shape[0] // 3
    return out[:hidden] + out[hidden : 2 * hidden] + out[2 * hidden :]


def dec_table(z, batch_row, kinds):
    high, mid, low = three(z)
    return jnp.concatenate((one_hot(batch_row, kinds).astype(BF), high, mid, low), axis=0)


def row_sums(value):
    return nt(jnp.ones((8, value.shape[1]), F32), value, HI)


def stat_rows(first, second, at):
    sums, squares = row_sums(first), row_sums(second)
    row = lax.broadcasted_iota(jnp.int32, sums.shape, 0)
    return jnp.where(row == at, sums, jnp.where(row == at + 1, squares, 0.0))


def enc_kernel(low, count, share, near, me_ref, x_ref, w_ref, keep_ref, send_ref, weight_ref, turn_ref, arrived, *buffers):
    def at(i):
        return pl.ds(pl.multiple_of(((low + i) ^ me_ref[0]) * share, share), share)

    weight = pltpu.make_async_copy(w_ref, weight_ref, arrived.at[count])
    weight.start()
    if not near:
        (buffer_ref,) = buffers

        def block(i):
            return pltpu.make_async_copy(x_ref.at[:, at(i)], buffer_ref.at[i], arrived.at[i])

        for i in range(count):
            block(i).start()
    weight.wait()
    turn_ref[...] = jnp.transpose(weight_ref[...]).astype(BF)

    def pair(half, carry):
        for odd in range(2):
            i = 2 * half + odd
            if near:
                x = x_ref[:, at(i)]
            else:
                block(i).wait()
                x = buffer_ref[i]
            part = nn(turn_ref[...], jnp.log(1.0 + x.astype(F32)).astype(BF))
            if odd:
                send_ref[half] = part.astype(BF)
            else:
                keep_ref[half] = part
        return carry

    lax.fori_loop(0, count // 2, pair, 0)


def lines(rows8, count):
    wide = rows8.shape[1]
    if wide < 128 * count:
        rows8 = jnp.concatenate((rows8, jnp.zeros((8, 128 * count - wide), F32)), axis=1)
    return jnp.concatenate([rows8[:, i * 128 : (i + 1) * 128] for i in range(count)], axis=0)


def counts_kernel(rows, span, x_ref, lg_ref, dg_ref, par_ref, batch_ref, lib_ref, logc_ref, mask_ref, side_ref, lib_out, cell_ref, disp_ref, line_ref, held_ref):
    step = pl.program_id(0)
    genes, width = mask_ref.shape

    @pl.when(step == 0)
    def _():
        disp_ref[...] = jnp.zeros_like(disp_ref)
        held_ref[...] = jnp.zeros_like(held_ref)

    kinds = held_ref.shape[0]
    table = one_hot(batch_ref[0], kinds)
    held_ref[...] += sum(table[:, t : t + 128] for t in range(0, width, 128))
    row = lax.broadcasted_iota(jnp.int32, (16, width), 0)
    side_ref[0:kinds, part_of(step, width)] = table.astype(BF)
    side_ref[kinds:, part_of(step, width)] = jnp.where(row == 0, 1.0, 0.0).astype(BF)
    lib_out[...] = lib_ref[...]
    tiles = span // 128
    done = []
    for first in range(0, width, span):
        lanes = [slice(first + tile * 128, first + (tile + 1) * 128) for tile in range(tiles)]

        def chunk(g, cell):
            at = pl.ds(pl.multiple_of(g * rows, rows), rows)
            keep = par_ref[4, at, :].astype(BF)
            lows = [x_ref[at, lanes[tile]] for tile in range(tiles)]
            xs = [low.astype(F32) for low in lows]
            logs = [jnp.log(1.0 + x) for x in xs]
            for tile in range(tiles):
                logc_ref[at, lanes[tile]] = logs[tile].astype(BF)
                mask_ref[at, lanes[tile]] = lows[tile] * keep
            gams = [jnp.zeros_like(xs[0]) for _ in range(tiles)]
            digs = [jnp.zeros_like(xs[0]) for _ in range(tiles)]
            for k in range(COUNT_TOP):
                lg, dg = lg_ref[k, at, :], dg_ref[k, at, :]
                for tile in range(tiles):
                    more = xs[tile] > (k + 0.5)
                    gams[tile] = jnp.where(more, lg, gams[tile])
                    digs[tile] = jnp.where(more, dg, digs[tile])
            disp_ref[at, :] += sum(digs)
            out = []
            for tile in range(tiles):
                folded = cell[tile]
                for part in range(rows // 8):
                    folded = folded + gams[tile][part * 8 : (part + 1) * 8]
                out.append(folded)
            return tuple(out)

        zero = tuple(jnp.zeros((8, 128), F32) for _ in range(tiles))
        done += list(lax.fori_loop(0, genes // rows, chunk, zero))
    cell_ref[pl.ds(step, 1), :] = jnp.sum(jnp.concatenate(done, axis=1), axis=0, keepdims=True)

    @pl.when(step == pl.num_programs(0) - 1)
    def _():
        line_ref[...] = row_sums(held_ref[...])


def own_kernel(me_ref, keep_ref, got_ref, one_ref, two_ref, six_ref, batch_ref, enc_b_ref, pre_ref, stat_ref):
    kinds = enc_b_ref.shape[1]
    gathered = (keep_ref[0] + got_ref[0].astype(F32) + one_ref[0].astype(F32)) + (
        two_ref[0].astype(F32) + six_ref[0].astype(F32)
    )
    table = one_hot(batch_ref[0], kinds).astype(BF)
    pre = gathered + exact_rows(enc_b_ref[...], table)
    pre_ref[...] = pre
    stat_ref[...] = stat_rows(pre, pre * pre, 0)


def norm_columns(stat, first, cells):
    turned = jnp.transpose(stat)
    mean = turned[:, first : first + 1] / cells
    var = turned[:, first + 1 : first + 2] / cells - mean * mean
    return mean, lax.rsqrt(var + norm_epsilon)


def norm_rows(stat, first, cells):
    mean = stat[first : first + 1] / cells
    var = stat[first + 1 : first + 2] / cells - mean * mean
    return mean, lax.rsqrt(var + norm_epsilon)


def latent_kernel(cells, latent, me_ref, pre_ref, stat_ref, norm_ref, head_ref, bias_ref, noise_ref, batch_ref, dec_b_ref, pack_ref, aff_ref, kl_ref):
    kinds = dec_b_ref.shape[1] - 48
    hidden = pre_ref.shape[0]
    mean, inv = norm_columns(stat_ref[...], 0, cells)
    phat = (pre_ref[...] - mean) * inv
    affine = norm_ref[:, 0:1] * phat + norm_ref[:, 1:2]
    out = nn(head_ref[...], jnp.maximum(affine, 0.0), HI) + bias_ref[:, 0:1]
    lat_mean, lat_logvar = out[:latent], out[16 : 16 + latent]
    high, mid, _ = three(latent_rows(lat_logvar))
    aff_ref[...] = jnp.concatenate((affine.astype(BF), high, mid), axis=0)
    var = jnp.exp(lat_logvar) + 0.0001
    z = latent_rows(lat_mean + jnp.sqrt(var) * noise_ref[...])
    terms = var + lat_mean * lat_mean - 1.0 - jnp.log(var)
    kl_ref[...] = 0.5 * jnp.sum(terms, axis=0, keepdims=True)
    pre_dec = exact_rows(dec_b_ref[...], dec_table(z, batch_ref[0], kinds))
    stat = stat_rows(pre_dec, pre_dec * pre_dec, 0)
    pack_ref[...] = z
    pack_ref[latent : latent + 1, 0:hidden] = stat[0:1]
    pack_ref[latent + 1 : latent + 2, 0:hidden] = stat[1:2]


def latent_rows(z):
    if z.shape[0] == 16:
        return z
    return jnp.concatenate((z, jnp.zeros((16 - z.shape[0], z.shape[1]), F32)), axis=0)


def part_of(step, width):
    return pl.ds(pl.multiple_of(step * width, 128), width)


def relu_low(affine):
    return jnp.maximum(affine, jnp.zeros_like(affine))


def pick(step, me_ref, fast, near_ref, far_ref):
    if not fast:
        return near_ref[step]
    place = step ^ me_ref[0]
    return jnp.where(lax.rem(place, 2) == 0, near_ref[lax.div(place, 2)], far_ref[lax.div(place, 2)])


def decode_kernel(cells, latent, fast, me_ref, near_ref, far_ref, side_ref, stat_ref, norm_ref, plain_ref, w_ref, aff_ref, lse_ref, z_ref, top_ref, mass_ref, low_ref, score_ref, left_ref):
    kinds = plain_ref.shape[1] - 16
    step = pl.program_id(0)
    cells_at = part_of(step, score_ref.shape[1])
    genes = score_ref.shape[0]
    hidden_rows = aff_ref.shape[0]

    @pl.when(step == 0)
    def _():
        mean, inv = norm_columns(stat_ref[...], latent - 8, cells)
        scaled = norm_ref[:, 2:3] * inv
        weights = plain_ref[...] * scaled
        high, mid, _ = three(weights)
        lane = lax.broadcasted_iota(jnp.int32, (hidden_rows, 16), 1)
        shift = jnp.broadcast_to(norm_ref[:, 3:4] - scaled * mean, (hidden_rows, 16))
        one, two, rest = (part.astype(F32) for part in three(shift))
        tail = jnp.where(lane == 0, one, jnp.where(lane == 1, two, jnp.where(lane == 2, rest, 0.0))).astype(BF)
        zero = jnp.zeros_like(tail)
        left_ref[:hidden_rows, :] = jnp.concatenate((high, high[:, kinds:], tail), axis=1)
        left_ref[hidden_rows:, :] = jnp.concatenate((mid, zero, zero), axis=1)

    z = pick(step, me_ref, fast, near_ref, far_ref)
    z = jnp.where(lax.broadcasted_iota(jnp.int32, z.shape, 0) < latent, z, 0.0)
    z_ref[:, cells_at] = z
    z_high, z_mid, _ = three(z)
    ones = jnp.where(lax.broadcasted_iota(jnp.int32, z.shape, 0) < 3, 1.0, 0.0).astype(BF)
    table = jnp.concatenate((side_ref[0:kinds, cells_at], z_high, z_mid, ones), axis=0)
    both = nn(left_ref[...], table)
    affine = (both[:hidden_rows] + both[hidden_rows:]).astype(BF)
    aff_ref[:, cells_at] = affine
    hidden = relu_low(affine)
    width = score_ref.shape[1]
    score_ref[...] = nn(w_ref[0:genes, :], jnp.concatenate((hidden, ones), axis=0))
    tiles = width // 128
    rows = 32

    def top(g, best):
        at = pl.ds(pl.multiple_of(g * rows, rows), rows)
        new = []
        for tile in range(tiles):
            value = score_ref[at, slice(tile * 128, (tile + 1) * 128)]
            part = best[tile]
            for index in range(rows // 8):
                part = jnp.maximum(part, value[index * 8 : (index + 1) * 8])
            new.append(part)
        return tuple(new)

    best = lax.fori_loop(0, genes // rows, top, tuple(jnp.full((8, 128), -3e38, F32) for _ in range(tiles)), unroll=5)
    high = [jnp.max(part, axis=0, keepdims=True) for part in best]
    wide = [jnp.broadcast_to(part, (8, 128)) for part in high]

    far_lanes = [pl.ds(pl.multiple_of(step * width + tile * 128, 128), 128) for tile in range(tiles)]

    def mass(g, sums):
        at = pl.ds(pl.multiple_of(g * rows, rows), rows)
        new = []
        for tile in range(tiles):
            value = score_ref[at, slice(tile * 128, (tile + 1) * 128)]
            part = sums[tile]
            pieces = []
            for index in range(rows // 8):
                pieces.append(jnp.exp(value[index * 8 : (index + 1) * 8] - wide[tile]))
                part = part + pieces[-1]
            whole_piece = jnp.concatenate(pieces, axis=0)
            mass_ref[at, far_lanes[tile]] = whole_piece
            low_ref[at, far_lanes[tile]] = whole_piece.astype(BF)
            new.append(part)
        return tuple(new)

    sums = lax.fori_loop(0, genes // rows, mass, tuple(jnp.zeros((8, 128), F32) for _ in range(tiles)), unroll=5)
    top_ref[pl.ds(step, 1), :] = jnp.concatenate(high, axis=1)
    lse = [high[tile] + jnp.log(jnp.sum(sums[tile], axis=0, keepdims=True)) for tile in range(tiles)]
    lse_ref[pl.ds(step, 1), :] = jnp.concatenate(lse, axis=1)


def enc_sums_kernel(fast, me_ref, logc_ref, near_ref, far_ref, side_ref, line_ref, out_ref, sum_ref):
    step = pl.program_id(0)
    genes = logc_ref.shape[0]
    hidden = out_ref.shape[1]
    kinds = side_ref.shape[0] - 16

    @pl.when(step == 0)
    def _():
        out_ref[...] = jnp.zeros_like(out_ref)
        sum_ref[...] = jnp.zeros_like(sum_ref)

    cells_at = part_of(step, near_ref.shape[2])
    affine = pick(step, me_ref, fast, near_ref, far_ref)[:hidden]
    part = nt(logc_ref[:, cells_at], jnp.concatenate((affine, side_ref[kinds:, cells_at]), axis=0))
    out_ref[0:genes, :] += part[:, :hidden]
    sum_ref[...] += part[:, hidden:]
    out_ref[genes : genes + kinds, :] += nt(side_ref[0:kinds, cells_at], affine)

    @pl.when(step == pl.num_programs(0) - 1)
    def _():
        pick_first = jnp.where(lax.broadcasted_iota(jnp.int32, (8, 16), 1) == 0, 1.0, 0.0)
        base = genes + kinds
        count = pl.cdiv(genes, 128)
        out_ref[base : base + 8 * count, :] = lines(nt(pick_first, sum_ref[...], HI), count)
        out_ref[base + 8 * count :, :] = line_ref[...]


def zinb_kernel(rows, span, hid_ref, e_ref, top_ref, w_ref, x_ref, par_ref, lib_ref, lse_ref, gam_ref, g_ref, mass_ref, recon_ref, acc_ref, sc_ref):
    step = pl.program_id(0)
    genes, width = x_ref.shape

    @pl.when(step == 0)
    def _():
        acc_ref[...] = jnp.zeros_like(acc_ref)

    one_row = pl.ds(step, 1)
    gam_row = gam_ref[one_row, :]
    level = jnp.exp(top_ref[one_row, :] + (lib_ref[one_row, :] - lse_ref[one_row, :]))
    row = lax.broadcasted_iota(jnp.int32, (16, width), 0)
    ones = jnp.where(row < 3, 1.0, 0.0).astype(BF)
    sc_ref[...] = nn(w_ref[genes:, :], jnp.concatenate((relu_low(hid_ref[:, part_of(step, width)]), ones), axis=0))
    tiles = span // 128
    mass_out, recon_out = [], []
    for first in range(0, width, span):
        lanes = [slice(first + tile * 128, first + (tile + 1) * 128) for tile in range(tiles)]
        far_lanes = [pl.ds(pl.multiple_of(step * width + first + tile * 128, 128), 128) for tile in range(tiles)]
        scale = [jnp.broadcast_to(level[:, lanes[tile]], (rows, 128)) for tile in range(tiles)]

        def chunk(g, state):
            at = pl.ds(pl.multiple_of(g * rows, rows), rows)
            at_drop = pl.ds(pl.multiple_of(genes + g * rows, rows), rows)
            the, th, log_the, part_th = (par_ref[i, at, :] for i in range(4))
            sum_t = acc_ref[at, :]
            new = []
            for tile in range(tiles):
                rec, prod, back = state[tile]
                x = x_ref[at, lanes[tile]].astype(F32)
                mu = e_ref[at, far_lanes[tile]] * scale[tile]
                drop = sc_ref[at, lanes[tile]]
                both = mu + the
                r = 1.0 / both
                log_both = jnp.log(both)
                gap = log_the - log_both
                th_gap = th * gap
                u = jnp.where(x < 0.5, th_gap - drop, 1e30)
                eu = jnp.exp2(jnp.abs(u) * (-LOG2_E))
                ed = jnp.exp2(jnp.abs(drop) * (-LOG2_E))
                den = 1.0 + eu
                mu_eps = mu + zinb_epsilon
                rd = 1.0 / (1.0 + ed)
                w0 = jnp.where(u >= 0.0, 1.0, eu) * (1.0 / den)
                term = (th_gap - jnp.maximum(drop, 0.0)) + (x * (jnp.log(mu_eps) - log_both) - jnp.minimum(u, 0.0))
                factor = den * rd
                y = (x + w0 * th) * r
                g_mean = mu * (x * (1.0 / mu_eps) - y)
                g_drop = jnp.where(drop >= 0.0, ed, 1.0) * rd - w0
                g_disp = w0 * (gap + part_th) - y
                g_ref[at, far_lanes[tile]] = g_mean.astype(BF)
                g_ref[at_drop, far_lanes[tile]] = g_drop.astype(BF)
                sum_t = sum_t + g_disp
                for part in range(rows // 8):
                    sub = slice(part * 8, (part + 1) * 8)
                    rec = rec + term[sub]
                    prod = prod * factor[sub]
                    back = back + g_mean[sub]
                new.append((rec, prod, back))
            acc_ref[at, :] = sum_t
            return tuple(new)
        zero = jnp.zeros((8, 128), F32)
        state = tuple((zero, zero + 1.0, zero) for _ in range(tiles))
        state = lax.fori_loop(0, genes // rows, chunk, state)
        for tile in range(tiles):
            rec, prod, back = state[tile]
            mass_out.append(jnp.sum(back, axis=0, keepdims=True))
            recon_out.append(jnp.sum(rec + jnp.log(prod), axis=0, keepdims=True))
    mass_ref[one_row, :] = jnp.concatenate(mass_out, axis=1)
    recon_ref[one_row, :] = jnp.concatenate(recon_out, axis=1) + gam_row


def softmax_kernel(width, mass_ref, w_ref, r_ref):
    genes = mass_ref.shape[0]
    cells_at = part_of(pl.program_id(0), width)
    r_ref[:, cells_at] = nn(w_ref[:, :genes], mass_ref[:, cells_at])


def back_kernel(width, g_in_ref, w_ref, a_ref):
    cells_at = part_of(pl.program_id(0), width)
    a_ref[:, cells_at] = nn(w_ref[...], g_in_ref[:, cells_at])


def hidden_grad_kernel(cells, latent, me_ref, a_ref, r_ref, mass_ref, aff_ref, top_ref, lse_ref, stat_ref, gain_ref, lat_ref, recon_ref, z_ref, side_ref, keep_ref, send_ref, lane_ref, oh_ref):
    step = pl.program_id(0)
    steps = pl.num_programs(0)
    place = step ^ me_ref[0]
    hidden, width = a_ref.shape[0], mass_ref.shape[1]
    cells_at = part_of(step, width)
    kinds = side_ref.shape[0] - 16

    @pl.when(step == 0)
    def _():
        lane_ref[...] = jnp.zeros_like(lane_ref)
        oh_ref[...] = jnp.zeros_like(oh_ref)

    line = pl.ds(step, 1)
    back = mass_ref[line, :] * jnp.exp(top_ref[line, :] - lse_ref[line, :])
    wide = aff_ref[:, cells_at].astype(F32)
    dy = jnp.where(wide > 0, a_ref[:, cells_at] - back * r_ref[:, cells_at], 0.0)
    weighted = dy * wide
    lane_ref[...] += sum(weighted[:, t : t + 128] for t in range(0, width, 128))
    dy_low = dy.astype(BF)
    oh_ref[...] += nt(jnp.concatenate((side_ref[:, cells_at], z_ref[:, cells_at].astype(BF)), axis=0), dy_low)
    _, inv = norm_rows(stat_ref[...], latent - 8, cells)
    lat_high, lat_mid, _ = three(lat_ref[...] * (gain_ref[2:3] * inv) * (-1.0 / cells))
    both = nn(jnp.concatenate((lat_high, lat_mid), axis=0), dy_low)
    block = both[:16] + both[16:]
    row = lax.broadcasted_iota(jnp.int32, block.shape, 0)
    block = jnp.where(row == latent, recon_ref[pl.ds(step, 1), :], block)
    slot = lax.div(place, 2)

    @pl.when(lax.rem(place, 2) == 0)
    def _():
        keep_ref[slot] = block

    @pl.when(lax.rem(place, 2) == 1)
    def _():
        send_ref[slot] = block

    @pl.when(step == steps - 1)
    def _():
        scale = -1.0 / cells
        one, two = oh_ref[kinds : kinds + 1, :] * scale, row_sums(lane_ref[...])[0:1] * scale
        oh_ref[kinds : kinds + 16, :] = oh_ref[kinds + 16 :, :]
        part = (kinds + 16) // steps
        for core, ref in enumerate((keep_ref, send_ref)):
            for index in range(ref.shape[0]):
                ref[index, latent + 1 : latent + 2, 0:hidden] = one
                ref[index, latent + 2 : latent + 3, 0:hidden] = two
                owner = me_ref[0] ^ (2 * index + core)
                for k in range(part):
                    line = latent + 3 + k // 8
                    lanes = slice((k % 8) * hidden, (k % 8 + 1) * hidden)
                    ref[index, line : line + 1, lanes] = oh_ref[pl.ds(owner * part + k, 1), :] * scale


def dec_grad_kernel(cells, rt_ref, hid_ref, mass_ref, top_ref, lse_ref, g_in_ref, acc_ref, dig_ref, par_ref, dec_ref, mix_ref, g_ref):
    step = pl.program_id(0)
    steps = pl.num_programs(0)
    genes = rt_ref.shape[0]
    cells_at = part_of(step, mass_ref.shape[1])
    hidden = hid_ref.shape[0]

    @pl.when(step == 0)
    def _():
        mix_ref[...] = jnp.zeros_like(mix_ref)
        g_ref[...] = jnp.zeros_like(g_ref)

    line = pl.ds(step, 1)
    back = mass_ref[line, :] * jnp.exp(top_ref[line, :] - lse_ref[line, :])
    back_high, back_mid, back_low = three(back)
    row = lax.broadcasted_iota(jnp.int32, (16, back.shape[1]), 0)
    extra = jnp.where(row == 0, back_high.astype(F32), jnp.where(row == 1, back_mid.astype(F32), 0.0))
    hidden_low = relu_low(hid_ref[:, cells_at])
    ones = jnp.where(row == 0, 1.0, 0.0).astype(BF)
    g_ref[...] += nt(g_in_ref[:, cells_at], jnp.concatenate((hidden_low, ones), axis=0))
    scaled = (hidden_low.astype(F32) * back).astype(BF)
    mix_ref[...] += nt(rt_ref[:, cells_at], jnp.concatenate((scaled, extra.astype(BF)), axis=0))

    @pl.when(step == steps - 1)
    def _():
        scale = -1.0 / cells
        mix = mix_ref[...]
        dec_ref[:genes, :] = (g_ref[:genes, :hidden] - mix[:, :hidden]) * scale
        dec_ref[genes : 2 * genes, :] = g_ref[genes:, :hidden] * scale
        pick = jnp.where(lax.broadcasted_iota(jnp.int32, (8, 16), 1) < 2, 1.0, 0.0)
        score_row = nt(pick, g_ref[:genes, hidden:] - mix[:, hidden:], HI)
        drop_row = nt(pick, g_ref[genes:, hidden:], HI)
        disp_row = row_sums((acc_ref[...] + dig_ref[...]) * par_ref[1])
        row = lax.broadcasted_iota(jnp.int32, score_row.shape, 0)
        gene_rows = scale * jnp.where(
            row == 0, score_row, jnp.where(row == 1, drop_row, jnp.where(row == 2, disp_row, 0.0))
        )
        dec_ref[2 * genes :, :] = lines(gene_rows, pl.cdiv(genes, 128))


def enc_back_kernel(cells, latent, fast, span, me_ref, own_ref, dnear_ref, dfar_ref, aff_dec_ref, sums_ref, stat_ref, gain_ref, lat_ref, noise_ref, klw_ref, anear_ref, afar_ref, side_ref, held_ref, logc_ref, cols_ref, z_ref, out_ref, rest_ref, lane_ref, left_ref, fixed_ref, one_ref, kept_ref, sum_ref):
    step = pl.program_id(0)
    steps = kept_ref.shape[0]
    genes, width = logc_ref.shape[0], dnear_ref.shape[2]
    hidden = aff_dec_ref.shape[0]
    cells_at = part_of(step, width)
    place = (step ^ me_ref[0]) if fast else step
    kinds = (rest_ref.shape[0] - 64) // 2
    at = latent + 1 - 8
    m_one, m_two = norm_sums(sums_ref[at : at + 2], gain_ref, 2)
    m_two = m_two / gain_ref[2:3] * (1.0 / cells)
    m_one = m_one * (1.0 / cells) - m_two * gain_ref[3:4]

    @pl.when(step == 0)
    def _():
        out_ref[...] = jnp.zeros_like(out_ref)
        rest_ref[...] = jnp.zeros_like(rest_ref)
        lane_ref[...] = jnp.zeros_like(lane_ref)
        sum_ref[...] = jnp.zeros_like(sum_ref)
        _, inv = norm_rows(stat_ref[...], latent - 8, cells)
        lat = lat_ref[...] * (gain_ref[2:3] * inv)
        fixed_ref[...] = jnp.broadcast_to(jnp.sum(lat * m_one, axis=1, keepdims=True), fixed_ref.shape)
        high, mid, _ = three(lat * m_two)
        left_ref[...] = jnp.concatenate((high, mid), axis=0)

    index = lax.div(place, 2) if fast else place
    near = (lax.rem(place, 2) == 0) if fast else None

    def take(near_ref, far_ref, rows, lanes):
        if not fast:
            return near_ref[index, rows, lanes]
        return jnp.where(near, near_ref[index, rows, lanes], far_ref[index, rows, lanes])

    every = slice(0, width)
    scale = klw_ref[0:1, 0:1] * (1.0 / cells)
    affine_dec = aff_dec_ref[:, cells_at]
    both = nn(left_ref[...], affine_dec)
    block = take(dnear_ref, dfar_ref, slice(0, 16), every)
    kept_ref[step] = block[8:]
    grad_z = (block - fixed_ref[:, 0:1] - (both[:16] + both[16:]))[:latent]
    noise = noise_ref[:, cells_at]
    pieces = take(anear_ref, afar_ref, slice(hidden, hidden + 32), every).astype(F32)
    lat_logvar = pieces[:latent] + pieces[16 : 16 + latent]
    spread = jnp.exp(lat_logvar)
    var = spread + 0.0001
    inv_std = lax.rsqrt(var)
    z = z_ref[:, cells_at]
    lat_mean = z[0:latent] - var * inv_std * noise
    g_mean = latent_rows(grad_z + scale * lat_mean)
    g_var = latent_rows(spread * (grad_z * noise * (0.5 * inv_std) + (0.5 * scale) * (1.0 - inv_std * inv_std)))
    g_head = jnp.concatenate((g_mean, g_var), axis=0)
    sum_ref[0:32, :] += sum(g_head[:, t : t + 128] for t in range(0, width, 128))
    sum_ref[32:, :] += sum(z[:, t : t + 128] for t in range(0, width, 128))
    head_high, head_mid, _ = three(g_head)
    heads = jnp.concatenate((head_high, head_mid, head_high), axis=0)
    for begin in range(0, width, span):
        lanes = slice(begin, begin + span)
        affine = take(anear_ref, afar_ref, slice(0, hidden), lanes)
        one_ref[hidden:, lanes] = relu_low(affine)
        wide = affine.astype(F32)
        dy = jnp.where(wide > 0, nn(cols_ref[...], heads[:, lanes]), 0.0)
        one_ref[0:hidden, lanes] = dy.astype(BF)
        weighted = dy * wide
        lane_ref[...] += sum(weighted[:, t : t + 128] for t in range(0, span, 128))
    dy_low = one_ref[0:hidden, :]
    side = side_ref[:, cells_at]
    out_ref[0:genes, :] += nt(logc_ref[:, cells_at], dy_low)
    mixed = nt(side, dy_low)
    rest_ref[0:kinds, :] += mixed[:kinds]
    out_ref[genes : genes + 1, :] += mixed[kinds : kinds + 1]
    rest_ref[kinds : kinds + 32, :] += nt(head_high, one_ref[hidden:, :])
    base = kinds + 40
    product = nt(jnp.concatenate((side, z.astype(BF)), axis=0), affine_dec)
    rest_ref[base : base + kinds, :] -= product[:kinds] * m_two
    rest_ref[base + kinds : base + kinds + 16, :] -= product[kinds + 16 :] * m_two

    @pl.when(step == steps - 1)
    def _():
        out_ref[genes + 1 : genes + 2, :] = row_sums(lane_ref[...])[0:1]
        rest_ref[kinds + 32 : kinds + 40, 0:32] = row_sums(sum_ref[0:32, :])
        held = jnp.concatenate((held_ref[...], sum_ref[32:, :]), axis=0)
        rest_ref[base : base + kinds + 16, :] -= jnp.sum(held, axis=1, keepdims=True) * m_one
        count = (kinds + 16) // steps
        for owner in range(steps):
            for k in range(count):
                line = latent + 3 + k // 8 - 8
                at = slice(base + owner * count + k, base + owner * count + k + 1)
                rest_ref[at, :] += kept_ref[owner, line : line + 1, (k % 8) * hidden : (k % 8 + 1) * hidden]
        size = rest_ref.shape[0] // 8
        out_ref[genes + 8 :, :] = rest_ref[pl.ds(pl.multiple_of((own_ref[0] & 7) * size, 8), size), :]


def whole_gradient(part, product, plain, gain, shift, inv, one, two):
    return (gain * inv) * (part - plain * one - ((product - plain * shift) / gain) * two)


def norm_sums(rows, norm_ref, at):
    return rows[0:1], (rows[1:2] - norm_ref[at + 1 : at + 2] * rows[0:1]) / norm_ref[at : at + 1]


def finish_kernel(cells, latent, sum_ref, dec_ref, fixed_ref, stat_enc_ref, norm_ref, kl_ref, klw_ref, own_ref, enc_out, tail_out, loss_out):
    genes = enc_out.shape[0]
    size = tail_out.shape[0] - 8
    count = pl.cdiv(genes, 128)
    kinds = fixed_ref.shape[0] - genes - 8 * count - 8
    loss_out[...] = klw_ref[0:1, 0:1] * kl_ref[...] - own_ref[latent : latent + 1, :]
    _, inv = norm_rows(stat_enc_ref[...], 0, cells)
    n_one, n_two = norm_sums(sum_ref[genes : genes + 8, :], norm_ref, 0)
    at = genes + kinds
    logs = jnp.concatenate([fixed_ref[at + 8 * i : at + 8 * (i + 1), :] for i in range(count)], axis=1)
    log_sum = jnp.transpose(logs)[:genes, 0:1]
    enc = whole_gradient(
        sum_ref[0:genes, :], fixed_ref[0:genes, :], log_sum, norm_ref[0:1], norm_ref[1:2], inv, n_one * (1.0 / cells), n_two * (1.0 / cells)
    )
    enc_out[...] = enc
    dec = dec_ref[...]
    lane = jnp.sum(enc * enc, axis=0, keepdims=True) + jnp.sum(dec * dec, axis=0, keepdims=True)
    tail_out[0:size, :] = sum_ref[genes + 8 :, :]
    tail_out[size:, :] = jnp.broadcast_to(jnp.sum(lane, axis=1, keepdims=True), (8, tail_out.shape[1]))


def step_of(weight, gradient, first, second, rate):
    first = beta_one * first + (1.0 - beta_one) * gradient
    second = beta_two * second + (1.0 - beta_two) * gradient * gradient
    fixed_one = first * (1.0 / (1.0 - beta_one**step_number))
    fixed_two = second * (1.0 / (1.0 - beta_two**step_number))
    update = fixed_one / (jnp.sqrt(fixed_two) + 1e-08) + decay_rate * weight
    return weight - rate * update, first, second


def update_kernel(cells, latent, me_ref, near_ref, far_ref, enc_g_ref, dec_g_ref, sum_ref, fixed_ref, stat_enc_ref, stat_dec_ref, sums_ref, *refs):
    ins, outs, (rest_ref, small_g_ref, head_g_ref, norm_g_ref) = refs[:18], refs[18:-4], refs[-4:]
    enc, dec, gene, small, head, norm = (ins[3 * i : 3 * i + 3] for i in range(6))
    genes, hidden = enc[0].shape
    rows = small[0].shape[0]
    kinds = (rows - latent) // 2
    count = pl.cdiv(genes, 128)
    size = near_ref.shape[1]
    for core, ref in enumerate((near_ref, far_ref)):
        for index in range(ref.shape[0]):
            owner = me_ref[0] ^ (2 * index + core)
            rest_ref[pl.ds(pl.multiple_of(owner * size, 8), size), :] = ref[index]
    whole_rest = [rest_ref[i * size : i * size + size - 8, :] for i in range(8)]
    square = jnp.zeros((1, 1), F32)
    for i in range(8):
        square = square + rest_ref[(i + 1) * size - 8 : (i + 1) * size - 7, 0:1]
    rest = jnp.concatenate(whole_rest, axis=0)
    gains = norm[0]
    gain, shift = gains[0:1], gains[1:2]
    n_one, n_two = norm_sums(sum_ref[genes : genes + 8, :], gains, 0)
    _, inv = norm_rows(stat_enc_ref[...], 0, cells)
    _, inv_dec = norm_rows(stat_dec_ref[...], latent - 8, cells)
    at = genes + kinds + 8 * count
    batch_sum = jnp.transpose(fixed_ref[at : at + 8, :])[:kinds, 0:1]
    small_g_ref[0:kinds, :] = whole_gradient(
        rest[0:kinds], fixed_ref[genes : genes + kinds, :], batch_sum, gain, shift, inv, n_one * (1.0 / cells), n_two * (1.0 / cells)
    )
    small_g_ref[kinds:, :] = (gains[2:3] * inv_dec) * rest[kinds + 40 : 2 * kinds + 56]
    bias = jnp.transpose(rest[kinds + 32 : kinds + 40])
    for half in range(2):
        into = slice(half * latent, (half + 1) * latent)
        head_g_ref[into, 0:hidden] = rest[kinds + 16 * half : kinds + 16 * half + latent]
        head_g_ref[into, hidden : hidden + 1] = bias[16 * half : 16 * half + latent, 0:1]
    at = latent + 1 - 8
    norm_g_ref[0:1] = n_two
    norm_g_ref[1:2] = n_one
    m_one, m_two = norm_sums(sums_ref[at : at + 2], gains, 2)
    norm_g_ref[2:3] = m_two
    norm_g_ref[3:4] = m_one
    small_square = jnp.zeros((1, 1), F32)
    for part in (small_g_ref[0:rows, :], head_g_ref[...], norm_g_ref[...]):
        small_square = small_square + jnp.sum(jnp.sum(part * part, axis=0, keepdims=True), axis=1, keepdims=True)
    value = jnp.sqrt(square + small_square)
    factor = jnp.minimum(1.0, max_norm / value)
    (enc_n, enc_m, enc_v, enc_l, dec_n, dec_m, dec_v, dec_l, gene_n, gene_m, gene_v, small_n, small_m, small_v, head_n, head_m, head_v, norm_n, norm_m, norm_v, norm_out) = outs
    norm_out[...] = value
    new, first, second = step_of(enc[0][...], enc_g_ref[...] * factor, enc[1][...], enc[2][...], rate_genes)
    enc_n[...], enc_m[...], enc_v[...], enc_l[...] = new, first, second, new.astype(BF)
    for index in range(2):
        gradient = dec_g_ref[index * genes : (index + 1) * genes, :] * factor
        new, first, second = step_of(dec[0][index], gradient, dec[1][index], dec[2][index], rate_genes)
        dec_n[index], dec_m[index], dec_v[index], dec_l[index] = new, first, second, new.astype(BF)
    for index in range(pl.cdiv(genes, 128)):
        span = slice(index * 128, min(genes, (index + 1) * 128))
        gradient = dec_g_ref[2 * genes + index * 8 : 2 * genes + index * 8 + 3, 0 : span.stop - span.start] * factor
        new, first, second = step_of(gene[0][:, span], gradient, gene[1][:, span], gene[2][:, span], rate_small)
        gene_n[:, span], gene_m[:, span], gene_v[:, span] = new, first, second
    new, first, second = step_of(small[0][...], small_g_ref[0:rows, :] * factor, small[1][...], small[2][...], rate_small)
    small_n[...], small_m[...], small_v[...] = new, first, second
    new, first, second = step_of(head[0][...], head_g_ref[...] * factor, head[1][...], head[2][...], rate_small)
    head_n[...], head_m[...], head_v[...] = new, first, second
    new, first, second = step_of(norm[0][...], norm_g_ref[...] * factor, norm[1][...], norm[2][...], rate_small)
    norm_n[...], norm_m[...], norm_v[...] = new, first, second


def gather_genes(value, fast, blocks, width, late=None):
    if fast:
        near = jnp.stack([value] + [swap(value, "genes", 2 * k) for k in (1, 2, 3)])
        near = near if late is None else after(near, late)
        return near, swap(near, "genes", 1)
    rows = value.shape[0]
    whole_rows = lax.all_gather(value, "genes", axis=0).transpose(1, 0, 2)
    near = whole_rows.reshape(rows, blocks, width).transpose(1, 0, 2)
    return near, near


def per_device(counts, library, noise, batch_ids, gene_mask, kl_weight, enc_w, enc_m, enc_v, dec_w, dec_m, dec_v, gene_par, gene_m, gene_v, small_w, small_m, small_v, head_w, head_m, head_v, norm_par, norm_m, norm_v):
    rows_all, genes = counts.shape
    cells = float(rows_all * lax.axis_size("cells"))
    groups = lax.axis_size("genes")
    hidden = enc_w.shape[1]
    latent = head_w.shape[1] // 2
    kinds = (small_w.shape[0] - latent) // 2
    share = rows_all // groups
    width = min(1024, rows_all)
    blocks = rows_all // width
    fast = groups == 8 and blocks == 8
    me = lax.axis_index("genes").astype(jnp.int32).reshape(1)
    gene_lines = -(-genes // 128)

    def turn(value):
        return value.transpose(0, 2, 1)

    x_t = counts.T
    noise_t = noise.T
    dec_t = turn(dec_w)
    head_t = head_w.T
    lib8 = library.reshape(blocks, width)
    batch_all = batch_ids.reshape(blocks, 1, width)
    batch_own = batch_ids.reshape(groups, 1, share)
    klw = jnp.broadcast_to(kl_weight.reshape(1, 1), (8, 128))

    own_block = pl.BlockSpec((1, 1, share), lambda i, m: (m[0], 0, 0))
    own_lanes = lambda rows: pl.BlockSpec((rows, share), lambda i, m: (0, m[0]))
    lane_block = lambda rows: pl.BlockSpec((rows, width), lambda i, *_: (0, i))
    here = pl.BlockSpec(memory_space=pltpu.VMEM)
    full = lambda array: (array, here)
    out_of = lambda shape, dtype=F32: (shape, dtype, whole(shape))
    new = lambda shape, dtype=F32: (shape, dtype, here)

    def encode(low, count, weight, near=False):
        return call(
            lambda *refs: enc_kernel(low, count, share, near, *refs),
            (1,),
            [
                (me if fast else me & 1, None),
                (x_t, here) if near else (in_hbm(x_t), pl.BlockSpec(memory_space=pl.ANY)),
                (in_hbm(weight), pl.BlockSpec(memory_space=pl.ANY)),
            ],
            [new((count // 2, hidden, share)), new((count // 2, hidden, share), BF)],
            scratch=[
                pltpu.VMEM((genes, hidden), F32),
                pltpu.VMEM((hidden, genes), BF),
                pltpu.SemaphoreType.DMA((count + 1,)),
            ]
            + ([] if near else [pltpu.VMEM((count, genes, share), BF)]),
            scalars=1,
            us=2.0 if near else 3.0,
            mib=6 if near else 8,
        )

    slot = pl.BlockSpec((1, hidden, share), lambda i, m: (0, 0, 0))
    if fast:
        keep_far, send_far = encode(4, 4, enc_w)
        got_far = swap(send_far, "genes", 1)
        keep_near, send_near = encode(0, 4, after(enc_w, send_far), True)
        far = [
            swap((keep_far[k : k + 1] + got_far[k : k + 1].astype(F32)).astype(BF), "genes", 4 + 2 * k)
            for k in range(2)
        ]
        got = swap(send_near, "genes", 1)
        ready = (keep_near[1:2] + got[1:2].astype(F32)).astype(BF)
        far.append(swap(ready, "genes", 2))
        kept = keep_near
    else:
        keep_part, send_part = encode(0, groups, enc_w)
        got = swap(send_part, "genes", 1)
        summed = lax.psum_scatter(
            keep_part + got.astype(F32),
            "genes",
            scatter_dimension=0,
            axis_index_groups=[list(range(c, groups, 2)) for c in range(2)],
            tiled=True,
        )
        zero = jnp.zeros((1, hidden, share), BF)
        kept, got, far = summed, zero, [zero] * 3
        ready = keep_part

    mask_late = after(gene_mask.reshape(1, genes), ready)
    aug, dec_n, par, lg_tab, dg_tab, enc_pieces, dec_pieces, dec_plain, lat_row, head_rows, head_bias, head_cols, norm_t = call(
        prep_kernel,
        (1,),
        [full(gene_par), full(mask_late), full(dec_t), full(small_w), full(head_t), full(norm_par)],
        [
            new((2 * genes, hidden + 16), BF),
            new((hidden, 2 * genes), BF),
            new((5, genes, 128)),
            new((COUNT_TOP, genes, 128)),
            new((COUNT_TOP, genes, 128)),
            new((3 * hidden, kinds), BF),
            new((3 * hidden, kinds + 48), BF),
            new((hidden, kinds + 16)),
            new((16, hidden)),
            new((32, hidden)),
            new((32, 128)),
            new((hidden, 96), BF),
            new((hidden, 8)),
        ],
    )
    batch_spec = pl.BlockSpec((1, 1, width), lambda i, *_: (i, 0, 0))
    logc, x_kept, side, lib8, gam_cell, dig_acc, log_lines, held = call(
        lambda *refs: counts_kernel(16, min(512, width), *refs),
        (blocks,),
        [
            (in_hbm(x_t), lane_block(genes)),
            full(lg_tab),
            full(dg_tab),
            full(par),
            (batch_all, batch_spec),
            full(lib8),
        ],
        [
            ((genes, rows_all), BF, lane_block(genes), True),
            ((genes, rows_all), BF, lane_block(genes), True),
            ((kinds + 16, rows_all), BF, here),
            new((blocks, width)),
            new((blocks, width)),
            new((genes, 128)),
            new((8, 128)),
            new((kinds, 128)),
        ],
        mib=8,
        us=15.0,
    )
    enc_late = after(enc_pieces, log_lines)
    stat8 = whole((8, hidden))
    pre_enc, stat_enc = call(
        own_kernel,
        (1,),
        [(me, None), (kept, slot), (got, slot)]
        + [(part, slot) for part in far]
        + [(batch_own, own_block), full(enc_late)],
        [new((hidden, share)), new((8, hidden))],
        scalars=1,
    )
    stat_enc = total(total(stat_enc, "genes"), "cells")

    pack, aff_own, kl_row = call(
        lambda *refs: latent_kernel(cells, latent, *refs),
        (1,),
        [
            (me, None),
            full(pre_enc),
            full(stat_enc),
            full(norm_t),
            full(head_rows),
            full(head_bias),
            (noise_t, own_lanes(latent)),
            (batch_own, own_block),
            full(dec_pieces),
        ],
        [new((16, share)), new((hidden + 32, share), BF), new((1, share))],
        scalars=1,
    )
    near, far_pack = gather_genes(pack, fast, blocks, width)
    if fast:
        stat_dec = jnp.sum(near[:, 8:16, :hidden], axis=0) + jnp.sum(far_pack[:, 8:16, :hidden], axis=0)
    else:
        stat_dec = lax.psum(pack[8:16, :hidden], "genes")
    stat_dec = total(stat_dec, "cells")

    aff_dec, lse, z_all, top, mass_all, mass_low_all = call(
        lambda *refs: decode_kernel(cells, latent, fast, *refs),
        (blocks,),
        [
            (me, None),
            (near, here),
            (far_pack, here),
            (side, here),
            full(stat_dec),
            full(norm_t),
            full(dec_plain),
            full(aug),
        ],
        [
            ((hidden, rows_all), BF, here),
            new((blocks, width)),
            ((16, rows_all), F32, here),
            new((blocks, width)),
            ((genes, rows_all), F32, here),
            ((genes, rows_all), BF, here),
        ],
        scratch=[pltpu.VMEM((genes, width), F32), pltpu.VMEM((2 * hidden, kinds + 48), BF)],
        scalars=1,
        us=8.0,
    )
    (part_r,) = call(
        lambda *refs: softmax_kernel(width, *refs),
        (blocks,),
        [(mass_low_all, here), full(dec_n)],
        [((hidden, rows_all), F32, here)],
        us=2.5,
    )
    lse_all = after(log_total_of(lse, "genes"), part_r)

    full8 = whole((blocks, width))
    g_both, mass, recon, gene_acc = call(
        lambda *refs: zinb_kernel(64, min(1024, width), *refs),
        (blocks,),
        [
            (aff_dec, here),
            (mass_all, here),
            full(top),
            full(aug),
            (in_hbm(x_kept), lane_block(genes)),
            full(par),
            full(lib8),
            full(lse_all),
            full(gam_cell),
        ],
        [((2 * genes, rows_all), BF, here)]
        + [new((blocks, width)), new((blocks, width)), new((genes, 128))],
        scratch=[pltpu.VMEM((genes, width), F32)],
        mib=16,
        us=28.0,
    )
    mass_low = mass + swap(mass, "genes", 1)
    mass = total(mass_low, "genes", 1)
    (part_a,) = call(
        lambda *refs: back_kernel(width, *refs),
        (blocks,),
        [(g_both, here), full(dec_n)],
        [((hidden, rows_all), F32, here)],
        us=4.0,
    )

    aff_near, aff_far = gather_genes(after(aff_own, lse_all), fast, blocks, width, mass_low)
    fixed_rows = genes + kinds + 8 * gene_lines + 8
    (fixed,) = call(
        lambda *refs: enc_sums_kernel(fast, *refs),
        (blocks,),
        [
            (me, None),
            (logc, here),
            (aff_near, here),
            (aff_far, here),
            (side, here),
            full(log_lines),
        ],
        [new((fixed_rows, hidden))],
        scratch=[pltpu.VMEM((genes, 16), F32)],
        scalars=1,
        us=4.0,
    )
    fixed = total_by_halves(fixed, "cells", (1, 2))

    keep_d, send_d = call(
        lambda *refs: hidden_grad_kernel(cells, latent, *refs),
        (blocks,),
        [
            (me if fast else jnp.zeros_like(me), None),
            (part_a, here),
            (part_r, here),
            (mass, here),
            (aff_dec, here),
            full(top),
            full(lse_all),
            full(stat_dec),
            full(norm_par),
            full(lat_row),
            full(recon),
            (z_all, here),
            (side, here),
        ],
        [
            new((blocks // 2, 16, width)),
            new((blocks // 2, 16, width)),
        ],
        scratch=[pltpu.VMEM((hidden, 128), F32), pltpu.VMEM((kinds + 32, hidden), F32)],
        scalars=1,
        us=5.0,
    )
    (dec_part,) = call(
        lambda *refs: dec_grad_kernel(cells, *refs),
        (blocks,),
        [
            (mass_low_all, here),
            (aff_dec, here),
            (mass, here),
            full(top),
            full(lse_all),
            (g_both, here),
            full(gene_acc),
            full(dig_acc),
            full(par),
        ],
        [new((2 * genes + 8 * gene_lines, hidden))],
        scratch=[pltpu.VMEM((genes, hidden + 16), F32), pltpu.VMEM((2 * genes, hidden + 16), F32)],
        us=6.0,
    )
    if fast:
        got_d = swap(send_d, "genes", 1)
        pieces = [swap(keep_d[k] + got_d[k], "genes", 2 * k) for k in (1, 2, 3)]
        pieces = [after(piece, dec_part) for piece in pieces]
        own_d = (keep_d[0] + got_d[0] + pieces[0]) + (pieces[1] + pieces[2])
        sums_dec = own_d[8:, :hidden]
    else:
        both = jnp.stack([keep_d, send_d], axis=1).reshape(blocks, 16, width)
        sums_dec = lax.psum(both[0, 8:, :hidden], "genes")
        both = both.transpose(1, 0, 2).reshape(16, groups, share).transpose(1, 0, 2)
        own_d = lax.psum_scatter(both, "genes", scatter_dimension=0, tiled=True)[0]
    sums_dec = total(sums_dec, "cells")
    d_near, d_far = gather_genes(own_d, fast, blocks, width)
    dec_g = total_by_halves(dec_part, "cells", (2, 1))

    size = (2 * kinds + 64) // 8
    (enc_part,) = call(
        lambda *refs: enc_back_kernel(cells, latent, fast, min(256, width), *refs),
        (blocks,),
        [
            (me, None),
            (me, None),
            (d_near, here),
            (d_far, here),
            (aff_dec, here),
            full(sums_dec),
            full(stat_dec),
            full(norm_par),
            full(lat_row),
            (noise_t, here),
            full(klw),
            (aff_near, here),
            (aff_far, here),
            (side, here),
            full(held),
            (logc, here),
            full(head_cols),
            (z_all, here),
        ],
        [new((genes + 8 + size, hidden))],
        scratch=[
            pltpu.VMEM((2 * kinds + 64, hidden), F32),
            pltpu.VMEM((hidden, 128), F32),
            pltpu.VMEM((32, hidden), BF),
            pltpu.VMEM((16, 128), F32),
            pltpu.VMEM((2 * hidden, width), BF),
            pltpu.VMEM((blocks, 8, width), F32),
            pltpu.VMEM((48, 128), F32),
        ],
        scalars=2,
        us=11.0,
    )
    enc_sum = total_by_halves(enc_part, "cells", (1, 2))
    enc_g, tail, loss = call(
        lambda *refs: finish_kernel(cells, latent, *refs),
        (1,),
        [full(a) for a in (enc_sum, dec_g, fixed, stat_enc, norm_par, kl_row, klw, own_d)],
        [new((genes, hidden)), new((size + 8, hidden)), new((1, share))],
    )
    if fast:
        tail_near = jnp.stack([tail] + [swap(tail, "genes", 2 * k) for k in (1, 2, 3)])
        tail_far = swap(tail_near, "genes", 1)
    else:
        tails = lax.all_gather(tail, "genes", axis=0)
        square = jnp.sum(tails[:, size:], axis=0)
        tails = tails[:8].at[:, size:].set(0.0).at[0, size:].set(square)
        tail_near, tail_far = tails[0::2], tails[1::2]

    state = [
        enc_w, enc_m, enc_v, dec_t, turn(dec_m), turn(dec_v), gene_par, gene_m, gene_v,
        small_w, small_m, small_v, head_t, head_m.T, head_v.T, norm_par, norm_m, norm_v,
    ]
    ins = [tail_near, tail_far, enc_g, dec_g, enc_sum, fixed, stat_enc, stat_dec, sums_dec] + state
    outs = []
    for index in range(6):
        one = state[3 * index]
        outs += [(one.shape, F32)] * 3
        if index < 2:
            outs.append((one.shape, BF))
    outs.append(((1, 1), F32))
    res = call(
        lambda *refs: update_kernel(cells, latent, *refs),
        (1,),
        [(me if fast else jnp.zeros_like(me), None)] + [full(array) for array in ins],
        [out_of(shape, dtype) for shape, dtype in outs],
        scratch=[
            pltpu.VMEM((8 * (size + 8), hidden), F32),
            pltpu.VMEM((2 * kinds + 16, hidden), F32),
            pltpu.VMEM((2 * latent, hidden + 1), F32),
            pltpu.VMEM((4, hidden), F32),
        ],
        scalars=1,
        mib=16,
    )
    enc_res, dec_res = res[0:4], [turn(part) for part in res[4:8]]
    head_res = [part.T for part in res[14:17]]
    return (
        *enc_res,
        *dec_res,
        *res[8:14],
        *head_res,
        *res[17:20],
        res[20].reshape(()),
        loss.reshape(share),
    )


def solution(mesh):
    placed = (
        P("cells", "genes"), P("cells"), P("cells", None), P("cells"), P("genes"), P(),
        P("genes", None), P("genes", None), P("genes", None),
        P(None, None, "genes"), P(None, None, "genes"), P(None, None, "genes"),
        P(None, "genes"), P(None, "genes"), P(None, "genes"),
        P(), P(), P(), P(), P(), P(), P(), P(), P(),
    )
    return jax.shard_map(
        per_device,
        mesh=mesh,
        in_specs=placed,
        out_specs=(
            P("genes", None), P("genes", None), P("genes", None), P("genes", None),
            P(None, None, "genes"), P(None, None, "genes"), P(None, None, "genes"), P(None, None, "genes"),
            P(None, "genes"), P(None, "genes"), P(None, "genes"),
            P(), P(), P(), P(), P(), P(), P(), P(), P(), P(),
            P(("cells", "genes")),
        ),
        check_vma=False,
    )
```

```python
import jax
import jax.numpy as jnp
from jax import lax
from jax.experimental import pallas as pl
from jax.experimental.pallas import tpu as pltpu
from jax.sharding import PartitionSpec as P

norm_epsilon = 0.001
zinb_epsilon = 1e-08
beta_one = 0.9
beta_two = 0.999
step_number = 5.0
decay_rate = 0.01
rate_genes = 0.03
rate_small = 0.2
max_norm = 0.1

F32 = jnp.float32
BF = jnp.bfloat16
HI = lax.Precision.HIGHEST
COUNT_TOP = 8
LOG2_E = 1.4426950408889634


def nn(left, right, precision=None):
    return lax.dot_general(
        left, right, (((1,), (0,)), ((), ())), precision=precision, preferred_element_type=F32
    )


def nt(left, right, precision=None):
    return lax.dot_general(
        left, right, (((1,), (1,)), ((), ())), precision=precision, preferred_element_type=F32
    )


def whole(shape):
    return pl.BlockSpec(shape, lambda *_: (0,) * len(shape))


def in_hbm(array):
    return pltpu.with_memory_space_constraint(array, pltpu.HBM)


def call(kernel, grid, ins, outs, scratch=(), scalars=0, us=2.0, mib=12):
    return pl.pallas_call(
        kernel,
        out_shape=[pltpu.HBM(out[0], out[1]) if len(out) == 4 else jax.ShapeDtypeStruct(out[0], out[1]) for out in outs],
        grid_spec=pltpu.PrefetchScalarGridSpec(
            num_scalar_prefetch=scalars,
            grid=grid,
            in_specs=[spec for _, spec in ins[scalars:]],
            out_specs=[out[2] for out in outs],
            scratch_shapes=list(scratch),
        ),
        compiler_params=pltpu.CompilerParams(vmem_limit_bytes=mib * 1024 * 1024),
        cost_estimate=pl.CostEstimate(flops=0, bytes_accessed=int(us * 3.69e6), transcendentals=0),
    )(*[array for array, _ in ins])


def swap(value, axis, bit):
    count = lax.axis_size(axis)
    return lax.ppermute(value, axis, [(i, i ^ bit) for i in range(count)])


def bit_groups(axis):
    count = lax.axis_size(axis)
    if axis == "genes":
        groups, bit = [[1]], 2
    else:
        groups, bit = [], 1
    while bit < count:
        groups.append([bit, 2 * bit] if 2 * bit < count else [bit])
        bit *= 4
    return groups


def total(value, axis, done=0):
    for group in bit_groups(axis)[done:]:
        if len(group) == 1:
            value = value + swap(value, axis, group[0])
        else:
            low, high = group
            value = (value + swap(value, axis, low)) + (
                swap(value, axis, high) + swap(value, axis, low ^ high)
            )
    return value


def log_total_of(value, axis):
    for group in bit_groups(axis):
        if len(group) == 1:
            parts = [value, swap(value, axis, group[0])]
        else:
            low, high = group
            parts = [value] + [swap(value, axis, k) for k in (low, high, low ^ high)]
        top = parts[0]
        for part in parts[1:]:
            top = jnp.maximum(top, part)
        mass = sum(jnp.exp(part - top) for part in parts)
        value = top + jnp.log(mass)
    return value


def total_by_halves(value, axis, order):
    for bit in order:
        value = value + swap(value, axis, bit)
    return value


def after(value, *others):
    return lax.optimization_barrier((value,) + others)[0]


def three(value):
    high = value.astype(BF)
    rest = value - high.astype(F32)
    mid = rest.astype(BF)
    low = (rest - mid.astype(F32)).astype(BF)
    return high, mid, low


def one_hot(batch_row, kinds):
    ids = lax.broadcasted_iota(jnp.int32, (kinds, batch_row.shape[1]), 0)
    return jnp.where(ids == batch_row, 1.0, 0.0)


def columns(rows):
    return jnp.transpose(rows)


def prep_kernel(gene_ref, mask_ref, dec_ref, small_ref, head_ref, norm_ref, aug_ref, turn_ref, par_ref, lg_ref, dg_ref, enc_out, dec_out, plain_out, lat_out, head_out, bias_out, cols_out, norm_out):
    genes = gene_ref.shape[1]
    hidden = norm_ref.shape[1]
    latent = head_ref.shape[0] // 2
    kinds = (small_ref.shape[0] - latent) // 2
    padded = pl.cdiv(genes, 128) * 128
    keep = mask_ref[...] > 0
    score_b = jnp.where(keep, gene_ref[0:1], -1e30)
    drop_b = jnp.where(keep, gene_ref[1:2], 1e30)
    th = jnp.exp(gene_ref[2:3])
    kept = jnp.where(keep, 1.0, 0.0)
    rows = jnp.concatenate((score_b, drop_b, th, kept, th, th, th, th), axis=0)
    if padded > genes:
        rows = jnp.concatenate((rows, jnp.ones((8, padded - genes), F32)), axis=1)
    turned = jnp.transpose(rows)[:genes]
    lane = lax.broadcasted_iota(jnp.int32, (genes, 16), 1)
    for half in range(2):
        at = slice(half * genes, (half + 1) * genes)
        aug_ref[at, 0:hidden] = dec_ref[half].astype(BF)
        high, mid, low = (jnp.broadcast_to(part.astype(F32), (genes, 16)) for part in three(turned[:, half : half + 1]))
        tail = jnp.where(lane == 0, high, jnp.where(lane == 1, mid, jnp.where(lane == 2, low, 0.0)))
        if half == 0:
            tail = jnp.where((lane >= 3) & (lane < 6), 1.0, tail)
        aug_ref[at, hidden : hidden + 16] = tail.astype(BF)
        turn_ref[:, at] = jnp.transpose(dec_ref[half]).astype(BF)
    th_w = jnp.broadcast_to(turned[:, 2:3], (genes, 128))
    keep_w = jnp.broadcast_to(turned[:, 3:4], (genes, 128))
    the_w = th_w + zinb_epsilon
    par_ref[0] = the_w
    par_ref[1] = th_w
    par_ref[2] = jnp.log(the_w)
    par_ref[3] = th_w / the_w
    par_ref[4] = keep_w
    gam = jnp.zeros_like(th_w)
    dig = jnp.zeros_like(th_w)
    for k in range(COUNT_TOP):
        more = th_w + float(k)
        gam = gam + keep_w * jnp.log(more * (1.0 / (1.0 + k)))
        dig = dig + keep_w / more
        lg_ref[k] = gam
        dg_ref[k] = dig
    for index, piece in enumerate(three(jnp.transpose(small_ref[0:kinds, :]))):
        enc_out[index * hidden : (index + 1) * hidden, :] = piece
    row = lax.broadcasted_iota(jnp.int32, (16, hidden), 0)
    lat_row = jnp.zeros((16, hidden), F32)
    for index in range(latent):
        lat_row = jnp.where(row == index, small_ref[2 * kinds + index : 2 * kinds + index + 1, :], lat_row)
    lat_out[...] = lat_row
    batch_turned, lat_turned = jnp.transpose(small_ref[kinds : 2 * kinds, :]), jnp.transpose(lat_row)
    plain_out[...] = jnp.concatenate((batch_turned, lat_turned), axis=1)
    batch_pieces = three(batch_turned)
    lat = three(lat_turned)
    zero = jnp.zeros_like(lat[0])
    tails = ((lat[0], lat[0], lat[0]), (lat[1], lat[1], zero), (lat[2], zero, zero))
    for index in range(3):
        at = slice(index * hidden, (index + 1) * hidden)
        dec_out[at, :] = jnp.concatenate((batch_pieces[index],) + tails[index], axis=1)
    full = lax.broadcasted_iota(jnp.int32, (32, hidden), 0)
    head = jnp.zeros((32, hidden), F32)
    bias = jnp.zeros((32, 1), F32)
    for index in range(2 * latent):
        to = index if index < latent else index - latent + 16
        head = jnp.where(full == to, head_ref[index : index + 1, 0:hidden], head)
        bias = jnp.where(full[:, 0:1] == to, head_ref[index : index + 1, hidden : hidden + 1], bias)
    head_out[...] = head
    bias_out[...] = jnp.broadcast_to(bias, (32, 128))
    high, mid, _ = three(jnp.transpose(head))
    cols_out[...] = jnp.concatenate((high, high, mid), axis=1)
    norm_out[...] = jnp.transpose(jnp.concatenate((norm_ref[...], norm_ref[...]), axis=0))


def exact_rows(stacked, table):
    out = nn(stacked, table)
    hidden = out.shape[0] // 3
    return out[:hidden] + out[hidden : 2 * hidden] + out[2 * hidden :]


def dec_table(z, batch_row, kinds):
    high, mid, low = three(z)
    return jnp.concatenate((one_hot(batch_row, kinds).astype(BF), high, mid, low), axis=0)


def row_sums(value):
    return nt(jnp.ones((8, value.shape[1]), F32), value, HI)


def stat_rows(first, second, at):
    sums, squares = row_sums(first), row_sums(second)
    row = lax.broadcasted_iota(jnp.int32, sums.shape, 0)
    return jnp.where(row == at, sums, jnp.where(row == at + 1, squares, 0.0))


def enc_kernel(low, count, share, near, me_ref, x_ref, w_ref, keep_ref, send_ref, weight_ref, turn_ref, arrived, *buffers):
    def at(i):
        return pl.ds(pl.multiple_of(((low + i) ^ me_ref[0]) * share, share), share)

    weight = pltpu.make_async_copy(w_ref, weight_ref, arrived.at[count])
    weight.start()
    if not near:
        (buffer_ref,) = buffers

        def block(i):
            return pltpu.make_async_copy(x_ref.at[:, at(i)], buffer_ref.at[i], arrived.at[i])

        for i in range(count):
            block(i).start()
    weight.wait()
    turn_ref[...] = jnp.transpose(weight_ref[...]).astype(BF)

    def pair(half, carry):
        for odd in range(2):
            i = 2 * half + odd
            if near:
                x = x_ref[:, at(i)]
            else:
                block(i).wait()
                x = buffer_ref[i]
            part = nn(turn_ref[...], jnp.log(1.0 + x.astype(F32)).astype(BF))
            if odd:
                send_ref[half] = part.astype(BF)
            else:
                keep_ref[half] = part
        return carry

    lax.fori_loop(0, count // 2, pair, 0)


def lines(rows8, count):
    wide = rows8.shape[1]
    if wide < 128 * count:
        rows8 = jnp.concatenate((rows8, jnp.zeros((8, 128 * count - wide), F32)), axis=1)
    return jnp.concatenate([rows8[:, i * 128 : (i + 1) * 128] for i in range(count)], axis=0)


def counts_kernel(rows, span, x_ref, lg_ref, dg_ref, par_ref, batch_ref, lib_ref, logc_ref, mask_ref, side_ref, lib_out, cell_ref, disp_ref, line_ref, held_ref):
    step = pl.program_id(0)
    genes, width = mask_ref.shape

    @pl.when(step == 0)
    def _():
        disp_ref[...] = jnp.zeros_like(disp_ref)
        held_ref[...] = jnp.zeros_like(held_ref)

    kinds = held_ref.shape[0]
    table = one_hot(batch_ref[0], kinds)
    held_ref[...] += sum(table[:, t : t + 128] for t in range(0, width, 128))
    row = lax.broadcasted_iota(jnp.int32, (16, width), 0)
    side_ref[0:kinds, part_of(step, width)] = table.astype(BF)
    side_ref[kinds:, part_of(step, width)] = jnp.where(row == 0, 1.0, 0.0).astype(BF)
    lib_out[...] = lib_ref[...]
    tiles = span // 128
    done = []
    for first in range(0, width, span):
        lanes = [slice(first + tile * 128, first + (tile + 1) * 128) for tile in range(tiles)]

        def chunk(g, cell):
            at = pl.ds(pl.multiple_of(g * rows, rows), rows)
            keep = par_ref[4, at, :].astype(BF)
            lows = [x_ref[at, lanes[tile]] for tile in range(tiles)]
            xs = [low.astype(F32) for low in lows]
            logs = [jnp.log(1.0 + x) for x in xs]
            for tile in range(tiles):
                logc_ref[at, lanes[tile]] = logs[tile].astype(BF)
                mask_ref[at, lanes[tile]] = lows[tile] * keep
            gams = [jnp.zeros_like(xs[0]) for _ in range(tiles)]
            digs = [jnp.zeros_like(xs[0]) for _ in range(tiles)]
            for k in range(COUNT_TOP):
                lg, dg = lg_ref[k, at, :], dg_ref[k, at, :]
                for tile in range(tiles):
                    more = xs[tile] > (k + 0.5)
                    gams[tile] = jnp.where(more, lg, gams[tile])
                    digs[tile] = jnp.where(more, dg, digs[tile])
            disp_ref[at, :] += sum(digs)
            out = []
            for tile in range(tiles):
                folded = cell[tile]
                for part in range(rows // 8):
                    folded = folded + gams[tile][part * 8 : (part + 1) * 8]
                out.append(folded)
            return tuple(out)

        zero = tuple(jnp.zeros((8, 128), F32) for _ in range(tiles))
        done += list(lax.fori_loop(0, genes // rows, chunk, zero))
    cell_ref[pl.ds(step, 1), :] = jnp.sum(jnp.concatenate(done, axis=1), axis=0, keepdims=True)

    @pl.when(step == pl.num_programs(0) - 1)
    def _():
        line_ref[...] = row_sums(held_ref[...])


def own_kernel(me_ref, keep_ref, got_ref, one_ref, two_ref, six_ref, batch_ref, enc_b_ref, pre_ref, stat_ref):
    kinds = enc_b_ref.shape[1]
    gathered = (keep_ref[0] + got_ref[0].astype(F32) + one_ref[0].astype(F32)) + (
        two_ref[0].astype(F32) + six_ref[0].astype(F32)
    )
    table = one_hot(batch_ref[0], kinds).astype(BF)
    pre = gathered + exact_rows(enc_b_ref[...], table)
    pre_ref[...] = pre
    stat_ref[...] = stat_rows(pre, pre * pre, 0)


def norm_columns(stat, first, cells):
    turned = jnp.transpose(stat)
    mean = turned[:, first : first + 1] / cells
    var = turned[:, first + 1 : first + 2] / cells - mean * mean
    return mean, lax.rsqrt(var + norm_epsilon)


def norm_rows(stat, first, cells):
    mean = stat[first : first + 1] / cells
    var = stat[first + 1 : first + 2] / cells - mean * mean
    return mean, lax.rsqrt(var + norm_epsilon)


def latent_kernel(cells, latent, me_ref, pre_ref, stat_ref, norm_ref, head_ref, bias_ref, noise_ref, batch_ref, dec_b_ref, pack_ref, aff_ref, kl_ref):
    kinds = dec_b_ref.shape[1] - 48
    hidden = pre_ref.shape[0]
    mean, inv = norm_columns(stat_ref[...], 0, cells)
    phat = (pre_ref[...] - mean) * inv
    affine = norm_ref[:, 0:1] * phat + norm_ref[:, 1:2]
    out = nn(head_ref[...], jnp.maximum(affine, 0.0), HI) + bias_ref[:, 0:1]
    lat_mean, lat_logvar = out[:latent], out[16 : 16 + latent]
    high, mid, _ = three(latent_rows(lat_logvar))
    aff_ref[...] = jnp.concatenate((affine.astype(BF), high, mid), axis=0)
    var = jnp.exp(lat_logvar) + 0.0001
    z = latent_rows(lat_mean + jnp.sqrt(var) * noise_ref[...])
    terms = var + lat_mean * lat_mean - 1.0 - jnp.log(var)
    kl_ref[...] = 0.5 * jnp.sum(terms, axis=0, keepdims=True)
    pre_dec = exact_rows(dec_b_ref[...], dec_table(z, batch_ref[0], kinds))
    stat = stat_rows(pre_dec, pre_dec * pre_dec, 0)
    pack_ref[...] = z
    pack_ref[latent : latent + 1, 0:hidden] = stat[0:1]
    pack_ref[latent + 1 : latent + 2, 0:hidden] = stat[1:2]


def latent_rows(z):
    if z.shape[0] == 16:
        return z
    return jnp.concatenate((z, jnp.zeros((16 - z.shape[0], z.shape[1]), F32)), axis=0)


def part_of(step, width):
    return pl.ds(pl.multiple_of(step * width, 128), width)


def relu_low(affine):
    return jnp.maximum(affine, jnp.zeros_like(affine))


def pick(step, me_ref, fast, near_ref, far_ref):
    if not fast:
        return near_ref[step]
    place = step ^ me_ref[0]
    return jnp.where(lax.rem(place, 2) == 0, near_ref[lax.div(place, 2)], far_ref[lax.div(place, 2)])


def decode_kernel(cells, latent, fast, me_ref, near_ref, far_ref, side_ref, stat_ref, norm_ref, plain_ref, w_ref, aff_ref, lse_ref, z_ref, top_ref, mass_ref, low_ref, score_ref, left_ref):
    kinds = plain_ref.shape[1] - 16
    step = pl.program_id(0)
    cells_at = part_of(step, score_ref.shape[1])
    genes = score_ref.shape[0]
    hidden_rows = aff_ref.shape[0]

    @pl.when(step == 0)
    def _():
        mean, inv = norm_columns(stat_ref[...], latent - 8, cells)
        scaled = norm_ref[:, 2:3] * inv
        weights = plain_ref[...] * scaled
        high, mid, _ = three(weights)
        lane = lax.broadcasted_iota(jnp.int32, (hidden_rows, 16), 1)
        shift = jnp.broadcast_to(norm_ref[:, 3:4] - scaled * mean, (hidden_rows, 16))
        one, two, rest = (part.astype(F32) for part in three(shift))
        tail = jnp.where(lane == 0, one, jnp.where(lane == 1, two, jnp.where(lane == 2, rest, 0.0))).astype(BF)
        zero = jnp.zeros_like(tail)
        left_ref[:hidden_rows, :] = jnp.concatenate((high, high[:, kinds:], tail), axis=1)
        left_ref[hidden_rows:, :] = jnp.concatenate((mid, zero, zero), axis=1)

    z = pick(step, me_ref, fast, near_ref, far_ref)
    z = jnp.where(lax.broadcasted_iota(jnp.int32, z.shape, 0) < latent, z, 0.0)
    z_ref[:, cells_at] = z
    z_high, z_mid, _ = three(z)
    ones = jnp.where(lax.broadcasted_iota(jnp.int32, z.shape, 0) < 3, 1.0, 0.0).astype(BF)
    table = jnp.concatenate((side_ref[0:kinds, cells_at], z_high, z_mid, ones), axis=0)
    both = nn(left_ref[...], table)
    affine = (both[:hidden_rows] + both[hidden_rows:]).astype(BF)
    aff_ref[:, cells_at] = affine
    hidden = relu_low(affine)
    width = score_ref.shape[1]
    score_ref[...] = nn(w_ref[0:genes, :], jnp.concatenate((hidden, ones), axis=0))
    tiles = width // 128
    rows = 32

    def top(g, best):
        at = pl.ds(pl.multiple_of(g * rows, rows), rows)
        new = []
        for tile in range(tiles):
            value = score_ref[at, slice(tile * 128, (tile + 1) * 128)]
            part = best[tile]
            for index in range(rows // 8):
                part = jnp.maximum(part, value[index * 8 : (index + 1) * 8])
            new.append(part)
        return tuple(new)

    best = lax.fori_loop(0, genes // rows, top, tuple(jnp.full((8, 128), -3e38, F32) for _ in range(tiles)), unroll=5)
    high = [jnp.max(part, axis=0, keepdims=True) for part in best]
    wide = [jnp.broadcast_to(part, (8, 128)) for part in high]

    far_lanes = [pl.ds(pl.multiple_of(step * width + tile * 128, 128), 128) for tile in range(tiles)]

    def mass(g, sums):
        at = pl.ds(pl.multiple_of(g * rows, rows), rows)
        new = []
        for tile in range(tiles):
            value = score_ref[at, slice(tile * 128, (tile + 1) * 128)]
            part = sums[tile]
            pieces = []
            for index in range(rows // 8):
                pieces.append(jnp.exp(value[index * 8 : (index + 1) * 8] - wide[tile]))
                part = part + pieces[-1]
            whole_piece = jnp.concatenate(pieces, axis=0)
            mass_ref[at, far_lanes[tile]] = whole_piece
            low_ref[at, far_lanes[tile]] = whole_piece.astype(BF)
            new.append(part)
        return tuple(new)

    sums = lax.fori_loop(0, genes // rows, mass, tuple(jnp.zeros((8, 128), F32) for _ in range(tiles)), unroll=5)
    top_ref[pl.ds(step, 1), :] = jnp.concatenate(high, axis=1)
    lse = [high[tile] + jnp.log(jnp.sum(sums[tile], axis=0, keepdims=True)) for tile in range(tiles)]
    lse_ref[pl.ds(step, 1), :] = jnp.concatenate(lse, axis=1)


def enc_sums_kernel(fast, me_ref, logc_ref, near_ref, far_ref, side_ref, line_ref, out_ref, sum_ref):
    step = pl.program_id(0)
    genes = logc_ref.shape[0]
    hidden = out_ref.shape[1]
    kinds = side_ref.shape[0] - 16

    @pl.when(step == 0)
    def _():
        out_ref[...] = jnp.zeros_like(out_ref)
        sum_ref[...] = jnp.zeros_like(sum_ref)

    cells_at = part_of(step, near_ref.shape[2])
    affine = pick(step, me_ref, fast, near_ref, far_ref)[:hidden]
    part = nt(logc_ref[:, cells_at], jnp.concatenate((affine, side_ref[kinds:, cells_at]), axis=0))
    out_ref[0:genes, :] += part[:, :hidden]
    sum_ref[...] += part[:, hidden:]
    out_ref[genes : genes + kinds, :] += nt(side_ref[0:kinds, cells_at], affine)

    @pl.when(step == pl.num_programs(0) - 1)
    def _():
        pick_first = jnp.where(lax.broadcasted_iota(jnp.int32, (8, 16), 1) == 0, 1.0, 0.0)
        base = genes + kinds
        count = pl.cdiv(genes, 128)
        out_ref[base : base + 8 * count, :] = lines(nt(pick_first, sum_ref[...], HI), count)
        out_ref[base + 8 * count :, :] = line_ref[...]


def zinb_kernel(rows, span, hid_ref, e_ref, top_ref, w_ref, x_ref, par_ref, lib_ref, lse_ref, gam_ref, g_ref, mass_ref, recon_ref, acc_ref, sc_ref):
    step = pl.program_id(0)
    genes, width = x_ref.shape

    @pl.when(step == 0)
    def _():
        acc_ref[...] = jnp.zeros_like(acc_ref)

    one_row = pl.ds(step, 1)
    gam_row = gam_ref[one_row, :]
    level = jnp.exp(top_ref[one_row, :] + (lib_ref[one_row, :] - lse_ref[one_row, :]))
    row = lax.broadcasted_iota(jnp.int32, (16, width), 0)
    ones = jnp.where(row < 3, 1.0, 0.0).astype(BF)
    sc_ref[...] = nn(w_ref[genes:, :], jnp.concatenate((relu_low(hid_ref[:, part_of(step, width)]), ones), axis=0))
    tiles = span // 128
    mass_out, recon_out = [], []
    for first in range(0, width, span):
        lanes = [slice(first + tile * 128, first + (tile + 1) * 128) for tile in range(tiles)]
        far_lanes = [pl.ds(pl.multiple_of(step * width + first + tile * 128, 128), 128) for tile in range(tiles)]
        scale = [jnp.broadcast_to(level[:, lanes[tile]], (rows, 128)) for tile in range(tiles)]

        def chunk(g, state):
            at = pl.ds(pl.multiple_of(g * rows, rows), rows)
            at_drop = pl.ds(pl.multiple_of(genes + g * rows, rows), rows)
            the, th, log_the, part_th = (par_ref[i, at, :] for i in range(4))
            sum_t = acc_ref[at, :]
            new = []
            for tile in range(tiles):
                rec, prod, back = state[tile]
                x = x_ref[at, lanes[tile]].astype(F32)
                mu = e_ref[at, far_lanes[tile]] * scale[tile]
                drop = sc_ref[at, lanes[tile]]
                both = mu + the
                r = 1.0 / both
                log_both = jnp.log(both)
                gap = log_the - log_both
                th_gap = th * gap
                u = jnp.where(x < 0.5, th_gap - drop, 1e30)
                eu = jnp.exp2(jnp.abs(u) * (-LOG2_E))
                ed = jnp.exp2(jnp.abs(drop) * (-LOG2_E))
                den = 1.0 + eu
                mu_eps = mu + zinb_epsilon
                rd = 1.0 / (1.0 + ed)
                w0 = jnp.where(u >= 0.0, 1.0, eu) * (1.0 / den)
                term = (th_gap - jnp.maximum(drop, 0.0)) + (x * (jnp.log(mu_eps) - log_both) - jnp.minimum(u, 0.0))
                factor = den * rd
                y = (x + w0 * th) * r
                g_mean = mu * (x * (1.0 / mu_eps) - y)
                g_drop = jnp.where(drop >= 0.0, ed, 1.0) * rd - w0
                g_disp = w0 * (gap + part_th) - y
                g_ref[at, far_lanes[tile]] = g_mean.astype(BF)
                g_ref[at_drop, far_lanes[tile]] = g_drop.astype(BF)
                sum_t = sum_t + g_disp
                for part in range(rows // 8):
                    sub = slice(part * 8, (part + 1) * 8)
                    rec = rec + term[sub]
                    prod = prod * factor[sub]
                    back = back + g_mean[sub]
                new.append((rec, prod, back))
            acc_ref[at, :] = sum_t
            return tuple(new)
        zero = jnp.zeros((8, 128), F32)
        state = tuple((zero, zero + 1.0, zero) for _ in range(tiles))
        state = lax.fori_loop(0, genes // rows, chunk, state)
        for tile in range(tiles):
            rec, prod, back = state[tile]
            mass_out.append(jnp.sum(back, axis=0, keepdims=True))
            recon_out.append(jnp.sum(rec + jnp.log(prod), axis=0, keepdims=True))
    mass_ref[one_row, :] = jnp.concatenate(mass_out, axis=1)
    recon_ref[one_row, :] = jnp.concatenate(recon_out, axis=1) + gam_row


def softmax_kernel(width, mass_ref, w_ref, side_ref, z_ref, aff_ref, r_ref, product_ref):
    genes = mass_ref.shape[0]
    step = pl.program_id(0)
    cells_at = part_of(step, width)

    @pl.when(step == 0)
    def _():
        product_ref[...] = jnp.zeros_like(product_ref)

    r_ref[:, cells_at] = nn(w_ref[:, :genes], mass_ref[:, cells_at])
    left = jnp.concatenate((side_ref[:, cells_at], z_ref[:, cells_at].astype(BF)), axis=0)
    product_ref[...] += nt(left, aff_ref[:, cells_at])


def back_kernel(width, g_in_ref, w_ref, a_ref):
    cells_at = part_of(pl.program_id(0), width)
    a_ref[:, cells_at] = nn(w_ref[...], g_in_ref[:, cells_at])


def hidden_grad_kernel(cells, latent, me_ref, a_ref, r_ref, mass_ref, aff_ref, top_ref, lse_ref, stat_ref, gain_ref, lat_ref, recon_ref, z_ref, side_ref, keep_ref, send_ref, lane_ref, oh_ref):
    step = pl.program_id(0)
    steps = pl.num_programs(0)
    place = step ^ me_ref[0]
    hidden, width = a_ref.shape[0], mass_ref.shape[1]
    cells_at = part_of(step, width)
    kinds = side_ref.shape[0] - 16

    @pl.when(step == 0)
    def _():
        lane_ref[...] = jnp.zeros_like(lane_ref)
        oh_ref[...] = jnp.zeros_like(oh_ref)

    line = pl.ds(step, 1)
    back = mass_ref[line, :] * jnp.exp(top_ref[line, :] - lse_ref[line, :])
    wide = aff_ref[:, cells_at].astype(F32)
    dy = jnp.where(wide > 0, a_ref[:, cells_at] - back * r_ref[:, cells_at], 0.0)
    weighted = dy * wide
    lane_ref[...] += sum(weighted[:, t : t + 128] for t in range(0, width, 128))
    dy_low = dy.astype(BF)
    oh_ref[...] += nt(jnp.concatenate((side_ref[:, cells_at], z_ref[:, cells_at].astype(BF)), axis=0), dy_low)
    _, inv = norm_rows(stat_ref[...], latent - 8, cells)
    lat_high, lat_mid, _ = three(lat_ref[...] * (gain_ref[2:3] * inv) * (-1.0 / cells))
    both = nn(jnp.concatenate((lat_high, lat_mid), axis=0), dy_low)
    block = both[:16] + both[16:]
    row = lax.broadcasted_iota(jnp.int32, block.shape, 0)
    block = jnp.where(row == latent, recon_ref[pl.ds(step, 1), :], block)
    slot = lax.div(place, 2)

    @pl.when(lax.rem(place, 2) == 0)
    def _():
        keep_ref[slot] = block

    @pl.when(lax.rem(place, 2) == 1)
    def _():
        send_ref[slot] = block

    @pl.when(step == steps - 1)
    def _():
        scale = -1.0 / cells
        one, two = oh_ref[kinds : kinds + 1, :] * scale, row_sums(lane_ref[...])[0:1] * scale
        oh_ref[kinds : kinds + 16, :] = oh_ref[kinds + 16 :, :]
        part = (kinds + 16) // steps
        for core, ref in enumerate((keep_ref, send_ref)):
            for index in range(ref.shape[0]):
                ref[index, latent + 1 : latent + 2, 0:hidden] = one
                ref[index, latent + 2 : latent + 3, 0:hidden] = two
                owner = me_ref[0] ^ (2 * index + core)
                for k in range(part):
                    line = latent + 3 + k // 8
                    lanes = slice((k % 8) * hidden, (k % 8 + 1) * hidden)
                    ref[index, line : line + 1, lanes] = oh_ref[pl.ds(owner * part + k, 1), :] * scale


def dec_grad_kernel(cells, rt_ref, hid_ref, mass_ref, top_ref, lse_ref, g_in_ref, acc_ref, dig_ref, par_ref, dec_ref, mix_ref, g_ref):
    step = pl.program_id(0)
    steps = pl.num_programs(0)
    genes = rt_ref.shape[0]
    cells_at = part_of(step, mass_ref.shape[1])
    hidden = hid_ref.shape[0]

    @pl.when(step == 0)
    def _():
        mix_ref[...] = jnp.zeros_like(mix_ref)
        g_ref[...] = jnp.zeros_like(g_ref)

    line = pl.ds(step, 1)
    back = mass_ref[line, :] * jnp.exp(top_ref[line, :] - lse_ref[line, :])
    back_high, back_mid, back_low = three(back)
    row = lax.broadcasted_iota(jnp.int32, (16, back.shape[1]), 0)
    extra = jnp.where(row == 0, back_high.astype(F32), jnp.where(row == 1, back_mid.astype(F32), 0.0))
    hidden_low = relu_low(hid_ref[:, cells_at])
    ones = jnp.where(row == 0, 1.0, 0.0).astype(BF)
    g_ref[...] += nt(g_in_ref[:, cells_at], jnp.concatenate((hidden_low, ones), axis=0))
    scaled = (hidden_low.astype(F32) * back).astype(BF)
    mix_ref[...] += nt(rt_ref[:, cells_at], jnp.concatenate((scaled, extra.astype(BF)), axis=0))

    @pl.when(step == steps - 1)
    def _():
        scale = -1.0 / cells
        mix = mix_ref[...]
        dec_ref[:genes, :] = (g_ref[:genes, :hidden] - mix[:, :hidden]) * scale
        dec_ref[genes : 2 * genes, :] = g_ref[genes:, :hidden] * scale
        pick = jnp.where(lax.broadcasted_iota(jnp.int32, (8, 16), 1) < 2, 1.0, 0.0)
        score_row = nt(pick, g_ref[:genes, hidden:] - mix[:, hidden:], HI)
        drop_row = nt(pick, g_ref[genes:, hidden:], HI)
        disp_row = row_sums((acc_ref[...] + dig_ref[...]) * par_ref[1])
        row = lax.broadcasted_iota(jnp.int32, score_row.shape, 0)
        gene_rows = scale * jnp.where(
            row == 0, score_row, jnp.where(row == 1, drop_row, jnp.where(row == 2, disp_row, 0.0))
        )
        dec_ref[2 * genes :, :] = lines(gene_rows, pl.cdiv(genes, 128))


def enc_back_kernel(cells, latent, fast, span, me_ref, own_ref, dnear_ref, dfar_ref, aff_dec_ref, sums_ref, stat_ref, gain_ref, lat_ref, noise_ref, klw_ref, anear_ref, afar_ref, side_ref, held_ref, product_ref, logc_ref, cols_ref, z_ref, out_ref, rest_ref, lane_ref, left_ref, fixed_ref, one_ref, kept_ref, sum_ref):
    step = pl.program_id(0)
    steps = kept_ref.shape[0]
    genes, width = logc_ref.shape[0], dnear_ref.shape[2]
    hidden = aff_dec_ref.shape[0]
    cells_at = part_of(step, width)
    place = (step ^ me_ref[0]) if fast else step
    kinds = (rest_ref.shape[0] - 64) // 2
    at = latent + 1 - 8
    m_one, m_two = norm_sums(sums_ref[at : at + 2], gain_ref, 2)
    m_two = m_two / gain_ref[2:3] * (1.0 / cells)
    m_one = m_one * (1.0 / cells) - m_two * gain_ref[3:4]

    @pl.when(step == 0)
    def _():
        out_ref[...] = jnp.zeros_like(out_ref)
        rest_ref[...] = jnp.zeros_like(rest_ref)
        lane_ref[...] = jnp.zeros_like(lane_ref)
        sum_ref[...] = jnp.zeros_like(sum_ref)
        _, inv = norm_rows(stat_ref[...], latent - 8, cells)
        lat = lat_ref[...] * (gain_ref[2:3] * inv)
        fixed_ref[...] = jnp.broadcast_to(jnp.sum(lat * m_one, axis=1, keepdims=True), fixed_ref.shape)
        high, mid, _ = three(lat * m_two)
        left_ref[...] = jnp.concatenate((high, mid), axis=0)

    index = lax.div(place, 2) if fast else place
    near = (lax.rem(place, 2) == 0) if fast else None

    def take(near_ref, far_ref, rows, lanes):
        if not fast:
            return near_ref[index, rows, lanes]
        return jnp.where(near, near_ref[index, rows, lanes], far_ref[index, rows, lanes])

    every = slice(0, width)
    scale = klw_ref[0:1, 0:1] * (1.0 / cells)
    affine_dec = aff_dec_ref[:, cells_at]
    both = nn(left_ref[...], affine_dec)
    block = take(dnear_ref, dfar_ref, slice(0, 16), every)
    kept_ref[step] = block[8:]
    grad_z = (block - fixed_ref[:, 0:1] - (both[:16] + both[16:]))[:latent]
    noise = noise_ref[:, cells_at]
    pieces = take(anear_ref, afar_ref, slice(hidden, hidden + 32), every).astype(F32)
    lat_logvar = pieces[:latent] + pieces[16 : 16 + latent]
    spread = jnp.exp(lat_logvar)
    var = spread + 0.0001
    inv_std = lax.rsqrt(var)
    z = z_ref[:, cells_at]
    lat_mean = z[0:latent] - var * inv_std * noise
    g_mean = latent_rows(grad_z + scale * lat_mean)
    g_var = latent_rows(spread * (grad_z * noise * (0.5 * inv_std) + (0.5 * scale) * (1.0 - inv_std * inv_std)))
    g_head = jnp.concatenate((g_mean, g_var), axis=0)
    sum_ref[0:32, :] += sum(g_head[:, t : t + 128] for t in range(0, width, 128))
    sum_ref[32:, :] += sum(z[:, t : t + 128] for t in range(0, width, 128))
    head_high, head_mid, _ = three(g_head)
    heads = jnp.concatenate((head_high, head_mid, head_high), axis=0)
    for begin in range(0, width, span):
        lanes = slice(begin, begin + span)
        affine = take(anear_ref, afar_ref, slice(0, hidden), lanes)
        one_ref[hidden:, lanes] = relu_low(affine)
        wide = affine.astype(F32)
        dy = jnp.where(wide > 0, nn(cols_ref[...], heads[:, lanes]), 0.0)
        one_ref[0:hidden, lanes] = dy.astype(BF)
        weighted = dy * wide
        lane_ref[...] += sum(weighted[:, t : t + 128] for t in range(0, span, 128))
    dy_low = one_ref[0:hidden, :]
    side = side_ref[:, cells_at]
    out_ref[0:genes, :] += nt(logc_ref[:, cells_at], dy_low)
    mixed = nt(side, dy_low)
    rest_ref[0:kinds, :] += mixed[:kinds]
    out_ref[genes : genes + 1, :] += mixed[kinds : kinds + 1]
    rest_ref[kinds : kinds + 32, :] += nt(head_high, one_ref[hidden:, :])
    base = kinds + 40

    @pl.when(step == steps - 1)
    def _():
        out_ref[genes + 1 : genes + 2, :] = row_sums(lane_ref[...])[0:1]
        rest_ref[kinds + 32 : kinds + 40, 0:32] = row_sums(sum_ref[0:32, :])
        held = jnp.concatenate((held_ref[...], sum_ref[32:, :]), axis=0)
        rest_ref[base : base + kinds + 16, :] -= jnp.sum(held, axis=1, keepdims=True) * m_one
        rest_ref[base : base + kinds, :] -= product_ref[:kinds, :] * m_two
        rest_ref[base + kinds : base + kinds + 16, :] -= product_ref[kinds + 16 :, :] * m_two
        count = (kinds + 16) // steps
        for owner in range(steps):
            for k in range(count):
                line = latent + 3 + k // 8 - 8
                at = slice(base + owner * count + k, base + owner * count + k + 1)
                rest_ref[at, :] += kept_ref[owner, line : line + 1, (k % 8) * hidden : (k % 8 + 1) * hidden]
        size = rest_ref.shape[0] // 8
        out_ref[genes + 8 :, :] = rest_ref[pl.ds(pl.multiple_of((own_ref[0] & 7) * size, 8), size), :]


def whole_gradient(part, product, plain, gain, shift, inv, one, two):
    return (gain * inv) * (part - plain * one - ((product - plain * shift) / gain) * two)


def norm_sums(rows, norm_ref, at):
    return rows[0:1], (rows[1:2] - norm_ref[at + 1 : at + 2] * rows[0:1]) / norm_ref[at : at + 1]


def finish_kernel(cells, latent, sum_ref, dec_ref, fixed_ref, stat_enc_ref, norm_ref, kl_ref, klw_ref, own_ref, enc_out, tail_out, loss_out):
    genes = enc_out.shape[0]
    size = tail_out.shape[0] - 8
    count = pl.cdiv(genes, 128)
    kinds = fixed_ref.shape[0] - genes - 8 * count - 8
    loss_out[...] = klw_ref[0:1, 0:1] * kl_ref[...] - own_ref[latent : latent + 1, :]
    _, inv = norm_rows(stat_enc_ref[...], 0, cells)
    n_one, n_two = norm_sums(sum_ref[genes : genes + 8, :], norm_ref, 0)
    at = genes + kinds
    logs = jnp.concatenate([fixed_ref[at + 8 * i : at + 8 * (i + 1), :] for i in range(count)], axis=1)
    log_sum = jnp.transpose(logs)[:genes, 0:1]
    enc = whole_gradient(
        sum_ref[0:genes, :], fixed_ref[0:genes, :], log_sum, norm_ref[0:1], norm_ref[1:2], inv, n_one * (1.0 / cells), n_two * (1.0 / cells)
    )
    enc_out[...] = enc
    dec = dec_ref[...]
    lane = jnp.sum(enc * enc, axis=0, keepdims=True) + jnp.sum(dec * dec, axis=0, keepdims=True)
    tail_out[0:size, :] = sum_ref[genes + 8 :, :]
    tail_out[size:, :] = jnp.broadcast_to(jnp.sum(lane, axis=1, keepdims=True), (8, tail_out.shape[1]))


def step_of(weight, gradient, first, second, rate):
    first = beta_one * first + (1.0 - beta_one) * gradient
    second = beta_two * second + (1.0 - beta_two) * gradient * gradient
    fixed_one = first * (1.0 / (1.0 - beta_one**step_number))
    fixed_two = second * (1.0 / (1.0 - beta_two**step_number))
    update = fixed_one / (jnp.sqrt(fixed_two) + 1e-08) + decay_rate * weight
    return weight - rate * update, first, second


def update_kernel(cells, latent, me_ref, near_ref, far_ref, enc_g_ref, dec_g_ref, sum_ref, fixed_ref, stat_enc_ref, stat_dec_ref, sums_ref, *refs):
    ins, outs, (rest_ref, small_g_ref, head_g_ref, norm_g_ref) = refs[:18], refs[18:-4], refs[-4:]
    enc, dec, gene, small, head, norm = (ins[3 * i : 3 * i + 3] for i in range(6))
    genes, hidden = enc[0].shape
    rows = small[0].shape[0]
    kinds = (rows - latent) // 2
    count = pl.cdiv(genes, 128)
    size = near_ref.shape[1]
    for core, ref in enumerate((near_ref, far_ref)):
        for index in range(ref.shape[0]):
            owner = me_ref[0] ^ (2 * index + core)
            rest_ref[pl.ds(pl.multiple_of(owner * size, 8), size), :] = ref[index]
    whole_rest = [rest_ref[i * size : i * size + size - 8, :] for i in range(8)]
    square = jnp.zeros((1, 1), F32)
    for i in range(8):
        square = square + rest_ref[(i + 1) * size - 8 : (i + 1) * size - 7, 0:1]
    rest = jnp.concatenate(whole_rest, axis=0)
    gains = norm[0]
    gain, shift = gains[0:1], gains[1:2]
    n_one, n_two = norm_sums(sum_ref[genes : genes + 8, :], gains, 0)
    _, inv = norm_rows(stat_enc_ref[...], 0, cells)
    _, inv_dec = norm_rows(stat_dec_ref[...], latent - 8, cells)
    at = genes + kinds + 8 * count
    batch_sum = jnp.transpose(fixed_ref[at : at + 8, :])[:kinds, 0:1]
    small_g_ref[0:kinds, :] = whole_gradient(
        rest[0:kinds], fixed_ref[genes : genes + kinds, :], batch_sum, gain, shift, inv, n_one * (1.0 / cells), n_two * (1.0 / cells)
    )
    small_g_ref[kinds:, :] = (gains[2:3] * inv_dec) * rest[kinds + 40 : 2 * kinds + 56]
    bias = jnp.transpose(rest[kinds + 32 : kinds + 40])
    for half in range(2):
        into = slice(half * latent, (half + 1) * latent)
        head_g_ref[into, 0:hidden] = rest[kinds + 16 * half : kinds + 16 * half + latent]
        head_g_ref[into, hidden : hidden + 1] = bias[16 * half : 16 * half + latent, 0:1]
    at = latent + 1 - 8
    norm_g_ref[0:1] = n_two
    norm_g_ref[1:2] = n_one
    m_one, m_two = norm_sums(sums_ref[at : at + 2], gains, 2)
    norm_g_ref[2:3] = m_two
    norm_g_ref[3:4] = m_one
    small_square = jnp.zeros((1, 1), F32)
    for part in (small_g_ref[0:rows, :], head_g_ref[...], norm_g_ref[...]):
        small_square = small_square + jnp.sum(jnp.sum(part * part, axis=0, keepdims=True), axis=1, keepdims=True)
    value = jnp.sqrt(square + small_square)
    factor = jnp.minimum(1.0, max_norm / value)
    (enc_n, enc_m, enc_v, enc_l, dec_n, dec_m, dec_v, dec_l, gene_n, gene_m, gene_v, small_n, small_m, small_v, head_n, head_m, head_v, norm_n, norm_m, norm_v, norm_out) = outs
    norm_out[...] = value
    new, first, second = step_of(enc[0][...], enc_g_ref[...] * factor, enc[1][...], enc[2][...], rate_genes)
    enc_n[...], enc_m[...], enc_v[...], enc_l[...] = new, first, second, new.astype(BF)
    for index in range(2):
        gradient = dec_g_ref[index * genes : (index + 1) * genes, :] * factor
        new, first, second = step_of(dec[0][index], gradient, dec[1][index], dec[2][index], rate_genes)
        dec_n[index], dec_m[index], dec_v[index], dec_l[index] = new, first, second, new.astype(BF)
    for index in range(pl.cdiv(genes, 128)):
        span = slice(index * 128, min(genes, (index + 1) * 128))
        gradient = dec_g_ref[2 * genes + index * 8 : 2 * genes + index * 8 + 3, 0 : span.stop - span.start] * factor
        new, first, second = step_of(gene[0][:, span], gradient, gene[1][:, span], gene[2][:, span], rate_small)
        gene_n[:, span], gene_m[:, span], gene_v[:, span] = new, first, second
    new, first, second = step_of(small[0][...], small_g_ref[0:rows, :] * factor, small[1][...], small[2][...], rate_small)
    small_n[...], small_m[...], small_v[...] = new, first, second
    new, first, second = step_of(head[0][...], head_g_ref[...] * factor, head[1][...], head[2][...], rate_small)
    head_n[...], head_m[...], head_v[...] = new, first, second
    new, first, second = step_of(norm[0][...], norm_g_ref[...] * factor, norm[1][...], norm[2][...], rate_small)
    norm_n[...], norm_m[...], norm_v[...] = new, first, second


def gather_genes(value, fast, blocks, width, late=None):
    if fast:
        near = jnp.stack([value] + [swap(value, "genes", 2 * k) for k in (1, 2, 3)])
        near = near if late is None else after(near, late)
        return near, swap(near, "genes", 1)
    rows = value.shape[0]
    whole_rows = lax.all_gather(value, "genes", axis=0).transpose(1, 0, 2)
    near = whole_rows.reshape(rows, blocks, width).transpose(1, 0, 2)
    return near, near


def per_device(counts, library, noise, batch_ids, gene_mask, kl_weight, enc_w, enc_m, enc_v, dec_w, dec_m, dec_v, gene_par, gene_m, gene_v, small_w, small_m, small_v, head_w, head_m, head_v, norm_par, norm_m, norm_v):
    rows_all, genes = counts.shape
    cells = float(rows_all * lax.axis_size("cells"))
    groups = lax.axis_size("genes")
    hidden = enc_w.shape[1]
    latent = head_w.shape[1] // 2
    kinds = (small_w.shape[0] - latent) // 2
    share = rows_all // groups
    width = min(1024, rows_all)
    blocks = rows_all // width
    fast = groups == 8 and blocks == 8
    me = lax.axis_index("genes").astype(jnp.int32).reshape(1)
    gene_lines = -(-genes // 128)

    def turn(value):
        return value.transpose(0, 2, 1)

    x_t = counts.T
    noise_t = noise.T
    dec_t = turn(dec_w)
    head_t = head_w.T
    lib8 = library.reshape(blocks, width)
    batch_all = batch_ids.reshape(blocks, 1, width)
    batch_own = batch_ids.reshape(groups, 1, share)
    klw = jnp.broadcast_to(kl_weight.reshape(1, 1), (8, 128))

    own_block = pl.BlockSpec((1, 1, share), lambda i, m: (m[0], 0, 0))
    own_lanes = lambda rows: pl.BlockSpec((rows, share), lambda i, m: (0, m[0]))
    lane_block = lambda rows: pl.BlockSpec((rows, width), lambda i, *_: (0, i))
    here = pl.BlockSpec(memory_space=pltpu.VMEM)
    full = lambda array: (array, here)
    out_of = lambda shape, dtype=F32: (shape, dtype, whole(shape))
    new = lambda shape, dtype=F32: (shape, dtype, here)

    def encode(low, count, weight, near=False):
        return call(
            lambda *refs: enc_kernel(low, count, share, near, *refs),
            (1,),
            [
                (me if fast else me & 1, None),
                (x_t, here) if near else (in_hbm(x_t), pl.BlockSpec(memory_space=pl.ANY)),
                (in_hbm(weight), pl.BlockSpec(memory_space=pl.ANY)),
            ],
            [new((count // 2, hidden, share)), new((count // 2, hidden, share), BF)],
            scratch=[
                pltpu.VMEM((genes, hidden), F32),
                pltpu.VMEM((hidden, genes), BF),
                pltpu.SemaphoreType.DMA((count + 1,)),
            ]
            + ([] if near else [pltpu.VMEM((count, genes, share), BF)]),
            scalars=1,
            us=2.0 if near else 3.0,
            mib=6 if near else 8,
        )

    slot = pl.BlockSpec((1, hidden, share), lambda i, m: (0, 0, 0))
    if fast:
        keep_far, send_far = encode(4, 4, enc_w)
        got_far = swap(send_far, "genes", 1)
        keep_near, send_near = encode(0, 4, after(enc_w, send_far), True)
        far = [
            swap((keep_far[k : k + 1] + got_far[k : k + 1].astype(F32)).astype(BF), "genes", 4 + 2 * k)
            for k in range(2)
        ]
        got = swap(send_near, "genes", 1)
        ready = (keep_near[1:2] + got[1:2].astype(F32)).astype(BF)
        far.append(swap(ready, "genes", 2))
        kept = keep_near
    else:
        keep_part, send_part = encode(0, groups, enc_w)
        got = swap(send_part, "genes", 1)
        summed = lax.psum_scatter(
            keep_part + got.astype(F32),
            "genes",
            scatter_dimension=0,
            axis_index_groups=[list(range(c, groups, 2)) for c in range(2)],
            tiled=True,
        )
        zero = jnp.zeros((1, hidden, share), BF)
        kept, got, far = summed, zero, [zero] * 3
        ready = keep_part

    mask_late = after(gene_mask.reshape(1, genes), ready)
    aug, dec_n, par, lg_tab, dg_tab, enc_pieces, dec_pieces, dec_plain, lat_row, head_rows, head_bias, head_cols, norm_t = call(
        prep_kernel,
        (1,),
        [full(gene_par), full(mask_late), full(dec_t), full(small_w), full(head_t), full(norm_par)],
        [
            new((2 * genes, hidden + 16), BF),
            new((hidden, 2 * genes), BF),
            new((5, genes, 128)),
            new((COUNT_TOP, genes, 128)),
            new((COUNT_TOP, genes, 128)),
            new((3 * hidden, kinds), BF),
            new((3 * hidden, kinds + 48), BF),
            new((hidden, kinds + 16)),
            new((16, hidden)),
            new((32, hidden)),
            new((32, 128)),
            new((hidden, 96), BF),
            new((hidden, 8)),
        ],
    )
    batch_spec = pl.BlockSpec((1, 1, width), lambda i, *_: (i, 0, 0))
    logc, x_kept, side, lib8, gam_cell, dig_acc, log_lines, held = call(
        lambda *refs: counts_kernel(16, min(512, width), *refs),
        (blocks,),
        [
            (in_hbm(x_t), lane_block(genes)),
            full(lg_tab),
            full(dg_tab),
            full(par),
            (batch_all, batch_spec),
            full(lib8),
        ],
        [
            ((genes, rows_all), BF, lane_block(genes), True),
            ((genes, rows_all), BF, lane_block(genes), True),
            ((kinds + 16, rows_all), BF, here),
            new((blocks, width)),
            new((blocks, width)),
            new((genes, 128)),
            new((8, 128)),
            new((kinds, 128)),
        ],
        mib=8,
        us=15.0,
    )
    enc_late = after(enc_pieces, log_lines)
    stat8 = whole((8, hidden))
    pre_enc, stat_enc = call(
        own_kernel,
        (1,),
        [(me, None), (kept, slot), (got, slot)]
        + [(part, slot) for part in far]
        + [(batch_own, own_block), full(enc_late)],
        [new((hidden, share)), new((8, hidden))],
        scalars=1,
    )
    stat_enc = total(total(stat_enc, "genes"), "cells")

    pack, aff_own, kl_row = call(
        lambda *refs: latent_kernel(cells, latent, *refs),
        (1,),
        [
            (me, None),
            full(pre_enc),
            full(stat_enc),
            full(norm_t),
            full(head_rows),
            full(head_bias),
            (noise_t, own_lanes(latent)),
            (batch_own, own_block),
            full(dec_pieces),
        ],
        [new((16, share)), new((hidden + 32, share), BF), new((1, share))],
        scalars=1,
    )
    near, far_pack = gather_genes(pack, fast, blocks, width)
    if fast:
        stat_dec = jnp.sum(near[:, 8:16, :hidden], axis=0) + jnp.sum(far_pack[:, 8:16, :hidden], axis=0)
    else:
        stat_dec = lax.psum(pack[8:16, :hidden], "genes")
    stat_dec = total(stat_dec, "cells")

    aff_dec, lse, z_all, top, mass_all, mass_low_all = call(
        lambda *refs: decode_kernel(cells, latent, fast, *refs),
        (blocks,),
        [
            (me, None),
            (near, here),
            (far_pack, here),
            (side, here),
            full(stat_dec),
            full(norm_t),
            full(dec_plain),
            full(aug),
        ],
        [
            ((hidden, rows_all), BF, here),
            new((blocks, width)),
            ((16, rows_all), F32, here),
            new((blocks, width)),
            ((genes, rows_all), F32, here),
            ((genes, rows_all), BF, here),
        ],
        scratch=[pltpu.VMEM((genes, width), F32), pltpu.VMEM((2 * hidden, kinds + 48), BF)],
        scalars=1,
        us=8.0,
    )
    part_r, product = call(
        lambda *refs: softmax_kernel(width, *refs),
        (blocks,),
        [(mass_low_all, here), full(dec_n), (side, here), (z_all, here), (aff_dec, here)],
        [((hidden, rows_all), F32, here), new((kinds + 32, hidden))],
        us=3.0,
    )
    lse_all = after(log_total_of(lse, "genes"), part_r)

    full8 = whole((blocks, width))
    g_both, mass, recon, gene_acc = call(
        lambda *refs: zinb_kernel(64, min(1024, width), *refs),
        (blocks,),
        [
            (aff_dec, here),
            (mass_all, here),
            full(top),
            full(aug),
            (in_hbm(x_kept), lane_block(genes)),
            full(par),
            full(lib8),
            full(lse_all),
            full(gam_cell),
        ],
        [((2 * genes, rows_all), BF, here)]
        + [new((blocks, width)), new((blocks, width)), new((genes, 128))],
        scratch=[pltpu.VMEM((genes, width), F32)],
        mib=16,
        us=28.0,
    )
    mass_low = mass + swap(mass, "genes", 1)
    mass = total(mass_low, "genes", 1)
    (part_a,) = call(
        lambda *refs: back_kernel(width, *refs),
        (blocks,),
        [(g_both, here), full(dec_n)],
        [((hidden, rows_all), F32, here)],
        us=4.0,
    )

    aff_near, aff_far = gather_genes(after(aff_own, lse_all), fast, blocks, width, mass_low)
    fixed_rows = genes + kinds + 8 * gene_lines + 8
    (fixed,) = call(
        lambda *refs: enc_sums_kernel(fast, *refs),
        (blocks,),
        [
            (me, None),
            (logc, here),
            (aff_near, here),
            (aff_far, here),
            (side, here),
            full(log_lines),
        ],
        [new((fixed_rows, hidden))],
        scratch=[pltpu.VMEM((genes, 16), F32)],
        scalars=1,
        us=4.0,
    )
    fixed = total_by_halves(fixed, "cells", (1, 2))

    keep_d, send_d = call(
        lambda *refs: hidden_grad_kernel(cells, latent, *refs),
        (blocks,),
        [
            (me if fast else jnp.zeros_like(me), None),
            (part_a, here),
            (part_r, here),
            (mass, here),
            (aff_dec, here),
            full(top),
            full(lse_all),
            full(stat_dec),
            full(norm_par),
            full(lat_row),
            full(recon),
            (z_all, here),
            (side, here),
        ],
        [
            new((blocks // 2, 16, width)),
            new((blocks // 2, 16, width)),
        ],
        scratch=[pltpu.VMEM((hidden, 128), F32), pltpu.VMEM((kinds + 32, hidden), F32)],
        scalars=1,
        us=5.0,
    )
    (dec_part,) = call(
        lambda *refs: dec_grad_kernel(cells, *refs),
        (blocks,),
        [
            (mass_low_all, here),
            (aff_dec, here),
            (mass, here),
            full(top),
            full(lse_all),
            (g_both, here),
            full(gene_acc),
            full(dig_acc),
            full(par),
        ],
        [new((2 * genes + 8 * gene_lines, hidden))],
        scratch=[pltpu.VMEM((genes, hidden + 16), F32), pltpu.VMEM((2 * genes, hidden + 16), F32)],
        us=6.0,
    )
    if fast:
        got_d = swap(send_d, "genes", 1)
        pieces = [swap(keep_d[k] + got_d[k], "genes", 2 * k) for k in (1, 2, 3)]
        pieces = [after(piece, dec_part) for piece in pieces]
        own_d = (keep_d[0] + got_d[0] + pieces[0]) + (pieces[1] + pieces[2])
        sums_dec = own_d[8:, :hidden]
    else:
        both = jnp.stack([keep_d, send_d], axis=1).reshape(blocks, 16, width)
        sums_dec = lax.psum(both[0, 8:, :hidden], "genes")
        both = both.transpose(1, 0, 2).reshape(16, groups, share).transpose(1, 0, 2)
        own_d = lax.psum_scatter(both, "genes", scatter_dimension=0, tiled=True)[0]
    sums_dec = total(sums_dec, "cells")
    d_near, d_far = gather_genes(own_d, fast, blocks, width)
    dec_g = total_by_halves(dec_part, "cells", (2, 1))

    size = (2 * kinds + 64) // 8
    (enc_part,) = call(
        lambda *refs: enc_back_kernel(cells, latent, fast, min(256, width), *refs),
        (blocks,),
        [
            (me, None),
            (me, None),
            (d_near, here),
            (d_far, here),
            (aff_dec, here),
            full(sums_dec),
            full(stat_dec),
            full(norm_par),
            full(lat_row),
            (noise_t, here),
            full(klw),
            (aff_near, here),
            (aff_far, here),
            (side, here),
            full(held),
            full(product),
            (logc, here),
            full(head_cols),
            (z_all, here),
        ],
        [new((genes + 8 + size, hidden))],
        scratch=[
            pltpu.VMEM((2 * kinds + 64, hidden), F32),
            pltpu.VMEM((hidden, 128), F32),
            pltpu.VMEM((32, hidden), BF),
            pltpu.VMEM((16, 128), F32),
            pltpu.VMEM((2 * hidden, width), BF),
            pltpu.VMEM((blocks, 8, width), F32),
            pltpu.VMEM((48, 128), F32),
        ],
        scalars=2,
        us=11.0,
    )
    enc_sum = total_by_halves(enc_part, "cells", (1, 2))
    enc_g, tail, loss = call(
        lambda *refs: finish_kernel(cells, latent, *refs),
        (1,),
        [full(a) for a in (enc_sum, dec_g, fixed, stat_enc, norm_par, kl_row, klw, own_d)],
        [new((genes, hidden)), new((size + 8, hidden)), new((1, share))],
    )
    if fast:
        tail_near = jnp.stack([tail] + [swap(tail, "genes", 2 * k) for k in (1, 2, 3)])
        tail_far = swap(tail_near, "genes", 1)
    else:
        tails = lax.all_gather(tail, "genes", axis=0)
        square = jnp.sum(tails[:, size:], axis=0)
        tails = tails[:8].at[:, size:].set(0.0).at[0, size:].set(square)
        tail_near, tail_far = tails[0::2], tails[1::2]

    state = [
        enc_w, enc_m, enc_v, dec_t, turn(dec_m), turn(dec_v), gene_par, gene_m, gene_v,
        small_w, small_m, small_v, head_t, head_m.T, head_v.T, norm_par, norm_m, norm_v,
    ]
    ins = [tail_near, tail_far, enc_g, dec_g, enc_sum, fixed, stat_enc, stat_dec, sums_dec] + state
    outs = []
    for index in range(6):
        one = state[3 * index]
        outs += [(one.shape, F32)] * 3
        if index < 2:
            outs.append((one.shape, BF))
    outs.append(((1, 1), F32))
    res = call(
        lambda *refs: update_kernel(cells, latent, *refs),
        (1,),
        [(me if fast else jnp.zeros_like(me), None)] + [full(array) for array in ins],
        [out_of(shape, dtype) for shape, dtype in outs],
        scratch=[
            pltpu.VMEM((8 * (size + 8), hidden), F32),
            pltpu.VMEM((2 * kinds + 16, hidden), F32),
            pltpu.VMEM((2 * latent, hidden + 1), F32),
            pltpu.VMEM((4, hidden), F32),
        ],
        scalars=1,
        mib=16,
    )
    enc_res, dec_res = res[0:4], [turn(part) for part in res[4:8]]
    head_res = [part.T for part in res[14:17]]
    return (
        *enc_res,
        *dec_res,
        *res[8:14],
        *head_res,
        *res[17:20],
        res[20].reshape(()),
        loss.reshape(share),
    )


def solution(mesh):
    placed = (
        P("cells", "genes"), P("cells"), P("cells", None), P("cells"), P("genes"), P(),
        P("genes", None), P("genes", None), P("genes", None),
        P(None, None, "genes"), P(None, None, "genes"), P(None, None, "genes"),
        P(None, "genes"), P(None, "genes"), P(None, "genes"),
        P(), P(), P(), P(), P(), P(), P(), P(), P(),
    )
    return jax.shard_map(
        per_device,
        mesh=mesh,
        in_specs=placed,
        out_specs=(
            P("genes", None), P("genes", None), P("genes", None), P("genes", None),
            P(None, None, "genes"), P(None, None, "genes"), P(None, None, "genes"), P(None, None, "genes"),
            P(None, "genes"), P(None, "genes"), P(None, "genes"),
            P(), P(), P(), P(), P(), P(), P(), P(), P(), P(),
            P(("cells", "genes")),
        ),
        check_vma=False,
    )
```

```python
import jax
import jax.numpy as jnp
from jax import lax
from jax.experimental import pallas as pl
from jax.experimental.pallas import tpu as pltpu
from jax.sharding import PartitionSpec as P

norm_epsilon = 0.001
zinb_epsilon = 1e-08
beta_one = 0.9
beta_two = 0.999
step_number = 5.0
decay_rate = 0.01
rate_genes = 0.03
rate_small = 0.2
max_norm = 0.1

F32 = jnp.float32
BF = jnp.bfloat16
HI = lax.Precision.HIGHEST
COUNT_TOP = 8
LOG2_E = 1.4426950408889634


def nn(left, right, precision=None):
    return lax.dot_general(
        left, right, (((1,), (0,)), ((), ())), precision=precision, preferred_element_type=F32
    )


def nt(left, right, precision=None):
    return lax.dot_general(
        left, right, (((1,), (1,)), ((), ())), precision=precision, preferred_element_type=F32
    )


def whole(shape):
    return pl.BlockSpec(shape, lambda *_: (0,) * len(shape))


def in_hbm(array):
    return pltpu.with_memory_space_constraint(array, pltpu.HBM)


def call(kernel, grid, ins, outs, scratch=(), scalars=0, us=2.0, mib=12):
    return pl.pallas_call(
        kernel,
        out_shape=[pltpu.HBM(out[0], out[1]) if len(out) == 4 else jax.ShapeDtypeStruct(out[0], out[1]) for out in outs],
        grid_spec=pltpu.PrefetchScalarGridSpec(
            num_scalar_prefetch=scalars,
            grid=grid,
            in_specs=[spec for _, spec in ins[scalars:]],
            out_specs=[out[2] for out in outs],
            scratch_shapes=list(scratch),
        ),
        compiler_params=pltpu.CompilerParams(vmem_limit_bytes=mib * 1024 * 1024),
        cost_estimate=pl.CostEstimate(flops=0, bytes_accessed=int(us * 3.69e6), transcendentals=0),
    )(*[array for array, _ in ins])


def swap(value, axis, bit):
    count = lax.axis_size(axis)
    return lax.ppermute(value, axis, [(i, i ^ bit) for i in range(count)])


def bit_groups(axis):
    count = lax.axis_size(axis)
    if axis == "genes":
        groups, bit = [[1]], 2
    else:
        groups, bit = [], 1
    while bit < count:
        groups.append([bit, 2 * bit] if 2 * bit < count else [bit])
        bit *= 4
    return groups


def total(value, axis, done=0):
    for group in bit_groups(axis)[done:]:
        if len(group) == 1:
            value = value + swap(value, axis, group[0])
        else:
            low, high = group
            value = (value + swap(value, axis, low)) + (
                swap(value, axis, high) + swap(value, axis, low ^ high)
            )
    return value


def log_total_of(value, axis):
    for group in bit_groups(axis):
        if len(group) == 1:
            parts = [value, swap(value, axis, group[0])]
        else:
            low, high = group
            parts = [value] + [swap(value, axis, k) for k in (low, high, low ^ high)]
        top = parts[0]
        for part in parts[1:]:
            top = jnp.maximum(top, part)
        mass = sum(jnp.exp(part - top) for part in parts)
        value = top + jnp.log(mass)
    return value


def total_by_halves(value, axis, order):
    for bit in order:
        value = value + swap(value, axis, bit)
    return value


def after(value, *others):
    return lax.optimization_barrier((value,) + others)[0]


def three(value):
    high = value.astype(BF)
    rest = value - high.astype(F32)
    mid = rest.astype(BF)
    low = (rest - mid.astype(F32)).astype(BF)
    return high, mid, low


def one_hot(batch_row, kinds):
    ids = lax.broadcasted_iota(jnp.int32, (kinds, batch_row.shape[1]), 0)
    return jnp.where(ids == batch_row, 1.0, 0.0)


def columns(rows):
    return jnp.transpose(rows)


def prep_kernel(gene_ref, mask_ref, dec_ref, small_ref, head_ref, norm_ref, aug_ref, turn_ref, par_ref, lg_ref, dg_ref, enc_out, dec_out, plain_out, lat_out, head_out, bias_out, cols_out, norm_out):
    genes = gene_ref.shape[1]
    hidden = norm_ref.shape[1]
    latent = head_ref.shape[0] // 2
    kinds = (small_ref.shape[0] - latent) // 2
    padded = pl.cdiv(genes, 128) * 128
    keep = mask_ref[...] > 0
    score_b = jnp.where(keep, gene_ref[0:1], -1e30)
    drop_b = jnp.where(keep, gene_ref[1:2], 1e30)
    th = jnp.exp(gene_ref[2:3])
    kept = jnp.where(keep, 1.0, 0.0)
    rows = jnp.concatenate((score_b, drop_b, th, kept, th, th, th, th), axis=0)
    if padded > genes:
        rows = jnp.concatenate((rows, jnp.ones((8, padded - genes), F32)), axis=1)
    turned = jnp.transpose(rows)[:genes]
    lane = lax.broadcasted_iota(jnp.int32, (genes, 16), 1)
    for half in range(2):
        at = slice(half * genes, (half + 1) * genes)
        aug_ref[at, 0:hidden] = dec_ref[half].astype(BF)
        high, mid, low = (jnp.broadcast_to(part.astype(F32), (genes, 16)) for part in three(turned[:, half : half + 1]))
        tail = jnp.where(lane == 0, high, jnp.where(lane == 1, mid, jnp.where(lane == 2, low, 0.0)))
        if half == 0:
            tail = jnp.where((lane >= 3) & (lane < 6), 1.0, tail)
        aug_ref[at, hidden : hidden + 16] = tail.astype(BF)
        turn_ref[:, at] = jnp.transpose(dec_ref[half]).astype(BF)
    th_w = jnp.broadcast_to(turned[:, 2:3], (genes, 128))
    keep_w = jnp.broadcast_to(turned[:, 3:4], (genes, 128))
    the_w = th_w + zinb_epsilon
    par_ref[0] = the_w
    par_ref[1] = th_w
    par_ref[2] = jnp.log(the_w)
    par_ref[3] = th_w / the_w
    par_ref[4] = keep_w
    gam = jnp.zeros_like(th_w)
    dig = jnp.zeros_like(th_w)
    for k in range(COUNT_TOP):
        more = th_w + float(k)
        gam = gam + keep_w * jnp.log(more * (1.0 / (1.0 + k)))
        dig = dig + keep_w / more
        lg_ref[k] = gam
        dg_ref[k] = dig
    for index, piece in enumerate(three(jnp.transpose(small_ref[0:kinds, :]))):
        enc_out[index * hidden : (index + 1) * hidden, :] = piece
    row = lax.broadcasted_iota(jnp.int32, (16, hidden), 0)
    lat_row = jnp.zeros((16, hidden), F32)
    for index in range(latent):
        lat_row = jnp.where(row == index, small_ref[2 * kinds + index : 2 * kinds + index + 1, :], lat_row)
    lat_out[...] = lat_row
    batch_turned, lat_turned = jnp.transpose(small_ref[kinds : 2 * kinds, :]), jnp.transpose(lat_row)
    plain_out[...] = jnp.concatenate((batch_turned, lat_turned), axis=1)
    batch_pieces = three(batch_turned)
    lat = three(lat_turned)
    zero = jnp.zeros_like(lat[0])
    tails = ((lat[0], lat[0], lat[0]), (lat[1], lat[1], zero), (lat[2], zero, zero))
    for index in range(3):
        at = slice(index * hidden, (index + 1) * hidden)
        dec_out[at, :] = jnp.concatenate((batch_pieces[index],) + tails[index], axis=1)
    full = lax.broadcasted_iota(jnp.int32, (32, hidden), 0)
    head = jnp.zeros((32, hidden), F32)
    bias = jnp.zeros((32, 1), F32)
    for index in range(2 * latent):
        to = index if index < latent else index - latent + 16
        head = jnp.where(full == to, head_ref[index : index + 1, 0:hidden], head)
        bias = jnp.where(full[:, 0:1] == to, head_ref[index : index + 1, hidden : hidden + 1], bias)
    head_out[...] = head
    bias_out[...] = jnp.broadcast_to(bias, (32, 128))
    high, mid, _ = three(jnp.transpose(head))
    cols_out[...] = jnp.concatenate((high, high, mid), axis=1)
    norm_out[...] = jnp.transpose(jnp.concatenate((norm_ref[...], norm_ref[...]), axis=0))


def exact_rows(stacked, table):
    out = nn(stacked, table)
    hidden = out.shape[0] // 3
    return out[:hidden] + out[hidden : 2 * hidden] + out[2 * hidden :]


def dec_table(z, batch_row, kinds):
    high, mid, low = three(z)
    return jnp.concatenate((one_hot(batch_row, kinds).astype(BF), high, mid, low), axis=0)


def row_sums(value):
    return nt(jnp.ones((8, value.shape[1]), F32), value, HI)


def stat_rows(first, second, at):
    sums, squares = row_sums(first), row_sums(second)
    row = lax.broadcasted_iota(jnp.int32, sums.shape, 0)
    return jnp.where(row == at, sums, jnp.where(row == at + 1, squares, 0.0))


def enc_kernel(low, count, share, near, me_ref, x_ref, w_ref, keep_ref, send_ref, weight_ref, turn_ref, arrived, *buffers):
    def at(i):
        return pl.ds(pl.multiple_of(((low + i) ^ me_ref[0]) * share, share), share)

    weight = pltpu.make_async_copy(w_ref, weight_ref, arrived.at[count])
    weight.start()
    if not near:
        (buffer_ref,) = buffers

        def block(i):
            return pltpu.make_async_copy(x_ref.at[:, at(i)], buffer_ref.at[i], arrived.at[i])

        for i in range(count):
            block(i).start()
    weight.wait()
    turn_ref[...] = jnp.transpose(weight_ref[...]).astype(BF)

    def pair(half, carry):
        for odd in range(2):
            i = 2 * half + odd
            if near:
                x = x_ref[:, at(i)]
            else:
                block(i).wait()
                x = buffer_ref[i]
            part = nn(turn_ref[...], jnp.log(1.0 + x.astype(F32)).astype(BF))
            if odd:
                send_ref[half] = part.astype(BF)
            else:
                keep_ref[half] = part
        return carry

    lax.fori_loop(0, count // 2, pair, 0)


def lines(rows8, count):
    wide = rows8.shape[1]
    if wide < 128 * count:
        rows8 = jnp.concatenate((rows8, jnp.zeros((8, 128 * count - wide), F32)), axis=1)
    return jnp.concatenate([rows8[:, i * 128 : (i + 1) * 128] for i in range(count)], axis=0)


def counts_kernel(rows, span, x_ref, lg_ref, dg_ref, par_ref, batch_ref, lib_ref, logc_ref, mask_ref, side_ref, lib_out, cell_ref, disp_ref, line_ref, held_ref):
    step = pl.program_id(0)
    genes, width = mask_ref.shape

    @pl.when(step == 0)
    def _():
        disp_ref[...] = jnp.zeros_like(disp_ref)
        held_ref[...] = jnp.zeros_like(held_ref)

    kinds = held_ref.shape[0]
    table = one_hot(batch_ref[0], kinds)
    held_ref[...] += sum(table[:, t : t + 128] for t in range(0, width, 128))
    row = lax.broadcasted_iota(jnp.int32, (16, width), 0)
    side_ref[0:kinds, part_of(step, width)] = table.astype(BF)
    side_ref[kinds:, part_of(step, width)] = jnp.where(row == 0, 1.0, 0.0).astype(BF)
    lib_out[...] = lib_ref[...]
    tiles = span // 128
    done = []
    for first in range(0, width, span):
        lanes = [slice(first + tile * 128, first + (tile + 1) * 128) for tile in range(tiles)]

        def chunk(g, cell):
            at = pl.ds(pl.multiple_of(g * rows, rows), rows)
            keep = par_ref[4, at, :].astype(BF)
            lows = [x_ref[at, lanes[tile]] for tile in range(tiles)]
            xs = [low.astype(F32) for low in lows]
            logs = [jnp.log(1.0 + x) for x in xs]
            for tile in range(tiles):
                logc_ref[at, lanes[tile]] = logs[tile].astype(BF)
                mask_ref[at, lanes[tile]] = lows[tile] * keep
            gams = [jnp.zeros_like(xs[0]) for _ in range(tiles)]
            digs = [jnp.zeros_like(xs[0]) for _ in range(tiles)]
            for k in range(COUNT_TOP):
                lg, dg = lg_ref[k, at, :], dg_ref[k, at, :]
                for tile in range(tiles):
                    more = xs[tile] > (k + 0.5)
                    gams[tile] = jnp.where(more, lg, gams[tile])
                    digs[tile] = jnp.where(more, dg, digs[tile])
            disp_ref[at, :] += sum(digs)
            out = []
            for tile in range(tiles):
                folded = cell[tile]
                for part in range(rows // 8):
                    folded = folded + gams[tile][part * 8 : (part + 1) * 8]
                out.append(folded)
            return tuple(out)

        zero = tuple(jnp.zeros((8, 128), F32) for _ in range(tiles))
        done += list(lax.fori_loop(0, genes // rows, chunk, zero))
    cell_ref[pl.ds(step, 1), :] = jnp.sum(jnp.concatenate(done, axis=1), axis=0, keepdims=True)

    @pl.when(step == pl.num_programs(0) - 1)
    def _():
        line_ref[...] = row_sums(held_ref[...])


def own_kernel(me_ref, keep_ref, got_ref, one_ref, two_ref, six_ref, batch_ref, enc_b_ref, pre_ref, stat_ref):
    kinds = enc_b_ref.shape[1]
    gathered = (keep_ref[0] + got_ref[0].astype(F32) + one_ref[0].astype(F32)) + (
        two_ref[0].astype(F32) + six_ref[0].astype(F32)
    )
    table = one_hot(batch_ref[0], kinds).astype(BF)
    pre = gathered + exact_rows(enc_b_ref[...], table)
    pre_ref[...] = pre
    stat_ref[...] = stat_rows(pre, pre * pre, 0)


def norm_columns(stat, first, cells):
    turned = jnp.transpose(stat)
    mean = turned[:, first : first + 1] / cells
    var = turned[:, first + 1 : first + 2] / cells - mean * mean
    return mean, lax.rsqrt(var + norm_epsilon)


def norm_rows(stat, first, cells):
    mean = stat[first : first + 1] / cells
    var = stat[first + 1 : first + 2] / cells - mean * mean
    return mean, lax.rsqrt(var + norm_epsilon)


def latent_kernel(cells, latent, me_ref, pre_ref, stat_ref, norm_ref, head_ref, bias_ref, noise_ref, batch_ref, dec_b_ref, pack_ref, aff_ref, kl_ref):
    kinds = dec_b_ref.shape[1] - 48
    hidden = pre_ref.shape[0]
    mean, inv = norm_columns(stat_ref[...], 0, cells)
    phat = (pre_ref[...] - mean) * inv
    affine = norm_ref[:, 0:1] * phat + norm_ref[:, 1:2]
    out = nn(head_ref[...], jnp.maximum(affine, 0.0), HI) + bias_ref[:, 0:1]
    lat_mean, lat_logvar = out[:latent], out[16 : 16 + latent]
    high, mid, _ = three(latent_rows(lat_logvar))
    aff_ref[...] = jnp.concatenate((affine.astype(BF), high, mid), axis=0)
    var = jnp.exp(lat_logvar) + 0.0001
    z = latent_rows(lat_mean + jnp.sqrt(var) * noise_ref[...])
    terms = var + lat_mean * lat_mean - 1.0 - jnp.log(var)
    kl_ref[...] = 0.5 * jnp.sum(terms, axis=0, keepdims=True)
    pre_dec = exact_rows(dec_b_ref[...], dec_table(z, batch_ref[0], kinds))
    stat = stat_rows(pre_dec, pre_dec * pre_dec, 0)
    pack_ref[...] = z
    pack_ref[latent : latent + 1, 0:hidden] = stat[0:1]
    pack_ref[latent + 1 : latent + 2, 0:hidden] = stat[1:2]


def latent_rows(z):
    if z.shape[0] == 16:
        return z
    return jnp.concatenate((z, jnp.zeros((16 - z.shape[0], z.shape[1]), F32)), axis=0)


def part_of(step, width):
    return pl.ds(pl.multiple_of(step * width, 128), width)


def relu_low(affine):
    return jnp.maximum(affine, jnp.zeros_like(affine))


def pick(step, me_ref, fast, near_ref, far_ref):
    if not fast:
        return near_ref[step]
    place = step ^ me_ref[0]
    return jnp.where(lax.rem(place, 2) == 0, near_ref[lax.div(place, 2)], far_ref[lax.div(place, 2)])


def decode_kernel(cells, latent, fast, me_ref, near_ref, far_ref, side_ref, stat_ref, norm_ref, plain_ref, w_ref, aff_ref, lse_ref, z_ref, top_ref, mass_ref, low_ref, score_ref, left_ref):
    kinds = plain_ref.shape[1] - 16
    step = pl.program_id(0)
    cells_at = part_of(step, score_ref.shape[1])
    genes = score_ref.shape[0]
    hidden_rows = aff_ref.shape[0]

    @pl.when(step == 0)
    def _():
        mean, inv = norm_columns(stat_ref[...], latent - 8, cells)
        scaled = norm_ref[:, 2:3] * inv
        weights = plain_ref[...] * scaled
        high, mid, _ = three(weights)
        lane = lax.broadcasted_iota(jnp.int32, (hidden_rows, 16), 1)
        shift = jnp.broadcast_to(norm_ref[:, 3:4] - scaled * mean, (hidden_rows, 16))
        one, two, rest = (part.astype(F32) for part in three(shift))
        tail = jnp.where(lane == 0, one, jnp.where(lane == 1, two, jnp.where(lane == 2, rest, 0.0))).astype(BF)
        zero = jnp.zeros_like(tail)
        left_ref[:hidden_rows, :] = jnp.concatenate((high, high[:, kinds:], tail), axis=1)
        left_ref[hidden_rows:, :] = jnp.concatenate((mid, zero, zero), axis=1)

    z = pick(step, me_ref, fast, near_ref, far_ref)
    z = jnp.where(lax.broadcasted_iota(jnp.int32, z.shape, 0) < latent, z, 0.0)
    z_ref[:, cells_at] = z
    z_high, z_mid, _ = three(z)
    ones = jnp.where(lax.broadcasted_iota(jnp.int32, z.shape, 0) < 3, 1.0, 0.0).astype(BF)
    table = jnp.concatenate((side_ref[0:kinds, cells_at], z_high, z_mid, ones), axis=0)
    both = nn(left_ref[...], table)
    affine = (both[:hidden_rows] + both[hidden_rows:]).astype(BF)
    aff_ref[:, cells_at] = affine
    hidden = relu_low(affine)
    width = score_ref.shape[1]
    score_ref[...] = nn(w_ref[0:genes, :], jnp.concatenate((hidden, ones), axis=0))
    tiles = width // 128
    rows = 32

    def top(g, best):
        at = pl.ds(pl.multiple_of(g * rows, rows), rows)
        new = []
        for tile in range(tiles):
            value = score_ref[at, slice(tile * 128, (tile + 1) * 128)]
            part = best[tile]
            for index in range(rows // 8):
                part = jnp.maximum(part, value[index * 8 : (index + 1) * 8])
            new.append(part)
        return tuple(new)

    best = lax.fori_loop(0, genes // rows, top, tuple(jnp.full((8, 128), -3e38, F32) for _ in range(tiles)), unroll=10)
    high = [jnp.max(part, axis=0, keepdims=True) for part in best]
    wide = [jnp.broadcast_to(part, (8, 128)) for part in high]

    far_lanes = [pl.ds(pl.multiple_of(step * width + tile * 128, 128), 128) for tile in range(tiles)]

    def mass(g, sums):
        at = pl.ds(pl.multiple_of(g * rows, rows), rows)
        new = []
        for tile in range(tiles):
            value = score_ref[at, slice(tile * 128, (tile + 1) * 128)]
            part = sums[tile]
            pieces = []
            for index in range(rows // 8):
                pieces.append(jnp.exp(value[index * 8 : (index + 1) * 8] - wide[tile]))
                part = part + pieces[-1]
            whole_piece = jnp.concatenate(pieces, axis=0)
            mass_ref[at, far_lanes[tile]] = whole_piece
            low_ref[at, far_lanes[tile]] = whole_piece.astype(BF)
            new.append(part)
        return tuple(new)

    sums = lax.fori_loop(0, genes // rows, mass, tuple(jnp.zeros((8, 128), F32) for _ in range(tiles)), unroll=10)
    top_ref[pl.ds(step, 1), :] = jnp.concatenate(high, axis=1)
    lse = [high[tile] + jnp.log(jnp.sum(sums[tile], axis=0, keepdims=True)) for tile in range(tiles)]
    lse_ref[pl.ds(step, 1), :] = jnp.concatenate(lse, axis=1)


def enc_sums_kernel(fast, me_ref, logc_ref, near_ref, far_ref, side_ref, line_ref, out_ref, sum_ref):
    step = pl.program_id(0)
    genes = logc_ref.shape[0]
    hidden = out_ref.shape[1]
    kinds = side_ref.shape[0] - 16

    @pl.when(step == 0)
    def _():
        out_ref[...] = jnp.zeros_like(out_ref)
        sum_ref[...] = jnp.zeros_like(sum_ref)

    cells_at = part_of(step, near_ref.shape[2])
    affine = pick(step, me_ref, fast, near_ref, far_ref)[:hidden]
    part = nt(logc_ref[:, cells_at], jnp.concatenate((affine, side_ref[kinds:, cells_at]), axis=0))
    out_ref[0:genes, :] += part[:, :hidden]
    sum_ref[...] += part[:, hidden:]
    out_ref[genes : genes + kinds, :] += nt(side_ref[0:kinds, cells_at], affine)

    @pl.when(step == pl.num_programs(0) - 1)
    def _():
        pick_first = jnp.where(lax.broadcasted_iota(jnp.int32, (8, 16), 1) == 0, 1.0, 0.0)
        base = genes + kinds
        count = pl.cdiv(genes, 128)
        out_ref[base : base + 8 * count, :] = lines(nt(pick_first, sum_ref[...], HI), count)
        out_ref[base + 8 * count :, :] = line_ref[...]


def zinb_kernel(rows, span, hid_ref, e_ref, top_ref, w_ref, x_ref, par_ref, lib_ref, lse_ref, gam_ref, g_ref, mass_ref, recon_ref, acc_ref, sc_ref):
    step = pl.program_id(0)
    genes, width = x_ref.shape

    @pl.when(step == 0)
    def _():
        acc_ref[...] = jnp.zeros_like(acc_ref)

    one_row = pl.ds(step, 1)
    gam_row = gam_ref[one_row, :]
    level = jnp.exp(top_ref[one_row, :] + (lib_ref[one_row, :] - lse_ref[one_row, :]))
    row = lax.broadcasted_iota(jnp.int32, (16, width), 0)
    ones = jnp.where(row < 3, 1.0, 0.0).astype(BF)
    sc_ref[...] = nn(w_ref[genes:, :], jnp.concatenate((relu_low(hid_ref[:, part_of(step, width)]), ones), axis=0))
    tiles = span // 128
    mass_out, recon_out = [], []
    for first in range(0, width, span):
        lanes = [slice(first + tile * 128, first + (tile + 1) * 128) for tile in range(tiles)]
        far_lanes = [pl.ds(pl.multiple_of(step * width + first + tile * 128, 128), 128) for tile in range(tiles)]
        scale = [jnp.broadcast_to(level[:, lanes[tile]], (rows, 128)) for tile in range(tiles)]

        def chunk(g, state):
            at = pl.ds(pl.multiple_of(g * rows, rows), rows)
            at_drop = pl.ds(pl.multiple_of(genes + g * rows, rows), rows)
            the, th, log_the, part_th = (par_ref[i, at, :] for i in range(4))
            sum_t = acc_ref[at, :]
            new = []
            for tile in range(tiles):
                rec, prod, back = state[tile]
                x = x_ref[at, lanes[tile]].astype(F32)
                mu = e_ref[at, far_lanes[tile]] * scale[tile]
                drop = sc_ref[at, lanes[tile]]
                both = mu + the
                r = 1.0 / both
                log_both = jnp.log(both)
                gap = log_the - log_both
                th_gap = th * gap
                u = jnp.where(x < 0.5, th_gap - drop, 1e30)
                eu = jnp.exp2(jnp.abs(u) * (-LOG2_E))
                ed = jnp.exp2(jnp.abs(drop) * (-LOG2_E))
                den = 1.0 + eu
                mu_eps = mu + zinb_epsilon
                rd = 1.0 / (1.0 + ed)
                w0 = jnp.where(u >= 0.0, 1.0, eu) * (1.0 / den)
                term = (th_gap - jnp.maximum(drop, 0.0)) + (x * (jnp.log(mu_eps) - log_both) - jnp.minimum(u, 0.0))
                factor = den * rd
                y = (x + w0 * th) * r
                g_mean = mu * (x * (1.0 / mu_eps) - y)
                g_drop = jnp.where(drop >= 0.0, ed, 1.0) * rd - w0
                g_disp = w0 * (gap + part_th) - y
                g_ref[at, far_lanes[tile]] = g_mean.astype(BF)
                g_ref[at_drop, far_lanes[tile]] = g_drop.astype(BF)
                sum_t = sum_t + g_disp
                for part in range(rows // 8):
                    sub = slice(part * 8, (part + 1) * 8)
                    rec = rec + term[sub]
                    prod = prod * factor[sub]
                    back = back + g_mean[sub]
                new.append((rec, prod, back))
            acc_ref[at, :] = sum_t
            return tuple(new)
        zero = jnp.zeros((8, 128), F32)
        state = tuple((zero, zero + 1.0, zero) for _ in range(tiles))
        state = lax.fori_loop(0, genes // rows, chunk, state)
        for tile in range(tiles):
            rec, prod, back = state[tile]
            mass_out.append(jnp.sum(back, axis=0, keepdims=True))
            recon_out.append(jnp.sum(rec + jnp.log(prod), axis=0, keepdims=True))
    mass_ref[one_row, :] = jnp.concatenate(mass_out, axis=1)
    recon_ref[one_row, :] = jnp.concatenate(recon_out, axis=1) + gam_row


def softmax_kernel(width, mass_ref, w_ref, side_ref, z_ref, aff_ref, r_ref, product_ref):
    genes = mass_ref.shape[0]
    step = pl.program_id(0)
    cells_at = part_of(step, width)

    @pl.when(step == 0)
    def _():
        product_ref[...] = jnp.zeros_like(product_ref)

    r_ref[:, cells_at] = nn(w_ref[:, :genes], mass_ref[:, cells_at])
    left = jnp.concatenate((side_ref[:, cells_at], z_ref[:, cells_at].astype(BF)), axis=0)
    product_ref[...] += nt(left, aff_ref[:, cells_at])


def back_kernel(width, g_in_ref, w_ref, a_ref):
    cells_at = part_of(pl.program_id(0), width)
    a_ref[:, cells_at] = nn(w_ref[...], g_in_ref[:, cells_at])


def hidden_grad_kernel(cells, latent, me_ref, a_ref, r_ref, mass_ref, aff_ref, top_ref, lse_ref, stat_ref, gain_ref, lat_ref, recon_ref, z_ref, side_ref, keep_ref, send_ref, lane_ref, oh_ref):
    step = pl.program_id(0)
    steps = pl.num_programs(0)
    place = step ^ me_ref[0]
    hidden, width = a_ref.shape[0], mass_ref.shape[1]
    cells_at = part_of(step, width)
    kinds = side_ref.shape[0] - 16

    @pl.when(step == 0)
    def _():
        lane_ref[...] = jnp.zeros_like(lane_ref)
        oh_ref[...] = jnp.zeros_like(oh_ref)

    line = pl.ds(step, 1)
    back = mass_ref[line, :] * jnp.exp(top_ref[line, :] - lse_ref[line, :])
    wide = aff_ref[:, cells_at].astype(F32)
    dy = jnp.where(wide > 0, a_ref[:, cells_at] - back * r_ref[:, cells_at], 0.0)
    weighted = dy * wide
    lane_ref[...] += sum(weighted[:, t : t + 128] for t in range(0, width, 128))
    dy_low = dy.astype(BF)
    oh_ref[...] += nt(jnp.concatenate((side_ref[:, cells_at], z_ref[:, cells_at].astype(BF)), axis=0), dy_low)
    _, inv = norm_rows(stat_ref[...], latent - 8, cells)
    lat_high, lat_mid, _ = three(lat_ref[...] * (gain_ref[2:3] * inv) * (-1.0 / cells))
    both = nn(jnp.concatenate((lat_high, lat_mid), axis=0), dy_low)
    block = both[:16] + both[16:]
    row = lax.broadcasted_iota(jnp.int32, block.shape, 0)
    block = jnp.where(row == latent, recon_ref[pl.ds(step, 1), :], block)
    slot = lax.div(place, 2)

    @pl.when(lax.rem(place, 2) == 0)
    def _():
        keep_ref[slot] = block

    @pl.when(lax.rem(place, 2) == 1)
    def _():
        send_ref[slot] = block

    @pl.when(step == steps - 1)
    def _():
        scale = -1.0 / cells
        one, two = oh_ref[kinds : kinds + 1, :] * scale, row_sums(lane_ref[...])[0:1] * scale
        oh_ref[kinds : kinds + 16, :] = oh_ref[kinds + 16 :, :]
        part = (kinds + 16) // steps
        for core, ref in enumerate((keep_ref, send_ref)):
            for index in range(ref.shape[0]):
                ref[index, latent + 1 : latent + 2, 0:hidden] = one
                ref[index, latent + 2 : latent + 3, 0:hidden] = two
                owner = me_ref[0] ^ (2 * index + core)
                for k in range(part):
                    line = latent + 3 + k // 8
                    lanes = slice((k % 8) * hidden, (k % 8 + 1) * hidden)
                    ref[index, line : line + 1, lanes] = oh_ref[pl.ds(owner * part + k, 1), :] * scale


def dec_grad_kernel(cells, rt_ref, hid_ref, mass_ref, top_ref, lse_ref, g_in_ref, acc_ref, dig_ref, par_ref, dec_ref, mix_ref, g_ref):
    step = pl.program_id(0)
    steps = pl.num_programs(0)
    genes = rt_ref.shape[0]
    cells_at = part_of(step, mass_ref.shape[1])
    hidden = hid_ref.shape[0]

    @pl.when(step == 0)
    def _():
        mix_ref[...] = jnp.zeros_like(mix_ref)
        g_ref[...] = jnp.zeros_like(g_ref)

    line = pl.ds(step, 1)
    back = mass_ref[line, :] * jnp.exp(top_ref[line, :] - lse_ref[line, :])
    back_high, back_mid, back_low = three(back)
    row = lax.broadcasted_iota(jnp.int32, (16, back.shape[1]), 0)
    extra = jnp.where(row == 0, back_high.astype(F32), jnp.where(row == 1, back_mid.astype(F32), 0.0))
    hidden_low = relu_low(hid_ref[:, cells_at])
    ones = jnp.where(row == 0, 1.0, 0.0).astype(BF)
    g_ref[...] += nt(g_in_ref[:, cells_at], jnp.concatenate((hidden_low, ones), axis=0))
    scaled = (hidden_low.astype(F32) * back).astype(BF)
    mix_ref[...] += nt(rt_ref[:, cells_at], jnp.concatenate((scaled, extra.astype(BF)), axis=0))

    @pl.when(step == steps - 1)
    def _():
        scale = -1.0 / cells
        mix = mix_ref[...]
        dec_ref[:genes, :] = (g_ref[:genes, :hidden] - mix[:, :hidden]) * scale
        dec_ref[genes : 2 * genes, :] = g_ref[genes:, :hidden] * scale
        pick = jnp.where(lax.broadcasted_iota(jnp.int32, (8, 16), 1) < 2, 1.0, 0.0)
        score_row = nt(pick, g_ref[:genes, hidden:] - mix[:, hidden:], HI)
        drop_row = nt(pick, g_ref[genes:, hidden:], HI)
        disp_row = row_sums((acc_ref[...] + dig_ref[...]) * par_ref[1])
        row = lax.broadcasted_iota(jnp.int32, score_row.shape, 0)
        gene_rows = scale * jnp.where(
            row == 0, score_row, jnp.where(row == 1, drop_row, jnp.where(row == 2, disp_row, 0.0))
        )
        dec_ref[2 * genes :, :] = lines(gene_rows, pl.cdiv(genes, 128))


def enc_back_kernel(cells, latent, fast, span, me_ref, own_ref, dnear_ref, dfar_ref, aff_dec_ref, sums_ref, stat_ref, gain_ref, lat_ref, noise_ref, klw_ref, anear_ref, afar_ref, side_ref, held_ref, product_ref, logc_ref, cols_ref, z_ref, out_ref, rest_ref, lane_ref, left_ref, fixed_ref, one_ref, kept_ref, sum_ref):
    step = pl.program_id(0)
    steps = kept_ref.shape[0]
    genes, width = logc_ref.shape[0], dnear_ref.shape[2]
    hidden = aff_dec_ref.shape[0]
    cells_at = part_of(step, width)
    place = (step ^ me_ref[0]) if fast else step
    kinds = (rest_ref.shape[0] - 64) // 2
    at = latent + 1 - 8
    m_one, m_two = norm_sums(sums_ref[at : at + 2], gain_ref, 2)
    m_two = m_two / gain_ref[2:3] * (1.0 / cells)
    m_one = m_one * (1.0 / cells) - m_two * gain_ref[3:4]

    @pl.when(step == 0)
    def _():
        out_ref[...] = jnp.zeros_like(out_ref)
        rest_ref[...] = jnp.zeros_like(rest_ref)
        lane_ref[...] = jnp.zeros_like(lane_ref)
        sum_ref[...] = jnp.zeros_like(sum_ref)
        _, inv = norm_rows(stat_ref[...], latent - 8, cells)
        lat = lat_ref[...] * (gain_ref[2:3] * inv)
        fixed_ref[...] = jnp.broadcast_to(jnp.sum(lat * m_one, axis=1, keepdims=True), fixed_ref.shape)
        high, mid, _ = three(lat * m_two)
        left_ref[...] = jnp.concatenate((high, mid), axis=0)

    index = lax.div(place, 2) if fast else place
    near = (lax.rem(place, 2) == 0) if fast else None

    def take(near_ref, far_ref, rows, lanes):
        if not fast:
            return near_ref[index, rows, lanes]
        return jnp.where(near, near_ref[index, rows, lanes], far_ref[index, rows, lanes])

    every = slice(0, width)
    scale = klw_ref[0:1, 0:1] * (1.0 / cells)
    affine_dec = aff_dec_ref[:, cells_at]
    both = nn(left_ref[...], affine_dec)
    block = take(dnear_ref, dfar_ref, slice(0, 16), every)
    kept_ref[step] = block[8:]
    grad_z = (block - fixed_ref[:, 0:1] - (both[:16] + both[16:]))[:latent]
    noise = noise_ref[:, cells_at]
    pieces = take(anear_ref, afar_ref, slice(hidden, hidden + 32), every).astype(F32)
    lat_logvar = pieces[:latent] + pieces[16 : 16 + latent]
    spread = jnp.exp(lat_logvar)
    var = spread + 0.0001
    inv_std = lax.rsqrt(var)
    z = z_ref[:, cells_at]
    lat_mean = z[0:latent] - var * inv_std * noise
    g_mean = latent_rows(grad_z + scale * lat_mean)
    g_var = latent_rows(spread * (grad_z * noise * (0.5 * inv_std) + (0.5 * scale) * (1.0 - inv_std * inv_std)))
    g_head = jnp.concatenate((g_mean, g_var), axis=0)
    sum_ref[0:32, :] += sum(g_head[:, t : t + 128] for t in range(0, width, 128))
    sum_ref[32:, :] += sum(z[:, t : t + 128] for t in range(0, width, 128))
    head_high, head_mid, _ = three(g_head)
    heads = jnp.concatenate((head_high, head_mid, head_high), axis=0)
    for begin in range(0, width, span):
        lanes = slice(begin, begin + span)
        affine = take(anear_ref, afar_ref, slice(0, hidden), lanes)
        one_ref[hidden:, lanes] = relu_low(affine)
        wide = affine.astype(F32)
        dy = jnp.where(wide > 0, nn(cols_ref[...], heads[:, lanes]), 0.0)
        one_ref[0:hidden, lanes] = dy.astype(BF)
        weighted = dy * wide
        lane_ref[...] += sum(weighted[:, t : t + 128] for t in range(0, span, 128))
    dy_low = one_ref[0:hidden, :]
    side = side_ref[:, cells_at]
    out_ref[0:genes, :] += nt(logc_ref[:, cells_at], dy_low)
    mixed = nt(side, dy_low)
    rest_ref[0:kinds, :] += mixed[:kinds]
    out_ref[genes : genes + 1, :] += mixed[kinds : kinds + 1]
    rest_ref[kinds : kinds + 32, :] += nt(head_high, one_ref[hidden:, :])
    base = kinds + 40

    @pl.when(step == steps - 1)
    def _():
        out_ref[genes + 1 : genes + 2, :] = row_sums(lane_ref[...])[0:1]
        rest_ref[kinds + 32 : kinds + 40, 0:32] = row_sums(sum_ref[0:32, :])
        held = jnp.concatenate((held_ref[...], sum_ref[32:, :]), axis=0)
        rest_ref[base : base + kinds + 16, :] -= jnp.sum(held, axis=1, keepdims=True) * m_one
        rest_ref[base : base + kinds, :] -= product_ref[:kinds, :] * m_two
        rest_ref[base + kinds : base + kinds + 16, :] -= product_ref[kinds + 16 :, :] * m_two
        count = (kinds + 16) // steps
        for owner in range(steps):
            for k in range(count):
                line = latent + 3 + k // 8 - 8
                at = slice(base + owner * count + k, base + owner * count + k + 1)
                rest_ref[at, :] += kept_ref[owner, line : line + 1, (k % 8) * hidden : (k % 8 + 1) * hidden]
        size = rest_ref.shape[0] // 8
        out_ref[genes + 8 :, :] = rest_ref[pl.ds(pl.multiple_of((own_ref[0] & 7) * size, 8), size), :]


def whole_gradient(part, product, plain, gain, shift, inv, one, two):
    return (gain * inv) * (part - plain * one - ((product - plain * shift) / gain) * two)


def norm_sums(rows, norm_ref, at):
    return rows[0:1], (rows[1:2] - norm_ref[at + 1 : at + 2] * rows[0:1]) / norm_ref[at : at + 1]


def finish_kernel(cells, latent, sum_ref, dec_ref, fixed_ref, stat_enc_ref, norm_ref, kl_ref, klw_ref, own_ref, enc_out, tail_out, loss_out):
    genes = enc_out.shape[0]
    size = tail_out.shape[0] - 8
    count = pl.cdiv(genes, 128)
    kinds = fixed_ref.shape[0] - genes - 8 * count - 8
    loss_out[...] = klw_ref[0:1, 0:1] * kl_ref[...] - own_ref[latent : latent + 1, :]
    _, inv = norm_rows(stat_enc_ref[...], 0, cells)
    n_one, n_two = norm_sums(sum_ref[genes : genes + 8, :], norm_ref, 0)
    at = genes + kinds
    logs = jnp.concatenate([fixed_ref[at + 8 * i : at + 8 * (i + 1), :] for i in range(count)], axis=1)
    log_sum = jnp.transpose(logs)[:genes, 0:1]
    enc = whole_gradient(
        sum_ref[0:genes, :], fixed_ref[0:genes, :], log_sum, norm_ref[0:1], norm_ref[1:2], inv, n_one * (1.0 / cells), n_two * (1.0 / cells)
    )
    enc_out[...] = enc
    dec = dec_ref[...]
    lane = jnp.sum(enc * enc, axis=0, keepdims=True) + jnp.sum(dec * dec, axis=0, keepdims=True)
    tail_out[0:size, :] = sum_ref[genes + 8 :, :]
    tail_out[size:, :] = jnp.broadcast_to(jnp.sum(lane, axis=1, keepdims=True), (8, tail_out.shape[1]))


def step_of(weight, gradient, first, second, rate):
    first = beta_one * first + (1.0 - beta_one) * gradient
    second = beta_two * second + (1.0 - beta_two) * gradient * gradient
    fixed_one = first * (1.0 / (1.0 - beta_one**step_number))
    fixed_two = second * (1.0 / (1.0 - beta_two**step_number))
    update = fixed_one / (jnp.sqrt(fixed_two) + 1e-08) + decay_rate * weight
    return weight - rate * update, first, second


def update_kernel(cells, latent, me_ref, near_ref, far_ref, enc_g_ref, dec_g_ref, sum_ref, fixed_ref, stat_enc_ref, stat_dec_ref, sums_ref, *refs):
    ins, outs, (rest_ref, small_g_ref, head_g_ref, norm_g_ref) = refs[:18], refs[18:-4], refs[-4:]
    enc, dec, gene, small, head, norm = (ins[3 * i : 3 * i + 3] for i in range(6))
    genes, hidden = enc[0].shape
    rows = small[0].shape[0]
    kinds = (rows - latent) // 2
    count = pl.cdiv(genes, 128)
    size = near_ref.shape[1]
    for core, ref in enumerate((near_ref, far_ref)):
        for index in range(ref.shape[0]):
            owner = me_ref[0] ^ (2 * index + core)
            rest_ref[pl.ds(pl.multiple_of(owner * size, 8), size), :] = ref[index]
    whole_rest = [rest_ref[i * size : i * size + size - 8, :] for i in range(8)]
    square = jnp.zeros((1, 1), F32)
    for i in range(8):
        square = square + rest_ref[(i + 1) * size - 8 : (i + 1) * size - 7, 0:1]
    rest = jnp.concatenate(whole_rest, axis=0)
    gains = norm[0]
    gain, shift = gains[0:1], gains[1:2]
    n_one, n_two = norm_sums(sum_ref[genes : genes + 8, :], gains, 0)
    _, inv = norm_rows(stat_enc_ref[...], 0, cells)
    _, inv_dec = norm_rows(stat_dec_ref[...], latent - 8, cells)
    at = genes + kinds + 8 * count
    batch_sum = jnp.transpose(fixed_ref[at : at + 8, :])[:kinds, 0:1]
    small_g_ref[0:kinds, :] = whole_gradient(
        rest[0:kinds], fixed_ref[genes : genes + kinds, :], batch_sum, gain, shift, inv, n_one * (1.0 / cells), n_two * (1.0 / cells)
    )
    small_g_ref[kinds:, :] = (gains[2:3] * inv_dec) * rest[kinds + 40 : 2 * kinds + 56]
    bias = jnp.transpose(rest[kinds + 32 : kinds + 40])
    for half in range(2):
        into = slice(half * latent, (half + 1) * latent)
        head_g_ref[into, 0:hidden] = rest[kinds + 16 * half : kinds + 16 * half + latent]
        head_g_ref[into, hidden : hidden + 1] = bias[16 * half : 16 * half + latent, 0:1]
    at = latent + 1 - 8
    norm_g_ref[0:1] = n_two
    norm_g_ref[1:2] = n_one
    m_one, m_two = norm_sums(sums_ref[at : at + 2], gains, 2)
    norm_g_ref[2:3] = m_two
    norm_g_ref[3:4] = m_one
    small_square = jnp.zeros((1, 1), F32)
    for part in (small_g_ref[0:rows, :], head_g_ref[...], norm_g_ref[...]):
        small_square = small_square + jnp.sum(jnp.sum(part * part, axis=0, keepdims=True), axis=1, keepdims=True)
    value = jnp.sqrt(square + small_square)
    factor = jnp.minimum(1.0, max_norm / value)
    (enc_n, enc_m, enc_v, enc_l, dec_n, dec_m, dec_v, dec_l, gene_n, gene_m, gene_v, small_n, small_m, small_v, head_n, head_m, head_v, norm_n, norm_m, norm_v, norm_out) = outs
    norm_out[...] = value
    new, first, second = step_of(enc[0][...], enc_g_ref[...] * factor, enc[1][...], enc[2][...], rate_genes)
    enc_n[...], enc_m[...], enc_v[...], enc_l[...] = new, first, second, new.astype(BF)
    for index in range(2):
        gradient = dec_g_ref[index * genes : (index + 1) * genes, :] * factor
        new, first, second = step_of(dec[0][index], gradient, dec[1][index], dec[2][index], rate_genes)
        dec_n[index], dec_m[index], dec_v[index], dec_l[index] = new, first, second, new.astype(BF)
    for index in range(pl.cdiv(genes, 128)):
        span = slice(index * 128, min(genes, (index + 1) * 128))
        gradient = dec_g_ref[2 * genes + index * 8 : 2 * genes + index * 8 + 3, 0 : span.stop - span.start] * factor
        new, first, second = step_of(gene[0][:, span], gradient, gene[1][:, span], gene[2][:, span], rate_small)
        gene_n[:, span], gene_m[:, span], gene_v[:, span] = new, first, second
    new, first, second = step_of(small[0][...], small_g_ref[0:rows, :] * factor, small[1][...], small[2][...], rate_small)
    small_n[...], small_m[...], small_v[...] = new, first, second
    new, first, second = step_of(head[0][...], head_g_ref[...] * factor, head[1][...], head[2][...], rate_small)
    head_n[...], head_m[...], head_v[...] = new, first, second
    new, first, second = step_of(norm[0][...], norm_g_ref[...] * factor, norm[1][...], norm[2][...], rate_small)
    norm_n[...], norm_m[...], norm_v[...] = new, first, second


def gather_genes(value, fast, blocks, width, late=None):
    if fast:
        near = jnp.stack([value] + [swap(value, "genes", 2 * k) for k in (1, 2, 3)])
        near = near if late is None else after(near, late)
        return near, swap(near, "genes", 1)
    rows = value.shape[0]
    whole_rows = lax.all_gather(value, "genes", axis=0).transpose(1, 0, 2)
    near = whole_rows.reshape(rows, blocks, width).transpose(1, 0, 2)
    return near, near


def per_device(counts, library, noise, batch_ids, gene_mask, kl_weight, enc_w, enc_m, enc_v, dec_w, dec_m, dec_v, gene_par, gene_m, gene_v, small_w, small_m, small_v, head_w, head_m, head_v, norm_par, norm_m, norm_v):
    rows_all, genes = counts.shape
    cells = float(rows_all * lax.axis_size("cells"))
    groups = lax.axis_size("genes")
    hidden = enc_w.shape[1]
    latent = head_w.shape[1] // 2
    kinds = (small_w.shape[0] - latent) // 2
    share = rows_all // groups
    width = min(1024, rows_all)
    blocks = rows_all // width
    fast = groups == 8 and blocks == 8
    me = lax.axis_index("genes").astype(jnp.int32).reshape(1)
    gene_lines = -(-genes // 128)

    def turn(value):
        return value.transpose(0, 2, 1)

    x_t = counts.T
    noise_t = noise.T
    dec_t = turn(dec_w)
    head_t = head_w.T
    lib8 = library.reshape(blocks, width)
    batch_all = batch_ids.reshape(blocks, 1, width)
    batch_own = batch_ids.reshape(groups, 1, share)
    klw = jnp.broadcast_to(kl_weight.reshape(1, 1), (8, 128))

    own_block = pl.BlockSpec((1, 1, share), lambda i, m: (m[0], 0, 0))
    own_lanes = lambda rows: pl.BlockSpec((rows, share), lambda i, m: (0, m[0]))
    lane_block = lambda rows: pl.BlockSpec((rows, width), lambda i, *_: (0, i))
    here = pl.BlockSpec(memory_space=pltpu.VMEM)
    full = lambda array: (array, here)
    out_of = lambda shape, dtype=F32: (shape, dtype, whole(shape))
    new = lambda shape, dtype=F32: (shape, dtype, here)

    def encode(low, count, weight, near=False):
        return call(
            lambda *refs: enc_kernel(low, count, share, near, *refs),
            (1,),
            [
                (me if fast else me & 1, None),
                (x_t, here) if near else (in_hbm(x_t), pl.BlockSpec(memory_space=pl.ANY)),
                (in_hbm(weight), pl.BlockSpec(memory_space=pl.ANY)),
            ],
            [new((count // 2, hidden, share)), new((count // 2, hidden, share), BF)],
            scratch=[
                pltpu.VMEM((genes, hidden), F32),
                pltpu.VMEM((hidden, genes), BF),
                pltpu.SemaphoreType.DMA((count + 1,)),
            ]
            + ([] if near else [pltpu.VMEM((count, genes, share), BF)]),
            scalars=1,
            us=2.0 if near else 3.0,
            mib=6 if near else 8,
        )

    slot = pl.BlockSpec((1, hidden, share), lambda i, m: (0, 0, 0))
    if fast:
        keep_far, send_far = encode(4, 4, enc_w)
        got_far = swap(send_far, "genes", 1)
        keep_near, send_near = encode(0, 4, after(enc_w, send_far), True)
        far = [
            swap((keep_far[k : k + 1] + got_far[k : k + 1].astype(F32)).astype(BF), "genes", 4 + 2 * k)
            for k in range(2)
        ]
        got = swap(send_near, "genes", 1)
        ready = (keep_near[1:2] + got[1:2].astype(F32)).astype(BF)
        far.append(swap(ready, "genes", 2))
        kept = keep_near
    else:
        keep_part, send_part = encode(0, groups, enc_w)
        got = swap(send_part, "genes", 1)
        summed = lax.psum_scatter(
            keep_part + got.astype(F32),
            "genes",
            scatter_dimension=0,
            axis_index_groups=[list(range(c, groups, 2)) for c in range(2)],
            tiled=True,
        )
        zero = jnp.zeros((1, hidden, share), BF)
        kept, got, far = summed, zero, [zero] * 3
        ready = keep_part

    mask_late = after(gene_mask.reshape(1, genes), ready)
    aug, dec_n, par, lg_tab, dg_tab, enc_pieces, dec_pieces, dec_plain, lat_row, head_rows, head_bias, head_cols, norm_t = call(
        prep_kernel,
        (1,),
        [full(gene_par), full(mask_late), full(dec_t), full(small_w), full(head_t), full(norm_par)],
        [
            new((2 * genes, hidden + 16), BF),
            new((hidden, 2 * genes), BF),
            new((5, genes, 128)),
            new((COUNT_TOP, genes, 128)),
            new((COUNT_TOP, genes, 128)),
            new((3 * hidden, kinds), BF),
            new((3 * hidden, kinds + 48), BF),
            new((hidden, kinds + 16)),
            new((16, hidden)),
            new((32, hidden)),
            new((32, 128)),
            new((hidden, 96), BF),
            new((hidden, 8)),
        ],
    )
    batch_spec = pl.BlockSpec((1, 1, width), lambda i, *_: (i, 0, 0))
    logc, x_kept, side, lib8, gam_cell, dig_acc, log_lines, held = call(
        lambda *refs: counts_kernel(16, min(512, width), *refs),
        (blocks,),
        [
            (in_hbm(x_t), lane_block(genes)),
            full(lg_tab),
            full(dg_tab),
            full(par),
            (batch_all, batch_spec),
            full(lib8),
        ],
        [
            ((genes, rows_all), BF, lane_block(genes), True),
            ((genes, rows_all), BF, lane_block(genes), True),
            ((kinds + 16, rows_all), BF, here),
            new((blocks, width)),
            new((blocks, width)),
            new((genes, 128)),
            new((8, 128)),
            new((kinds, 128)),
        ],
        mib=8,
        us=15.0,
    )
    enc_late = after(enc_pieces, log_lines)
    stat8 = whole((8, hidden))
    pre_enc, stat_enc = call(
        own_kernel,
        (1,),
        [(me, None), (kept, slot), (got, slot)]
        + [(part, slot) for part in far]
        + [(batch_own, own_block), full(enc_late)],
        [new((hidden, share)), new((8, hidden))],
        scalars=1,
    )
    stat_enc = total(total(stat_enc, "genes"), "cells")

    pack, aff_own, kl_row = call(
        lambda *refs: latent_kernel(cells, latent, *refs),
        (1,),
        [
            (me, None),
            full(pre_enc),
            full(stat_enc),
            full(norm_t),
            full(head_rows),
            full(head_bias),
            (noise_t, own_lanes(latent)),
            (batch_own, own_block),
            full(dec_pieces),
        ],
        [new((16, share)), new((hidden + 32, share), BF), new((1, share))],
        scalars=1,
    )
    near, far_pack = gather_genes(pack, fast, blocks, width)
    if fast:
        stat_dec = jnp.sum(near[:, 8:16, :hidden], axis=0) + jnp.sum(far_pack[:, 8:16, :hidden], axis=0)
    else:
        stat_dec = lax.psum(pack[8:16, :hidden], "genes")
    stat_dec = total(stat_dec, "cells")

    aff_dec, lse, z_all, top, mass_all, mass_low_all = call(
        lambda *refs: decode_kernel(cells, latent, fast, *refs),
        (blocks,),
        [
            (me, None),
            (near, here),
            (far_pack, here),
            (side, here),
            full(stat_dec),
            full(norm_t),
            full(dec_plain),
            full(aug),
        ],
        [
            ((hidden, rows_all), BF, here),
            new((blocks, width)),
            ((16, rows_all), F32, here),
            new((blocks, width)),
            ((genes, rows_all), F32, here),
            ((genes, rows_all), BF, here),
        ],
        scratch=[pltpu.VMEM((genes, width), F32), pltpu.VMEM((2 * hidden, kinds + 48), BF)],
        scalars=1,
        us=8.0,
    )
    part_r, product = call(
        lambda *refs: softmax_kernel(width, *refs),
        (blocks,),
        [(mass_low_all, here), full(dec_n), (side, here), (z_all, here), (aff_dec, here)],
        [((hidden, rows_all), F32, here), new((kinds + 32, hidden))],
        us=3.0,
    )
    lse_all = after(log_total_of(lse, "genes"), part_r)

    full8 = whole((blocks, width))
    g_both, mass, recon, gene_acc = call(
        lambda *refs: zinb_kernel(64, min(1024, width), *refs),
        (blocks,),
        [
            (aff_dec, here),
            (mass_all, here),
            full(top),
            full(aug),
            (in_hbm(x_kept), lane_block(genes)),
            full(par),
            full(lib8),
            full(lse_all),
            full(gam_cell),
        ],
        [((2 * genes, rows_all), BF, here)]
        + [new((blocks, width)), new((blocks, width)), new((genes, 128))],
        scratch=[pltpu.VMEM((genes, width), F32)],
        mib=16,
        us=28.0,
    )
    mass_low = mass + swap(mass, "genes", 1)
    mass = total(mass_low, "genes", 1)
    (part_a,) = call(
        lambda *refs: back_kernel(width, *refs),
        (blocks,),
        [(g_both, here), full(dec_n)],
        [((hidden, rows_all), F32, here)],
        us=4.0,
    )

    aff_near, aff_far = gather_genes(after(aff_own, lse_all), fast, blocks, width, mass_low)
    fixed_rows = genes + kinds + 8 * gene_lines + 8
    (fixed,) = call(
        lambda *refs: enc_sums_kernel(fast, *refs),
        (blocks,),
        [
            (me, None),
            (logc, here),
            (aff_near, here),
            (aff_far, here),
            (side, here),
            full(log_lines),
        ],
        [new((fixed_rows, hidden))],
        scratch=[pltpu.VMEM((genes, 16), F32)],
        scalars=1,
        us=4.0,
    )
    fixed = total_by_halves(fixed, "cells", (1, 2))

    keep_d, send_d = call(
        lambda *refs: hidden_grad_kernel(cells, latent, *refs),
        (blocks,),
        [
            (me if fast else jnp.zeros_like(me), None),
            (part_a, here),
            (part_r, here),
            (mass, here),
            (aff_dec, here),
            full(top),
            full(lse_all),
            full(stat_dec),
            full(norm_par),
            full(lat_row),
            full(recon),
            (z_all, here),
            (side, here),
        ],
        [
            new((blocks // 2, 16, width)),
            new((blocks // 2, 16, width)),
        ],
        scratch=[pltpu.VMEM((hidden, 128), F32), pltpu.VMEM((kinds + 32, hidden), F32)],
        scalars=1,
        us=5.0,
    )
    (dec_part,) = call(
        lambda *refs: dec_grad_kernel(cells, *refs),
        (blocks,),
        [
            (mass_low_all, here),
            (aff_dec, here),
            (mass, here),
            full(top),
            full(lse_all),
            (g_both, here),
            full(gene_acc),
            full(dig_acc),
            full(par),
        ],
        [new((2 * genes + 8 * gene_lines, hidden))],
        scratch=[pltpu.VMEM((genes, hidden + 16), F32), pltpu.VMEM((2 * genes, hidden + 16), F32)],
        us=6.0,
    )
    if fast:
        got_d = swap(send_d, "genes", 1)
        pieces = [swap(keep_d[k] + got_d[k], "genes", 2 * k) for k in (1, 2, 3)]
        pieces = [after(piece, dec_part) for piece in pieces]
        own_d = (keep_d[0] + got_d[0] + pieces[0]) + (pieces[1] + pieces[2])
        sums_dec = own_d[8:, :hidden]
    else:
        both = jnp.stack([keep_d, send_d], axis=1).reshape(blocks, 16, width)
        sums_dec = lax.psum(both[0, 8:, :hidden], "genes")
        both = both.transpose(1, 0, 2).reshape(16, groups, share).transpose(1, 0, 2)
        own_d = lax.psum_scatter(both, "genes", scatter_dimension=0, tiled=True)[0]
    sums_dec = total(sums_dec, "cells")
    d_near, d_far = gather_genes(own_d, fast, blocks, width)
    dec_g = total_by_halves(dec_part, "cells", (2, 1))

    size = (2 * kinds + 64) // 8
    (enc_part,) = call(
        lambda *refs: enc_back_kernel(cells, latent, fast, min(256, width), *refs),
        (blocks,),
        [
            (me, None),
            (me, None),
            (d_near, here),
            (d_far, here),
            (aff_dec, here),
            full(sums_dec),
            full(stat_dec),
            full(norm_par),
            full(lat_row),
            (noise_t, here),
            full(klw),
            (aff_near, here),
            (aff_far, here),
            (side, here),
            full(held),
            full(product),
            (logc, here),
            full(head_cols),
            (z_all, here),
        ],
        [new((genes + 8 + size, hidden))],
        scratch=[
            pltpu.VMEM((2 * kinds + 64, hidden), F32),
            pltpu.VMEM((hidden, 128), F32),
            pltpu.VMEM((32, hidden), BF),
            pltpu.VMEM((16, 128), F32),
            pltpu.VMEM((2 * hidden, width), BF),
            pltpu.VMEM((blocks, 8, width), F32),
            pltpu.VMEM((48, 128), F32),
        ],
        scalars=2,
        us=11.0,
    )
    enc_sum = total_by_halves(enc_part, "cells", (1, 2))
    enc_g, tail, loss = call(
        lambda *refs: finish_kernel(cells, latent, *refs),
        (1,),
        [full(a) for a in (enc_sum, dec_g, fixed, stat_enc, norm_par, kl_row, klw, own_d)],
        [new((genes, hidden)), new((size + 8, hidden)), new((1, share))],
    )
    if fast:
        tail_near = jnp.stack([tail] + [swap(tail, "genes", 2 * k) for k in (1, 2, 3)])
        tail_far = swap(tail_near, "genes", 1)
    else:
        tails = lax.all_gather(tail, "genes", axis=0)
        square = jnp.sum(tails[:, size:], axis=0)
        tails = tails[:8].at[:, size:].set(0.0).at[0, size:].set(square)
        tail_near, tail_far = tails[0::2], tails[1::2]

    state = [
        enc_w, enc_m, enc_v, dec_t, turn(dec_m), turn(dec_v), gene_par, gene_m, gene_v,
        small_w, small_m, small_v, head_t, head_m.T, head_v.T, norm_par, norm_m, norm_v,
    ]
    ins = [tail_near, tail_far, enc_g, dec_g, enc_sum, fixed, stat_enc, stat_dec, sums_dec] + state
    outs = []
    for index in range(6):
        one = state[3 * index]
        outs += [(one.shape, F32)] * 3
        if index < 2:
            outs.append((one.shape, BF))
    outs.append(((1, 1), F32))
    res = call(
        lambda *refs: update_kernel(cells, latent, *refs),
        (1,),
        [(me if fast else jnp.zeros_like(me), None)] + [full(array) for array in ins],
        [out_of(shape, dtype) for shape, dtype in outs],
        scratch=[
            pltpu.VMEM((8 * (size + 8), hidden), F32),
            pltpu.VMEM((2 * kinds + 16, hidden), F32),
            pltpu.VMEM((2 * latent, hidden + 1), F32),
            pltpu.VMEM((4, hidden), F32),
        ],
        scalars=1,
        mib=16,
    )
    enc_res, dec_res = res[0:4], [turn(part) for part in res[4:8]]
    head_res = [part.T for part in res[14:17]]
    return (
        *enc_res,
        *dec_res,
        *res[8:14],
        *head_res,
        *res[17:20],
        res[20].reshape(()),
        loss.reshape(share),
    )


def solution(mesh):
    placed = (
        P("cells", "genes"), P("cells"), P("cells", None), P("cells"), P("genes"), P(),
        P("genes", None), P("genes", None), P("genes", None),
        P(None, None, "genes"), P(None, None, "genes"), P(None, None, "genes"),
        P(None, "genes"), P(None, "genes"), P(None, "genes"),
        P(), P(), P(), P(), P(), P(), P(), P(), P(),
    )
    return jax.shard_map(
        per_device,
        mesh=mesh,
        in_specs=placed,
        out_specs=(
            P("genes", None), P("genes", None), P("genes", None), P("genes", None),
            P(None, None, "genes"), P(None, None, "genes"), P(None, None, "genes"), P(None, None, "genes"),
            P(None, "genes"), P(None, "genes"), P(None, "genes"),
            P(), P(), P(), P(), P(), P(), P(), P(), P(), P(),
            P(("cells", "genes")),
        ),
        check_vma=False,
    )
```
